32 devices in a mesh: section: 2 (over core), dp: 4 (over z), seq: 4 (over y, x).
Axes of the slice: x: 2, y: 2, z: 4, core: 2. Of those that a mesh axis runs over, the one named last changes fastest.
Arguments:
- ends: bfloat16 [2, 2, 4, 1024, 1024], P('section', None, 'dp', 'seq'), may hold values from -6 to 6
- mixer_input_weight: bfloat16 [2, 1024, 3072], P('section', 'dp'), may hold values from -0.1875 to 0.1875
- forget_first_map: bfloat16 [2, 1024, 16], P('section', 'dp'), may hold values from -0.1875 to 0.1875
- forget_second_map: bfloat16 [2, 16, 512], P('section'), may hold values from -1.5 to 1.5
- forget_logit_bias: float32 [2, 512], P('section'), may hold values from -2 to 6
- mixer_output_weight: bfloat16 [2, 1024, 1024], P('section', 'dp'), may hold values from -0.1875 to 0.1875
- feedforward_input_weight: bfloat16 [2, 1024, 5632], P('section', 'dp'), may hold values from -0.1875 to 0.1875
- feedforward_output_weight: bfloat16 [2, 2816, 1024], P('section', 'dp'), may hold values from -0.109375 to 0.109375
- adapter_model_first: bfloat16 [2, 1024, 768], P('section'), may hold values from -0.1875 to 0.1875
- adapter_hidden_first: bfloat16 [2, 3840, 128], P('section'), may hold values from -0.125 to 0.125
- adapter_second_maps: bfloat16 [2, 128, 10752], P('section'), may hold values from -0.75 to 0.75
- lengths: int32 [2, 4], P(None, 'dp'), may hold values from 256 to 1024, as said below
- dealt_block_order: int32 [2, 4, 16], P(None, 'dp'), may hold values from 0 to 15, each once within a row
- adapter_choice_per_seq: int32 [2, 4], P(None, 'dp'), may hold values from 0 to 7
Outputs:
- results: bfloat16 [2, 2, 4, 1024, 1024], P('section', None, 'dp', 'seq')
- grad_lora_model: float32 [2, 1024, 768], P('section', None, ('dp', 'seq'))
- grad_lora_hidden: float32 [2, 3840, 128], P('section', None, ('dp', 'seq'))
- grad_lora_up: float32 [2, 128, 10752], P('section', None, ('dp', 'seq'))
The draws below stay inside these ranges and needn't reach their ends.
Inputs may be any that keep to these rules, and one draw needn't show every extreme that they name: `lengths`: in every micro-batch some sequence has 1024 live positions. `dealt_block_order`: each row is a permutation of the block numbers.
All inputs are finite; a program needn't handle non-finite values.
Results may differ from the reference program's by a relative error of at most 0.025.
Values may be sent and summed in bfloat16 or wider, within the bound.
A program may use at most 384 MiB of HBM per device.

```python
import jax
import jax.numpy as jnp
from jax import lax

MODEL_WIDTH = 1024
HEADS = 4
KEY = 512
VALUE_WIDTH = 1024
HIDDEN_UNITS = 2816
FGATE_RANK = 16
GROUP = 64
ADAPTER_RANK = 16
ADAPTERS = 8
MICRO = 2
SEQ_LEN = 1024
SEQS_MB = 4
GROUPS = 16
ADAPTER_COLUMNS = 128
RAISED_COLUMNS = 10752


def draw_lengths(key, part):
    key = jax.random.fold_in(key, 5)
    first_key, second_key, third_key = jax.random.split(key, 3)
    shorter = jax.random.randint(first_key, (MICRO, SEQS_MB), SEQ_LEN // 4, SEQ_LEN + 1)
    whole = jax.random.randint(second_key, (MICRO, SEQS_MB), 0, 4) > 0
    picked = jax.random.randint(third_key, (MICRO,), 0, SEQS_MB)
    forced = jnp.arange(SEQS_MB)[None, :] == picked[:, None]
    return jnp.where(whole | forced, SEQ_LEN, shorter).astype(jnp.int32)


def touch_ends(result, stream_key, smallest, high):
    shape = result.shape
    spot = [jax.random.randint(jax.random.fold_in(stream_key, axis), (), 0, shape[axis]) for axis in range(len(shape))]
    result = result.at[tuple(spot)].set(smallest)
    longest = shape.index(max(shape))
    spot[longest] = (spot[longest] + 1) % shape[longest]
    return result.at[tuple(spot)].set(high)


def levels(key, extent, cuts, least, high):
    loudness, own = 1.0, jax.random.fold_in(key, 6)
    for axis_at, shards_of in cuts:
        heights = jnp.exp(jax.random.uniform(jax.random.fold_in(own, axis_at), (shards_of,), jnp.float32, least / len(cuts), high / len(cuts)))
        loudness = loudness * jnp.repeat(heights, extent[axis_at] // shards_of).reshape([-1 if axis == axis_at else 1 for axis in range(len(extent))])
    return loudness


def noise(key, shape, width, reach, shards=(), kind=jnp.bfloat16):
    values = width * jax.random.normal(key, shape, jnp.float32)
    if shards:
        values = values * levels(key, shape, shards, -0.22, 0.18)
    return jnp.clip(values, -reach, reach).astype(kind)


def setup_inputs(seed: int = 0) -> dict:
    splits = jax.random.split(jax.random.key(seed), 15)
    ends = noise(splits[0], (2, MICRO, SEQS_MB, SEQ_LEN, MODEL_WIDTH), 1.0, 6.0, ((0, 2), (2, 4), (3, 4)))
    mixer_input_weight = noise(splits[1], (2, MODEL_WIDTH, 2 * KEY + 2 * VALUE_WIDTH), MODEL_WIDTH ** -0.5, 0.1875, ((0, 2), (1, 4)))
    forget_first_map = noise(splits[2], (2, MODEL_WIDTH, FGATE_RANK), MODEL_WIDTH ** -0.5, 0.1875, ((0, 2), (1, 4)))
    forget_second_map = noise(splits[3], (2, FGATE_RANK, KEY), FGATE_RANK ** -0.5, 1.5, ((0, 2),))
    forget_logit_bias = jnp.clip(-2.0 + 8.0 * jax.random.uniform(splits[4], (2, KEY), jnp.float32) ** levels(splits[4], (2, KEY), ((0, 2),), -0.2, 0.2), -2.0, 6.0)
    mixer_output_weight = noise(splits[5], (2, VALUE_WIDTH, MODEL_WIDTH), VALUE_WIDTH ** -0.5, 0.1875, ((0, 2), (1, 4)))
    feedforward_input_weight = noise(splits[6], (2, MODEL_WIDTH, 2 * HIDDEN_UNITS), MODEL_WIDTH ** -0.5, 0.1875, ((0, 2), (1, 4)))
    feedforward_output_weight = noise(splits[7], (2, HIDDEN_UNITS, MODEL_WIDTH), HIDDEN_UNITS ** -0.5, 0.109375, ((0, 2), (1, 4)))
    adapter_model_first = noise(splits[8], (2, MODEL_WIDTH, 6 * ADAPTER_COLUMNS), MODEL_WIDTH ** -0.5, 0.1875, ((0, 2),))
    adapter_hidden_first = noise(splits[9], (2, VALUE_WIDTH + HIDDEN_UNITS, ADAPTER_COLUMNS), ((VALUE_WIDTH + HIDDEN_UNITS) // 2) ** -0.5, 0.125, ((0, 2),))
    adapter_second_maps = noise(splits[10], (2, ADAPTER_COLUMNS, RAISED_COLUMNS), (4 * ADAPTER_RANK) ** -0.5, 0.75, ((0, 2),))
    lengths = draw_lengths(jax.random.fold_in(splits[14], 71), 0)
    dealt_block_order = jax.vmap(lambda own: jax.random.permutation(own, GROUPS))(jax.random.split(splits[12], MICRO * SEQS_MB)).reshape((MICRO, SEQS_MB, GROUPS)).astype(jnp.int32)
    adapter_choice_per_seq = touch_ends(jax.random.randint(splits[13], (MICRO, SEQS_MB), 0, ADAPTERS), jax.random.fold_in(splits[13], 1), 0, ADAPTERS - 1).astype(jnp.int32)
    return dict(ends=ends, mixer_input_weight=mixer_input_weight, forget_first_map=forget_first_map, forget_second_map=forget_second_map, forget_logit_bias=forget_logit_bias, mixer_output_weight=mixer_output_weight, feedforward_input_weight=feedforward_input_weight, feedforward_output_weight=feedforward_output_weight, adapter_model_first=adapter_model_first, adapter_hidden_first=adapter_hidden_first, adapter_second_maps=adapter_second_maps, lengths=lengths, dealt_block_order=dealt_block_order, adapter_choice_per_seq=adapter_choice_per_seq)


@jax.custom_vjp
def low(v):
    return lax.optimization_barrier(v.astype(jnp.bfloat16)).astype(jnp.float32)

@jax.custom_vjp
def low_back(v):
    return v

def low_keep(v):
    return (low(v), None)

def low_pass(kept, grad):
    return (grad,)

def back_keep(v):
    return (v, None)

def back_low(kept, grad):
    return (low(grad),)
low.defvjp(low_keep, low_pass)
low_back.defvjp(back_keep, back_low)

def matrix_product(left, right):
    return jnp.dot(left, right, precision=lax.Precision.HIGHEST)

def rms_norm(values, epsilon):
    return values * lax.rsqrt(lax.optimization_barrier(jnp.mean(values * values, axis=-1, keepdims=True)) + epsilon)

def describe(seq_length, order_row, adapter_pick):
    group_count = order_row.shape[0]
    offsets = jnp.arange(GROUP, dtype=jnp.int32)
    positions = jnp.arange(group_count, dtype=jnp.int32)
    dealt_tokens = (order_row[:, None].astype(jnp.int32) * GROUP + offsets[None, :]).reshape(-1).astype(jnp.int32)
    inverse = lax.optimization_barrier(jnp.sum(positions[:, None] * (order_row[:, None] == positions[None, :]).astype(jnp.int32), axis=0)).astype(jnp.int32)
    source_tokens = (inverse[:, None] * GROUP + offsets[None, :]).reshape(-1).astype(jnp.int32)
    live = (jnp.arange(group_count * GROUP, dtype=jnp.int32) < seq_length).astype(jnp.float32)
    adapter_select_mask = (jnp.arange(ADAPTERS * ADAPTER_RANK, dtype=jnp.int32) // ADAPTER_RANK == adapter_pick).astype(jnp.float32)
    return (adapter_select_mask, source_tokens, dealt_tokens, live)

def head_mix(queries, keys, values, forget, source_tokens, dealt_tokens, live):
    key_dim = KEY // HEADS
    value_dim = VALUE_WIDTH // HEADS
    seq_total = queries.shape[0]
    head_count = queries.shape[1] // key_dim
    block_count = seq_total // GROUP
    highest = lax.Precision.HIGHEST
    queries = jnp.take(queries, source_tokens, axis=0) * key_dim ** (-0.5)
    keys = jnp.take(keys, source_tokens, axis=0) * live[:, None]
    values = jnp.take(values, source_tokens, axis=0)
    forget = jnp.take(forget, source_tokens, axis=0)
    queries = queries.reshape(block_count, GROUP, head_count, key_dim)
    keys = keys.reshape(block_count, GROUP, head_count, key_dim)
    values = values.reshape(block_count, GROUP, head_count, value_dim)
    forget = forget.reshape(block_count, GROUP, head_count, key_dim)
    summed = jnp.cumsum(forget, axis=1)
    middle = summed[:, GROUP // 2:GROUP // 2 + 1]
    block_total = summed[:, -1]
    scores = jnp.einsum('nihk,njhk->nhij', queries * jnp.exp(summed - middle), keys * jnp.exp(middle - summed), precision=highest)
    causal = (jnp.arange(GROUP, dtype=jnp.int32)[:, None] >= jnp.arange(GROUP, dtype=jnp.int32)[None, :]).astype(jnp.float32)
    inner = jnp.einsum('nhij,njhv->nihv', scores * causal, values, precision=highest)
    update = jnp.einsum('njhk,njhv->nhkv', keys * jnp.exp(block_total[:, None] - summed), values, precision=highest)

    def advance(state, inputs_now):
        decay, addend = inputs_now
        return (decay[..., None] * state + addend, state)
    _, states = lax.scan(advance, jnp.zeros((head_count, key_dim, value_dim), jnp.float32), (jnp.exp(block_total), update))
    cross = jnp.einsum('nihk,nhkv->nihv', queries * jnp.exp(summed), states, precision=highest)
    layer_result = (inner + cross).reshape(seq_total, head_count, value_dim)
    layer_result = layer_result * lax.rsqrt(lax.optimization_barrier(jnp.mean(layer_result * layer_result, axis=-1, keepdims=True)) + 1.0)
    return jnp.take(layer_result.reshape(seq_total, head_count * value_dim), dealt_tokens, axis=0)

def apply_adapter(values, down, up, spans, adapter_select_mask):
    rank_block = down.shape[1] // len(spans)
    adapted = low_back(low(matrix_product(values, down) * jnp.tile(adapter_select_mask, len(spans))))
    pieces = []
    for block_index, (col_start, col_width) in enumerate(spans):
        pieces.append(matrix_product(adapted[:, block_index * rank_block:(block_index + 1) * rank_block], up[:, col_start:col_start + col_width]))
    return jnp.concatenate(pieces, axis=1)

def layer(residual_stream, frozen, trainable_params, sequence_details):
    mixer_input_weight, forget_first_map, forget_second_map, forget_logit_bias, mixer_output_weight, feedforward_input_weight, feedforward_output_weight = frozen
    adapter_model_first, adapter_hidden_first, adapter_second_maps = trainable_params
    adapter_select_mask, source_tokens, dealt_tokens, live = sequence_details
    frozen_base = 2 * KEY + 2 * VALUE_WIDTH
    mixer_column_ranges = ((0, KEY), (KEY, KEY), (2 * KEY, VALUE_WIDTH), (2 * KEY + VALUE_WIDTH, VALUE_WIDTH))
    feedforward_ranges = ((frozen_base, HIDDEN_UNITS), (frozen_base + HIDDEN_UNITS, HIDDEN_UNITS))
    normalized_input = low(rms_norm(residual_stream, 1e-06))
    projected_features = matrix_product(normalized_input, mixer_input_weight) + apply_adapter(normalized_input, adapter_model_first[:, :4 * ADAPTER_COLUMNS], adapter_second_maps, mixer_column_ranges, adapter_select_mask)
    queries = low_back(low(projected_features[:, :KEY]))
    keys = low_back(low(projected_features[:, KEY:2 * KEY]))
    values = low_back(low(projected_features[:, 2 * KEY:2 * KEY + VALUE_WIDTH]))
    out_gate = low_back(projected_features[:, 2 * KEY + VALUE_WIDTH:])
    gate_low = low_back(low(matrix_product(normalized_input, forget_first_map)))
    gate_logit = low_back(matrix_product(gate_low, forget_second_map) + forget_logit_bias)
    forget = low_back(low(jax.nn.log_sigmoid(gate_logit) / 16.0))
    mixed = low_back(low(head_mix(queries, keys, values, forget, source_tokens, dealt_tokens, live)))
    gated_output = low(mixed * jax.nn.silu(out_gate))
    attention_output = low_back(matrix_product(gated_output, mixer_output_weight) + apply_adapter(gated_output, adapter_hidden_first[:VALUE_WIDTH], adapter_second_maps, ((frozen_base + 2 * HIDDEN_UNITS, MODEL_WIDTH),), adapter_select_mask))
    resid_mid = residual_stream + attention_output
    normalized_middle = low(rms_norm(resid_mid, 1e-06))
    gate_and_up = low_back(matrix_product(normalized_middle, feedforward_input_weight) + apply_adapter(normalized_middle, adapter_model_first[:, 4 * ADAPTER_COLUMNS:], adapter_second_maps, feedforward_ranges, adapter_select_mask))
    hidden_features = low(jax.nn.silu(gate_and_up[:, :HIDDEN_UNITS]) * gate_and_up[:, HIDDEN_UNITS:])
    feedforward_branch = low_back(matrix_product(hidden_features, feedforward_output_weight) + apply_adapter(hidden_features, adapter_hidden_first[VALUE_WIDTH:], adapter_second_maps, ((frozen_base + 2 * HIDDEN_UNITS + MODEL_WIDTH, MODEL_WIDTH),), adapter_select_mask))
    return resid_mid + feedforward_branch

def reference(ends, mixer_input_weight, forget_first_map, forget_second_map, forget_logit_bias, mixer_output_weight, feedforward_input_weight, feedforward_output_weight, adapter_model_first, adapter_hidden_first, adapter_second_maps, lengths, dealt_block_order, adapter_choice_per_seq):
    frozen = []
    for section_index in range(2):
        frozen.append(tuple((tensor[section_index].astype(jnp.float32) for tensor in (mixer_input_weight, forget_first_map, forget_second_map, forget_logit_bias, mixer_output_weight, feedforward_input_weight, feedforward_output_weight))))
    trainable_params = (adapter_model_first.astype(jnp.float32), adapter_hidden_first.astype(jnp.float32), adapter_second_maps.astype(jnp.float32))
    count = MICRO * SEQS_MB
    block_ins = ends[0].reshape(count, SEQ_LEN, MODEL_WIDTH)
    cotangents = ends[1].reshape(count, SEQ_LEN, MODEL_WIDTH)
    flat_lengths = lengths.reshape(count).astype(jnp.int32)
    flat_orders = dealt_block_order.reshape(count, GROUPS).astype(jnp.int32)
    flat_ids = adapter_choice_per_seq.reshape(count).astype(jnp.int32)

    def per_sequence(carry, item):
        block_in, cotangent, seq_length, order_row, adapter_pick = item
        sequence_details = describe(seq_length, order_row, adapter_pick)

        def forward(model_part, hidden_part, up_part, entry):
            first_out = layer(entry, frozen[0], (model_part[0], hidden_part[0], up_part[0]), sequence_details)
            passed = low_back(low(first_out))
            return layer(passed, frozen[1], (model_part[1], hidden_part[1], up_part[1]), sequence_details)
        output, pullback = jax.vjp(forward, trainable_params[0], trainable_params[1], trainable_params[2], block_in.astype(jnp.float32))
        grad_model, grad_hidden, grad_up, entry_gradient = pullback(cotangent.astype(jnp.float32))
        carry = (carry[0] + grad_model, carry[1] + grad_hidden, carry[2] + grad_up)
        return (carry, (output.astype(jnp.bfloat16), entry_gradient.astype(jnp.bfloat16)))
    start = tuple((jnp.zeros_like(tensor) for tensor in trainable_params))
    grad_sums, (outputs_all, entry_grads) = lax.scan(per_sequence, start, (block_ins, cotangents, flat_lengths, flat_orders, flat_ids))
    results = jnp.stack([entry_grads.reshape(MICRO, SEQS_MB, SEQ_LEN, MODEL_WIDTH), outputs_all.reshape(MICRO, SEQS_MB, SEQ_LEN, MODEL_WIDTH)])
    return (results, grad_sums[0], grad_sums[1], grad_sums[2])
```

```python
import functools
import jax
import jax.numpy as jnp
from jax import lax
from jax.experimental import pallas as pl
from jax.experimental.pallas import tpu as pltpu

from jax.sharding import PartitionSpec as P

MODEL_WIDTH = 1024
HEADS = 4
KEY = 512
VALUE_WIDTH = 1024
HIDDEN_UNITS = 2816
FGATE_RANK = 16
GROUP = 64
ADAPTER_RANK = 16
ADAPTERS = 8
ADAPTER_COLUMNS = 128
VMEM_LIMIT = 60 << 20

MESH = pl.DeviceIdType.MESH
ANY = pl.BlockSpec(memory_space=pl.ANY)


def gather_kernel(*refs):
    n_w, n_s = 4, 6
    shards = refs[:n_w]
    f1_ref, ends_ref = refs[n_w : n_w + 2]
    small = refs[n_w + 2 : n_w + 2 + n_s - 1]
    at = n_w + 2 + len(small)
    outs = refs[at : at + n_w]
    f1_out, x_out, c_out = refs[at + n_w : at + n_w + 3]
    small_out = refs[at + n_w + 3 : at + n_w + 3 + len(small)]
    at += n_w + 3 + len(small)
    held, held_small, held_ends, held_f1 = refs[at : at + n_w], refs[at + n_w : at + n_w + len(small)], refs[-23], refs[-22]
    ins = refs[-21]
    (zs, zr, xs, xr, ys, yr, fxs, fxr, fys, fyr, cs, cr, own, ms, mr, es, er, f1s, f1r, f1c) = refs[-20:]
    core, z, s = lax.axis_index("section"), lax.axis_index("dp"), lax.axis_index("seq")
    other = 1 - core
    n_z = 4
    fetch = [pltpu.make_async_copy(shards[w].at[0], held[w], ins.at[w]) for w in range(n_w)]
    fetch += [pltpu.make_async_copy(a.at[0], b, ins.at[n_w + i]) for i, (a, b) in enumerate(zip(small, held_small))]
    fetch.append(pltpu.make_async_copy(ends_ref.at[0, :, 0], held_ends, ins.at[n_w + len(small)]))
    fetch.append(pltpu.make_async_copy(f1_ref, held_f1, ins.at[n_w + len(small) + 1]))
    for f in fetch:
        f.start()
    barrier = pltpu.get_barrier_semaphore()

    def greet(**where):
        pl.semaphore_signal(barrier, inc=1, device_id=where, device_id_type=MESH)

    greet(section=other)
    greet(seq=s ^ 1)
    greet(seq=s ^ 2)
    for gap in range(1, n_z):
        greet(dp=lax.rem(z + gap, n_z))
    pl.semaphore_wait(barrier, 3 + n_z - 1)

    finals = []

    def remote(src, dst, ssem, rsem, **where):
        return pltpu.make_async_remote_copy(
            src_ref=src, dst_ref=dst, send_sem=ssem, recv_sem=rsem, device_id=where, device_id_type=MESH
        )

    def rows_of(w, j):
        return shards[w].shape[1] * j

    def piece(w, j, q):
        r = shards[w].shape[1]
        return outs[w].at[core, pl.ds(pl.multiple_of(j * r + q * (r // 4), 16), r // 4)]

    def half(w, j, q, low):
        r = shards[w].shape[1]
        cut = (r // 8 + 15) // 16 * 16
        start, size = (0, cut) if low else (cut, r // 4 - cut)
        return outs[w].at[core, pl.ds(pl.multiple_of(j * r + q * (r // 4) + start, 16), size)]

    def block(w, j):
        r = shards[w].shape[1]
        return outs[w].at[core, pl.ds(pl.multiple_of(j * r, 16), r)]

    def own_shard(w):
        return held[w]

    def own_piece(w):
        r = shards[w].shape[1]
        return held[w].at[pl.ds(pl.multiple_of(s * (r // 4), 16), r // 4)]

    def step(d):
        return 1 if d == 0 else -1

    def can_send(d, t):
        has_next = (z < n_z - 1) if d == 0 else (z > 0)
        origin = z - step(d) * (t - 1)
        return jnp.logical_and(has_next, jnp.logical_and(origin >= 0, origin < n_z))

    def gets(d, t):
        origin = z - step(d) * t
        return jnp.logical_and(origin >= 0, origin < n_z)

    def z_copy(w, d, t):
        j = z - step(d) * (t - 1)
        src = own_piece(w) if t == 1 else piece(w, j, s)
        return remote(src, piece(w, j, s), zs.at[w, d, t - 1], zr.at[w, d, t - 1], dp=z + step(d))

    def origin(d, t):
        return z - step(d) * t

    def x_copy(w, d, t):
        return remote(piece(w, origin(d, t), s), piece(w, origin(d, t), s), xs.at[w, d, t - 1], xr.at[w, d, t - 1], seq=s ^ 1)

    def y_copy(w, d, t):
        return remote(piece(w, origin(d, t), s), piece(w, origin(d, t), s), ys.at[w, d, t - 1], yr.at[w, d, t - 1], seq=s ^ 2)

    def fx_copy(w, d, t):
        ref = half(w, origin(d, t), s ^ 2, False)
        return remote(ref, ref, fxs.at[w, d, t - 1], fxr.at[w, d, t - 1], seq=s ^ 1)

    def fy_copy(w, d, t):
        ref = half(w, origin(d, t), s ^ 1, True)
        return remote(ref, ref, fys.at[w, d, t - 1], fyr.at[w, d, t - 1], seq=s ^ 2)

    def c_copy(w, d, t):
        if t == 0:
            return remote(own_shard(w), block(w, z), cs.at[w, 0, 3], cr.at[w, 0, 3], section=other)
        ref = block(w, origin(d, t))
        return remote(ref, ref, cs.at[w, d, t - 1], cr.at[w, d, t - 1], section=other)

    def own_copy(w):
        return pltpu.make_async_copy(own_shard(w), block(w, z), own.at[w])

    def start_own(w):
        for d in range(2):
            @pl.when(can_send(d, 1))
            def _():
                z_copy(w, d, 1).start()

    def take_z(w, t):
        for d in range(2):
            @pl.when(gets(d, t))
            def _():
                z_copy(w, d, t).wait_recv()
            if t < n_z - 1:
                @pl.when(can_send(d, t + 1))
                def _():
                    z_copy(w, d, t + 1).start()
            @pl.when(gets(d, t))
            def _():
                x_copy(w, d, t).start()
                y_copy(w, d, t).start()

    def take_xy(w, t):
        for d in range(2):
            @pl.when(gets(d, t))
            def _():
                x_copy(w, d, t).wait_recv()
                fy_copy(w, d, t).start()
                y_copy(w, d, t).wait_recv()
                fx_copy(w, d, t).start()

    def take_diagonal(w, t):
        for d in range(2):
            @pl.when(gets(d, t))
            def _():
                fy_copy(w, d, t).wait_recv()
                fx_copy(w, d, t).wait_recv()
                c_copy(w, d, t).start()

    ends_to_x = remote(held_ends.at[1], x_out, es, er, section=other)
    ends_to_c = remote(held_ends.at[0], c_out, es, er, section=other)
    ends_x = pltpu.make_async_copy(held_ends.at[0], x_out, own.at[n_w])
    ends_c = pltpu.make_async_copy(held_ends.at[1], c_out, own.at[n_w])

    for f in fetch:
        f.wait()
    start_own(0)
    @pl.when(core == 0)
    def _():
        ends_to_x.start()
        ends_x.start()

    @pl.when(core == 1)
    def _():
        ends_to_c.start()
        ends_c.start()

    def f1_copy(gap):
        return remote(
            held_f1, f1_out.at[core, z], f1s.at[gap], f1r.at[gap], dp=lax.rem(z + gap, n_z)
        )
    for gap in range(1, n_z):
        f1_copy(gap).start()
    f1_own = pltpu.make_async_copy(held_f1, f1_out.at[core, z], own.at[n_w + 1])
    f1_own.start()
    smalls = []
    for i, (a, b) in enumerate(zip(held_small, small_out)):
        mine = pltpu.make_async_copy(a, b.at[core], own.at[n_w + 2 + i])
        theirs = remote(a, b.at[core], ms.at[i], mr.at[i], section=other)
        mine.start()
        theirs.start()
        smalls.append((mine, theirs))
    for w in range(n_w):
        own_copy(w).start()
        c_copy(w, 0, 0).start()
    items = [(w, t) for w in range(n_w) for t in range(1, n_z)]
    f1_sends = [f1_copy(gap) for gap in range(1, n_z)]
    f1_cross = remote(f1_out.at[core], f1_out.at[core], f1c.at[0], f1c.at[1], section=other)
    for i in range(len(items) + 2):
        if i < len(items):
            w, t = items[i]
            if t == 1 and w + 1 < n_w:
                start_own(w + 1)
            take_z(w, t)
        if 0 <= i - 1 < len(items):
            take_xy(*items[i - 1])
        if 0 <= i - 2 < len(items):
            take_diagonal(*items[i - 2])
        if i == 1:
            f1_own.wait()
            for c in f1_sends:
                c.wait_recv()
            f1_cross.start()
    for w in range(n_w):
        own_copy(w).wait()
        c_copy(w, 0, 0).wait()
        for d in range(2):
            for t in range(1, n_z):
                @pl.when(can_send(d, t))
                def _():
                    z_copy(w, d, t).wait_send()
                @pl.when(gets(d, t))
                def _():
                    x_copy(w, d, t).wait_send()
                    y_copy(w, d, t).wait_send()
                    fx_copy(w, d, t).wait_send()
                    fy_copy(w, d, t).wait_send()
                    c_copy(w, d, t).wait()
    for mine, theirs in smalls:
        mine.wait()
        theirs.wait()
    for c in f1_sends:
        c.wait_send()
    f1_cross.wait()
    ends_x.wait()
    ends_to_x.wait()


def gather_all(shards, f1t, ends, small):
    n_w = 4
    shape = jax.ShapeDtypeStruct
    outs = [shape((2, 4 * w.shape[1], w.shape[2]), w.dtype) for w in shards]
    outs.append(shape((2, 4) + f1t.shape, f1t.dtype))
    outs += [shape(ends.shape[3:], ends.dtype)] * 2
    outs += [shape((2,) + a.shape[1:], a.dtype) for a in small]
    dma = pltpu.SemaphoreType.DMA
    per = [dma((n_w, 2, 3)) for _ in range(10)] + [dma((n_w, 2, 4)) for _ in range(2)]
    return pl.pallas_call(
        gather_kernel,
        out_shape=outs,
        in_specs=[ANY] * (n_w + 2 + len(small)),
        out_specs=[ANY] * len(outs),
        scratch_shapes=[pltpu.VMEM(w.shape[1:], w.dtype) for w in shards]
        + [pltpu.VMEM(a.shape[1:], a.dtype) for a in small]
        + [pltpu.VMEM((2,) + ends.shape[3:], ends.dtype), pltpu.VMEM(f1t.shape, f1t.dtype)]
        + [dma((n_w + len(small) + 2,))]
        + per
        + [dma((n_w + 2 + len(small),)), dma((len(small),)), dma((len(small),)), dma, dma, dma((4,)), dma((4,)), dma((2,))],
        compiler_params=pltpu.CompilerParams(collective_id=0, has_side_effects=True, vmem_limit_bytes=VMEM_LIMIT),
    )(*shards, f1t, ends, *small)


BF = jnp.bfloat16
F32 = jnp.float32


def nn(a, b):
    return lax.dot_general(a, b, (((1,), (0,)), ((), ())), preferred_element_type=F32)


def nt(a, b):
    return lax.dot_general(a, b, (((1,), (1,)), ((), ())), preferred_element_type=F32)


def tn(a, b):
    return lax.dot_general(a, b, (((0,), (0,)), ((), ())), preferred_element_type=F32)


def silu_parts(v):
    sig = lax.logistic(v)
    return v * sig, sig


def inverse_rms(v):
    return lax.rsqrt(jnp.mean(v * v, axis=-1, keepdims=True) + 1e-06)


def rms_back(v, grad):
    r = inverse_rms(v)
    n = v * r
    return r * (grad - n * jnp.mean(grad * n, axis=-1, keepdims=True))


def lanes(start, size):
    return pl.ds(pl.multiple_of(start, 128), size)


def rows(start, size):
    return pl.ds(pl.multiple_of(start, size if size <= 64 else 64), size)


def greet_peers(me):
    barrier = pltpu.get_barrier_semaphore()
    for d in range(1, HEADS):
        pl.semaphore_signal(barrier, inc=1, device_id={"seq": me ^ d}, device_id_type=MESH)
    pl.semaphore_wait(barrier, HEADS - 1)


def to_peer(src, dst, ssem, rsem, peer):
    return pltpu.make_async_remote_copy(
        src_ref=src, dst_ref=dst, send_sem=ssem, recv_sem=rsem,
        device_id={"seq": peer}, device_id_type=MESH,
    )


class Local:
    def __init__(self, sems):
        self.sems, self.used, self.open = sems, 0, []

    def start(self, src, dst, wait_at_end=False):
        copy = pltpu.make_async_copy(src, dst, self.sems.at[self.used])
        self.used += 1
        copy.start()
        if wait_at_end:
            self.open.append(copy)
        return copy

    def finish(self):
        for copy in self.open:
            copy.wait()


def picked(adapter, width):
    row = lax.broadcasted_iota(jnp.int32, (width, ADAPTER_RANK), 0)
    col = lax.broadcasted_iota(jnp.int32, (width, ADAPTER_RANK), 1)
    return (row == adapter * ADAPTER_RANK + col).astype(BF)


def column_mask(adapter):
    col = lax.broadcasted_iota(jnp.int32, (1, ADAPTER_COLUMNS), 1)
    low = adapter * ADAPTER_RANK
    return jnp.logical_and(col >= low, col < low + ADAPTER_RANK).astype(F32)


def lower_triangle(dtype):
    i = lax.broadcasted_iota(jnp.int32, (GROUP, GROUP), 0)
    j = lax.broadcasted_iota(jnp.int32, (GROUP, GROUP), 1)
    return (i >= j).astype(dtype)


DK = KEY // HEADS
DV = VALUE_WIDTH // HEADS
CHUNK = 2 * DK + DV
FROZEN = 2 * KEY + 2 * VALUE_WIDTH
TILE = 256
SCALE = DK ** (-0.5)

U_G = FROZEN
U_U = FROZEN + HIDDEN_UNITS
U_O = FROZEN + 2 * HIDDEN_UNITS
U_D = U_O + MODEL_WIDTH


def live_rows(n, length):
    at = lax.broadcasted_iota(jnp.int32, (GROUP, 1), 0) + n * GROUP
    return (at < length).astype(F32)


def forward_kernel(
    layer, n_blocks, meta, h_in, w_mi, w_mo, w_fi, w_fo, w_f1, w_f2, w_b, w_am, w_ah, w_au,
    y_out, o_ad, o_og, o_qkv, o_gl, o_st, o_mix, o_yh, o_rh, o_ao, o_mid, o_af, o_gu, o_dn,
    h, mi, mo, fi, fo, f1, f2, bias, am, ah, au,
    y, ad, og, qkv, gl, st, mix, yh, rh, ao, mid, af, gu, dn,
    normed, send, glsend, fg, state, gated, hidden,
    lsem, ssem, rsem,
):
    me = lax.axis_index("seq")
    T = h.shape[0]
    per = T // GROUP
    adapter = meta[2 * n_blocks]
    length = meta[2 * n_blocks + 1]
    loc = Local(lsem)
    l_h = loc.start(h_in, h)
    l_f1 = loc.start(w_f1.at[layer], f1)
    l_f2 = loc.start(w_f2.at[layer], f2)
    l_b = loc.start(w_b.at[layer], bias)
    l_am = loc.start(w_am.at[layer], am)
    l_au = loc.start(w_au.at[layer], au)
    l_mi = loc.start(w_mi.at[layer], mi)
    greet_peers(me)
    l_ah = loc.start(w_ah.at[layer], ah)
    l_mo = loc.start(w_mo.at[layer], mo)
    l_fi = loc.start(w_fi.at[layer], fi)
    l_fo = loc.start(w_fo.at[layer], fo)
    mask = column_mask(adapter)

    l_h.wait()
    hv = h[...].astype(F32)
    normed[...] = (hv * inverse_rms(hv)).astype(BF)
    l_f1.wait()
    z_w = f1.shape[2]
    low = nt(f1[0], normed[:, 0:z_w])
    for j in range(1, f1.shape[0]):
        low += nt(f1[j], normed[:, j * z_w : (j + 1) * z_w])
    glsend[...] = low.astype(BF)
    low_copies = [to_peer(glsend, gl.at[me], ssem.at[0, d], rsem.at[0, d], me ^ d) for d in range(1, HEADS)]
    for c in low_copies:
        c.start()
    gl[me] = glsend[...]
    l_am.wait()
    for p in range(4):
        cols = pl.ds(p * ADAPTER_COLUMNS, ADAPTER_COLUMNS)
        ad[:, cols] = (nn(normed[...], am[:, cols]) * mask).astype(BF)
    l_au.wait()
    l_mi.wait()

    def project(w_start, p, width):
        cols = lanes(w_start, width)
        return nn(normed[...], mi[:, cols]) + nn(ad[:, p * ADAPTER_COLUMNS : (p + 1) * ADAPTER_COLUMNS], au[:, cols])

    def chunk(head, ref):
        ref[:, 0:DK] = project(head * DK, 0, DK).astype(BF)
        ref[:, DK : 2 * DK] = project(KEY + head * DK, 1, DK).astype(BF)
        ref[:, 2 * DK : CHUNK] = project(2 * KEY + head * DV, 2, DV).astype(BF)

    qkv_copies = []
    for d in range(1, HEADS):
        chunk(me ^ d, send.at[d - 1])
        copy = to_peer(send.at[d - 1], qkv.at[rows(me * T, T)], ssem.at[1, d], rsem.at[1, d], me ^ d)
        copy.start()
        qkv_copies.append(copy)
    chunk(me, qkv.at[rows(me * T, T)])
    loc.start(ad, o_ad, True)
    for j in range(VALUE_WIDTH // TILE):
        og[:, j * TILE : (j + 1) * TILE] = project(2 * KEY + VALUE_WIDTH + j * TILE, 3, TILE)
    loc.start(og, o_og, True)
    l_f2.wait()
    l_b.wait()
    for c in low_copies:
        c.wait_recv()
    f2h = f2[:, lanes(me * DK, DK)]
    bh = bias[:, lanes(me * DK, DK)]
    for src in range(HEADS):
        logit = tn(gl[src], f2h) + bh
        fg[src * T : (src + 1) * T, :] = (jax.nn.log_sigmoid(logit) / 16.0).astype(BF)
    for c in qkv_copies:
        c.wait_recv()
    loc.start(gl, o_gl, True)
    loc.start(qkv, o_qkv, True)
    tri = lower_triangle(BF)
    causal = lower_triangle(F32)

    state[...] = jnp.zeros_like(state)

    def advance(n, carry):
        at = pl.ds(meta[n_blocks + n] * GROUP, GROUP)
        summed = nn(tri, fg[at, :])
        total = summed[GROUP - 1 : GROUP]
        k = qkv[at, DK : 2 * DK].astype(F32) * live_rows(n, length)
        ku = (k * jnp.exp(total - summed)).astype(BF)
        update = tn(qkv[at, 2 * DK : CHUNK], ku)
        now = state[...]
        st[n] = now.astype(BF)
        state[...] = jnp.exp(total) * now + update
        return carry

    lax.fori_loop(0, n_blocks, advance, 0, unroll=4)
    loc.start(st, o_st, True)

    def mix_block(p):
        n = meta[p]
        at = rows(p * GROUP, GROUP)
        summed = nn(tri, fg[at, :])
        middle = summed[GROUP // 2 : GROUP // 2 + 1]
        q = qkv[at, 0:DK].astype(F32) * SCALE
        k = qkv[at, DK : 2 * DK].astype(F32) * live_rows(n, length)
        qe = (q * jnp.exp(summed - middle)).astype(BF)
        ke = (k * jnp.exp(middle - summed)).astype(BF)
        scores = jnp.where(causal > 0, nt(qe, ke), 0.0).astype(BF)
        o = nn(scores, qkv[at, 2 * DK : CHUNK]) + nt((q * jnp.exp(summed)).astype(BF), st[n])
        r = lax.rsqrt(jnp.mean(o * o, axis=-1, keepdims=True) + 1.0)
        yh[at, :] = (o * r).astype(BF)
        rh[at, :] = jnp.broadcast_to(r, (GROUP, DK))

    mix_copies = []
    for d in range(1, HEADS):
        peer = me ^ d
        lax.fori_loop(0, per, lambda j, c, peer=peer: (mix_block(peer * per + j), c)[1], 0, unroll=True)
        copy = to_peer(yh.at[rows(peer * T, T)], mix.at[me], ssem.at[2, d], rsem.at[2, d], peer)
        copy.start()
        mix_copies.append(copy)
    lax.fori_loop(0, per, lambda j, c: (mix_block(me * per + j), c)[1], 0, unroll=True)
    mix[me] = yh[rows(me * T, T), :]
    loc.start(yh, o_yh, True)
    loc.start(rh, o_rh, True)
    for c in mix_copies:
        c.wait_recv()
    loc.start(mix, o_mix, True)
    for hd in range(HEADS):
        cols = slice(hd * DV, (hd + 1) * DV)
        gated[:, cols] = (mix[hd].astype(F32) * silu_parts(og[:, cols])[0]).astype(BF)
    l_ah.wait()
    l_mo.wait()
    ao[...] = (nn(gated[...], ah[0:VALUE_WIDTH, :]) * mask).astype(BF)
    for j in range(MODEL_WIDTH // TILE):
        cols = slice(j * TILE, (j + 1) * TILE)
        mid[:, cols] = (
            h[:, cols].astype(F32) + nn(gated[...], mo[:, cols]) + nn(ao[...], au[:, U_O + j * TILE : U_O + (j + 1) * TILE])
        )
    loc.start(ao, o_ao, True)
    loc.start(mid, o_mid, True)
    mv = mid[...]
    normed[...] = (mv * inverse_rms(mv)).astype(BF)
    for p in range(2):
        cols = slice(p * ADAPTER_COLUMNS, (p + 1) * ADAPTER_COLUMNS)
        wide = slice((4 + p) * ADAPTER_COLUMNS, (5 + p) * ADAPTER_COLUMNS)
        af[:, cols] = (nn(normed[...], am[:, wide]) * mask).astype(BF)
    loc.start(af, o_af, True)
    l_fi.wait()

    def up_tile(i, carry):
        a, b = lanes(i * TILE, TILE), lanes(HIDDEN_UNITS + i * TILE, TILE)
        gate = nn(normed[...], fi[:, a]) + nn(af[:, 0:ADAPTER_COLUMNS], au[:, lanes(U_G + i * TILE, TILE)])
        up = nn(normed[...], fi[:, b]) + nn(af[:, ADAPTER_COLUMNS:], au[:, lanes(U_U + i * TILE, TILE)])
        gu[:, a] = gate.astype(gu.dtype)
        gu[:, b] = up.astype(gu.dtype)
        hidden[:, a] = (silu_parts(gate)[0] * up).astype(BF)
        return carry

    lax.fori_loop(0, HIDDEN_UNITS // TILE, up_tile, 0)
    loc.start(gu, o_gu, True)
    l_fo.wait()
    dn[...] = (nn(hidden[...], ah[VALUE_WIDTH:, :]) * mask).astype(BF)
    loc.start(dn, o_dn, True)
    for j in range(MODEL_WIDTH // TILE):
        cols = slice(j * TILE, (j + 1) * TILE)
        y[:, cols] = (
            mid[:, cols] + nn(hidden[...], fo[:, cols]) + nn(dn[...], au[:, U_D + j * TILE : U_D + (j + 1) * TILE])
        ).astype(BF)
    loc.start(y, y_out, True)
    loc.finish()
    for c in low_copies + qkv_copies + mix_copies:
        c.wait_send()


def weight_scratch(weights):
    return [pltpu.VMEM(w.shape[1:], w.dtype) for w in weights]


def saved_shapes(T, L, n_blocks):
    s = lambda shape, dtype=BF: (shape, dtype)
    return [
        s((T, MODEL_WIDTH)),
        s((T, 4 * ADAPTER_COLUMNS)),
        s((T, VALUE_WIDTH), F32),
        s((L, CHUNK)),
        s((HEADS, FGATE_RANK, T)),
        s((n_blocks, DV, DK)),
        s((HEADS, T, DV)),
        s((L, DV)),
        s((L, DK), F32),
        s((T, ADAPTER_COLUMNS)),
        s((T, MODEL_WIDTH), F32),
        s((T, 2 * ADAPTER_COLUMNS)),
        s((T, 2 * HIDDEN_UNITS)),
        s((T, ADAPTER_COLUMNS)),
    ]


def forward(layer, meta, h, weights):
    T = h.shape[0]
    L = T * HEADS
    n_blocks = L // GROUP
    saved = saved_shapes(T, L, n_blocks)
    vm = pltpu.VMEM
    dma = pltpu.SemaphoreType.DMA
    return pl.pallas_call(
        functools.partial(forward_kernel, layer, n_blocks),
        out_shape=[jax.ShapeDtypeStruct(*s) for s in saved],
        in_specs=[pl.BlockSpec(memory_space=pltpu.SMEM)] + [ANY] * (1 + len(weights)),
        out_specs=[ANY] * len(saved),
        scratch_shapes=[vm(h.shape, h.dtype)]
        + weight_scratch(weights)
        + [vm(*s) for s in saved]
        + [
            vm((T, MODEL_WIDTH), BF),
            vm((HEADS - 1, T, CHUNK), BF),
            vm((FGATE_RANK, T), BF),
            vm((L, DK), BF),
            vm((DV, DK), F32),
            vm((T, VALUE_WIDTH), BF),
            vm((T, HIDDEN_UNITS), BF),
            dma((1 + len(weights) + len(saved),)),
            dma((3, HEADS)),
            dma((3, HEADS)),
        ],
        compiler_params=pltpu.CompilerParams(
            collective_id=1 + layer, has_side_effects=True, vmem_limit_bytes=VMEM_LIMIT
        ),
        cost_estimate=pl.CostEstimate(flops=2 * T * 13_000_000, bytes_accessed=40 << 20, transcendentals=T * 8192),
    )(meta, h, *weights)


def backward_kernel(
    layer, n_blocks, meta, d_in, h_in, w_mi, w_mo, w_fi, w_fo, w_f1, w_f2, w_b, w_am, w_ah, w_au,
    i_ad, i_og, i_qkv, i_gl, i_st, i_mix, i_yh, i_rh, i_ao, i_mid, i_af, i_gu, i_dn,
    e_out, gm_out, gh_out, gp_out,
    d, h, mi, mo, fi, fo, f1, f2, bias, am, ah, au,
    ad, og, qkv, gl, st, mix, yh, rh, ao, mid, af, gu, dn,
    e, gm, gh, gp,
    hidden, wide, gad, big, grad, dog, sendm, dmr, logit, fg, gstate, gt, dt, don, hidden_gated, sendq, dqkv, dlog, sendl, dlr, dproj,
    lsem, ssem, rsem,
):
    me = lax.axis_index("seq")
    T = h.shape[0]
    per = T // GROUP
    adapter = meta[2 * n_blocks]
    length = meta[2 * n_blocks + 1]
    loc = Local(lsem)
    l_d = loc.start(d_in, d)
    l_au = loc.start(w_au.at[layer], au)
    l_ah = loc.start(w_ah.at[layer], ah)
    l_fo = loc.start(w_fo.at[layer], fo)
    l_gu = loc.start(i_gu, gu)
    l_dn = loc.start(i_dn, dn)
    greet_peers(me)
    l_fi = loc.start(w_fi.at[layer], fi)
    l_am = loc.start(w_am.at[layer], am)
    l_mid = loc.start(i_mid, mid)
    l_af = loc.start(i_af, af)
    l_mo = loc.start(w_mo.at[layer], mo)
    l_og = loc.start(i_og, og)
    l_mix = loc.start(i_mix, mix)
    l_ao = loc.start(i_ao, ao)
    l_mixer = [
        loc.start(a, b)
        for a, b in (
            (w_f2.at[layer], f2), (w_b.at[layer], bias), (i_qkv, qkv), (i_gl, gl), (i_st, st), (i_yh, yh), (i_rh, rh),
        )
    ]
    l_last = [
        loc.start(a, b) for a, b in ((w_mi.at[layer], mi), (w_f1.at[layer], f1), (i_ad, ad), (h_in, h))
    ]
    mask = column_mask(adapter)
    pick = picked(adapter, ADAPTER_COLUMNS)

    def narrow(v):
        return nn(v, pick).astype(BF)

    l_d.wait()
    l_au.wait()
    gdown = (nt(d[...], au[:, U_D : U_D + MODEL_WIDTH]).astype(BF).astype(F32) * mask).astype(BF)
    gdown16 = narrow(gdown)
    l_dn.wait()
    gp[:, U_D : U_D + MODEL_WIDTH] = tn(narrow(dn[...]), d[...])
    gad[...] = gdown
    l_ah.wait()
    l_fo.wait()
    l_gu.wait()

    def down_tile(i, carry):
        a, b = lanes(i * TILE, TILE), lanes(HIDDEN_UNITS + i * TILE, TILE)
        at = pl.ds(pl.multiple_of(i * TILE, TILE), TILE)
        dh = nt(d[...], fo[at, :]) + nt(gad[...], ah[pl.ds(pl.multiple_of(VALUE_WIDTH + i * TILE, TILE), TILE), :])
        gate, up = gu[:, a].astype(F32), gu[:, b].astype(F32)
        act, sig = silu_parts(gate)
        hidden[:, a] = (act * up).astype(BF)
        wide[:, a] = (dh * up * sig * (1.0 + gate * (1.0 - sig))).astype(BF)
        wide[:, b] = (dh * act).astype(BF)
        return carry

    lax.fori_loop(0, HIDDEN_UNITS // TILE, down_tile, 0)
    gate_cols, up_cols = slice(0, HIDDEN_UNITS), slice(HIDDEN_UNITS, 2 * HIDDEN_UNITS)
    gg = (nt(wide[:, gate_cols], au[:, U_G : U_G + HIDDEN_UNITS]).astype(BF).astype(F32) * mask).astype(BF)
    gu2 = (nt(wide[:, up_cols], au[:, U_U : U_U + HIDDEN_UNITS]).astype(BF).astype(F32) * mask).astype(BF)
    gad2 = jnp.concatenate([gg, gu2], axis=1)
    big[:, 0 : 2 * ADAPTER_COLUMNS] = gad2
    l_fi.wait()
    l_am.wait()

    def wide_tile(i, carry):
        at = pl.ds(pl.multiple_of(i * TILE, TILE), TILE)
        grad[:, lanes(i * TILE, TILE)] = nt(wide[...], fi[at, :]) + nt(
            big[:, 0 : 2 * ADAPTER_COLUMNS], am[at, 4 * ADAPTER_COLUMNS :]
        )
        return carry

    lax.fori_loop(0, MODEL_WIDTH // TILE, wide_tile, 0)
    l_mid.wait()
    mv = mid[...]
    grad_mid = d[...].astype(F32) + rms_back(mv, grad[...])
    grad[...] = grad_mid
    attn = grad_mid.astype(BF)
    e[...] = attn
    gout = (nt(attn, au[:, U_O : U_O + MODEL_WIDTH]).astype(BF).astype(F32) * mask).astype(BF)
    gad[...] = gout
    l_mo.wait()
    l_og.wait()
    l_mix.wait()

    def gate_back(head, out):
        at = rows(head * DV, DV)
        cols = lanes(head * DV, DV)
        gg_ = nt(e[...], mo[at, :]) + nt(gad[...], ah[at, :])
        o = og[:, cols]
        act, sig = silu_parts(o)
        out[...] = (gg_ * act).astype(BF)
        m = mix[head].astype(F32)
        dog[:, cols] = (gg_ * m * sig * (1.0 + o * (1.0 - sig))).astype(BF)
        hidden_gated[:, cols] = (m * act).astype(BF)

    mix_copies = []
    for k in range(1, HEADS):
        peer = me ^ k
        gate_back(peer, sendm.at[k - 1])
        copy = to_peer(sendm.at[k - 1], dmr.at[rows(me * T, T)], ssem.at[0, k], rsem.at[0, k], peer)
        copy.start()
        mix_copies.append(copy)
    gate_back(me, dmr.at[rows(me * T, T)])

    l_af.wait()
    l_ao.wait()
    normed_mid = (mv * inverse_rms(mv)).astype(BF)
    gh[:, VALUE_WIDTH:] = tn(gdown16, hidden[...])
    gm[4 * ADAPTER_RANK : 5 * ADAPTER_RANK, :] = tn(narrow(gg), normed_mid)
    gm[5 * ADAPTER_RANK : 6 * ADAPTER_RANK, :] = tn(narrow(gu2), normed_mid)
    gp[:, U_G : U_G + HIDDEN_UNITS] = tn(narrow(af[:, 0:ADAPTER_COLUMNS]), wide[:, gate_cols])
    gp[:, U_U : U_U + HIDDEN_UNITS] = tn(narrow(af[:, ADAPTER_COLUMNS:]), wide[:, up_cols])
    gp[:, U_O : U_O + MODEL_WIDTH] = tn(narrow(ao[...]), e[...])
    gh[:, 0:VALUE_WIDTH] = tn(narrow(gad[...]), hidden_gated[...])

    for c in l_mixer:
        c.wait()
    f2h = f2[:, lanes(me * DK, DK)]
    bh = bias[:, lanes(me * DK, DK)]
    for src in range(HEADS):
        lg = tn(gl[src], f2h) + bh
        logit[src * T : (src + 1) * T, :] = lg
        fg[src * T : (src + 1) * T, :] = (jax.nn.log_sigmoid(lg) / 16.0).astype(BF)
    tri = lower_triangle(BF)
    causal = lower_triangle(F32)
    for c in mix_copies:
        c.wait_recv()
    gstate[...] = jnp.zeros_like(gstate)

    def retreat(i, carry):
        n = n_blocks - 1 - i
        at = pl.ds(meta[n_blocks + n] * GROUP, GROUP)
        here = rows(n * GROUP, GROUP)
        dm = dmr[at, :].astype(F32)
        yv = yh[at, :].astype(F32)
        r = rh[at, 0:1]
        do = (r * (dm - yv * jnp.mean(dm * yv, axis=-1, keepdims=True))).astype(BF)
        don[here, :] = do
        summed = nn(tri, fg[at, :])
        total = jnp.exp(summed[GROUP - 1 : GROUP])
        qs = (qkv[at, 0:DK].astype(F32) * SCALE * jnp.exp(summed)).astype(BF)
        now = gstate[...]
        gt[n] = now.astype(BF)
        decayed = total * now
        dt[n] = jnp.sum(decayed * st[n].astype(F32), axis=0, keepdims=True)
        gstate[...] = decayed + tn(do, qs)
        return carry

    lax.fori_loop(0, n_blocks, retreat, 0, unroll=4)

    def back_block(p, out, j):
        n = meta[p]
        at = rows(p * GROUP, GROUP)
        here = pl.ds(n * GROUP, GROUP)
        to = rows(j * GROUP, GROUP)
        live = live_rows(n, length)
        summed = nn(tri, fg[at, :])
        middle = summed[GROUP // 2 : GROUP // 2 + 1]
        total = summed[GROUP - 1 : GROUP]
        e1, e2 = jnp.exp(summed - middle), jnp.exp(middle - summed)
        es, eu = jnp.exp(summed), jnp.exp(total - summed)
        q = qkv[at, 0:DK].astype(F32) * SCALE
        k = qkv[at, DK : 2 * DK].astype(F32) * live
        v = qkv[at, 2 * DK : CHUNK]
        do, state_t, grad_t = don[here, :], st[n], gt[n]
        qe, ke, qs, ku = q * e1, k * e2, q * es, k * eu
        qeb, keb = qe.astype(BF), ke.astype(BF)
        scores = jnp.where(causal > 0, nt(qeb, keb), 0.0).astype(BF)
        dscores = jnp.where(causal > 0, nt(do, v), 0.0).astype(BF)
        dv = tn(scores, do) + nt(ku.astype(BF), grad_t)
        dqs = nn(do, state_t)
        dku = nn(v, grad_t)
        dqe = nn(dscores, keb)
        dke = tn(dscores, qeb)
        out[to, 0:DK] = (SCALE * (dqe * e1 + dqs * es)).astype(BF)
        out[to, DK : 2 * DK] = (live * (dke * e2 + dku * eu)).astype(BF)
        out[to, 2 * DK : CHUNK] = dv.astype(BF)
        kk = dku * ku
        dsum = dqe * qe + dqs * qs - dke * ke - kk
        dtotal = dt[n] + jnp.sum(kk, axis=0, keepdims=True)
        high = dsum.astype(BF)
        lowp = (dsum - high.astype(F32)).astype(BF)
        df = tn(tri, high) + tn(tri, lowp) + dtotal
        df = df.astype(BF).astype(F32)
        dlog[to, :] = (df * lax.logistic(-logit[at, :]) / 16.0).astype(BF)

    q_copies = []

    def back_rows(dest, out, low_out):
        lax.fori_loop(0, per, lambda j, c: (back_block(dest * per + j, out, j), c)[1], 0, unroll=2)
        low_out[...] = nt(f2h, dlog[...]).astype(BF)

    for k in range(1, HEADS):
        peer = me ^ k
        back_rows(peer, sendq.at[k - 1], sendl.at[k - 1])
        copies = (
            to_peer(sendq.at[k - 1], dqkv.at[me], ssem.at[1, k], rsem.at[1, k], peer),
            to_peer(sendl.at[k - 1], dlr.at[me], ssem.at[2, k], rsem.at[2, k], peer),
        )
        for copy in copies:
            copy.start()
        q_copies += copies
    back_rows(me, dqkv.at[me], dlr.at[me])

    for c in l_last:
        c.wait()
    hv = h[...].astype(F32)
    hr = inverse_rms(hv)
    big[...] = (hv * hr).astype(BF)
    for c in q_copies:
        c.wait_recv()
    for hd in range(HEADS):
        dproj[:, hd * DK : (hd + 1) * DK] = dqkv[hd, :, 0:DK]
        dproj[:, KEY + hd * DK : KEY + (hd + 1) * DK] = dqkv[hd, :, DK : 2 * DK]
        dproj[:, 2 * KEY + hd * DV : 2 * KEY + (hd + 1) * DV] = dqkv[hd, :, 2 * DK : CHUNK]
    dproj[:, 2 * KEY + VALUE_WIDTH :] = dog[...]
    dlow = dlr[0].astype(F32)
    for hd in range(1, HEADS):
        dlow += dlr[hd].astype(F32)
    dlowb = dlow.astype(BF)
    spans = ((0, KEY), (KEY, KEY), (2 * KEY, VALUE_WIDTH), (2 * KEY + VALUE_WIDTH, VALUE_WIDTH))
    for p, (start, width) in enumerate(spans):
        block = slice(p * ADAPTER_COLUMNS, (p + 1) * ADAPTER_COLUMNS)
        piece = dproj[:, start : start + width]
        ga = (nt(piece, au[:, start : start + width]).astype(BF).astype(F32) * mask).astype(BF)
        wide[:, block] = ga
        gm[p * ADAPTER_RANK : (p + 1) * ADAPTER_RANK, :] = tn(narrow(ga), big[...])
        gp[:, start : start + width] = tn(narrow(ad[:, block]), piece)
    z_w = f1.shape[2]
    tiles = f1.shape[0]
    back = []
    for j in range(tiles):
        at = slice(j * z_w, (j + 1) * z_w)
        back.append(
            nt(dproj[...], mi[at, :]) + nt(wide[:, 0 : 4 * ADAPTER_COLUMNS], am[at, 0 : 4 * ADAPTER_COLUMNS]) + tn(dlowb, f1[j])
        )
    dn_ = jnp.concatenate(back, axis=1)
    n = hv * hr
    e[...] = (grad[...] + hr * (dn_ - n * jnp.mean(dn_ * n, axis=-1, keepdims=True))).astype(BF)
    for a, b in ((e, e_out), (gm, gm_out), (gh, gh_out), (gp, gp_out)):
        loc.start(a, b, True)
    loc.finish()
    for c in mix_copies + q_copies:
        c.wait_send()


def backward(layer, meta, d, h, weights, saved):
    T = h.shape[0]
    L = T * HEADS
    n_blocks = L // GROUP
    outs = [
        ((T, MODEL_WIDTH), BF),
        ((6 * ADAPTER_RANK, MODEL_WIDTH), F32),
        ((ADAPTER_RANK, VALUE_WIDTH + HIDDEN_UNITS), F32),
        ((ADAPTER_RANK, U_D + MODEL_WIDTH), F32),
    ]
    vm = pltpu.VMEM
    dma = pltpu.SemaphoreType.DMA
    return pl.pallas_call(
        functools.partial(backward_kernel, layer, n_blocks),
        out_shape=[jax.ShapeDtypeStruct(*s) for s in outs],
        in_specs=[pl.BlockSpec(memory_space=pltpu.SMEM)] + [ANY] * (2 + len(weights) + len(saved)),
        out_specs=[ANY] * len(outs),
        scratch_shapes=[vm(d.shape, d.dtype), vm(h.shape, h.dtype)]
        + weight_scratch(weights)
        + [vm(s.shape, s.dtype) for s in saved]
        + [vm(*s) for s in outs]
        + [
            vm((T, HIDDEN_UNITS), BF),
            vm((T, 2 * HIDDEN_UNITS), BF),
            vm((T, ADAPTER_COLUMNS), BF),
            vm((T, MODEL_WIDTH), BF),
            vm((T, MODEL_WIDTH), F32),
            vm((T, VALUE_WIDTH), BF),
            vm((HEADS - 1, T, DV), BF),
            vm((L, DV), BF),
            vm((L, DK), F32),
            vm((L, DK), BF),
            vm((DV, DK), F32),
            vm((n_blocks, DV, DK), BF),
            vm((n_blocks, 1, DK), F32),
            vm((L, DV), BF),
            vm((T, VALUE_WIDTH), BF),
            vm((HEADS - 1, T, CHUNK), BF),
            vm((HEADS, T, CHUNK), BF),
            vm((T, DK), BF),
            vm((HEADS - 1, FGATE_RANK, T), BF),
            vm((HEADS, FGATE_RANK, T), BF),
            vm((T, FROZEN), BF),
            dma((2 + len(weights) + len(saved) + len(outs),)),
            dma((3, HEADS)),
            dma((3, HEADS)),
        ],
        compiler_params=pltpu.CompilerParams(
            collective_id=3 + layer, has_side_effects=True, vmem_limit_bytes=VMEM_LIMIT
        ),
        cost_estimate=pl.CostEstimate(flops=2 * T * 16_000_000, bytes_accessed=45 << 20, transcendentals=T * 8192),
    )(meta, d, h, *weights, *saved)


def swap_sections(v):
    return lax.ppermute(v, "section", [(0, 1), (1, 0)])


def plain_gather(shards, f1t, ends, small):
    first = lax.axis_index("section") == 0
    both = lambda a: lax.all_gather(a, "section", axis=0)
    outs = [both(lax.all_gather(w[0], "dp", axis=0, tiled=True)) for w in shards]
    low = lax.all_gather(f1t, "dp", axis=1, tiled=True)
    outs.append(both(jnp.stack(jnp.split(low, 4, axis=1))))
    sent = swap_sections(jnp.where(first, ends[0, 1, 0], ends[0, 0, 0]))
    outs.append(jnp.where(first, ends[0, 0, 0], sent))
    outs.append(jnp.where(first, sent, ends[0, 1, 0]))
    return outs + [both(a[0]) for a in small]


def spread(parts, chosen):
    hot = (chosen[:, None] == jnp.arange(ADAPTERS, dtype=jnp.int32)[None, :]).astype(F32)
    return sum(parts[n][:, None] * hot[n][None, :, None, None] for n in range(parts.shape[0]))


def reduce_gradients(early, late, chosen, first):
    n_dp, n_seq = lax.axis_size("dp"), lax.axis_size("seq")
    dp = lax.axis_index("dp")
    kept = [jnp.where(first, b, a) for a, b in zip(early, late)]
    got = [swap_sections(jnp.where(first, a, b)) for a, b in zip(early, late)]
    gm, gh, gp = [jnp.stack(pair) for pair in zip(kept, got)]
    wide = gp.shape[-1] // (n_dp * n_seq)
    gm = lax.psum_scatter(gm, "seq", scatter_dimension=2, tiled=True)
    gh = lax.psum_scatter(gh, "seq", scatter_dimension=2, tiled=True)
    gp = jnp.transpose(gp.reshape(2, ADAPTER_RANK, n_dp, n_seq, wide), (3, 2, 0, 1, 4))
    gp = lax.psum_scatter(gp, "seq", scatter_dimension=0, tiled=True)[0]
    gm = lax.all_gather(gm, "dp", axis=0)
    gh = lax.all_gather(gh, "dp", axis=0)
    gp = lax.all_to_all(gp, "dp", split_axis=0, concat_axis=0, tiled=True)
    chosen = chosen.reshape(-1)
    n = chosen.shape[0]
    gm = spread(gm.reshape(n, 6, ADAPTER_RANK, -1), chosen).reshape(6 * ADAPTER_COLUMNS, -1)
    gh = spread(gh.reshape(n, 1, ADAPTER_RANK, -1), chosen).reshape(ADAPTER_COLUMNS, -1)
    gp = spread(gp.reshape(n, 1, ADAPTER_RANK, -1), chosen).reshape(ADAPTER_COLUMNS, -1)

    def columns(v):
        size = v.shape[0] // n_dp
        v = lax.dynamic_slice_in_dim(v, dp * size, size, 0)
        return lax.all_to_all(v, "seq", split_axis=0, concat_axis=1, tiled=True).T

    return columns(gm), columns(gh), gp


def local(
    ends,
    mixer_input_weight,
    forget_first_map,
    forget_second_map,
    forget_logit_bias,
    mixer_output_weight,
    feedforward_input_weight,
    feedforward_output_weight,
    adapter_model_first,
    adapter_hidden_first,
    adapter_second_maps,
    lengths,
    dealt_block_order,
    adapter_choice_per_seq,
):
    first = lax.axis_index("section") == 0
    mine = lambda a: jnp.where(first, a[0], a[1])
    order = mine(dealt_block_order)[0]
    n_blocks = order.shape[0]
    at = jnp.arange(n_blocks, dtype=jnp.int32)
    inverse = jnp.sum(at[:, None] * (order[:, None] == at[None, :]).astype(jnp.int32), axis=0)
    meta = jnp.concatenate([order, inverse, mine(adapter_choice_per_seq), mine(lengths)])
    picks = lax.all_gather(adapter_choice_per_seq[:, 0], "dp", axis=0)
    picks = jnp.where(first, picks, picks[:, ::-1])
    shards = [mixer_input_weight, mixer_output_weight, feedforward_input_weight, feedforward_output_weight]
    small = [
        forget_second_map,
        forget_logit_bias[:, None],
        adapter_model_first,
        adapter_hidden_first,
        adapter_second_maps,
    ]
    gather = gather_all if lax.axis_size("dp") == 4 and lax.axis_size("seq") == 4 else plain_gather
    out = gather(shards, forget_first_map[0].T, ends, small)
    weights = list(out[:5]) + list(out[7:])
    x, cotangent = out[5], out[6]
    early = forward(0, meta, x, weights)
    late = forward(1, meta, early[0], weights)
    middle, *grads_late = backward(1, meta, cotangent, early[0], weights, late[1:])
    entry, *grads_early = backward(0, meta, middle, x, weights, early[1:])
    sent = swap_sections(jnp.where(first, late[0], entry))
    results = jnp.where(first, jnp.stack([entry, sent]), jnp.stack([sent, late[0]]))
    model, hidden, up = reduce_gradients(grads_late, grads_early, picks, first)
    return (results[None, :, None], model[None], hidden[None], up[None])


def solution(mesh):
    return jax.shard_map(
        local,
        mesh=mesh,
        in_specs=(
            P("section", None, "dp", "seq", None),
            P("section", "dp", None),
            P("section", "dp", None),
            P("section", None, None),
            P("section", None),
            P("section", "dp", None),
            P("section", "dp", None),
            P("section", "dp", None),
            P("section", None, None),
            P("section", None, None),
            P("section", None, None),
            P(None, "dp"),
            P(None, "dp", None),
            P(None, "dp"),
        ),
        out_specs=(
            P("section", None, "dp", "seq", None),
            P("section", None, ("dp", "seq")),
            P("section", None, ("dp", "seq")),
            P("section", None, ("dp", "seq")),
        ),
        check_vma=False,
    )
```

```python
import functools
import jax
import jax.numpy as jnp
from jax import lax
from jax.experimental import pallas as pl
from jax.experimental.pallas import tpu as pltpu

from jax.sharding import PartitionSpec as P

MODEL_WIDTH = 1024
HEADS = 4
KEY = 512
VALUE_WIDTH = 1024
HIDDEN_UNITS = 2816
FGATE_RANK = 16
GROUP = 64
ADAPTER_RANK = 16
ADAPTERS = 8
ADAPTER_COLUMNS = 128
VMEM_LIMIT = 60 << 20

MESH = pl.DeviceIdType.MESH
ANY = pl.BlockSpec(memory_space=pl.ANY)


def gather_kernel(*refs):
    n_w, n_s = 4, 6
    shards = refs[:n_w]
    f1_ref, ends_ref = refs[n_w : n_w + 2]
    small = refs[n_w + 2 : n_w + 2 + n_s - 1]
    at = n_w + 2 + len(small)
    outs = refs[at : at + n_w]
    f1_out, x_out, c_out = refs[at + n_w : at + n_w + 3]
    small_out = refs[at + n_w + 3 : at + n_w + 3 + len(small)]
    at += n_w + 3 + len(small)
    held, held_small, held_ends, held_f1 = refs[at : at + n_w], refs[at + n_w : at + n_w + len(small)], refs[-23], refs[-22]
    ins = refs[-21]
    (zs, zr, xs, xr, ys, yr, fxs, fxr, fys, fyr, cs, cr, own, ms, mr, es, er, f1s, f1r, f1c) = refs[-20:]
    core, z, s = lax.axis_index("section"), lax.axis_index("dp"), lax.axis_index("seq")
    other = 1 - core
    n_z = 4
    fetch = [pltpu.make_async_copy(shards[w].at[0], held[w], ins.at[w]) for w in range(n_w)]
    fetch += [pltpu.make_async_copy(a.at[0], b, ins.at[n_w + i]) for i, (a, b) in enumerate(zip(small, held_small))]
    fetch.append(pltpu.make_async_copy(ends_ref.at[0, :, 0], held_ends, ins.at[n_w + len(small)]))
    fetch.append(pltpu.make_async_copy(f1_ref, held_f1, ins.at[n_w + len(small) + 1]))
    for f in fetch:
        f.start()
    barrier = pltpu.get_barrier_semaphore()

    def greet(**where):
        pl.semaphore_signal(barrier, inc=1, device_id=where, device_id_type=MESH)

    greet(section=other)
    greet(seq=s ^ 1)
    greet(seq=s ^ 2)
    for gap in range(1, n_z):
        greet(dp=lax.rem(z + gap, n_z))
    pl.semaphore_wait(barrier, 3 + n_z - 1)

    finals = []

    def remote(src, dst, ssem, rsem, **where):
        return pltpu.make_async_remote_copy(
            src_ref=src, dst_ref=dst, send_sem=ssem, recv_sem=rsem, device_id=where, device_id_type=MESH
        )

    def rows_of(w, j):
        return shards[w].shape[1] * j

    def piece(w, j, q):
        r = shards[w].shape[1]
        return outs[w].at[core, pl.ds(pl.multiple_of(j * r + q * (r // 4), 16), r // 4)]

    def half(w, j, q, low):
        r = shards[w].shape[1]
        cut = (r // 8 + 15) // 16 * 16
        start, size = (0, cut) if low else (cut, r // 4 - cut)
        return outs[w].at[core, pl.ds(pl.multiple_of(j * r + q * (r // 4) + start, 16), size)]

    def block(w, j):
        r = shards[w].shape[1]
        return outs[w].at[core, pl.ds(pl.multiple_of(j * r, 16), r)]

    def own_shard(w):
        return held[w]

    def own_piece(w):
        r = shards[w].shape[1]
        return held[w].at[pl.ds(pl.multiple_of(s * (r // 4), 16), r // 4)]

    def step(d):
        return 1 if d == 0 else -1

    def can_send(d, t):
        has_next = (z < n_z - 1) if d == 0 else (z > 0)
        origin = z - step(d) * (t - 1)
        return jnp.logical_and(has_next, jnp.logical_and(origin >= 0, origin < n_z))

    def gets(d, t):
        origin = z - step(d) * t
        return jnp.logical_and(origin >= 0, origin < n_z)

    def z_copy(w, d, t):
        j = z - step(d) * (t - 1)
        src = own_piece(w) if t == 1 else piece(w, j, s)
        return remote(src, piece(w, j, s), zs.at[w, d, t - 1], zr.at[w, d, t - 1], dp=z + step(d))

    def origin(d, t):
        return z - step(d) * t

    def x_copy(w, d, t):
        return remote(piece(w, origin(d, t), s), piece(w, origin(d, t), s), xs.at[w, d, t - 1], xr.at[w, d, t - 1], seq=s ^ 1)

    def y_copy(w, d, t):
        return remote(piece(w, origin(d, t), s), piece(w, origin(d, t), s), ys.at[w, d, t - 1], yr.at[w, d, t - 1], seq=s ^ 2)

    def fx_copy(w, d, t):
        ref = half(w, origin(d, t), s ^ 2, False)
        return remote(ref, ref, fxs.at[w, d, t - 1], fxr.at[w, d, t - 1], seq=s ^ 1)

    def fy_copy(w, d, t):
        ref = half(w, origin(d, t), s ^ 1, True)
        return remote(ref, ref, fys.at[w, d, t - 1], fyr.at[w, d, t - 1], seq=s ^ 2)

    def c_copy(w, d, t):
        if t == 0:
            return remote(own_shard(w), block(w, z), cs.at[w, 0, 3], cr.at[w, 0, 3], section=other)
        ref = block(w, origin(d, t))
        return remote(ref, ref, cs.at[w, d, t - 1], cr.at[w, d, t - 1], section=other)

    def own_copy(w):
        return pltpu.make_async_copy(own_shard(w), block(w, z), own.at[w])

    def start_own(w):
        for d in range(2):
            @pl.when(can_send(d, 1))
            def _():
                z_copy(w, d, 1).start()

    def take_z(w, t):
        for d in range(2):
            @pl.when(gets(d, t))
            def _():
                z_copy(w, d, t).wait_recv()
            if t < n_z - 1:
                @pl.when(can_send(d, t + 1))
                def _():
                    z_copy(w, d, t + 1).start()
            @pl.when(gets(d, t))
            def _():
                x_copy(w, d, t).start()
                y_copy(w, d, t).start()

    def take_xy(w, t):
        for d in range(2):
            @pl.when(gets(d, t))
            def _():
                x_copy(w, d, t).wait_recv()
                fy_copy(w, d, t).start()
                y_copy(w, d, t).wait_recv()
                fx_copy(w, d, t).start()

    def take_diagonal(w, t):
        for d in range(2):
            @pl.when(gets(d, t))
            def _():
                fy_copy(w, d, t).wait_recv()
                fx_copy(w, d, t).wait_recv()
                c_copy(w, d, t).start()

    ends_to_x = remote(held_ends.at[1], x_out, es, er, section=other)
    ends_to_c = remote(held_ends.at[0], c_out, es, er, section=other)
    ends_x = pltpu.make_async_copy(held_ends.at[0], x_out, own.at[n_w])
    ends_c = pltpu.make_async_copy(held_ends.at[1], c_out, own.at[n_w])

    for f in fetch:
        f.wait()
    start_own(0)
    @pl.when(core == 0)
    def _():
        ends_to_x.start()
        ends_x.start()

    @pl.when(core == 1)
    def _():
        ends_to_c.start()
        ends_c.start()

    def f1_copy(gap):
        return remote(
            held_f1, f1_out.at[core, z], f1s.at[gap], f1r.at[gap], dp=lax.rem(z + gap, n_z)
        )
    for gap in range(1, n_z):
        f1_copy(gap).start()
    f1_own = pltpu.make_async_copy(held_f1, f1_out.at[core, z], own.at[n_w + 1])
    f1_own.start()
    smalls = []
    for i, (a, b) in enumerate(zip(held_small, small_out)):
        mine = pltpu.make_async_copy(a, b.at[core], own.at[n_w + 2 + i])
        theirs = remote(a, b.at[core], ms.at[i], mr.at[i], section=other)
        mine.start()
        theirs.start()
        smalls.append((mine, theirs))
    for w in range(n_w):
        own_copy(w).start()
        c_copy(w, 0, 0).start()
    items = [(w, t) for w in range(n_w) for t in range(1, n_z)]
    f1_sends = [f1_copy(gap) for gap in range(1, n_z)]
    f1_cross = remote(f1_out.at[core], f1_out.at[core], f1c.at[0], f1c.at[1], section=other)
    for i in range(len(items) + 2):
        if i < len(items):
            w, t = items[i]
            if t == 1 and w + 1 < n_w:
                start_own(w + 1)
            take_z(w, t)
        if 0 <= i - 1 < len(items):
            take_xy(*items[i - 1])
        if 0 <= i - 2 < len(items):
            take_diagonal(*items[i - 2])
        if i == 1:
            f1_own.wait()
            for c in f1_sends:
                c.wait_recv()
            f1_cross.start()
    for w in range(n_w):
        own_copy(w).wait()
        c_copy(w, 0, 0).wait()
        for d in range(2):
            for t in range(1, n_z):
                @pl.when(can_send(d, t))
                def _():
                    z_copy(w, d, t).wait_send()
                @pl.when(gets(d, t))
                def _():
                    x_copy(w, d, t).wait_send()
                    y_copy(w, d, t).wait_send()
                    fx_copy(w, d, t).wait_send()
                    fy_copy(w, d, t).wait_send()
                    c_copy(w, d, t).wait()
    for mine, theirs in smalls:
        mine.wait()
        theirs.wait()
    for c in f1_sends:
        c.wait_send()
    f1_cross.wait()
    ends_x.wait()
    ends_to_x.wait()


def gather_all(shards, f1t, ends, small):
    n_w = 4
    shape = jax.ShapeDtypeStruct
    outs = [shape((2, 4 * w.shape[1], w.shape[2]), w.dtype) for w in shards]
    outs.append(shape((2, 4) + f1t.shape, f1t.dtype))
    outs += [shape(ends.shape[3:], ends.dtype)] * 2
    outs += [shape((2,) + a.shape[1:], a.dtype) for a in small]
    dma = pltpu.SemaphoreType.DMA
    per = [dma((n_w, 2, 3)) for _ in range(10)] + [dma((n_w, 2, 4)) for _ in range(2)]
    return pl.pallas_call(
        gather_kernel,
        out_shape=outs,
        in_specs=[ANY] * (n_w + 2 + len(small)),
        out_specs=[ANY] * len(outs),
        scratch_shapes=[pltpu.VMEM(w.shape[1:], w.dtype) for w in shards]
        + [pltpu.VMEM(a.shape[1:], a.dtype) for a in small]
        + [pltpu.VMEM((2,) + ends.shape[3:], ends.dtype), pltpu.VMEM(f1t.shape, f1t.dtype)]
        + [dma((n_w + len(small) + 2,))]
        + per
        + [dma((n_w + 2 + len(small),)), dma((len(small),)), dma((len(small),)), dma, dma, dma((4,)), dma((4,)), dma((2,))],
        compiler_params=pltpu.CompilerParams(collective_id=0, has_side_effects=True, vmem_limit_bytes=VMEM_LIMIT),
    )(*shards, f1t, ends, *small)


BF = jnp.bfloat16
F32 = jnp.float32


def nn(a, b):
    return lax.dot_general(a, b, (((1,), (0,)), ((), ())), preferred_element_type=F32)


def nt(a, b):
    return lax.dot_general(a, b, (((1,), (1,)), ((), ())), preferred_element_type=F32)


def tn(a, b):
    return lax.dot_general(a, b, (((0,), (0,)), ((), ())), preferred_element_type=F32)


def silu_parts(v):
    sig = lax.logistic(v)
    return v * sig, sig


def inverse_rms(v):
    return lax.rsqrt(jnp.mean(v * v, axis=-1, keepdims=True) + 1e-06)


def rms_back(v, grad):
    r = inverse_rms(v)
    n = v * r
    return r * (grad - n * jnp.mean(grad * n, axis=-1, keepdims=True))


def lanes(start, size):
    return pl.ds(pl.multiple_of(start, 128), size)


def rows(start, size):
    return pl.ds(pl.multiple_of(start, size if size <= 64 else 64), size)


def greet_peers(me):
    barrier = pltpu.get_barrier_semaphore()
    for d in range(1, HEADS):
        pl.semaphore_signal(barrier, inc=1, device_id={"seq": me ^ d}, device_id_type=MESH)
    pl.semaphore_wait(barrier, HEADS - 1)


def to_peer(src, dst, ssem, rsem, peer):
    return pltpu.make_async_remote_copy(
        src_ref=src, dst_ref=dst, send_sem=ssem, recv_sem=rsem,
        device_id={"seq": peer}, device_id_type=MESH,
    )


class Local:
    def __init__(self, sems):
        self.sems, self.used, self.open = sems, 0, []

    def start(self, src, dst, wait_at_end=False):
        copy = pltpu.make_async_copy(src, dst, self.sems.at[self.used])
        self.used += 1
        copy.start()
        if wait_at_end:
            self.open.append(copy)
        return copy

    def finish(self):
        for copy in self.open:
            copy.wait()


def picked(adapter, width):
    row = lax.broadcasted_iota(jnp.int32, (width, ADAPTER_RANK), 0)
    col = lax.broadcasted_iota(jnp.int32, (width, ADAPTER_RANK), 1)
    return (row == adapter * ADAPTER_RANK + col).astype(BF)


def column_mask(adapter):
    col = lax.broadcasted_iota(jnp.int32, (1, ADAPTER_COLUMNS), 1)
    low = adapter * ADAPTER_RANK
    return jnp.logical_and(col >= low, col < low + ADAPTER_RANK).astype(F32)


def lower_triangle(dtype):
    i = lax.broadcasted_iota(jnp.int32, (GROUP, GROUP), 0)
    j = lax.broadcasted_iota(jnp.int32, (GROUP, GROUP), 1)
    return (i >= j).astype(dtype)


DK = KEY // HEADS
DV = VALUE_WIDTH // HEADS
CHUNK = 2 * DK + DV
FROZEN = 2 * KEY + 2 * VALUE_WIDTH
TILE = 256
SCALE = DK ** (-0.5)

U_G = FROZEN
U_U = FROZEN + HIDDEN_UNITS
U_O = FROZEN + 2 * HIDDEN_UNITS
U_D = U_O + MODEL_WIDTH


def live_rows(n, length):
    at = lax.broadcasted_iota(jnp.int32, (GROUP, 1), 0) + n * GROUP
    return (at < length).astype(F32)


def forward_kernel(
    layer, n_blocks, meta, h_in, w_mi, w_mo, w_fi, w_fo, w_f1, w_f2, w_b, w_am, w_ah, w_au,
    y_out, o_ad, o_og, o_qkv, o_gl, o_st, o_mix, o_yh, o_rh, o_ao, o_mid, o_af, o_gu, o_dn,
    h, mi, mo, fi, fo, f1, f2, bias, am, ah, au,
    y, ad, og, qkv, gl, st, mix, yh, rh, ao, mid, af, gu, dn,
    normed, send, glsend, fg, state, gated, hidden,
    lsem, ssem, rsem,
):
    me = lax.axis_index("seq")
    T = h.shape[0]
    per = T // GROUP
    adapter = meta[2 * n_blocks]
    length = meta[2 * n_blocks + 1]
    loc = Local(lsem)
    l_h = loc.start(h_in, h)
    l_f1 = loc.start(w_f1.at[layer], f1)
    l_f2 = loc.start(w_f2.at[layer], f2)
    l_b = loc.start(w_b.at[layer], bias)
    l_am = loc.start(w_am.at[layer], am)
    l_au = loc.start(w_au.at[layer], au)
    l_mi = loc.start(w_mi.at[layer], mi)
    greet_peers(me)
    l_ah = loc.start(w_ah.at[layer], ah)
    l_mo = loc.start(w_mo.at[layer], mo)
    l_fi = loc.start(w_fi.at[layer], fi)
    l_fo = loc.start(w_fo.at[layer], fo)
    mask = column_mask(adapter)

    l_h.wait()
    hv = h[...].astype(F32)
    normed[...] = (hv * inverse_rms(hv)).astype(BF)
    l_f1.wait()
    z_w = f1.shape[2]
    low = nt(f1[0], normed[:, 0:z_w])
    for j in range(1, f1.shape[0]):
        low += nt(f1[j], normed[:, j * z_w : (j + 1) * z_w])
    glsend[...] = low.astype(BF)
    low_copies = [to_peer(glsend, gl.at[me], ssem.at[0, d], rsem.at[0, d], me ^ d) for d in range(1, HEADS)]
    for c in low_copies:
        c.start()
    gl[me] = glsend[...]
    l_am.wait()
    for p in range(4):
        cols = pl.ds(p * ADAPTER_COLUMNS, ADAPTER_COLUMNS)
        ad[:, cols] = (nn(normed[...], am[:, cols]) * mask).astype(BF)
    l_au.wait()
    l_mi.wait()

    def project(w_start, p, width):
        cols = lanes(w_start, width)
        return nn(normed[...], mi[:, cols]) + nn(ad[:, p * ADAPTER_COLUMNS : (p + 1) * ADAPTER_COLUMNS], au[:, cols])

    def chunk(head, ref):
        ref[:, 0:DK] = project(head * DK, 0, DK).astype(BF)
        ref[:, DK : 2 * DK] = project(KEY + head * DK, 1, DK).astype(BF)
        ref[:, 2 * DK : CHUNK] = project(2 * KEY + head * DV, 2, DV).astype(BF)

    qkv_copies = []
    for d in range(1, HEADS):
        chunk(me ^ d, send.at[d - 1])
        copy = to_peer(send.at[d - 1], qkv.at[rows(me * T, T)], ssem.at[1, d], rsem.at[1, d], me ^ d)
        copy.start()
        qkv_copies.append(copy)
    chunk(me, qkv.at[rows(me * T, T)])
    loc.start(ad, o_ad, True)
    for j in range(VALUE_WIDTH // TILE):
        og[:, j * TILE : (j + 1) * TILE] = project(2 * KEY + VALUE_WIDTH + j * TILE, 3, TILE)
    loc.start(og, o_og, True)
    l_f2.wait()
    l_b.wait()
    for c in low_copies:
        c.wait_recv()
    f2h = f2[:, lanes(me * DK, DK)]
    bh = bias[:, lanes(me * DK, DK)]
    for src in range(HEADS):
        logit = tn(gl[src], f2h) + bh
        fg[src * T : (src + 1) * T, :] = (jax.nn.log_sigmoid(logit) / 16.0).astype(BF)
    for c in qkv_copies:
        c.wait_recv()
    loc.start(gl, o_gl, True)
    loc.start(qkv, o_qkv, True)
    tri = lower_triangle(BF)
    causal = lower_triangle(F32)

    state[...] = jnp.zeros_like(state)

    def advance(n, carry):
        at = pl.ds(meta[n_blocks + n] * GROUP, GROUP)
        summed = nn(tri, fg[at, :])
        total = summed[GROUP - 1 : GROUP]
        k = qkv[at, DK : 2 * DK].astype(F32) * live_rows(n, length)
        ku = (k * jnp.exp(total - summed)).astype(BF)
        update = tn(qkv[at, 2 * DK : CHUNK], ku)
        now = state[...]
        st[n] = now.astype(BF)
        state[...] = jnp.exp(total) * now + update
        return carry

    lax.fori_loop(0, n_blocks, advance, 0, unroll=4)
    loc.start(st, o_st, True)

    def mix_block(p):
        n = meta[p]
        at = rows(p * GROUP, GROUP)
        summed = nn(tri, fg[at, :])
        middle = summed[GROUP // 2 : GROUP // 2 + 1]
        q = qkv[at, 0:DK].astype(F32) * SCALE
        k = qkv[at, DK : 2 * DK].astype(F32) * live_rows(n, length)
        qe = (q * jnp.exp(summed - middle)).astype(BF)
        ke = (k * jnp.exp(middle - summed)).astype(BF)
        scores = jnp.where(causal > 0, nt(qe, ke), 0.0).astype(BF)
        o = nn(scores, qkv[at, 2 * DK : CHUNK]) + nt((q * jnp.exp(summed)).astype(BF), st[n])
        r = lax.rsqrt(jnp.mean(o * o, axis=-1, keepdims=True) + 1.0)
        yh[at, :] = (o * r).astype(BF)
        rh[at, :] = jnp.broadcast_to(r, (GROUP, DK))

    mix_copies = []
    for d in range(1, HEADS):
        peer = me ^ d
        lax.fori_loop(0, per, lambda j, c, peer=peer: (mix_block(peer * per + j), c)[1], 0, unroll=True)
        copy = to_peer(yh.at[rows(peer * T, T)], mix.at[me], ssem.at[2, d], rsem.at[2, d], peer)
        copy.start()
        mix_copies.append(copy)
    lax.fori_loop(0, per, lambda j, c: (mix_block(me * per + j), c)[1], 0, unroll=True)
    mix[me] = yh[rows(me * T, T), :]
    loc.start(yh, o_yh, True)
    loc.start(rh, o_rh, True)
    for c in mix_copies:
        c.wait_recv()
    loc.start(mix, o_mix, True)
    for hd in range(HEADS):
        cols = slice(hd * DV, (hd + 1) * DV)
        gated[:, cols] = (mix[hd].astype(F32) * silu_parts(og[:, cols])[0]).astype(BF)
    l_ah.wait()
    l_mo.wait()
    ao[...] = (nn(gated[...], ah[0:VALUE_WIDTH, :]) * mask).astype(BF)
    for j in range(MODEL_WIDTH // TILE):
        cols = slice(j * TILE, (j + 1) * TILE)
        mid[:, cols] = (
            h[:, cols].astype(F32) + nn(gated[...], mo[:, cols]) + nn(ao[...], au[:, U_O + j * TILE : U_O + (j + 1) * TILE])
        )
    loc.start(ao, o_ao, True)
    loc.start(mid, o_mid, True)
    mv = mid[...]
    normed[...] = (mv * inverse_rms(mv)).astype(BF)
    for p in range(2):
        cols = slice(p * ADAPTER_COLUMNS, (p + 1) * ADAPTER_COLUMNS)
        wide = slice((4 + p) * ADAPTER_COLUMNS, (5 + p) * ADAPTER_COLUMNS)
        af[:, cols] = (nn(normed[...], am[:, wide]) * mask).astype(BF)
    loc.start(af, o_af, True)
    l_fi.wait()

    def up_tile(i, carry):
        a, b = lanes(i * TILE, TILE), lanes(HIDDEN_UNITS + i * TILE, TILE)
        gate = nn(normed[...], fi[:, a]) + nn(af[:, 0:ADAPTER_COLUMNS], au[:, lanes(U_G + i * TILE, TILE)])
        up = nn(normed[...], fi[:, b]) + nn(af[:, ADAPTER_COLUMNS:], au[:, lanes(U_U + i * TILE, TILE)])
        gu[:, a] = gate.astype(gu.dtype)
        gu[:, b] = up.astype(gu.dtype)
        hidden[:, a] = (silu_parts(gate)[0] * up).astype(BF)
        return carry

    lax.fori_loop(0, HIDDEN_UNITS // TILE, up_tile, 0)
    loc.start(gu, o_gu, True)
    l_fo.wait()
    dn[...] = (nn(hidden[...], ah[VALUE_WIDTH:, :]) * mask).astype(BF)
    loc.start(dn, o_dn, True)
    for j in range(MODEL_WIDTH // TILE):
        cols = slice(j * TILE, (j + 1) * TILE)
        y[:, cols] = (
            mid[:, cols] + nn(hidden[...], fo[:, cols]) + nn(dn[...], au[:, U_D + j * TILE : U_D + (j + 1) * TILE])
        ).astype(BF)
    loc.start(y, y_out, True)
    loc.finish()
    for c in low_copies + qkv_copies + mix_copies:
        c.wait_send()


def weight_scratch(weights):
    return [pltpu.VMEM(w.shape[1:], w.dtype) for w in weights]


def saved_shapes(T, L, n_blocks):
    s = lambda shape, dtype=BF: (shape, dtype)
    return [
        s((T, MODEL_WIDTH)),
        s((T, 4 * ADAPTER_COLUMNS)),
        s((T, VALUE_WIDTH), F32),
        s((L, CHUNK)),
        s((HEADS, FGATE_RANK, T)),
        s((n_blocks, DV, DK)),
        s((HEADS, T, DV)),
        s((L, DV)),
        s((L, DK), F32),
        s((T, ADAPTER_COLUMNS)),
        s((T, MODEL_WIDTH), F32),
        s((T, 2 * ADAPTER_COLUMNS)),
        s((T, 2 * HIDDEN_UNITS)),
        s((T, ADAPTER_COLUMNS)),
    ]


def forward(layer, meta, h, weights):
    T = h.shape[0]
    L = T * HEADS
    n_blocks = L // GROUP
    saved = saved_shapes(T, L, n_blocks)
    vm = pltpu.VMEM
    dma = pltpu.SemaphoreType.DMA
    return pl.pallas_call(
        functools.partial(forward_kernel, layer, n_blocks),
        out_shape=[jax.ShapeDtypeStruct(*s) for s in saved],
        in_specs=[pl.BlockSpec(memory_space=pltpu.SMEM)] + [ANY] * (1 + len(weights)),
        out_specs=[ANY] * len(saved),
        scratch_shapes=[vm(h.shape, h.dtype)]
        + weight_scratch(weights)
        + [vm(*s) for s in saved]
        + [
            vm((T, MODEL_WIDTH), BF),
            vm((HEADS - 1, T, CHUNK), BF),
            vm((FGATE_RANK, T), BF),
            vm((L, DK), BF),
            vm((DV, DK), F32),
            vm((T, VALUE_WIDTH), BF),
            vm((T, HIDDEN_UNITS), BF),
            dma((1 + len(weights) + len(saved),)),
            dma((3, HEADS)),
            dma((3, HEADS)),
        ],
        compiler_params=pltpu.CompilerParams(
            collective_id=1 + layer, has_side_effects=True, vmem_limit_bytes=VMEM_LIMIT
        ),
        cost_estimate=pl.CostEstimate(flops=2 * T * 13_000_000, bytes_accessed=40 << 20, transcendentals=T * 8192),
    )(meta, h, *weights)


def backward_kernel(
    layer, n_blocks, meta, d_in, h_in, w_mi, w_mo, w_fi, w_fo, w_f1, w_f2, w_b, w_am, w_ah, w_au,
    i_ad, i_og, i_qkv, i_gl, i_st, i_mix, i_yh, i_rh, i_ao, i_mid, i_af, i_gu, i_dn,
    e_out, gm_out, gh_out, gp_out,
    d, h, mi, mo, fi, fo, f1, f2, bias, am, ah, au,
    ad, og, qkv, gl, st, mix, yh, rh, ao, mid, af, gu, dn,
    e, sgm, sgh, sgp,
    gm, gh, gp, gps, rgm, rgh, rgp, hidden, wide, gad, big, grad, dog, sendm, dmr, logit, fg, gstate, gt, dt, don, hidden_gated, sendq, dqkv, dlog, sendl, dlr, dproj,
    lsem, ssem, rsem, gssem, grsem,
):
    me = lax.axis_index("seq")
    T = h.shape[0]
    per = T // GROUP
    adapter = meta[2 * n_blocks]
    length = meta[2 * n_blocks + 1]
    loc = Local(lsem)
    l_d = loc.start(d_in, d)
    l_au = loc.start(w_au.at[layer], au)
    l_ah = loc.start(w_ah.at[layer], ah)
    l_fo = loc.start(w_fo.at[layer], fo)
    l_gu = loc.start(i_gu, gu)
    l_dn = loc.start(i_dn, dn)
    greet_peers(me)
    l_fi = loc.start(w_fi.at[layer], fi)
    l_am = loc.start(w_am.at[layer], am)
    l_mid = loc.start(i_mid, mid)
    l_af = loc.start(i_af, af)
    l_mo = loc.start(w_mo.at[layer], mo)
    l_og = loc.start(i_og, og)
    l_mix = loc.start(i_mix, mix)
    l_ao = loc.start(i_ao, ao)
    l_mixer = [
        loc.start(a, b)
        for a, b in (
            (w_f2.at[layer], f2), (w_b.at[layer], bias), (i_qkv, qkv), (i_gl, gl), (i_st, st), (i_yh, yh), (i_rh, rh),
        )
    ]
    l_last = [
        loc.start(a, b) for a, b in ((w_mi.at[layer], mi), (w_f1.at[layer], f1), (i_ad, ad), (h_in, h))
    ]
    mask = column_mask(adapter)
    pick = picked(adapter, ADAPTER_COLUMNS)

    def narrow(v):
        return nn(v, pick).astype(BF)

    def outer(u, v):
        return tn(narrow(u), v).astype(BF)

    n_dp, width, padded = gps.shape[1], gp.shape[1] // (HEADS * gps.shape[1]), gps.shape[3]
    quarter, hidden_quarter = MODEL_WIDTH // HEADS, gh.shape[1] // HEADS
    n_late = -(-FROZEN // (HEADS * width))
    mix_rows = 4 * ADAPTER_RANK

    def place(dps):
        for i in dps:
            for q in range(HEADS):
                piece = gp[:, (i * HEADS + q) * width : (i * HEADS + q + 1) * width]
                gps[q, i] = jnp.concatenate([piece, jnp.zeros((ADAPTER_RANK, padded - width), BF)], axis=1)

    def grad_copies(late):
        copies = []
        at = slice(0, mix_rows) if late else slice(mix_rows, 6 * ADAPTER_RANK)
        dps = slice(0, n_late) if late else slice(n_late, n_dp)
        for k in range(1, HEADS):
            peer = me ^ k
            pairs = [
                (gm.at[at, lanes(peer * quarter, quarter)], rgm.at[k - 1, at]),
                (gps.at[peer, dps], rgp.at[k - 1, dps]),
            ]
            if not late:
                pairs.append((gh.at[:, lanes(peer * hidden_quarter, hidden_quarter)], rgh.at[k - 1]))
            for i, (a, b) in enumerate(pairs):
                j = i if late else 2 + i
                copies.append(to_peer(a, b, gssem.at[j, k], grsem.at[j, k], peer))
        return copies

    l_d.wait()
    l_au.wait()
    gdown = (nt(d[...], au[:, U_D : U_D + MODEL_WIDTH]).astype(BF).astype(F32) * mask).astype(BF)
    gdown16 = narrow(gdown)
    gh[:, VALUE_WIDTH + HIDDEN_UNITS :] = jnp.zeros((ADAPTER_RANK, gh.shape[1] - VALUE_WIDTH - HIDDEN_UNITS), BF)
    l_dn.wait()
    gp[:, U_D : U_D + MODEL_WIDTH] = outer(dn[...], d[...])
    gad[...] = gdown
    l_ah.wait()
    l_fo.wait()
    l_gu.wait()

    def down_tile(i, carry):
        a, b = lanes(i * TILE, TILE), lanes(HIDDEN_UNITS + i * TILE, TILE)
        at = pl.ds(pl.multiple_of(i * TILE, TILE), TILE)
        dh = nt(d[...], fo[at, :]) + nt(gad[...], ah[pl.ds(pl.multiple_of(VALUE_WIDTH + i * TILE, TILE), TILE), :])
        gate, up = gu[:, a].astype(F32), gu[:, b].astype(F32)
        act, sig = silu_parts(gate)
        hidden[:, a] = (act * up).astype(BF)
        wide[:, a] = (dh * up * sig * (1.0 + gate * (1.0 - sig))).astype(BF)
        wide[:, b] = (dh * act).astype(BF)
        return carry

    lax.fori_loop(0, HIDDEN_UNITS // TILE, down_tile, 0)
    gate_cols, up_cols = slice(0, HIDDEN_UNITS), slice(HIDDEN_UNITS, 2 * HIDDEN_UNITS)
    gg = (nt(wide[:, gate_cols], au[:, U_G : U_G + HIDDEN_UNITS]).astype(BF).astype(F32) * mask).astype(BF)
    gu2 = (nt(wide[:, up_cols], au[:, U_U : U_U + HIDDEN_UNITS]).astype(BF).astype(F32) * mask).astype(BF)
    gad2 = jnp.concatenate([gg, gu2], axis=1)
    big[:, 0 : 2 * ADAPTER_COLUMNS] = gad2
    l_fi.wait()
    l_am.wait()

    def wide_tile(i, carry):
        at = pl.ds(pl.multiple_of(i * TILE, TILE), TILE)
        grad[:, lanes(i * TILE, TILE)] = nt(wide[...], fi[at, :]) + nt(
            big[:, 0 : 2 * ADAPTER_COLUMNS], am[at, 4 * ADAPTER_COLUMNS :]
        )
        return carry

    lax.fori_loop(0, MODEL_WIDTH // TILE, wide_tile, 0)
    l_mid.wait()
    mv = mid[...]
    grad_mid = d[...].astype(F32) + rms_back(mv, grad[...])
    grad[...] = grad_mid
    attn = grad_mid.astype(BF)
    e[...] = attn
    gout = (nt(attn, au[:, U_O : U_O + MODEL_WIDTH]).astype(BF).astype(F32) * mask).astype(BF)
    gad[...] = gout
    l_mo.wait()
    l_og.wait()
    l_mix.wait()

    def gate_back(head, out):
        at = rows(head * DV, DV)
        cols = lanes(head * DV, DV)
        gg_ = nt(e[...], mo[at, :]) + nt(gad[...], ah[at, :])
        o = og[:, cols]
        act, sig = silu_parts(o)
        out[...] = (gg_ * act).astype(BF)
        m = mix[head].astype(F32)
        dog[:, cols] = (gg_ * m * sig * (1.0 + o * (1.0 - sig))).astype(BF)
        hidden_gated[:, cols] = (m * act).astype(BF)

    mix_copies = []
    for k in range(1, HEADS):
        peer = me ^ k
        gate_back(peer, sendm.at[k - 1])
        copy = to_peer(sendm.at[k - 1], dmr.at[rows(me * T, T)], ssem.at[0, k], rsem.at[0, k], peer)
        copy.start()
        mix_copies.append(copy)
    gate_back(me, dmr.at[rows(me * T, T)])

    l_af.wait()
    l_ao.wait()
    normed_mid = (mv * inverse_rms(mv)).astype(BF)
    gh[:, VALUE_WIDTH : VALUE_WIDTH + HIDDEN_UNITS] = tn(gdown16, hidden[...]).astype(BF)
    gm[4 * ADAPTER_RANK : 5 * ADAPTER_RANK, :] = outer(gg, normed_mid)
    gm[5 * ADAPTER_RANK : 6 * ADAPTER_RANK, :] = outer(gu2, normed_mid)
    gp[:, U_G : U_G + HIDDEN_UNITS] = outer(af[:, 0:ADAPTER_COLUMNS], wide[:, gate_cols])
    gp[:, U_U : U_U + HIDDEN_UNITS] = outer(af[:, ADAPTER_COLUMNS:], wide[:, up_cols])
    gp[:, U_O : U_O + MODEL_WIDTH] = outer(ao[...], e[...])
    gh[:, 0:VALUE_WIDTH] = outer(gad[...], hidden_gated[...])
    place(range(n_late, n_dp))
    grads = grad_copies(False)
    for c in grads:
        c.start()

    for c in l_mixer:
        c.wait()
    f2h = f2[:, lanes(me * DK, DK)]
    bh = bias[:, lanes(me * DK, DK)]
    for src in range(HEADS):
        lg = tn(gl[src], f2h) + bh
        logit[src * T : (src + 1) * T, :] = lg
        fg[src * T : (src + 1) * T, :] = (jax.nn.log_sigmoid(lg) / 16.0).astype(BF)
    tri = lower_triangle(BF)
    causal = lower_triangle(F32)
    for c in mix_copies:
        c.wait_recv()
    gstate[...] = jnp.zeros_like(gstate)

    def retreat(i, carry):
        n = n_blocks - 1 - i
        at = pl.ds(meta[n_blocks + n] * GROUP, GROUP)
        here = rows(n * GROUP, GROUP)
        dm = dmr[at, :].astype(F32)
        yv = yh[at, :].astype(F32)
        r = rh[at, 0:1]
        do = (r * (dm - yv * jnp.mean(dm * yv, axis=-1, keepdims=True))).astype(BF)
        don[here, :] = do
        summed = nn(tri, fg[at, :])
        total = jnp.exp(summed[GROUP - 1 : GROUP])
        qs = (qkv[at, 0:DK].astype(F32) * SCALE * jnp.exp(summed)).astype(BF)
        now = gstate[...]
        gt[n] = now.astype(BF)
        decayed = total * now
        dt[n] = jnp.sum(decayed * st[n].astype(F32), axis=0, keepdims=True)
        gstate[...] = decayed + tn(do, qs)
        return carry

    lax.fori_loop(0, n_blocks, retreat, 0, unroll=4)

    def back_block(p, out, j):
        n = meta[p]
        at = rows(p * GROUP, GROUP)
        here = pl.ds(n * GROUP, GROUP)
        to = rows(j * GROUP, GROUP)
        live = live_rows(n, length)
        summed = nn(tri, fg[at, :])
        middle = summed[GROUP // 2 : GROUP // 2 + 1]
        total = summed[GROUP - 1 : GROUP]
        e1, e2 = jnp.exp(summed - middle), jnp.exp(middle - summed)
        es, eu = jnp.exp(summed), jnp.exp(total - summed)
        q = qkv[at, 0:DK].astype(F32) * SCALE
        k = qkv[at, DK : 2 * DK].astype(F32) * live
        v = qkv[at, 2 * DK : CHUNK]
        do, state_t, grad_t = don[here, :], st[n], gt[n]
        qe, ke, qs, ku = q * e1, k * e2, q * es, k * eu
        qeb, keb = qe.astype(BF), ke.astype(BF)
        scores = jnp.where(causal > 0, nt(qeb, keb), 0.0).astype(BF)
        dscores = jnp.where(causal > 0, nt(do, v), 0.0).astype(BF)
        dv = tn(scores, do) + nt(ku.astype(BF), grad_t)
        dqs = nn(do, state_t)
        dku = nn(v, grad_t)
        dqe = nn(dscores, keb)
        dke = tn(dscores, qeb)
        out[to, 0:DK] = (SCALE * (dqe * e1 + dqs * es)).astype(BF)
        out[to, DK : 2 * DK] = (live * (dke * e2 + dku * eu)).astype(BF)
        out[to, 2 * DK : CHUNK] = dv.astype(BF)
        kk = dku * ku
        dsum = dqe * qe + dqs * qs - dke * ke - kk
        dtotal = dt[n] + jnp.sum(kk, axis=0, keepdims=True)
        high = dsum.astype(BF)
        lowp = (dsum - high.astype(F32)).astype(BF)
        df = tn(tri, high) + tn(tri, lowp) + dtotal
        df = df.astype(BF).astype(F32)
        dlog[to, :] = (df * lax.logistic(-logit[at, :]) / 16.0).astype(BF)

    q_copies = []

    def back_rows(dest, out, low_out):
        lax.fori_loop(0, per, lambda j, c: (back_block(dest * per + j, out, j), c)[1], 0, unroll=2)
        low_out[...] = nt(f2h, dlog[...]).astype(BF)

    for k in range(1, HEADS):
        peer = me ^ k
        back_rows(peer, sendq.at[k - 1], sendl.at[k - 1])
        copies = (
            to_peer(sendq.at[k - 1], dqkv.at[me], ssem.at[1, k], rsem.at[1, k], peer),
            to_peer(sendl.at[k - 1], dlr.at[me], ssem.at[2, k], rsem.at[2, k], peer),
        )
        for copy in copies:
            copy.start()
        q_copies += copies
    back_rows(me, dqkv.at[me], dlr.at[me])

    for c in l_last:
        c.wait()
    hv = h[...].astype(F32)
    hr = inverse_rms(hv)
    big[...] = (hv * hr).astype(BF)
    for c in q_copies:
        c.wait_recv()
    for hd in range(HEADS):
        dproj[:, hd * DK : (hd + 1) * DK] = dqkv[hd, :, 0:DK]
        dproj[:, KEY + hd * DK : KEY + (hd + 1) * DK] = dqkv[hd, :, DK : 2 * DK]
        dproj[:, 2 * KEY + hd * DV : 2 * KEY + (hd + 1) * DV] = dqkv[hd, :, 2 * DK : CHUNK]
    dproj[:, 2 * KEY + VALUE_WIDTH :] = dog[...]
    dlow = dlr[0].astype(F32)
    for hd in range(1, HEADS):
        dlow += dlr[hd].astype(F32)
    dlowb = dlow.astype(BF)
    spans = ((0, KEY), (KEY, KEY), (2 * KEY, VALUE_WIDTH), (2 * KEY + VALUE_WIDTH, VALUE_WIDTH))
    for p, (start, span) in enumerate(spans):
        block = slice(p * ADAPTER_COLUMNS, (p + 1) * ADAPTER_COLUMNS)
        piece = dproj[:, start : start + span]
        ga = (nt(piece, au[:, start : start + span]).astype(BF).astype(F32) * mask).astype(BF)
        wide[:, block] = ga
        gm[p * ADAPTER_RANK : (p + 1) * ADAPTER_RANK, :] = outer(ga, big[...])
        gp[:, start : start + span] = outer(ad[:, block], piece)
    place(range(n_late))
    late_grads = grad_copies(True)
    for c in late_grads:
        c.start()
    z_w = f1.shape[2]
    tiles = f1.shape[0]
    back = []
    for j in range(tiles):
        at = slice(j * z_w, (j + 1) * z_w)
        back.append(
            nt(dproj[...], mi[at, :]) + nt(wide[:, 0 : 4 * ADAPTER_COLUMNS], am[at, 0 : 4 * ADAPTER_COLUMNS]) + tn(dlowb, f1[j])
        )
    dn_ = jnp.concatenate(back, axis=1)
    n = hv * hr
    e[...] = (grad[...] + hr * (dn_ - n * jnp.mean(dn_ * n, axis=-1, keepdims=True))).astype(BF)
    loc.start(e, e_out, True)
    grads += late_grads
    for c in grads:
        c.wait_recv()

    def summed_over_seq(own, got):
        total = own.astype(F32)
        for k in range(HEADS - 1):
            total += got[k].astype(F32)
        return total.astype(BF)

    sgm[...] = summed_over_seq(gm[:, lanes(me * quarter, quarter)], rgm)
    sgh[...] = summed_over_seq(gh[:, lanes(me * hidden_quarter, hidden_quarter)], rgh)
    spot = lax.broadcasted_iota(jnp.int32, (ADAPTER_RANK, padded), 1)
    for i in range(n_dp):
        total = gps[me, i].astype(F32)
        for k in range(HEADS - 1):
            total += rgp[k, i].astype(F32)
        sgp[i] = jnp.where(spot == width, adapter.astype(F32), total).astype(BF)
    for a, b in ((sgm, gm_out), (sgh, gh_out), (sgp, gp_out)):
        loc.start(a, b, True)
    loc.finish()
    for c in mix_copies + q_copies + grads:
        c.wait_send()


def backward(layer, meta, d, h, weights, saved, n_dp):
    T = h.shape[0]
    L = T * HEADS
    n_blocks = L // GROUP
    raised = U_D + MODEL_WIDTH
    padded = (raised // (n_dp * HEADS) // 128 + 1) * 128
    quarter = MODEL_WIDTH // HEADS
    hidden_quarter = -(-(VALUE_WIDTH + HIDDEN_UNITS) // (HEADS * 128)) * 128
    outs = [
        ((T, MODEL_WIDTH), BF),
        ((6 * ADAPTER_RANK, quarter), BF),
        ((ADAPTER_RANK, hidden_quarter), BF),
        ((n_dp, ADAPTER_RANK, padded), BF),
    ]
    vm = pltpu.VMEM
    dma = pltpu.SemaphoreType.DMA
    return pl.pallas_call(
        functools.partial(backward_kernel, layer, n_blocks),
        out_shape=[jax.ShapeDtypeStruct(*s) for s in outs],
        in_specs=[pl.BlockSpec(memory_space=pltpu.SMEM)] + [ANY] * (2 + len(weights) + len(saved)),
        out_specs=[ANY] * len(outs),
        scratch_shapes=[vm(d.shape, d.dtype), vm(h.shape, h.dtype)]
        + weight_scratch(weights)
        + [vm(s.shape, s.dtype) for s in saved]
        + [vm(*s) for s in outs]
        + [
            vm((6 * ADAPTER_RANK, MODEL_WIDTH), BF),
            vm((ADAPTER_RANK, HEADS * hidden_quarter), BF),
            vm((ADAPTER_RANK, raised), BF),
            vm((HEADS, n_dp, ADAPTER_RANK, padded), BF),
            vm((HEADS - 1, 6 * ADAPTER_RANK, quarter), BF),
            vm((HEADS - 1, ADAPTER_RANK, hidden_quarter), BF),
            vm((HEADS - 1, n_dp, ADAPTER_RANK, padded), BF),
            vm((T, HIDDEN_UNITS), BF),
            vm((T, 2 * HIDDEN_UNITS), BF),
            vm((T, ADAPTER_COLUMNS), BF),
            vm((T, MODEL_WIDTH), BF),
            vm((T, MODEL_WIDTH), F32),
            vm((T, VALUE_WIDTH), BF),
            vm((HEADS - 1, T, DV), BF),
            vm((L, DV), BF),
            vm((L, DK), F32),
            vm((L, DK), BF),
            vm((DV, DK), F32),
            vm((n_blocks, DV, DK), BF),
            vm((n_blocks, 1, DK), F32),
            vm((L, DV), BF),
            vm((T, VALUE_WIDTH), BF),
            vm((HEADS - 1, T, CHUNK), BF),
            vm((HEADS, T, CHUNK), BF),
            vm((T, DK), BF),
            vm((HEADS - 1, FGATE_RANK, T), BF),
            vm((HEADS, FGATE_RANK, T), BF),
            vm((T, FROZEN), BF),
            dma((2 + len(weights) + len(saved) + len(outs),)),
            dma((3, HEADS)),
            dma((3, HEADS)),
            dma((5, HEADS)),
            dma((5, HEADS)),
        ],
        compiler_params=pltpu.CompilerParams(
            collective_id=3 + layer, has_side_effects=True, vmem_limit_bytes=VMEM_LIMIT
        ),
        cost_estimate=pl.CostEstimate(flops=2 * T * 16_000_000, bytes_accessed=45 << 20, transcendentals=T * 8192),
    )(meta, d, h, *weights, *saved)


def swap_sections(v):
    return lax.ppermute(v, "section", [(0, 1), (1, 0)])


def plain_gather(shards, f1t, ends, small):
    first = lax.axis_index("section") == 0
    both = lambda a: lax.all_gather(a, "section", axis=0)
    outs = [both(lax.all_gather(w[0], "dp", axis=0, tiled=True)) for w in shards]
    low = lax.all_gather(f1t, "dp", axis=1, tiled=True)
    outs.append(both(jnp.stack(jnp.split(low, 4, axis=1))))
    sent = swap_sections(jnp.where(first, ends[0, 1, 0], ends[0, 0, 0]))
    outs.append(jnp.where(first, ends[0, 0, 0], sent))
    outs.append(jnp.where(first, sent, ends[0, 1, 0]))
    return outs + [both(a[0]) for a in small]


def spread(parts, chosen):
    hot = (chosen[:, None] == jnp.arange(ADAPTERS, dtype=jnp.int32)[None, :]).astype(F32)
    return sum(parts[n][:, None] * hot[n][None, :, None, None] for n in range(parts.shape[0]))


def reduce_kernel(
    gm0, gh0, gp0, gm1, gh1, gp1, m_out, h_out, u_out,
    vm_, vh, vp, rm, rh, rp, am, ah, em, eh, ls, ss, rs, es, er,
):
    core, dp, me = lax.axis_index("section"), lax.axis_index("dp"), lax.axis_index("seq")
    n_dp = vp.shape[1]
    width = u_out.shape[1]
    loads = [
        pltpu.make_async_copy(a, b.at[l], ls.at[l, i])
        for l, three in enumerate(((gm0, gh0, gp0), (gm1, gh1, gp1)))
        for i, (a, b) in enumerate(zip(three, (vm_, vh, vp)))
    ]
    for c in loads:
        c.start()
    barrier = pltpu.get_barrier_semaphore()
    places = [dict(section=1 - core)] + [dict(seq=me ^ k) for k in range(1, HEADS)]
    for gap in range(1, n_dp):
        to = lax.rem(dp + gap, n_dp)
        places += [dict(dp=to), dict(section=1 - core, dp=to)]
    for where in places:
        pl.semaphore_signal(barrier, inc=1, device_id=where, device_id_type=MESH)
    for c in loads:
        c.wait()
    pl.semaphore_wait(barrier, len(places))
    slot = dp * 2 + core
    size = 6 * ADAPTER_COLUMNS // n_dp

    def first_projection(i):
        return i * size // ADAPTER_COLUMNS

    def parts(layer, to):
        at = pl.ds(pl.multiple_of(first_projection(to) * ADAPTER_RANK, ADAPTER_RANK), 2 * ADAPTER_RANK)
        return ((vm_.at[layer, at], rm.at[slot]), (vh.at[layer], rh.at[slot]), (vp.at[layer, to], rp.at[slot]))

    copies = []
    for gap in range(n_dp - 1, -1, -1):
        to = lax.rem(dp + gap, n_dp)
        for crossing in (0, 1):
            if crossing == 0 and gap == 0:
                continue
            section = 1 - core if crossing else core
            for i, (a, b) in enumerate(parts(section, to)):
                c = pltpu.make_async_remote_copy(
                    src_ref=a, dst_ref=b, send_sem=ss.at[crossing, gap, i], recv_sem=rs.at[crossing, gap, i],
                    device_id=dict(section=section, dp=to), device_id_type=MESH,
                )
                c.start()
                copies.append(c)
    at = pl.ds(pl.multiple_of(first_projection(dp) * ADAPTER_RANK, ADAPTER_RANK), 2 * ADAPTER_RANK)
    rm[slot] = vm_[core, at]
    rh[slot] = vh[core]
    rp[slot] = vp[core, dp]
    for c in copies:
        c.wait_recv()
    n = rm.shape[0]
    chosen = [rp[j, :, width : width + 1].astype(F32) for j in range(n)]
    for a in range(ADAPTERS):
        hot = [(c == float(a)).astype(F32) for c in chosen]
        at = slice(a * ADAPTER_RANK, (a + 1) * ADAPTER_RANK)

        def total(values):
            out = hot[0] * values(0).astype(F32)
            for j in range(1, n):
                out += hot[j] * values(j).astype(F32)
            return out

        for p in range(2):
            am[p * ADAPTER_COLUMNS + a * ADAPTER_RANK : p * ADAPTER_COLUMNS + (a + 1) * ADAPTER_RANK, :] = total(
                lambda j, p=p: rm[j, p * ADAPTER_RANK : (p + 1) * ADAPTER_RANK]
            )
        ah[at, :] = total(lambda j: rh[j])
        u_out[at, :] = total(lambda j: rp[j])[:, 0:width]
    own_m, own_h = size // HEADS, ADAPTER_COLUMNS // n_dp // HEADS
    base = dp * size - first_projection(dp) * ADAPTER_COLUMNS

    def m_rows(q):
        return am.at[pl.ds(pl.multiple_of(base + q * own_m, 16), own_m)]

    def h_rows(q):
        return ah.at[pl.ds(pl.multiple_of(dp * HEADS * own_h + q * own_h, 8), own_h)]

    last = []
    for k in range(1, HEADS):
        for i, (a, b) in enumerate(((m_rows(me ^ k), em.at[me]), (h_rows(me ^ k), eh.at[me]))):
            c = to_peer(a, b, es.at[i, k], er.at[i, k], me ^ k)
            c.start()
            last.append(c)
    em[me] = m_rows(me)[...]
    eh[me] = h_rows(me)[...]
    for c in last:
        c.wait_recv()
    for q in range(HEADS):
        m_out[:, q * em.shape[2] : (q + 1) * em.shape[2]] = em[q]
        h_out[:, q * eh.shape[2] : (q + 1) * eh.shape[2]] = eh[q]
    for c in copies + last:
        c.wait_send()


def reduce_gradients(early, late, n_dp):
    gm, gh, gp = early
    n = 2 * n_dp
    width = (U_D + MODEL_WIDTH) // (n_dp * HEADS)
    own_m, own_h = 6 * ADAPTER_COLUMNS // (n_dp * HEADS), ADAPTER_COLUMNS // (n_dp * HEADS)
    vm, dma, VM = pltpu.VMEM, pltpu.SemaphoreType.DMA, pl.BlockSpec(memory_space=pltpu.VMEM)
    shape = jax.ShapeDtypeStruct
    model, hidden, up = pl.pallas_call(
        reduce_kernel,
        out_shape=[
            shape((own_m, MODEL_WIDTH), F32),
            shape((own_h, HEADS * gh.shape[1]), F32),
            shape((ADAPTER_COLUMNS, width), F32),
        ],
        in_specs=[ANY] * 6,
        out_specs=[VM] * 3,
        scratch_shapes=[
            vm((2,) + gm.shape, BF),
            vm((2,) + gh.shape, BF),
            vm((2,) + gp.shape, BF),
            vm((n, 2 * ADAPTER_RANK, gm.shape[1]), BF),
            vm((n,) + gh.shape, BF),
            vm((n,) + gp.shape[1:], BF),
            vm((2 * ADAPTER_COLUMNS, gm.shape[1]), F32),
            vm((ADAPTER_COLUMNS, gh.shape[1]), F32),
            vm((HEADS, own_m, gm.shape[1]), F32),
            vm((HEADS, own_h, gh.shape[1]), F32),
            dma((2, 3)),
            dma((2, n_dp, 3)),
            dma((2, n_dp, 3)),
            dma((2, HEADS)),
            dma((2, HEADS)),
        ],
        compiler_params=pltpu.CompilerParams(collective_id=5, has_side_effects=True, vmem_limit_bytes=32 << 20),
    )(*early, *late)
    return model.T, hidden[:, : VALUE_WIDTH + HIDDEN_UNITS].T, up


def plain_reduce(early, late, n_dp):
    first = lax.axis_index("section") == 0
    dp = lax.axis_index("dp")
    kept = [jnp.where(first, a, b) for a, b in zip(early, late)]
    got = [swap_sections(jnp.where(first, b, a)) for a, b in zip(early, late)]
    gm, gh, gp = [jnp.stack(pair) for pair in zip(kept, got)]
    width = (U_D + MODEL_WIDTH) // (n_dp * HEADS)
    gm = lax.all_gather(gm, "dp", axis=0)
    gh = lax.all_gather(gh, "dp", axis=0)
    gp = lax.all_to_all(jnp.swapaxes(gp, 0, 1), "dp", split_axis=0, concat_axis=0, tiled=True)
    gp = gp.reshape(2 * n_dp, 1, ADAPTER_RANK, -1)
    n = gp.shape[0]
    chosen = gp[:, 0, 0, width].astype(jnp.int32)
    gm = spread(gm.reshape(n, 6, ADAPTER_RANK, -1).astype(F32), chosen).reshape(6 * ADAPTER_COLUMNS, -1)
    gh = spread(gh.reshape(n, 1, ADAPTER_RANK, -1).astype(F32), chosen).reshape(ADAPTER_COLUMNS, -1)
    gp = spread(gp.astype(F32), chosen).reshape(ADAPTER_COLUMNS, -1)

    def columns(v):
        size = v.shape[0] // n_dp
        v = lax.dynamic_slice_in_dim(v, dp * size, size, 0)
        return lax.all_to_all(v, "seq", split_axis=0, concat_axis=1, tiled=True).T

    return columns(gm), columns(gh)[: VALUE_WIDTH + HIDDEN_UNITS], gp[:, :width]


def local(
    ends,
    mixer_input_weight,
    forget_first_map,
    forget_second_map,
    forget_logit_bias,
    mixer_output_weight,
    feedforward_input_weight,
    feedforward_output_weight,
    adapter_model_first,
    adapter_hidden_first,
    adapter_second_maps,
    lengths,
    dealt_block_order,
    adapter_choice_per_seq,
):
    first = lax.axis_index("section") == 0
    mine = lambda a: jnp.where(first, a[0], a[1])
    order = mine(dealt_block_order)[0]
    n_blocks = order.shape[0]
    at = jnp.arange(n_blocks, dtype=jnp.int32)
    inverse = jnp.sum(at[:, None] * (order[:, None] == at[None, :]).astype(jnp.int32), axis=0)
    meta = jnp.concatenate([order, inverse, mine(adapter_choice_per_seq), mine(lengths)])
    n_dp = lax.axis_size("dp")
    own_kernels = n_dp == 4 and lax.axis_size("seq") == 4
    shards = [mixer_input_weight, mixer_output_weight, feedforward_input_weight, feedforward_output_weight]
    small = [
        forget_second_map,
        forget_logit_bias[:, None],
        adapter_model_first,
        adapter_hidden_first,
        adapter_second_maps,
    ]
    gather = gather_all if own_kernels else plain_gather
    out = gather(shards, forget_first_map[0].T, ends, small)
    weights = list(out[:5]) + list(out[7:])
    x, cotangent = out[5], out[6]
    early = forward(0, meta, x, weights)
    late = forward(1, meta, early[0], weights)
    middle, *grads_late = backward(1, meta, cotangent, early[0], weights, late[1:], n_dp)
    entry, *grads_early = backward(0, meta, middle, x, weights, early[1:], n_dp)
    sent = swap_sections(jnp.where(first, late[0], entry))
    results = jnp.where(first, jnp.stack([entry, sent]), jnp.stack([sent, late[0]]))
    reduce = reduce_gradients if own_kernels else plain_reduce
    model, hidden, up = reduce(grads_early, grads_late, n_dp)
    return (results[None, :, None], model[None], hidden[None], up[None])


def solution(mesh):
    return jax.shard_map(
        local,
        mesh=mesh,
        in_specs=(
            P("section", None, "dp", "seq", None),
            P("section", "dp", None),
            P("section", "dp", None),
            P("section", None, None),
            P("section", None),
            P("section", "dp", None),
            P("section", "dp", None),
            P("section", "dp", None),
            P("section", None, None),
            P("section", None, None),
            P("section", None, None),
            P(None, "dp"),
            P(None, "dp", None),
            P(None, "dp"),
        ),
        out_specs=(
            P("section", None, "dp", "seq", None),
            P("section", None, ("dp", "seq")),
            P("section", None, ("dp", "seq")),
            P("section", None, ("dp", "seq")),
        ),
        check_vma=False,
    )
```

```python
import functools
import jax
import jax.numpy as jnp
from jax import lax
from jax.experimental import pallas as pl
from jax.experimental.pallas import tpu as pltpu

from jax.sharding import PartitionSpec as P

MODEL_WIDTH = 1024
HEADS = 4
KEY = 512
VALUE_WIDTH = 1024
HIDDEN_UNITS = 2816
FGATE_RANK = 16
GROUP = 64
ADAPTER_RANK = 16
ADAPTERS = 8
ADAPTER_COLUMNS = 128
VMEM_LIMIT = 60 << 20
LINK_BYTES_PER_US = 72e3
SKEW = (2, 4)
DELAYS = (8, 18, 12)
STRIPS = (256, 128, 384, 128)

MESH = pl.DeviceIdType.MESH
ANY = pl.BlockSpec(memory_space=pl.ANY)


BF = jnp.bfloat16
F32 = jnp.float32


def nn(a, b):
    return lax.dot_general(a, b, (((1,), (0,)), ((), ())), preferred_element_type=F32)


def nt(a, b):
    return lax.dot_general(a, b, (((1,), (1,)), ((), ())), preferred_element_type=F32)


def tn(a, b):
    return lax.dot_general(a, b, (((0,), (0,)), ((), ())), preferred_element_type=F32)


def silu_parts(v):
    sig = lax.logistic(v)
    return v * sig, sig


def inverse_rms(v):
    return lax.rsqrt(jnp.mean(v * v, axis=-1, keepdims=True) + 1e-06)


def rms_back(v, grad):
    r = inverse_rms(v)
    n = v * r
    return r * (grad - n * jnp.mean(grad * n, axis=-1, keepdims=True))


def lanes(start, size):
    return pl.ds(pl.multiple_of(start, 128), size)


def rows(start, size):
    return pl.ds(pl.multiple_of(start, size if size <= 64 else 64), size)


def greet_peers(me):
    barrier = pltpu.get_barrier_semaphore()
    for d in range(1, HEADS):
        pl.semaphore_signal(barrier, inc=1, device_id={"seq": me ^ d}, device_id_type=MESH)
    pl.semaphore_wait(barrier, HEADS - 1)


def to_peer(src, dst, ssem, rsem, peer):
    return pltpu.make_async_remote_copy(
        src_ref=src, dst_ref=dst, send_sem=ssem, recv_sem=rsem,
        device_id={"seq": peer}, device_id_type=MESH,
    )


class Local:
    def __init__(self, sems):
        self.sems, self.used, self.open = sems, 0, []

    def start(self, src, dst, wait_at_end=False):
        copy = pltpu.make_async_copy(src, dst, self.sems.at[self.used])
        self.used += 1
        copy.start()
        if wait_at_end:
            self.open.append(copy)
        return copy

    def finish(self):
        for copy in self.open:
            copy.wait()
        self.open = []


def picked(adapter, width):
    row = lax.broadcasted_iota(jnp.int32, (width, ADAPTER_RANK), 0)
    col = lax.broadcasted_iota(jnp.int32, (width, ADAPTER_RANK), 1)
    return (row == adapter * ADAPTER_RANK + col).astype(BF)


def column_mask(adapter):
    col = lax.broadcasted_iota(jnp.int32, (1, ADAPTER_COLUMNS), 1)
    low = adapter * ADAPTER_RANK
    return jnp.logical_and(col >= low, col < low + ADAPTER_RANK).astype(F32)


def lower_triangle(dtype):
    i = lax.broadcasted_iota(jnp.int32, (GROUP, GROUP), 0)
    j = lax.broadcasted_iota(jnp.int32, (GROUP, GROUP), 1)
    return (i >= j).astype(dtype)


DK = KEY // HEADS
DV = VALUE_WIDTH // HEADS
CHUNK = 2 * DK + DV
FROZEN = 2 * KEY + 2 * VALUE_WIDTH
TILE = 256
SCALE = DK ** (-0.5)

U_G = FROZEN
U_U = FROZEN + HIDDEN_UNITS
U_O = FROZEN + 2 * HIDDEN_UNITS
U_D = U_O + MODEL_WIDTH


def live_rows(n, length):
    at = lax.broadcasted_iota(jnp.int32, (GROUP, 1), 0) + n * GROUP
    return (at < length).astype(F32)


def forward_steps(layer, n_blocks, meta, loc, weights, buffers, work, outs, sems):
    w, v = weights, buffers
    (h, y, ad, og, qkv, gl, st, mix, yh, rh, ao, mid, af, gu, dn, normed, send, glsend, fg, state, gated, hidden) = work
    o_y, o_ad, o_og, o_qkv, o_gl, o_st, o_mix, o_yh, o_rh, o_ao, o_mid, o_af, o_gu, o_dn = outs
    ssem, rsem = sems
    me = lax.axis_index("seq")
    T = h.shape[0]
    per = T // GROUP
    adapter = meta[2 * n_blocks]
    length = meta[2 * n_blocks + 1]
    mask = column_mask(adapter)
    am, ah, au, mi, mo, fi, fo = [v[name] for name in ("am", "ah", "au", "mi", "mo", "fi", "fo")]

    def load(*names):
        return [loc.start(w[name], v[name]) for name in names]

    def wait(copies):
        for c in copies:
            c.wait()

    yield "small", 0
    small = load("f1", "f2", "b", "am", "au", "ah")
    yield None, 2
    hv = h[...].astype(F32)
    normed[...] = (hv * inverse_rms(hv)).astype(BF)
    wait(small)
    f1, f2, bias = v["f1"], v["f2"], v["b"]
    z_w = f1.shape[2]
    low = nt(f1[0], normed[:, 0:z_w])
    for j in range(1, f1.shape[0]):
        low += nt(f1[j], normed[:, j * z_w : (j + 1) * z_w])
    glsend[...] = low.astype(BF)
    low_copies = [to_peer(glsend, gl.at[me], ssem.at[0, d], rsem.at[0, d], me ^ d) for d in range(1, HEADS)]
    for c in low_copies:
        c.start()
    gl[me] = glsend[...]
    yield "delay", DELAYS[0]
    for p in range(4):
        cols = pl.ds(p * ADAPTER_COLUMNS, ADAPTER_COLUMNS)
        ad[:, cols] = (nn(normed[...], am[:, cols]) * mask).astype(BF)
    f2h = f2[:, lanes(me * DK, DK)]
    bh = bias[:, lanes(me * DK, DK)]
    for c in low_copies:
        c.wait_recv()
    for src in range(HEADS):
        logit = tn(gl[src], f2h) + bh
        fg[src * T : (src + 1) * T, :] = (jax.nn.log_sigmoid(logit) / 16.0).astype(BF)
    loc.start(gl, o_gl, True)
    loc.start(ad, o_ad, True)
    yield "mi", 0
    wait(load("mi"))

    def project(w_start, p, width):
        cols = lanes(w_start, width)
        return nn(normed[...], mi[:, cols]) + nn(ad[:, p * ADAPTER_COLUMNS : (p + 1) * ADAPTER_COLUMNS], au[:, cols])

    def chunk(head, ref):
        ref[:, 0:DK] = project(head * DK, 0, DK).astype(BF)
        ref[:, DK : 2 * DK] = project(KEY + head * DK, 1, DK).astype(BF)
        ref[:, 2 * DK : CHUNK] = project(2 * KEY + head * DV, 2, DV).astype(BF)

    qkv_copies = []
    for d in range(1, HEADS):
        yield None, 1
        chunk(me ^ d, send.at[d - 1])
        copy = to_peer(send.at[d - 1], qkv.at[rows(me * T, T)], ssem.at[1, d], rsem.at[1, d], me ^ d)
        copy.start()
        qkv_copies.append(copy)
    yield None, 1
    chunk(me, qkv.at[rows(me * T, T)])
    yield None, 1
    for j in range(VALUE_WIDTH // TILE):
        og[:, j * TILE : (j + 1) * TILE] = project(2 * KEY + VALUE_WIDTH + j * TILE, 3, TILE)
    loc.start(og, o_og, True)
    yield "delay", DELAYS[1]
    for c in qkv_copies:
        c.wait_recv()
    loc.start(qkv, o_qkv, True)
    tri = lower_triangle(BF)
    causal = lower_triangle(F32)
    state[...] = jnp.zeros_like(state)

    def advance(n, carry):
        at = pl.ds(meta[n_blocks + n] * GROUP, GROUP)
        summed = nn(tri, fg[at, :])
        total = summed[GROUP - 1 : GROUP]
        k = qkv[at, DK : 2 * DK].astype(F32) * live_rows(n, length)
        ku = (k * jnp.exp(total - summed)).astype(BF)
        update = tn(qkv[at, 2 * DK : CHUNK], ku)
        now = state[...]
        st[n] = now.astype(BF)
        state[...] = jnp.exp(total) * now + update
        return carry

    lax.fori_loop(0, n_blocks, advance, 0, unroll=4)
    loc.start(st, o_st, True)
    yield None, 4

    def mix_block(p):
        n = meta[p]
        at = rows(p * GROUP, GROUP)
        summed = nn(tri, fg[at, :])
        middle = summed[GROUP // 2 : GROUP // 2 + 1]
        q = qkv[at, 0:DK].astype(F32) * SCALE
        k = qkv[at, DK : 2 * DK].astype(F32) * live_rows(n, length)
        qe = (q * jnp.exp(summed - middle)).astype(BF)
        ke = (k * jnp.exp(middle - summed)).astype(BF)
        scores = jnp.where(causal > 0, nt(qe, ke), 0.0).astype(BF)
        o = nn(scores, qkv[at, 2 * DK : CHUNK]) + nt((q * jnp.exp(summed)).astype(BF), st[n])
        r = lax.rsqrt(jnp.mean(o * o, axis=-1, keepdims=True) + 1.0)
        yh[at, :] = (o * r).astype(BF)
        rh[at, :] = jnp.broadcast_to(r, (GROUP, DK))

    mix_copies = []
    for d in range(1, HEADS):
        yield None, 2
        peer = me ^ d
        lax.fori_loop(0, per, lambda j, c, peer=peer: (mix_block(peer * per + j), c)[1], 0, unroll=True)
        copy = to_peer(yh.at[rows(peer * T, T)], mix.at[me], ssem.at[2, d], rsem.at[2, d], peer)
        copy.start()
        mix_copies.append(copy)
    yield None, 2
    lax.fori_loop(0, per, lambda j, c: (mix_block(me * per + j), c)[1], 0, unroll=True)
    mix[me] = yh[rows(me * T, T), :]
    loc.start(yh, o_yh, True)
    loc.start(rh, o_rh, True)
    yield "mo", 0
    l_mo = load("mo")
    yield "delay", DELAYS[2]
    for c in mix_copies:
        c.wait_recv()
    loc.start(mix, o_mix, True)
    for hd in range(HEADS):
        cols = slice(hd * DV, (hd + 1) * DV)
        gated[:, cols] = (mix[hd].astype(F32) * silu_parts(og[:, cols])[0]).astype(BF)
    ao[...] = (nn(gated[...], ah[0:VALUE_WIDTH, :]) * mask).astype(BF)
    wait(l_mo)
    for j in range(MODEL_WIDTH // TILE):
        cols = slice(j * TILE, (j + 1) * TILE)
        mid[:, cols] = (
            h[:, cols].astype(F32) + nn(gated[...], mo[:, cols]) + nn(ao[...], au[:, U_O + j * TILE : U_O + (j + 1) * TILE])
        )
    loc.start(ao, o_ao, True)
    loc.start(mid, o_mid, True)
    yield None, 1
    mv = mid[...]
    normed[...] = (mv * inverse_rms(mv)).astype(BF)
    for p in range(2):
        cols = slice(p * ADAPTER_COLUMNS, (p + 1) * ADAPTER_COLUMNS)
        wide = slice((4 + p) * ADAPTER_COLUMNS, (5 + p) * ADAPTER_COLUMNS)
        af[:, cols] = (nn(normed[...], am[:, wide]) * mask).astype(BF)
    loc.start(af, o_af, True)
    yield "fi", 0
    wait(load("fi"))

    def up_tile(i, carry):
        a, b = lanes(i * TILE, TILE), lanes(HIDDEN_UNITS + i * TILE, TILE)
        gate = nn(normed[...], fi[:, a]) + nn(af[:, 0:ADAPTER_COLUMNS], au[:, lanes(U_G + i * TILE, TILE)])
        up = nn(normed[...], fi[:, b]) + nn(af[:, ADAPTER_COLUMNS:], au[:, lanes(U_U + i * TILE, TILE)])
        gu[:, a] = gate.astype(gu.dtype)
        gu[:, b] = up.astype(gu.dtype)
        hidden[:, a] = (silu_parts(gate)[0] * up).astype(BF)
        return carry

    tiles = HIDDEN_UNITS // TILE
    yield None, 3
    lax.fori_loop(0, tiles // 2, up_tile, 0)
    yield None, 3
    lax.fori_loop(tiles // 2, tiles, up_tile, 0)
    loc.start(gu, o_gu, True)
    dn[...] = (nn(hidden[...], ah[VALUE_WIDTH:, :]) * mask).astype(BF)
    loc.start(dn, o_dn, True)
    yield "fo", 0
    wait(load("fo"))
    yield None, 3
    for j in range(MODEL_WIDTH // TILE):
        cols = slice(j * TILE, (j + 1) * TILE)
        y[:, cols] = (
            mid[:, cols] + nn(hidden[...], fo[:, cols]) + nn(dn[...], au[:, U_D + j * TILE : U_D + (j + 1) * TILE])
        ).astype(BF)
    loc.start(y, o_y, True)
    loc.finish()
    for c in low_copies + qkv_copies + mix_copies:
        c.wait_send()


NAMES = ("mi", "mo", "fi", "fo", "f1", "f2", "b", "am", "ah", "au")


def forward_kernel(layer, n_blocks, meta, h_in, *refs):
    n_w, n_out = len(NAMES), 14
    ins, outs = refs[:n_w], refs[n_w : n_w + n_out]
    refs = refs[n_w + n_out :]
    buffers, work = dict(zip(NAMES, refs[:n_w])), refs[n_w:-3]
    lsem, ssem, rsem = refs[-3:]
    loc = Local(lsem)
    first = loc.start(h_in, work[0])
    greet_peers(lax.axis_index("seq"))
    first.wait()
    weights = {name: ref.at[layer] for name, ref in zip(NAMES, ins)}
    for _ in forward_steps(layer, n_blocks, meta, loc, weights, buffers, work, outs, (ssem, rsem)):
        pass


def weight_scratch(weights):
    return [pltpu.VMEM(w.shape[1:], w.dtype) for w in weights]


def saved_shapes(T, L, n_blocks):
    s = lambda shape, dtype=BF: (shape, dtype)
    return [
        s((T, MODEL_WIDTH)),
        s((T, 4 * ADAPTER_COLUMNS)),
        s((T, VALUE_WIDTH), F32),
        s((L, CHUNK)),
        s((HEADS, FGATE_RANK, T)),
        s((n_blocks, DV, DK)),
        s((HEADS, T, DV)),
        s((L, DV)),
        s((L, DK), F32),
        s((T, ADAPTER_COLUMNS)),
        s((T, MODEL_WIDTH), F32),
        s((T, 2 * ADAPTER_COLUMNS)),
        s((T, 2 * HIDDEN_UNITS)),
        s((T, ADAPTER_COLUMNS)),
    ]


def work_scratch(T, L, saved):
    vm = pltpu.VMEM
    return [vm((T, MODEL_WIDTH), BF)] + [vm(*s) for s in saved] + [
        vm((T, MODEL_WIDTH), BF),
        vm((HEADS - 1, T, CHUNK), BF),
        vm((FGATE_RANK, T), BF),
        vm((L, DK), BF),
        vm((DV, DK), F32),
        vm((T, VALUE_WIDTH), BF),
        vm((T, HIDDEN_UNITS), BF),
    ]


def forward(layer, meta, h, weights):
    T = h.shape[0]
    L = T * HEADS
    n_blocks = L // GROUP
    saved = saved_shapes(T, L, n_blocks)
    dma = pltpu.SemaphoreType.DMA
    return pl.pallas_call(
        functools.partial(forward_kernel, layer, n_blocks),
        out_shape=[jax.ShapeDtypeStruct(*s) for s in saved],
        in_specs=[pl.BlockSpec(memory_space=pltpu.SMEM)] + [ANY] * (1 + len(weights)),
        out_specs=[ANY] * len(saved),
        scratch_shapes=weight_scratch(weights)
        + work_scratch(T, L, saved)
        + [dma((1 + len(weights) + len(saved),)), dma((3, HEADS)), dma((3, HEADS))],
        compiler_params=pltpu.CompilerParams(
            collective_id=1 + layer, has_side_effects=True, vmem_limit_bytes=VMEM_LIMIT
        ),
    )(meta, h, *weights)


def backward_kernel(
    layer, n_blocks, meta, d_in, h_in, w_mi, w_mo, w_fi, w_fo, w_f1, w_f2, w_b, w_am, w_ah, w_au,
    i_ad, i_og, i_qkv, i_gl, i_st, i_mix, i_yh, i_rh, i_ao, i_mid, i_af, i_gu, i_dn,
    e_out, gm_out, gh_out, gp_out,
    d, h, mi, mo, fi, fo, f1, f2, bias, am, ah, au,
    ad, og, qkv, gl, st, mix, yh, rh, ao, mid, af, gu, dn,
    e, sgm, sgh, sgp,
    gm, gh, gp, gps, rgm, rgh, rgp, hidden, wide, gad, big, grad, dog, sendm, dmr, logit, fg, gstate, gt, dt, don, hidden_gated, sendq, dqkv, dlog, sendl, dlr, dproj,
    lsem, ssem, rsem, gssem, grsem,
):
    me = lax.axis_index("seq")
    T = h.shape[0]
    per = T // GROUP
    adapter = meta[2 * n_blocks]
    length = meta[2 * n_blocks + 1]
    loc = Local(lsem)
    l_d = loc.start(d_in, d)
    l_au = loc.start(w_au.at[layer], au)
    l_ah = loc.start(w_ah.at[layer], ah)
    l_fo = loc.start(w_fo.at[layer], fo)
    l_gu = loc.start(i_gu, gu)
    l_dn = loc.start(i_dn, dn)
    greet_peers(me)
    l_fi = loc.start(w_fi.at[layer], fi)
    l_am = loc.start(w_am.at[layer], am)
    l_mid = loc.start(i_mid, mid)
    l_af = loc.start(i_af, af)
    l_mo = loc.start(w_mo.at[layer], mo)
    l_og = loc.start(i_og, og)
    l_mix = loc.start(i_mix, mix)
    l_ao = loc.start(i_ao, ao)
    l_mixer = [
        loc.start(a, b)
        for a, b in (
            (w_f2.at[layer], f2), (w_b.at[layer], bias), (i_qkv, qkv), (i_gl, gl), (i_st, st), (i_yh, yh), (i_rh, rh),
        )
    ]
    l_last = [
        loc.start(a, b) for a, b in ((w_mi.at[layer], mi), (w_f1.at[layer], f1), (i_ad, ad), (h_in, h))
    ]
    mask = column_mask(adapter)
    pick = picked(adapter, ADAPTER_COLUMNS)

    def narrow(v):
        return nn(v, pick).astype(BF)

    def outer(u, v):
        return tn(narrow(u), v).astype(BF)

    n_dp, width, padded = gps.shape[1], gp.shape[1] // (HEADS * gps.shape[1]), gps.shape[3]
    quarter, hidden_quarter = MODEL_WIDTH // HEADS, gh.shape[1] // HEADS
    n_late = -(-FROZEN // (HEADS * width))
    mix_rows = 4 * ADAPTER_RANK

    def place(dps):
        for i in dps:
            for q in range(HEADS):
                piece = gp[:, (i * HEADS + q) * width : (i * HEADS + q + 1) * width]
                gps[q, i] = jnp.concatenate([piece, jnp.zeros((ADAPTER_RANK, padded - width), BF)], axis=1)

    def grad_copies(late):
        copies = []
        at = slice(0, mix_rows) if late else slice(mix_rows, 6 * ADAPTER_RANK)
        dps = slice(0, n_late) if late else slice(n_late, n_dp)
        for k in range(1, HEADS):
            peer = me ^ k
            pairs = [
                (gm.at[at, lanes(peer * quarter, quarter)], rgm.at[k - 1, at]),
                (gps.at[peer, dps], rgp.at[k - 1, dps]),
            ]
            if not late:
                pairs.append((gh.at[:, lanes(peer * hidden_quarter, hidden_quarter)], rgh.at[k - 1]))
            for i, (a, b) in enumerate(pairs):
                j = i if late else 2 + i
                copies.append(to_peer(a, b, gssem.at[j, k], grsem.at[j, k], peer))
        return copies

    l_d.wait()
    l_au.wait()
    gdown = (nt(d[...], au[:, U_D : U_D + MODEL_WIDTH]).astype(BF).astype(F32) * mask).astype(BF)
    gdown16 = narrow(gdown)
    gh[:, VALUE_WIDTH + HIDDEN_UNITS :] = jnp.zeros((ADAPTER_RANK, gh.shape[1] - VALUE_WIDTH - HIDDEN_UNITS), BF)
    l_dn.wait()
    gp[:, U_D : U_D + MODEL_WIDTH] = outer(dn[...], d[...])
    gad[...] = gdown
    l_ah.wait()
    l_fo.wait()
    l_gu.wait()

    def down_tile(i, carry):
        a, b = lanes(i * TILE, TILE), lanes(HIDDEN_UNITS + i * TILE, TILE)
        at = pl.ds(pl.multiple_of(i * TILE, TILE), TILE)
        dh = nt(d[...], fo[at, :]) + nt(gad[...], ah[pl.ds(pl.multiple_of(VALUE_WIDTH + i * TILE, TILE), TILE), :])
        gate, up = gu[:, a].astype(F32), gu[:, b].astype(F32)
        act, sig = silu_parts(gate)
        hidden[:, a] = (act * up).astype(BF)
        wide[:, a] = (dh * up * sig * (1.0 + gate * (1.0 - sig))).astype(BF)
        wide[:, b] = (dh * act).astype(BF)
        return carry

    lax.fori_loop(0, HIDDEN_UNITS // TILE, down_tile, 0)
    gate_cols, up_cols = slice(0, HIDDEN_UNITS), slice(HIDDEN_UNITS, 2 * HIDDEN_UNITS)
    gg = (nt(wide[:, gate_cols], au[:, U_G : U_G + HIDDEN_UNITS]).astype(BF).astype(F32) * mask).astype(BF)
    gu2 = (nt(wide[:, up_cols], au[:, U_U : U_U + HIDDEN_UNITS]).astype(BF).astype(F32) * mask).astype(BF)
    gad2 = jnp.concatenate([gg, gu2], axis=1)
    big[:, 0 : 2 * ADAPTER_COLUMNS] = gad2
    l_fi.wait()
    l_am.wait()

    def wide_tile(i, carry):
        at = pl.ds(pl.multiple_of(i * TILE, TILE), TILE)
        grad[:, lanes(i * TILE, TILE)] = nt(wide[...], fi[at, :]) + nt(
            big[:, 0 : 2 * ADAPTER_COLUMNS], am[at, 4 * ADAPTER_COLUMNS :]
        )
        return carry

    lax.fori_loop(0, MODEL_WIDTH // TILE, wide_tile, 0)
    l_mid.wait()
    mv = mid[...]
    grad_mid = d[...].astype(F32) + rms_back(mv, grad[...])
    grad[...] = grad_mid
    attn = grad_mid.astype(BF)
    e[...] = attn
    gout = (nt(attn, au[:, U_O : U_O + MODEL_WIDTH]).astype(BF).astype(F32) * mask).astype(BF)
    gad[...] = gout
    l_mo.wait()
    l_og.wait()
    l_mix.wait()

    def gate_back(head, out):
        at = rows(head * DV, DV)
        cols = lanes(head * DV, DV)
        gg_ = nt(e[...], mo[at, :]) + nt(gad[...], ah[at, :])
        o = og[:, cols]
        act, sig = silu_parts(o)
        out[...] = (gg_ * act).astype(BF)
        m = mix[head].astype(F32)
        dog[:, cols] = (gg_ * m * sig * (1.0 + o * (1.0 - sig))).astype(BF)
        hidden_gated[:, cols] = (m * act).astype(BF)

    mix_copies = []
    for k in range(1, HEADS):
        peer = me ^ k
        gate_back(peer, sendm.at[k - 1])
        copy = to_peer(sendm.at[k - 1], dmr.at[rows(me * T, T)], ssem.at[0, k], rsem.at[0, k], peer)
        copy.start()
        mix_copies.append(copy)
    gate_back(me, dmr.at[rows(me * T, T)])

    l_af.wait()
    l_ao.wait()
    normed_mid = (mv * inverse_rms(mv)).astype(BF)
    gh[:, VALUE_WIDTH : VALUE_WIDTH + HIDDEN_UNITS] = tn(gdown16, hidden[...]).astype(BF)
    gm[4 * ADAPTER_RANK : 5 * ADAPTER_RANK, :] = outer(gg, normed_mid)
    gm[5 * ADAPTER_RANK : 6 * ADAPTER_RANK, :] = outer(gu2, normed_mid)
    gp[:, U_G : U_G + HIDDEN_UNITS] = outer(af[:, 0:ADAPTER_COLUMNS], wide[:, gate_cols])
    gp[:, U_U : U_U + HIDDEN_UNITS] = outer(af[:, ADAPTER_COLUMNS:], wide[:, up_cols])
    gp[:, U_O : U_O + MODEL_WIDTH] = outer(ao[...], e[...])
    gh[:, 0:VALUE_WIDTH] = outer(gad[...], hidden_gated[...])
    place(range(n_late, n_dp))
    grads = grad_copies(False)
    for c in grads:
        c.start()

    for c in l_mixer:
        c.wait()
    f2h = f2[:, lanes(me * DK, DK)]
    bh = bias[:, lanes(me * DK, DK)]
    for src in range(HEADS):
        lg = tn(gl[src], f2h) + bh
        logit[src * T : (src + 1) * T, :] = lg
        fg[src * T : (src + 1) * T, :] = (jax.nn.log_sigmoid(lg) / 16.0).astype(BF)
    tri = lower_triangle(BF)
    causal = lower_triangle(F32)
    for c in mix_copies:
        c.wait_recv()
    gstate[...] = jnp.zeros_like(gstate)

    def retreat(i, carry):
        n = n_blocks - 1 - i
        at = pl.ds(meta[n_blocks + n] * GROUP, GROUP)
        here = rows(n * GROUP, GROUP)
        dm = dmr[at, :].astype(F32)
        yv = yh[at, :].astype(F32)
        r = rh[at, 0:1]
        do = (r * (dm - yv * jnp.mean(dm * yv, axis=-1, keepdims=True))).astype(BF)
        don[here, :] = do
        summed = nn(tri, fg[at, :])
        total = jnp.exp(summed[GROUP - 1 : GROUP])
        qs = (qkv[at, 0:DK].astype(F32) * SCALE * jnp.exp(summed)).astype(BF)
        now = gstate[...]
        gt[n] = now.astype(BF)
        decayed = total * now
        dt[n] = jnp.sum(decayed * st[n].astype(F32), axis=0, keepdims=True)
        gstate[...] = decayed + tn(do, qs)
        return carry

    lax.fori_loop(0, n_blocks, retreat, 0, unroll=4)

    def back_block(p, out, j):
        n = meta[p]
        at = rows(p * GROUP, GROUP)
        here = pl.ds(n * GROUP, GROUP)
        to = rows(j * GROUP, GROUP)
        live = live_rows(n, length)
        summed = nn(tri, fg[at, :])
        middle = summed[GROUP // 2 : GROUP // 2 + 1]
        total = summed[GROUP - 1 : GROUP]
        e1, e2 = jnp.exp(summed - middle), jnp.exp(middle - summed)
        es, eu = jnp.exp(summed), jnp.exp(total - summed)
        q = qkv[at, 0:DK].astype(F32) * SCALE
        k = qkv[at, DK : 2 * DK].astype(F32) * live
        v = qkv[at, 2 * DK : CHUNK]
        do, state_t, grad_t = don[here, :], st[n], gt[n]
        qe, ke, qs, ku = q * e1, k * e2, q * es, k * eu
        qeb, keb = qe.astype(BF), ke.astype(BF)
        scores = jnp.where(causal > 0, nt(qeb, keb), 0.0).astype(BF)
        dscores = jnp.where(causal > 0, nt(do, v), 0.0).astype(BF)
        dv = tn(scores, do) + nt(ku.astype(BF), grad_t)
        dqs = nn(do, state_t)
        dku = nn(v, grad_t)
        dqe = nn(dscores, keb)
        dke = tn(dscores, qeb)
        out[to, 0:DK] = (SCALE * (dqe * e1 + dqs * es)).astype(BF)
        out[to, DK : 2 * DK] = (live * (dke * e2 + dku * eu)).astype(BF)
        out[to, 2 * DK : CHUNK] = dv.astype(BF)
        kk = dku * ku
        dsum = dqe * qe + dqs * qs - dke * ke - kk
        dtotal = dt[n] + jnp.sum(kk, axis=0, keepdims=True)
        high = dsum.astype(BF)
        lowp = (dsum - high.astype(F32)).astype(BF)
        df = tn(tri, high) + tn(tri, lowp) + dtotal
        df = df.astype(BF).astype(F32)
        dlog[to, :] = (df * lax.logistic(-logit[at, :]) / 16.0).astype(BF)

    q_copies = []

    def back_rows(dest, out, low_out):
        lax.fori_loop(0, per, lambda j, c: (back_block(dest * per + j, out, j), c)[1], 0, unroll=2)
        low_out[...] = nt(f2h, dlog[...]).astype(BF)

    for k in range(1, HEADS):
        peer = me ^ k
        back_rows(peer, sendq.at[k - 1], sendl.at[k - 1])
        copies = (
            to_peer(sendq.at[k - 1], dqkv.at[me], ssem.at[1, k], rsem.at[1, k], peer),
            to_peer(sendl.at[k - 1], dlr.at[me], ssem.at[2, k], rsem.at[2, k], peer),
        )
        for copy in copies:
            copy.start()
        q_copies += copies
    back_rows(me, dqkv.at[me], dlr.at[me])

    for c in l_last:
        c.wait()
    hv = h[...].astype(F32)
    hr = inverse_rms(hv)
    big[...] = (hv * hr).astype(BF)
    for c in q_copies:
        c.wait_recv()
    for hd in range(HEADS):
        dproj[:, hd * DK : (hd + 1) * DK] = dqkv[hd, :, 0:DK]
        dproj[:, KEY + hd * DK : KEY + (hd + 1) * DK] = dqkv[hd, :, DK : 2 * DK]
        dproj[:, 2 * KEY + hd * DV : 2 * KEY + (hd + 1) * DV] = dqkv[hd, :, 2 * DK : CHUNK]
    dproj[:, 2 * KEY + VALUE_WIDTH :] = dog[...]
    dlow = dlr[0].astype(F32)
    for hd in range(1, HEADS):
        dlow += dlr[hd].astype(F32)
    dlowb = dlow.astype(BF)
    spans = ((0, KEY), (KEY, KEY), (2 * KEY, VALUE_WIDTH), (2 * KEY + VALUE_WIDTH, VALUE_WIDTH))
    for p, (start, span) in enumerate(spans):
        block = slice(p * ADAPTER_COLUMNS, (p + 1) * ADAPTER_COLUMNS)
        piece = dproj[:, start : start + span]
        ga = (nt(piece, au[:, start : start + span]).astype(BF).astype(F32) * mask).astype(BF)
        wide[:, block] = ga
        gm[p * ADAPTER_RANK : (p + 1) * ADAPTER_RANK, :] = outer(ga, big[...])
        gp[:, start : start + span] = outer(ad[:, block], piece)
    place(range(n_late))
    late_grads = grad_copies(True)
    for c in late_grads:
        c.start()
    z_w = f1.shape[2]
    tiles = f1.shape[0]
    back = []
    for j in range(tiles):
        at = slice(j * z_w, (j + 1) * z_w)
        back.append(
            nt(dproj[...], mi[at, :]) + nt(wide[:, 0 : 4 * ADAPTER_COLUMNS], am[at, 0 : 4 * ADAPTER_COLUMNS]) + tn(dlowb, f1[j])
        )
    dn_ = jnp.concatenate(back, axis=1)
    n = hv * hr
    e[...] = (grad[...] + hr * (dn_ - n * jnp.mean(dn_ * n, axis=-1, keepdims=True))).astype(BF)
    loc.start(e, e_out, True)
    grads += late_grads
    for c in grads:
        c.wait_recv()

    def summed_over_seq(own, got):
        total = own.astype(F32)
        for k in range(HEADS - 1):
            total += got[k].astype(F32)
        return total.astype(BF)

    sgm[...] = summed_over_seq(gm[:, lanes(me * quarter, quarter)], rgm)
    sgh[...] = summed_over_seq(gh[:, lanes(me * hidden_quarter, hidden_quarter)], rgh)
    spot = lax.broadcasted_iota(jnp.int32, (ADAPTER_RANK, padded), 1)
    for i in range(n_dp):
        total = gps[me, i].astype(F32)
        for k in range(HEADS - 1):
            total += rgp[k, i].astype(F32)
        sgp[i] = jnp.where(spot == width, adapter.astype(F32), total).astype(BF)
    for a, b in ((sgm, gm_out), (sgh, gh_out), (sgp, gp_out)):
        loc.start(a, b, True)
    loc.finish()
    for c in mix_copies + q_copies + grads:
        c.wait_send()


def backward(layer, meta, d, h, weights, saved, n_dp):
    T = h.shape[0]
    L = T * HEADS
    n_blocks = L // GROUP
    raised = U_D + MODEL_WIDTH
    padded = (raised // (n_dp * HEADS) // 128 + 1) * 128
    quarter = MODEL_WIDTH // HEADS
    hidden_quarter = -(-(VALUE_WIDTH + HIDDEN_UNITS) // (HEADS * 128)) * 128
    outs = [
        ((T, MODEL_WIDTH), BF),
        ((6 * ADAPTER_RANK, quarter), BF),
        ((ADAPTER_RANK, hidden_quarter), BF),
        ((n_dp, ADAPTER_RANK, padded), BF),
    ]
    vm = pltpu.VMEM
    dma = pltpu.SemaphoreType.DMA
    return pl.pallas_call(
        functools.partial(backward_kernel, layer, n_blocks),
        out_shape=[jax.ShapeDtypeStruct(*s) for s in outs],
        in_specs=[pl.BlockSpec(memory_space=pltpu.SMEM)] + [ANY] * (2 + len(weights) + len(saved)),
        out_specs=[ANY] * len(outs),
        scratch_shapes=[vm(d.shape, d.dtype), vm(h.shape, h.dtype)]
        + weight_scratch(weights)
        + [vm(s.shape, s.dtype) for s in saved]
        + [vm(*s) for s in outs]
        + [
            vm((6 * ADAPTER_RANK, MODEL_WIDTH), BF),
            vm((ADAPTER_RANK, HEADS * hidden_quarter), BF),
            vm((ADAPTER_RANK, raised), BF),
            vm((HEADS, n_dp, ADAPTER_RANK, padded), BF),
            vm((HEADS - 1, 6 * ADAPTER_RANK, quarter), BF),
            vm((HEADS - 1, ADAPTER_RANK, hidden_quarter), BF),
            vm((HEADS - 1, n_dp, ADAPTER_RANK, padded), BF),
            vm((T, HIDDEN_UNITS), BF),
            vm((T, 2 * HIDDEN_UNITS), BF),
            vm((T, ADAPTER_COLUMNS), BF),
            vm((T, MODEL_WIDTH), BF),
            vm((T, MODEL_WIDTH), F32),
            vm((T, VALUE_WIDTH), BF),
            vm((HEADS - 1, T, DV), BF),
            vm((L, DV), BF),
            vm((L, DK), F32),
            vm((L, DK), BF),
            vm((DV, DK), F32),
            vm((n_blocks, DV, DK), BF),
            vm((n_blocks, 1, DK), F32),
            vm((L, DV), BF),
            vm((T, VALUE_WIDTH), BF),
            vm((HEADS - 1, T, CHUNK), BF),
            vm((HEADS, T, CHUNK), BF),
            vm((T, DK), BF),
            vm((HEADS - 1, FGATE_RANK, T), BF),
            vm((HEADS, FGATE_RANK, T), BF),
            vm((T, FROZEN), BF),
            dma((2 + len(weights) + len(saved) + len(outs),)),
            dma((3, HEADS)),
            dma((3, HEADS)),
            dma((5, HEADS)),
            dma((5, HEADS)),
        ],
        compiler_params=pltpu.CompilerParams(
            collective_id=3 + layer, has_side_effects=True, vmem_limit_bytes=VMEM_LIMIT
        ),
        cost_estimate=pl.CostEstimate(flops=2 * T * 16_000_000, bytes_accessed=45 << 20, transcendentals=T * 8192),
    )(meta, d, h, *weights, *saved)


UNITS = [(layer, w) for layer in range(2) for w in range(4)]


def model_kernel(n_blocks, meta, *refs):
    n_w, n_small, n_saved, n_z = 4, 5, 14, 4
    refs = list(refs)

    def take(n):
        out = refs[:n]
        del refs[:n]
        return out

    shards = take(n_w)
    f1_ref, ends_ref = take(2)
    small = take(n_small)
    outs = take(n_w)
    (f1_out,) = take(1)
    (x_out, c_out) = take(2)
    small_out = take(n_small)
    saved = [take(n_saved), take(n_saved)]
    held = take(n_w)
    held_f1 = take(1)[0]
    held_small = take(n_small)
    work = take(1 + n_saved + 7)
    qkv2, gl2, mix2, held_ends = take(4)
    (ins, zs, zr, ts, tr, xs, xr, ys, yr, fxs, fxr, fys, fyr, cs, cr, own, ms, mr, es, er, f1s, f1r, f1c, lsem, ssem, rsem) = take(26)
    core, z, s = lax.axis_index("section"), lax.axis_index("dp"), lax.axis_index("seq")
    other = 1 - core

    def remote(src, dst, send_sem, recv_sem, **where):
        return pltpu.make_async_remote_copy(
            src_ref=src, dst_ref=dst, send_sem=send_sem, recv_sem=recv_sem, device_id=where, device_id_type=MESH
        )

    def height(w):
        return shards[w].shape[1]

    def staged(w):
        return held[w].at[pl.ds(pl.multiple_of(z * height(w), 16), height(w))]

    fetch = [pltpu.make_async_copy(shards[w].at[0], staged(w), ins.at[w]) for w in range(n_w)]
    fetch += [pltpu.make_async_copy(a.at[0], b, ins.at[n_w + i]) for i, (a, b) in enumerate(zip(small, held_small))]
    fetch.append(pltpu.make_async_copy(ends_ref.at[0, :, 0], held_ends, ins.at[n_w + n_small]))
    fetch.append(pltpu.make_async_copy(f1_ref, held_f1.at[z], ins.at[n_w + n_small + 1]))
    for f in fetch:
        f.start()

    barrier = pltpu.get_barrier_semaphore()
    greeted = [dict(section=other)] + [dict(seq=s ^ k) for k in range(1, HEADS)]
    greeted += [dict(dp=lax.rem(z + gap, n_z)) for gap in range(1, n_z)]
    for where in greeted:
        pl.semaphore_signal(barrier, inc=1, device_id=where, device_id_type=MESH)
    pl.semaphore_wait(barrier, len(greeted))

    def part(u, j, start, size, strip=False):
        layer, w = UNITS[u]
        cols = shards[w].shape[2] // 2
        at, wide = (cols - STRIPS[w], STRIPS[w]) if strip else (0, cols - STRIPS[w])
        return outs[w].at[layer, pl.ds(pl.multiple_of(j * height(w) + start, 16), size), lanes(core * cols + at, wide)]

    def piece(u, j, q):
        r = height(UNITS[u][1])
        return part(u, j, q * (r // 4), r // 4)

    def half(u, j, q, low):
        r = height(UNITS[u][1])
        cut = (r // 8 + 15) // 16 * 16
        start, size = (0, cut) if low else (cut, r // 4 - cut)
        return part(u, j, q * (r // 4) + start, size)

    def block(u, j):
        layer, w = UNITS[u]
        cols = shards[w].shape[2] // 2
        return outs[w].at[layer, pl.ds(pl.multiple_of(j * height(w), 16), height(w)), lanes(core * cols, cols)]

    def whole_block(layer, w):
        return outs[w].at[layer, pl.ds(pl.multiple_of(z * height(w), 16), height(w))]

    def step(d):
        return 1 if d == 0 else -1

    def can_send(d, t):
        has_next = (z < n_z - 1) if d == 0 else (z > 0)
        first = z - step(d) * (t - 1)
        return jnp.logical_and(has_next, jnp.logical_and(first >= 0, first < n_z))

    def gets(d, t):
        first = z - step(d) * t
        return jnp.logical_and(first >= 0, first < n_z)

    def origin(d, t):
        return z - step(d) * t

    def z_copy(u, d, t):
        ref = piece(u, z - step(d) * (t - 1), s)
        return remote(ref, ref, zs.at[u, d, t - 1], zr.at[u, d, t - 1], dp=z + step(d))

    def t_copy(u, d, t):
        ref = part(u, z - step(d) * (t - 1), 0, height(UNITS[u][1]), True)
        return remote(ref, ref, ts.at[u, d, t - 1], tr.at[u, d, t - 1], dp=z + step(d))

    def x_copy(u, d, t):
        ref = piece(u, origin(d, t), s)
        return remote(ref, ref, xs.at[u, d, t - 1], xr.at[u, d, t - 1], seq=s ^ 1)

    def y_copy(u, d, t):
        ref = piece(u, origin(d, t), s)
        return remote(ref, ref, ys.at[u, d, t - 1], yr.at[u, d, t - 1], seq=s ^ 2)

    def fx_copy(u, d, t):
        ref = half(u, origin(d, t), s ^ 2, False)
        return remote(ref, ref, fxs.at[u, d, t - 1], fxr.at[u, d, t - 1], seq=s ^ 1)

    def fy_copy(u, d, t):
        ref = half(u, origin(d, t), s ^ 1, True)
        return remote(ref, ref, fys.at[u, d, t - 1], fyr.at[u, d, t - 1], seq=s ^ 2)

    def c_copy(u, d, t):
        ref = block(u, origin(d, t))
        return remote(ref, ref, cs.at[u, d, t - 1], cr.at[u, d, t - 1], section=other)

    def own_copy(w):
        return pltpu.make_async_copy(staged(w), whole_block(core, w), own.at[w])

    def own_cross(w):
        return remote(staged(w), whole_block(core, w), ms.at[n_small + w], mr.at[n_small + w], section=other)

    def start_own(u):
        layer, w = UNITS[u]

        if layer == 0:
            own_copy(w).wait()

        @pl.when(core != layer)
        def _():
            own_cross(w).wait_recv()

        for d in range(2):
            @pl.when(can_send(d, 1))
            def _():
                z_copy(u, d, 1).start()
                t_copy(u, d, 1).start()

    def take_z(u, t):
        for d in range(2):
            @pl.when(gets(d, t))
            def _():
                z_copy(u, d, t).wait_recv()
            if t < n_z - 1:
                @pl.when(can_send(d, t + 1))
                def _():
                    z_copy(u, d, t + 1).start()
            @pl.when(gets(d, t))
            def _():
                x_copy(u, d, t).start()
                y_copy(u, d, t).start()
                t_copy(u, d, t).wait_recv()
            if t < n_z - 1:
                @pl.when(can_send(d, t + 1))
                def _():
                    t_copy(u, d, t + 1).start()

    def take_xy(u, t):
        for d in range(2):
            @pl.when(gets(d, t))
            def _():
                x_copy(u, d, t).wait_recv()
                fy_copy(u, d, t).start()
                y_copy(u, d, t).wait_recv()
                fx_copy(u, d, t).start()

    def take_diagonal(u, t):
        for d in range(2):
            @pl.when(gets(d, t))
            def _():
                fy_copy(u, d, t).wait_recv()
                fx_copy(u, d, t).wait_recv()
                c_copy(u, d, t).start()

    def take_core(u):
        for d in range(2):
            for t in range(1, n_z):
                @pl.when(gets(d, t))
                def _():
                    c_copy(u, d, t).wait_recv()

    for f in fetch:
        f.wait()
    for w in range(n_w):
        own_copy(w).start()
        own_cross(w).start()

    def f1_copy(gap):
        return remote(held_f1.at[z], f1_out.at[core, z], f1s.at[gap], f1r.at[gap], dp=lax.rem(z + gap, n_z))

    f1_sends = [f1_copy(gap) for gap in range(1, n_z)]
    for c in f1_sends:
        c.start()
    f1_own = pltpu.make_async_copy(held_f1.at[z], f1_out.at[core, z], own.at[n_w])
    f1_own.start()
    smalls = []
    for i, (a, b) in enumerate(zip(held_small, small_out)):
        mine = pltpu.make_async_copy(a, b.at[core], own.at[n_w + 2 + i])
        theirs = remote(a, b.at[core], ms.at[i], mr.at[i], section=other)
        mine.start()
        theirs.start()
        smalls.append((mine, theirs))
    ends_to_x = remote(held_ends.at[1], x_out, es, er, section=other)
    ends_to_c = remote(held_ends.at[0], c_out, es, er, section=other)
    ends_x = pltpu.make_async_copy(held_ends.at[0], x_out, own.at[n_w + 1])
    ends_c = pltpu.make_async_copy(held_ends.at[1], c_out, own.at[n_w + 1])

    @pl.when(core == 0)
    def _():
        ends_to_x.start()
        ends_x.start()

    @pl.when(core == 1)
    def _():
        ends_to_c.start()
        ends_c.start()

    f1_cross = remote(f1_out.at[core], f1_out.at[core], f1c.at[0], f1c.at[1], section=other)
    start_own(0)
    f1_own.wait()
    for c in f1_sends:
        c.wait_recv()
    f1_cross.start()
    for w in range(n_w):
        own_cross(w).wait_send()
    for mine, theirs in smalls:
        mine.wait()
        theirs.wait()
    for c in f1_sends:
        c.wait_send()
    f1_cross.wait()
    ends_x.wait()
    ends_to_x.wait()

    items = [(u, t) for u in range(len(UNITS)) for t in range(1, n_z)]
    ready, clock = [], 8.0
    for u, t in items:
        r, c = shards[UNITS[u][1]].shape[1:]
        clock += r // 4 * (c - 2 * STRIPS[UNITS[u][1]]) * 3 / LINK_BYTES_PER_US
        ready.append(clock)

    def gather_step(i):
        if i < len(items):
            u, t = items[i]
            if t == 1 and u + 1 < len(UNITS):
                start_own(u + 1)
            take_z(u, t)
        if 0 <= i - SKEW[0] < len(items):
            take_xy(*items[i - SKEW[0]])
        if 0 <= i - SKEW[1] < len(items):
            take_diagonal(*items[i - SKEW[1]])

    loc = Local(lsem)
    loaded = loc.start(x_out, work[0])
    loaded.wait()
    n_steps = len(items) + SKEW[1]
    works = [list(work), list(work)]
    for at, ref in ((4, qkv2), (5, gl2), (7, mix2)):
        works[1][at] = ref

    def both_layers():
        for layer in range(2):
            sources = dict(zip(NAMES[:4], outs))
            sources["f1"] = f1_out
            sources.update(zip(NAMES[5:], small_out))
            sources = {name: ref.at[layer] for name, ref in sources.items()}
            buffers = dict(zip(NAMES, held + [held_f1] + held_small))
            for what, us in forward_steps(
                layer, n_blocks, meta, loc, sources, buffers, works[layer], saved[layer], (ssem.at[layer], rsem.at[layer])
            ):
                yield layer, what, us
            if layer == 0:
                work[0][...] = work[1][...]

    steps, done, now, crossed, until = both_layers(), 0, 8.0, set(), None
    pending = next(steps)
    while pending is not None or done < n_steps:
        due = ready[min(max(done - 2, 0), len(ready) - 1)]
        blocked = False
        if pending is not None and pending[1] in NAMES[:4]:
            u = UNITS.index((pending[0], NAMES.index(pending[1])))
            blocked = done < min(3 * u + 3 + SKEW[1], n_steps)
            if not blocked:
                take_core(u)
                crossed.add(u)
        elif pending is not None and pending[1] == "delay":
            until = now + pending[2] if until is None else until
            blocked = now < until and due < until
        if done < n_steps and (pending is None or blocked or due <= now):
            now = max(now, due)
            gather_step(done)
            done += 1
            continue
        now = now + pending[2] if until is None else max(now, until)
        until = None
        pending = next(steps, None)
    for u in range(len(UNITS)):
        if u not in crossed:
            take_core(u)
        for d in range(2):
            for t in range(1, n_z):
                @pl.when(can_send(d, t))
                def _():
                    z_copy(u, d, t).wait_send()
                    t_copy(u, d, t).wait_send()
                @pl.when(gets(d, t))
                def _():
                    x_copy(u, d, t).wait_send()
                    y_copy(u, d, t).wait_send()
                    fx_copy(u, d, t).wait_send()
                    fy_copy(u, d, t).wait_send()
                    c_copy(u, d, t).wait_send()


def forward_model(meta, shards, f1t, ends, small):
    shape, dma, vm = jax.ShapeDtypeStruct, pltpu.SemaphoreType.DMA, pltpu.VMEM
    T = ends.shape[3]
    L = T * HEADS
    n_blocks = L // GROUP
    saved = saved_shapes(T, L, n_blocks)
    n_w, n_small, n_u = len(shards), len(small), len(UNITS)
    outs = [shape((2, 4 * w.shape[1], w.shape[2]), w.dtype) for w in shards]
    outs.append(shape((2, 4) + f1t.shape, f1t.dtype))
    outs += [shape(ends.shape[3:], ends.dtype)] * 2
    outs += [shape((2,) + a.shape[1:], a.dtype) for a in small]
    outs += [shape(*s) for s in saved] * 2
    full = [vm((4 * w.shape[1], w.shape[2]), w.dtype) for w in shards]
    out = pl.pallas_call(
        functools.partial(model_kernel, n_blocks),
        out_shape=outs,
        in_specs=[pl.BlockSpec(memory_space=pltpu.SMEM)] + [ANY] * (n_w + 2 + n_small),
        out_specs=[ANY] * len(outs),
        scratch_shapes=full
        + [vm((4,) + f1t.shape, f1t.dtype)]
        + [vm(a.shape[1:], a.dtype) for a in small]
        + work_scratch(T, L, saved)
        + [vm((L, CHUNK), BF), vm((HEADS, FGATE_RANK, T), BF), vm((HEADS, T, DV), BF), vm((2,) + ends.shape[3:], BF)]
        + [dma((n_w + n_small + 2,))]
        + [dma((n_u, 2, 3)) for _ in range(14)]
        + [dma((n_w + n_small + 2,)), dma((n_small + n_w,)), dma((n_small + n_w,)), dma, dma, dma((4,)), dma((4,)), dma((2,))]
        + [dma((1 + 2 * (len(NAMES) + len(saved)),)), dma((2, 3, HEADS)), dma((2, 3, HEADS))],
        compiler_params=pltpu.CompilerParams(collective_id=0, has_side_effects=True, vmem_limit_bytes=VMEM_LIMIT),
    )(meta, *shards, f1t, ends, *small)
    weights = list(out[:5]) + list(out[7:12])
    return weights, out[5], out[6], out[12 : 12 + len(saved)], out[12 + len(saved) :]


def swap_sections(v):
    return lax.ppermute(v, "section", [(0, 1), (1, 0)])


def plain_gather(shards, f1t, ends, small):
    first = lax.axis_index("section") == 0
    both = lambda a: lax.all_gather(a, "section", axis=0)
    outs = [both(lax.all_gather(w[0], "dp", axis=0, tiled=True)) for w in shards]
    low = lax.all_gather(f1t, "dp", axis=1, tiled=True)
    outs.append(both(jnp.stack(jnp.split(low, 4, axis=1))))
    sent = swap_sections(jnp.where(first, ends[0, 1, 0], ends[0, 0, 0]))
    outs.append(jnp.where(first, ends[0, 0, 0], sent))
    outs.append(jnp.where(first, sent, ends[0, 1, 0]))
    return outs + [both(a[0]) for a in small]


def spread(parts, chosen):
    hot = (chosen[:, None] == jnp.arange(ADAPTERS, dtype=jnp.int32)[None, :]).astype(F32)
    return sum(parts[n][:, None] * hot[n][None, :, None, None] for n in range(parts.shape[0]))


def reduce_kernel(
    gm0, gh0, gp0, gm1, gh1, gp1, m_out, h_out, u_out,
    vm_, vh, vp, rm, rh, rp, am, ah, em, eh, ls, ss, rs, es, er,
):
    core, dp, me = lax.axis_index("section"), lax.axis_index("dp"), lax.axis_index("seq")
    n_dp = vp.shape[1]
    width = u_out.shape[1]
    loads = [
        pltpu.make_async_copy(a, b.at[l], ls.at[l, i])
        for l, three in enumerate(((gm0, gh0, gp0), (gm1, gh1, gp1)))
        for i, (a, b) in enumerate(zip(three, (vm_, vh, vp)))
    ]
    for c in loads:
        c.start()
    barrier = pltpu.get_barrier_semaphore()
    places = [dict(section=1 - core)] + [dict(seq=me ^ k) for k in range(1, HEADS)]
    for gap in range(1, n_dp):
        to = lax.rem(dp + gap, n_dp)
        places += [dict(dp=to), dict(section=1 - core, dp=to)]
    for where in places:
        pl.semaphore_signal(barrier, inc=1, device_id=where, device_id_type=MESH)
    for c in loads:
        c.wait()
    pl.semaphore_wait(barrier, len(places))
    slot = dp * 2 + core
    size = 6 * ADAPTER_COLUMNS // n_dp

    def first_projection(i):
        return i * size // ADAPTER_COLUMNS

    def parts(layer, to):
        at = pl.ds(pl.multiple_of(first_projection(to) * ADAPTER_RANK, ADAPTER_RANK), 2 * ADAPTER_RANK)
        return ((vm_.at[layer, at], rm.at[slot]), (vh.at[layer], rh.at[slot]), (vp.at[layer, to], rp.at[slot]))

    copies = []
    for gap in range(n_dp - 1, -1, -1):
        to = lax.rem(dp + gap, n_dp)
        for crossing in (0, 1):
            if crossing == 0 and gap == 0:
                continue
            section = 1 - core if crossing else core
            for i, (a, b) in enumerate(parts(section, to)):
                c = pltpu.make_async_remote_copy(
                    src_ref=a, dst_ref=b, send_sem=ss.at[crossing, gap, i], recv_sem=rs.at[crossing, gap, i],
                    device_id=dict(section=section, dp=to), device_id_type=MESH,
                )
                c.start()
                copies.append(c)
    at = pl.ds(pl.multiple_of(first_projection(dp) * ADAPTER_RANK, ADAPTER_RANK), 2 * ADAPTER_RANK)
    rm[slot] = vm_[core, at]
    rh[slot] = vh[core]
    rp[slot] = vp[core, dp]
    for c in copies:
        c.wait_recv()
    n = rm.shape[0]
    chosen = [rp[j, :, width : width + 1].astype(F32) for j in range(n)]
    for a in range(ADAPTERS):
        hot = [(c == float(a)).astype(F32) for c in chosen]
        at = slice(a * ADAPTER_RANK, (a + 1) * ADAPTER_RANK)

        def total(values):
            out = hot[0] * values(0).astype(F32)
            for j in range(1, n):
                out += hot[j] * values(j).astype(F32)
            return out

        for p in range(2):
            am[p * ADAPTER_COLUMNS + a * ADAPTER_RANK : p * ADAPTER_COLUMNS + (a + 1) * ADAPTER_RANK, :] = total(
                lambda j, p=p: rm[j, p * ADAPTER_RANK : (p + 1) * ADAPTER_RANK]
            )
        ah[at, :] = total(lambda j: rh[j])
        u_out[at, :] = total(lambda j: rp[j])[:, 0:width]
    own_m, own_h = size // HEADS, ADAPTER_COLUMNS // n_dp // HEADS
    base = dp * size - first_projection(dp) * ADAPTER_COLUMNS

    def m_rows(q):
        return am.at[pl.ds(pl.multiple_of(base + q * own_m, 16), own_m)]

    def h_rows(q):
        return ah.at[pl.ds(pl.multiple_of(dp * HEADS * own_h + q * own_h, 8), own_h)]

    last = []
    for k in range(1, HEADS):
        for i, (a, b) in enumerate(((m_rows(me ^ k), em.at[me]), (h_rows(me ^ k), eh.at[me]))):
            c = to_peer(a, b, es.at[i, k], er.at[i, k], me ^ k)
            c.start()
            last.append(c)
    em[me] = m_rows(me)[...]
    eh[me] = h_rows(me)[...]
    for c in last:
        c.wait_recv()
    for q in range(HEADS):
        m_out[:, q * em.shape[2] : (q + 1) * em.shape[2]] = em[q]
        h_out[:, q * eh.shape[2] : (q + 1) * eh.shape[2]] = eh[q]
    for c in copies + last:
        c.wait_send()


def reduce_gradients(early, late, n_dp):
    gm, gh, gp = early
    n = 2 * n_dp
    width = (U_D + MODEL_WIDTH) // (n_dp * HEADS)
    own_m, own_h = 6 * ADAPTER_COLUMNS // (n_dp * HEADS), ADAPTER_COLUMNS // (n_dp * HEADS)
    vm, dma, VM = pltpu.VMEM, pltpu.SemaphoreType.DMA, pl.BlockSpec(memory_space=pltpu.VMEM)
    shape = jax.ShapeDtypeStruct
    model, hidden, up = pl.pallas_call(
        reduce_kernel,
        out_shape=[
            shape((own_m, MODEL_WIDTH), F32),
            shape((own_h, HEADS * gh.shape[1]), F32),
            shape((ADAPTER_COLUMNS, width), F32),
        ],
        in_specs=[ANY] * 6,
        out_specs=[VM] * 3,
        scratch_shapes=[
            vm((2,) + gm.shape, BF),
            vm((2,) + gh.shape, BF),
            vm((2,) + gp.shape, BF),
            vm((n, 2 * ADAPTER_RANK, gm.shape[1]), BF),
            vm((n,) + gh.shape, BF),
            vm((n,) + gp.shape[1:], BF),
            vm((2 * ADAPTER_COLUMNS, gm.shape[1]), F32),
            vm((ADAPTER_COLUMNS, gh.shape[1]), F32),
            vm((HEADS, own_m, gm.shape[1]), F32),
            vm((HEADS, own_h, gh.shape[1]), F32),
            dma((2, 3)),
            dma((2, n_dp, 3)),
            dma((2, n_dp, 3)),
            dma((2, HEADS)),
            dma((2, HEADS)),
        ],
        compiler_params=pltpu.CompilerParams(collective_id=5, has_side_effects=True, vmem_limit_bytes=32 << 20),
    )(*early, *late)
    return model.T, hidden[:, : VALUE_WIDTH + HIDDEN_UNITS].T, up


def plain_reduce(early, late, n_dp):
    first = lax.axis_index("section") == 0
    dp = lax.axis_index("dp")
    kept = [jnp.where(first, a, b) for a, b in zip(early, late)]
    got = [swap_sections(jnp.where(first, b, a)) for a, b in zip(early, late)]
    gm, gh, gp = [jnp.stack(pair) for pair in zip(kept, got)]
    width = (U_D + MODEL_WIDTH) // (n_dp * HEADS)
    gm = lax.all_gather(gm, "dp", axis=0)
    gh = lax.all_gather(gh, "dp", axis=0)
    gp = lax.all_to_all(jnp.swapaxes(gp, 0, 1), "dp", split_axis=0, concat_axis=0, tiled=True)
    gp = gp.reshape(2 * n_dp, 1, ADAPTER_RANK, -1)
    n = gp.shape[0]
    chosen = gp[:, 0, 0, width].astype(jnp.int32)
    gm = spread(gm.reshape(n, 6, ADAPTER_RANK, -1).astype(F32), chosen).reshape(6 * ADAPTER_COLUMNS, -1)
    gh = spread(gh.reshape(n, 1, ADAPTER_RANK, -1).astype(F32), chosen).reshape(ADAPTER_COLUMNS, -1)
    gp = spread(gp.astype(F32), chosen).reshape(ADAPTER_COLUMNS, -1)

    def columns(v):
        size = v.shape[0] // n_dp
        v = lax.dynamic_slice_in_dim(v, dp * size, size, 0)
        return lax.all_to_all(v, "seq", split_axis=0, concat_axis=1, tiled=True).T

    return columns(gm), columns(gh)[: VALUE_WIDTH + HIDDEN_UNITS], gp[:, :width]


def local(
    ends,
    mixer_input_weight,
    forget_first_map,
    forget_second_map,
    forget_logit_bias,
    mixer_output_weight,
    feedforward_input_weight,
    feedforward_output_weight,
    adapter_model_first,
    adapter_hidden_first,
    adapter_second_maps,
    lengths,
    dealt_block_order,
    adapter_choice_per_seq,
):
    first = lax.axis_index("section") == 0
    mine = lambda a: jnp.where(first, a[0], a[1])
    order = mine(dealt_block_order)[0]
    n_blocks = order.shape[0]
    at = jnp.arange(n_blocks, dtype=jnp.int32)
    inverse = jnp.sum(at[:, None] * (order[:, None] == at[None, :]).astype(jnp.int32), axis=0)
    meta = jnp.concatenate([order, inverse, mine(adapter_choice_per_seq), mine(lengths)])
    n_dp = lax.axis_size("dp")
    own_kernels = n_dp == 4 and lax.axis_size("seq") == 4
    shards = [mixer_input_weight, mixer_output_weight, feedforward_input_weight, feedforward_output_weight]
    small = [
        forget_second_map,
        forget_logit_bias[:, None],
        adapter_model_first,
        adapter_hidden_first,
        adapter_second_maps,
    ]
    if own_kernels:
        weights, x, cotangent, early, late = forward_model(meta, shards, forget_first_map[0].T, ends, small)
    else:
        out = plain_gather(shards, forget_first_map[0].T, ends, small)
        weights, x, cotangent = list(out[:5]) + list(out[7:]), out[5], out[6]
        early = forward(0, meta, x, weights)
        late = forward(1, meta, early[0], weights)
    middle, *grads_late = backward(1, meta, cotangent, early[0], weights, late[1:], n_dp)
    entry, *grads_early = backward(0, meta, middle, x, weights, early[1:], n_dp)
    sent = swap_sections(jnp.where(first, late[0], entry))
    results = jnp.where(first, jnp.stack([entry, sent]), jnp.stack([sent, late[0]]))
    reduce = reduce_gradients if own_kernels else plain_reduce
    model, hidden, up = reduce(grads_early, grads_late, n_dp)
    return (results[None, :, None], model[None], hidden[None], up[None])


def solution(mesh):
    return jax.shard_map(
        local,
        mesh=mesh,
        in_specs=(
            P("section", None, "dp", "seq", None),
            P("section", "dp", None),
            P("section", "dp", None),
            P("section", None, None),
            P("section", None),
            P("section", "dp", None),
            P("section", "dp", None),
            P("section", "dp", None),
            P("section", None, None),
            P("section", None, None),
            P("section", None, None),
            P(None, "dp"),
            P(None, "dp", None),
            P(None, "dp"),
        ),
        out_specs=(
            P("section", None, "dp", "seq", None),
            P("section", None, ("dp", "seq")),
            P("section", None, ("dp", "seq")),
            P("section", None, ("dp", "seq")),
        ),
        check_vma=False,
    )
```

```python
import functools
import jax
import jax.numpy as jnp
from jax import lax
from jax.experimental import pallas as pl
from jax.experimental.pallas import tpu as pltpu

from jax.sharding import PartitionSpec as P

MODEL_WIDTH = 1024
HEADS = 4
KEY = 512
VALUE_WIDTH = 1024
HIDDEN_UNITS = 2816
FGATE_RANK = 16
GROUP = 64
ADAPTER_RANK = 16
ADAPTERS = 8
ADAPTER_COLUMNS = 128
VMEM_LIMIT = 60 << 20
LINK_BYTES_PER_US = 72e3
SKEW = (2, 4)
DELAYS = (8, 18, 12)
STRIPS = (256, 128, 384, 128)

MESH = pl.DeviceIdType.MESH
ANY = pl.BlockSpec(memory_space=pl.ANY)


BF = jnp.bfloat16
F32 = jnp.float32


def nn(a, b):
    return lax.dot_general(a, b, (((1,), (0,)), ((), ())), preferred_element_type=F32)


def nt(a, b):
    return lax.dot_general(a, b, (((1,), (1,)), ((), ())), preferred_element_type=F32)


def tn(a, b):
    return lax.dot_general(a, b, (((0,), (0,)), ((), ())), preferred_element_type=F32)


def silu_parts(v):
    sig = lax.logistic(v)
    return v * sig, sig


def inverse_rms(v):
    return lax.rsqrt(jnp.mean(v * v, axis=-1, keepdims=True) + 1e-06)


def rms_back(v, grad):
    r = inverse_rms(v)
    n = v * r
    return r * (grad - n * jnp.mean(grad * n, axis=-1, keepdims=True))


def lanes(start, size):
    return pl.ds(pl.multiple_of(start, 128), size)


def rows(start, size):
    return pl.ds(pl.multiple_of(start, size if size <= 64 else 64), size)


def greet_peers(me):
    barrier = pltpu.get_barrier_semaphore()
    for d in range(1, HEADS):
        pl.semaphore_signal(barrier, inc=1, device_id={"seq": me ^ d}, device_id_type=MESH)
    pl.semaphore_wait(barrier, HEADS - 1)


def to_peer(src, dst, ssem, rsem, peer):
    return pltpu.make_async_remote_copy(
        src_ref=src, dst_ref=dst, send_sem=ssem, recv_sem=rsem,
        device_id={"seq": peer}, device_id_type=MESH,
    )


class Local:
    def __init__(self, sems):
        self.sems, self.used, self.open = sems, 0, []

    def start(self, src, dst, wait_at_end=False):
        copy = pltpu.make_async_copy(src, dst, self.sems.at[self.used])
        self.used += 1
        copy.start()
        if wait_at_end:
            self.open.append(copy)
        return copy

    def finish(self):
        for copy in self.open:
            copy.wait()
        self.open = []


def picked(adapter, width):
    row = lax.broadcasted_iota(jnp.int32, (width, ADAPTER_RANK), 0)
    col = lax.broadcasted_iota(jnp.int32, (width, ADAPTER_RANK), 1)
    return (row == adapter * ADAPTER_RANK + col).astype(BF)


def column_mask(adapter):
    col = lax.broadcasted_iota(jnp.int32, (1, ADAPTER_COLUMNS), 1)
    low = adapter * ADAPTER_RANK
    return jnp.logical_and(col >= low, col < low + ADAPTER_RANK).astype(F32)


def lower_triangle(dtype):
    i = lax.broadcasted_iota(jnp.int32, (GROUP, GROUP), 0)
    j = lax.broadcasted_iota(jnp.int32, (GROUP, GROUP), 1)
    return (i >= j).astype(dtype)


DK = KEY // HEADS
DV = VALUE_WIDTH // HEADS
CHUNK = 2 * DK + DV
FROZEN = 2 * KEY + 2 * VALUE_WIDTH
TILE = 256
SCALE = DK ** (-0.5)

U_G = FROZEN
U_U = FROZEN + HIDDEN_UNITS
U_O = FROZEN + 2 * HIDDEN_UNITS
U_D = U_O + MODEL_WIDTH


def live_rows(n, length):
    at = lax.broadcasted_iota(jnp.int32, (GROUP, 1), 0) + n * GROUP
    return (at < length).astype(F32)


def forward_steps(layer, n_blocks, meta, loc, weights, buffers, work, outs, sems):
    w, v = weights, buffers
    (h, y, ad, og, qkv, gl, st, mix, yh, rh, ao, mid, af, gu, dn, normed, send, glsend, fg, state, gated, hidden) = work
    o_y, o_ad, o_og, o_qkv, o_gl, o_st, o_mix, o_yh, o_rh, o_ao, o_mid, o_af, o_gu, o_dn = outs
    ssem, rsem = sems
    me = lax.axis_index("seq")
    T = h.shape[0]
    per = T // GROUP
    adapter = meta[2 * n_blocks]
    length = meta[2 * n_blocks + 1]
    mask = column_mask(adapter)
    am, ah, au, mi, mo, fi, fo = [v[name] for name in ("am", "ah", "au", "mi", "mo", "fi", "fo")]

    def load(*names):
        return [loc.start(w[name], v[name]) for name in names]

    def wait(copies):
        for c in copies:
            c.wait()

    yield "small", 0
    small = load("f1", "f2", "b", "am", "au", "ah")
    yield None, 2
    hv = h[...].astype(F32)
    normed[...] = (hv * inverse_rms(hv)).astype(BF)
    wait(small)
    f1, f2, bias = v["f1"], v["f2"], v["b"]
    z_w = f1.shape[2]
    low = nt(f1[0], normed[:, 0:z_w])
    for j in range(1, f1.shape[0]):
        low += nt(f1[j], normed[:, j * z_w : (j + 1) * z_w])
    glsend[...] = low.astype(BF)
    low_copies = [to_peer(glsend, gl.at[me], ssem.at[0, d], rsem.at[0, d], me ^ d) for d in range(1, HEADS)]
    for c in low_copies:
        c.start()
    gl[me] = glsend[...]
    yield "delay", DELAYS[0]
    for p in range(4):
        cols = pl.ds(p * ADAPTER_COLUMNS, ADAPTER_COLUMNS)
        ad[:, cols] = (nn(normed[...], am[:, cols]) * mask).astype(BF)
    f2h = f2[:, lanes(me * DK, DK)]
    bh = bias[:, lanes(me * DK, DK)]
    for c in low_copies:
        c.wait_recv()
    for src in range(HEADS):
        logit = tn(gl[src], f2h) + bh
        fg[src * T : (src + 1) * T, :] = (jax.nn.log_sigmoid(logit) / 16.0).astype(BF)
    loc.start(gl, o_gl, True)
    loc.start(ad, o_ad, True)
    yield "mi", 0
    wait(load("mi"))

    def project(w_start, p, width):
        cols = lanes(w_start, width)
        return nn(normed[...], mi[:, cols]) + nn(ad[:, p * ADAPTER_COLUMNS : (p + 1) * ADAPTER_COLUMNS], au[:, cols])

    def chunk(head, ref):
        ref[:, 0:DK] = project(head * DK, 0, DK).astype(BF)
        ref[:, DK : 2 * DK] = project(KEY + head * DK, 1, DK).astype(BF)
        ref[:, 2 * DK : CHUNK] = project(2 * KEY + head * DV, 2, DV).astype(BF)

    qkv_copies = []
    for d in range(1, HEADS):
        yield None, 1
        chunk(me ^ d, send.at[d - 1])
        copy = to_peer(send.at[d - 1], qkv.at[rows(me * T, T)], ssem.at[1, d], rsem.at[1, d], me ^ d)
        copy.start()
        qkv_copies.append(copy)
    yield None, 1
    chunk(me, qkv.at[rows(me * T, T)])
    yield None, 1
    for j in range(VALUE_WIDTH // TILE):
        og[:, j * TILE : (j + 1) * TILE] = project(2 * KEY + VALUE_WIDTH + j * TILE, 3, TILE)
    loc.start(og, o_og, True)
    yield "delay", DELAYS[1]
    for c in qkv_copies:
        c.wait_recv()
    loc.start(qkv, o_qkv, True)
    tri = lower_triangle(BF)
    causal = lower_triangle(F32)
    state[...] = jnp.zeros_like(state)

    def advance(n, carry):
        at = pl.ds(meta[n_blocks + n] * GROUP, GROUP)
        summed = nn(tri, fg[at, :])
        total = summed[GROUP - 1 : GROUP]
        k = qkv[at, DK : 2 * DK].astype(F32) * live_rows(n, length)
        ku = (k * jnp.exp(total - summed)).astype(BF)
        update = tn(qkv[at, 2 * DK : CHUNK], ku)
        now = state[...]
        st[n] = now.astype(BF)
        state[...] = jnp.exp(total) * now + update
        return carry

    lax.fori_loop(0, n_blocks, advance, 0, unroll=4)
    loc.start(st, o_st, True)
    yield None, 4

    def mix_block(p):
        n = meta[p]
        at = rows(p * GROUP, GROUP)
        summed = nn(tri, fg[at, :])
        middle = summed[GROUP // 2 : GROUP // 2 + 1]
        q = qkv[at, 0:DK].astype(F32) * SCALE
        k = qkv[at, DK : 2 * DK].astype(F32) * live_rows(n, length)
        qe = (q * jnp.exp(summed - middle)).astype(BF)
        ke = (k * jnp.exp(middle - summed)).astype(BF)
        scores = jnp.where(causal > 0, nt(qe, ke), 0.0).astype(BF)
        o = nn(scores, qkv[at, 2 * DK : CHUNK]) + nt((q * jnp.exp(summed)).astype(BF), st[n])
        r = lax.rsqrt(jnp.mean(o * o, axis=-1, keepdims=True) + 1.0)
        yh[at, :] = (o * r).astype(BF)
        rh[at, :] = jnp.broadcast_to(r, (GROUP, DK))

    mix_copies = []
    for d in range(1, HEADS):
        yield None, 2
        peer = me ^ d
        lax.fori_loop(0, per, lambda j, c, peer=peer: (mix_block(peer * per + j), c)[1], 0, unroll=True)
        copy = to_peer(yh.at[rows(peer * T, T)], mix.at[me], ssem.at[2, d], rsem.at[2, d], peer)
        copy.start()
        mix_copies.append(copy)
    yield None, 2
    lax.fori_loop(0, per, lambda j, c: (mix_block(me * per + j), c)[1], 0, unroll=True)
    mix[me] = yh[rows(me * T, T), :]
    loc.start(yh, o_yh, True)
    loc.start(rh, o_rh, True)
    yield "mo", 0
    l_mo = load("mo")
    yield "delay", DELAYS[2]
    for c in mix_copies:
        c.wait_recv()
    loc.start(mix, o_mix, True)
    for hd in range(HEADS):
        cols = slice(hd * DV, (hd + 1) * DV)
        gated[:, cols] = (mix[hd].astype(F32) * silu_parts(og[:, cols])[0]).astype(BF)
    ao[...] = (nn(gated[...], ah[0:VALUE_WIDTH, :]) * mask).astype(BF)
    wait(l_mo)
    for j in range(MODEL_WIDTH // TILE):
        cols = slice(j * TILE, (j + 1) * TILE)
        mid[:, cols] = (
            h[:, cols].astype(F32) + nn(gated[...], mo[:, cols]) + nn(ao[...], au[:, U_O + j * TILE : U_O + (j + 1) * TILE])
        )
    loc.start(ao, o_ao, True)
    loc.start(mid, o_mid, True)
    yield None, 1
    mv = mid[...]
    normed[...] = (mv * inverse_rms(mv)).astype(BF)
    for p in range(2):
        cols = slice(p * ADAPTER_COLUMNS, (p + 1) * ADAPTER_COLUMNS)
        wide = slice((4 + p) * ADAPTER_COLUMNS, (5 + p) * ADAPTER_COLUMNS)
        af[:, cols] = (nn(normed[...], am[:, wide]) * mask).astype(BF)
    loc.start(af, o_af, True)
    yield "fi", 0
    wait(load("fi"))

    def up_tile(i, carry):
        a, b = lanes(i * TILE, TILE), lanes(HIDDEN_UNITS + i * TILE, TILE)
        gate = nn(normed[...], fi[:, a]) + nn(af[:, 0:ADAPTER_COLUMNS], au[:, lanes(U_G + i * TILE, TILE)])
        up = nn(normed[...], fi[:, b]) + nn(af[:, ADAPTER_COLUMNS:], au[:, lanes(U_U + i * TILE, TILE)])
        gu[:, a] = gate.astype(gu.dtype)
        gu[:, b] = up.astype(gu.dtype)
        hidden[:, a] = (silu_parts(gate)[0] * up).astype(BF)
        return carry

    tiles = HIDDEN_UNITS // TILE
    yield None, 3
    lax.fori_loop(0, tiles // 2, up_tile, 0)
    yield None, 3
    lax.fori_loop(tiles // 2, tiles, up_tile, 0)
    loc.start(gu, o_gu, True)
    dn[...] = (nn(hidden[...], ah[VALUE_WIDTH:, :]) * mask).astype(BF)
    loc.start(dn, o_dn, True)
    yield "fo", 0
    wait(load("fo"))
    yield None, 3
    for j in range(MODEL_WIDTH // TILE):
        cols = slice(j * TILE, (j + 1) * TILE)
        y[:, cols] = (
            mid[:, cols] + nn(hidden[...], fo[:, cols]) + nn(dn[...], au[:, U_D + j * TILE : U_D + (j + 1) * TILE])
        ).astype(BF)
    loc.start(y, o_y, True)
    loc.finish()
    for c in low_copies + qkv_copies + mix_copies:
        c.wait_send()


NAMES = ("mi", "mo", "fi", "fo", "f1", "f2", "b", "am", "ah", "au")


def forward_kernel(layer, n_blocks, meta, h_in, *refs):
    n_w, n_out = len(NAMES), 14
    ins, outs = refs[:n_w], refs[n_w : n_w + n_out]
    refs = refs[n_w + n_out :]
    buffers, work = dict(zip(NAMES, refs[:n_w])), refs[n_w:-3]
    lsem, ssem, rsem = refs[-3:]
    loc = Local(lsem)
    first = loc.start(h_in, work[0])
    greet_peers(lax.axis_index("seq"))
    first.wait()
    weights = {name: ref.at[layer] for name, ref in zip(NAMES, ins)}
    for _ in forward_steps(layer, n_blocks, meta, loc, weights, buffers, work, outs, (ssem, rsem)):
        pass


def weight_scratch(weights):
    return [pltpu.VMEM(w.shape[1:], w.dtype) for w in weights]


def saved_shapes(T, L, n_blocks):
    s = lambda shape, dtype=BF: (shape, dtype)
    return [
        s((T, MODEL_WIDTH)),
        s((T, 4 * ADAPTER_COLUMNS)),
        s((T, VALUE_WIDTH), F32),
        s((L, CHUNK)),
        s((HEADS, FGATE_RANK, T)),
        s((n_blocks, DV, DK)),
        s((HEADS, T, DV)),
        s((L, DV)),
        s((L, DK), F32),
        s((T, ADAPTER_COLUMNS)),
        s((T, MODEL_WIDTH), F32),
        s((T, 2 * ADAPTER_COLUMNS)),
        s((T, 2 * HIDDEN_UNITS)),
        s((T, ADAPTER_COLUMNS)),
    ]


def work_scratch(T, L, saved):
    vm = pltpu.VMEM
    return [vm((T, MODEL_WIDTH), BF)] + [vm(*s) for s in saved] + [
        vm((T, MODEL_WIDTH), BF),
        vm((HEADS - 1, T, CHUNK), BF),
        vm((FGATE_RANK, T), BF),
        vm((L, DK), BF),
        vm((DV, DK), F32),
        vm((T, VALUE_WIDTH), BF),
        vm((T, HIDDEN_UNITS), BF),
    ]


def forward(layer, meta, h, weights):
    T = h.shape[0]
    L = T * HEADS
    n_blocks = L // GROUP
    saved = saved_shapes(T, L, n_blocks)
    dma = pltpu.SemaphoreType.DMA
    return pl.pallas_call(
        functools.partial(forward_kernel, layer, n_blocks),
        out_shape=[jax.ShapeDtypeStruct(*s) for s in saved],
        in_specs=[pl.BlockSpec(memory_space=pltpu.SMEM)] + [ANY] * (1 + len(weights)),
        out_specs=[ANY] * len(saved),
        scratch_shapes=weight_scratch(weights)
        + work_scratch(T, L, saved)
        + [dma((1 + len(weights) + len(saved),)), dma((3, HEADS)), dma((3, HEADS))],
        compiler_params=pltpu.CompilerParams(
            collective_id=1 + layer, has_side_effects=True, vmem_limit_bytes=VMEM_LIMIT
        ),
    )(meta, h, *weights)


def backward_kernel(
    layer, n_blocks, meta, d_in, h_in, w_mi, w_mo, w_fi, w_fo, w_f1, w_f2, w_b, w_am, w_ah, w_au,
    i_ad, i_og, i_qkv, i_gl, i_st, i_mix, i_yh, i_rh, i_ao, i_mid, i_af, i_gu, i_dn,
    e_out, gm_out, gh_out, gp_out,
    d, h, mi, mo, fi, fo, f1, f2, bias, am, ah, au,
    ad, og, qkv, gl, st, mix, yh, rh, ao, mid, af, gu, dn,
    e, sgm, sgh, sgp,
    gm, gh, gp, gps, rgm, rgh, rgp, hidden, wide, gad, big, grad, dog, sendm, dmr, logit, fg, gstate, gt, dt, don, hidden_gated, sendq, dqkv, dlog, sendl, dlr, dproj,
    lsem, ssem, rsem, gssem, grsem,
):
    me = lax.axis_index("seq")
    T = h.shape[0]
    per = T // GROUP
    adapter = meta[2 * n_blocks]
    length = meta[2 * n_blocks + 1]
    loc = Local(lsem)
    l_d = loc.start(d_in, d)
    l_au = loc.start(w_au.at[layer], au)
    l_ah = loc.start(w_ah.at[layer], ah)
    l_fo = loc.start(w_fo.at[layer], fo)
    l_gu = loc.start(i_gu, gu)
    l_dn = loc.start(i_dn, dn)
    greet_peers(me)
    l_fi = loc.start(w_fi.at[layer], fi)
    l_am = loc.start(w_am.at[layer], am)
    l_mid = loc.start(i_mid, mid)
    l_af = loc.start(i_af, af)
    l_mo = loc.start(w_mo.at[layer], mo)
    l_og = loc.start(i_og, og)
    l_mix = loc.start(i_mix, mix)
    l_ao = loc.start(i_ao, ao)
    l_mixer = [
        loc.start(a, b)
        for a, b in (
            (w_f2.at[layer], f2), (w_b.at[layer], bias), (i_qkv, qkv), (i_gl, gl), (i_st, st), (i_yh, yh), (i_rh, rh),
        )
    ]
    l_last = [
        loc.start(a, b) for a, b in ((w_mi.at[layer], mi), (w_f1.at[layer], f1), (i_ad, ad), (h_in, h))
    ]
    mask = column_mask(adapter)
    pick = picked(adapter, ADAPTER_COLUMNS)

    def narrow(v):
        return nn(v, pick).astype(BF)

    def outer(u, v):
        return tn(narrow(u), v).astype(BF)

    n_dp, width, padded = gps.shape[1], gp.shape[1] // (HEADS * gps.shape[1]), gps.shape[3]
    quarter, hidden_quarter = MODEL_WIDTH // HEADS, gh.shape[1] // HEADS
    n_late = -(-FROZEN // (HEADS * width))
    mix_rows = 4 * ADAPTER_RANK

    def place(dps):
        for i in dps:
            for q in range(HEADS):
                piece = gp[:, (i * HEADS + q) * width : (i * HEADS + q + 1) * width]
                gps[q, i] = jnp.concatenate([piece, jnp.zeros((ADAPTER_RANK, padded - width), BF)], axis=1)

    def grad_copies(late):
        copies = []
        at = slice(0, mix_rows) if late else slice(mix_rows, 6 * ADAPTER_RANK)
        dps = slice(0, n_late) if late else slice(n_late, n_dp)
        for k in range(1, HEADS):
            peer = me ^ k
            pairs = [
                (gm.at[at, lanes(peer * quarter, quarter)], rgm.at[k - 1, at]),
                (gps.at[peer, dps], rgp.at[k - 1, dps]),
            ]
            if not late:
                pairs.append((gh.at[:, lanes(peer * hidden_quarter, hidden_quarter)], rgh.at[k - 1]))
            for i, (a, b) in enumerate(pairs):
                j = i if late else 2 + i
                copies.append(to_peer(a, b, gssem.at[j, k], grsem.at[j, k], peer))
        return copies

    l_d.wait()
    l_au.wait()
    gdown = (nt(d[...], au[:, U_D : U_D + MODEL_WIDTH]).astype(BF).astype(F32) * mask).astype(BF)
    gdown16 = narrow(gdown)
    gh[:, VALUE_WIDTH + HIDDEN_UNITS :] = jnp.zeros((ADAPTER_RANK, gh.shape[1] - VALUE_WIDTH - HIDDEN_UNITS), BF)
    l_dn.wait()
    gp[:, U_D : U_D + MODEL_WIDTH] = outer(dn[...], d[...])
    gad[...] = gdown
    l_ah.wait()
    l_fo.wait()
    l_gu.wait()

    def down_tile(i, carry):
        a, b = lanes(i * TILE, TILE), lanes(HIDDEN_UNITS + i * TILE, TILE)
        at = pl.ds(pl.multiple_of(i * TILE, TILE), TILE)
        dh = nt(d[...], fo[at, :]) + nt(gad[...], ah[pl.ds(pl.multiple_of(VALUE_WIDTH + i * TILE, TILE), TILE), :])
        gate, up = gu[:, a].astype(F32), gu[:, b].astype(F32)
        act, sig = silu_parts(gate)
        hidden[:, a] = (act * up).astype(BF)
        wide[:, a] = (dh * up * sig * (1.0 + gate * (1.0 - sig))).astype(BF)
        wide[:, b] = (dh * act).astype(BF)
        return carry

    lax.fori_loop(0, HIDDEN_UNITS // TILE, down_tile, 0)
    gate_cols, up_cols = slice(0, HIDDEN_UNITS), slice(HIDDEN_UNITS, 2 * HIDDEN_UNITS)
    gg = (nt(wide[:, gate_cols], au[:, U_G : U_G + HIDDEN_UNITS]).astype(BF).astype(F32) * mask).astype(BF)
    gu2 = (nt(wide[:, up_cols], au[:, U_U : U_U + HIDDEN_UNITS]).astype(BF).astype(F32) * mask).astype(BF)
    gad2 = jnp.concatenate([gg, gu2], axis=1)
    big[:, 0 : 2 * ADAPTER_COLUMNS] = gad2
    l_fi.wait()
    l_am.wait()

    def wide_tile(i, carry):
        at = pl.ds(pl.multiple_of(i * TILE, TILE), TILE)
        grad[:, lanes(i * TILE, TILE)] = nt(wide[...], fi[at, :]) + nt(
            big[:, 0 : 2 * ADAPTER_COLUMNS], am[at, 4 * ADAPTER_COLUMNS :]
        )
        return carry

    lax.fori_loop(0, MODEL_WIDTH // TILE, wide_tile, 0)
    l_mid.wait()
    mv = mid[...]
    grad_mid = d[...].astype(F32) + rms_back(mv, grad[...])
    grad[...] = grad_mid
    attn = grad_mid.astype(BF)
    e[...] = attn
    gout = (nt(attn, au[:, U_O : U_O + MODEL_WIDTH]).astype(BF).astype(F32) * mask).astype(BF)
    gad[...] = gout
    l_mo.wait()
    l_og.wait()
    l_mix.wait()

    def gate_back(head, out):
        at = rows(head * DV, DV)
        cols = lanes(head * DV, DV)
        gg_ = nt(e[...], mo[at, :]) + nt(gad[...], ah[at, :])
        o = og[:, cols]
        act, sig = silu_parts(o)
        out[...] = (gg_ * act).astype(BF)
        m = mix[head].astype(F32)
        dog[:, cols] = (gg_ * m * sig * (1.0 + o * (1.0 - sig))).astype(BF)
        hidden_gated[:, cols] = (m * act).astype(BF)

    mix_copies = []
    for k in range(1, HEADS):
        peer = me ^ k
        gate_back(peer, sendm.at[k - 1])
        copy = to_peer(sendm.at[k - 1], dmr.at[rows(me * T, T)], ssem.at[0, k], rsem.at[0, k], peer)
        copy.start()
        mix_copies.append(copy)
    gate_back(me, dmr.at[rows(me * T, T)])

    l_af.wait()
    l_ao.wait()
    normed_mid = (mv * inverse_rms(mv)).astype(BF)
    gh[:, VALUE_WIDTH : VALUE_WIDTH + HIDDEN_UNITS] = tn(gdown16, hidden[...]).astype(BF)
    gm[4 * ADAPTER_RANK : 5 * ADAPTER_RANK, :] = outer(gg, normed_mid)
    gm[5 * ADAPTER_RANK : 6 * ADAPTER_RANK, :] = outer(gu2, normed_mid)
    gp[:, U_G : U_G + HIDDEN_UNITS] = outer(af[:, 0:ADAPTER_COLUMNS], wide[:, gate_cols])
    gp[:, U_U : U_U + HIDDEN_UNITS] = outer(af[:, ADAPTER_COLUMNS:], wide[:, up_cols])
    gp[:, U_O : U_O + MODEL_WIDTH] = outer(ao[...], e[...])
    gh[:, 0:VALUE_WIDTH] = outer(gad[...], hidden_gated[...])
    place(range(n_late, n_dp))
    grads = grad_copies(False)
    for c in grads:
        c.start()

    for c in l_mixer:
        c.wait()
    f2h = f2[:, lanes(me * DK, DK)]
    bh = bias[:, lanes(me * DK, DK)]
    for src in range(HEADS):
        lg = tn(gl[src], f2h) + bh
        logit[src * T : (src + 1) * T, :] = lg
        fg[src * T : (src + 1) * T, :] = (jax.nn.log_sigmoid(lg) / 16.0).astype(BF)
    tri = lower_triangle(BF)
    causal = lower_triangle(F32)
    for c in mix_copies:
        c.wait_recv()
    gstate[...] = jnp.zeros_like(gstate)

    def retreat(i, carry):
        n = n_blocks - 1 - i
        at = pl.ds(meta[n_blocks + n] * GROUP, GROUP)
        here = rows(n * GROUP, GROUP)
        dm = dmr[at, :].astype(F32)
        yv = yh[at, :].astype(F32)
        r = rh[at, 0:1]
        do = (r * (dm - yv * jnp.mean(dm * yv, axis=-1, keepdims=True))).astype(BF)
        don[here, :] = do
        summed = nn(tri, fg[at, :])
        total = jnp.exp(summed[GROUP - 1 : GROUP])
        qs = (qkv[at, 0:DK].astype(F32) * SCALE * jnp.exp(summed)).astype(BF)
        now = gstate[...]
        gt[n] = now.astype(BF)
        decayed = total * now
        dt[n] = jnp.sum(decayed * st[n].astype(F32), axis=0, keepdims=True)
        gstate[...] = decayed + tn(do, qs)
        return carry

    lax.fori_loop(0, n_blocks, retreat, 0, unroll=4)

    def back_block(p, out, j):
        n = meta[p]
        at = rows(p * GROUP, GROUP)
        here = pl.ds(n * GROUP, GROUP)
        to = rows(j * GROUP, GROUP)
        live = live_rows(n, length)
        summed = nn(tri, fg[at, :])
        middle = summed[GROUP // 2 : GROUP // 2 + 1]
        total = summed[GROUP - 1 : GROUP]
        e1, e2 = jnp.exp(summed - middle), jnp.exp(middle - summed)
        es, eu = jnp.exp(summed), jnp.exp(total - summed)
        q = qkv[at, 0:DK].astype(F32) * SCALE
        k = qkv[at, DK : 2 * DK].astype(F32) * live
        v = qkv[at, 2 * DK : CHUNK]
        do, state_t, grad_t = don[here, :], st[n], gt[n]
        qe, ke, qs, ku = q * e1, k * e2, q * es, k * eu
        qeb, keb = qe.astype(BF), ke.astype(BF)
        scores = jnp.where(causal > 0, nt(qeb, keb), 0.0).astype(BF)
        dscores = jnp.where(causal > 0, nt(do, v), 0.0).astype(BF)
        dv = tn(scores, do) + nt(ku.astype(BF), grad_t)
        dqs = nn(do, state_t)
        dku = nn(v, grad_t)
        dqe = nn(dscores, keb)
        dke = tn(dscores, qeb)
        out[to, 0:DK] = (SCALE * (dqe * e1 + dqs * es)).astype(BF)
        out[to, DK : 2 * DK] = (live * (dke * e2 + dku * eu)).astype(BF)
        out[to, 2 * DK : CHUNK] = dv.astype(BF)
        kk = dku * ku
        dsum = dqe * qe + dqs * qs - dke * ke - kk
        dtotal = dt[n] + jnp.sum(kk, axis=0, keepdims=True)
        high = dsum.astype(BF)
        lowp = (dsum - high.astype(F32)).astype(BF)
        df = tn(tri, high) + tn(tri, lowp) + dtotal
        df = df.astype(BF).astype(F32)
        dlog[to, :] = (df * lax.logistic(-logit[at, :]) / 16.0).astype(BF)

    q_copies = []

    def back_rows(dest, out, low_out):
        lax.fori_loop(0, per, lambda j, c: (back_block(dest * per + j, out, j), c)[1], 0, unroll=2)
        low_out[...] = nt(f2h, dlog[...]).astype(BF)

    for k in range(1, HEADS):
        peer = me ^ k
        back_rows(peer, sendq.at[k - 1], sendl.at[k - 1])
        copies = (
            to_peer(sendq.at[k - 1], dqkv.at[me], ssem.at[1, k], rsem.at[1, k], peer),
            to_peer(sendl.at[k - 1], dlr.at[me], ssem.at[2, k], rsem.at[2, k], peer),
        )
        for copy in copies:
            copy.start()
        q_copies += copies
    back_rows(me, dqkv.at[me], dlr.at[me])

    for c in l_last:
        c.wait()
    hv = h[...].astype(F32)
    hr = inverse_rms(hv)
    big[...] = (hv * hr).astype(BF)
    for c in q_copies:
        c.wait_recv()
    for hd in range(HEADS):
        dproj[:, hd * DK : (hd + 1) * DK] = dqkv[hd, :, 0:DK]
        dproj[:, KEY + hd * DK : KEY + (hd + 1) * DK] = dqkv[hd, :, DK : 2 * DK]
        dproj[:, 2 * KEY + hd * DV : 2 * KEY + (hd + 1) * DV] = dqkv[hd, :, 2 * DK : CHUNK]
    dproj[:, 2 * KEY + VALUE_WIDTH :] = dog[...]
    dlow = dlr[0].astype(F32)
    for hd in range(1, HEADS):
        dlow += dlr[hd].astype(F32)
    dlowb = dlow.astype(BF)
    spans = ((0, KEY), (KEY, KEY), (2 * KEY, VALUE_WIDTH), (2 * KEY + VALUE_WIDTH, VALUE_WIDTH))
    for p, (start, span) in enumerate(spans):
        block = slice(p * ADAPTER_COLUMNS, (p + 1) * ADAPTER_COLUMNS)
        piece = dproj[:, start : start + span]
        ga = (nt(piece, au[:, start : start + span]).astype(BF).astype(F32) * mask).astype(BF)
        wide[:, block] = ga
        gm[p * ADAPTER_RANK : (p + 1) * ADAPTER_RANK, :] = outer(ga, big[...])
        gp[:, start : start + span] = outer(ad[:, block], piece)
    place(range(n_late))
    late_grads = grad_copies(True)
    for c in late_grads:
        c.start()
    z_w = f1.shape[2]
    tiles = f1.shape[0]
    back = []
    for j in range(tiles):
        at = slice(j * z_w, (j + 1) * z_w)
        back.append(
            nt(dproj[...], mi[at, :]) + nt(wide[:, 0 : 4 * ADAPTER_COLUMNS], am[at, 0 : 4 * ADAPTER_COLUMNS]) + tn(dlowb, f1[j])
        )
    dn_ = jnp.concatenate(back, axis=1)
    n = hv * hr
    e[...] = (grad[...] + hr * (dn_ - n * jnp.mean(dn_ * n, axis=-1, keepdims=True))).astype(BF)
    loc.start(e, e_out, True)
    grads += late_grads
    for c in grads:
        c.wait_recv()

    def summed_over_seq(own, got):
        total = own.astype(F32)
        for k in range(HEADS - 1):
            total += got[k].astype(F32)
        return total.astype(BF)

    sgm[...] = summed_over_seq(gm[:, lanes(me * quarter, quarter)], rgm)
    sgh[...] = summed_over_seq(gh[:, lanes(me * hidden_quarter, hidden_quarter)], rgh)
    spot = lax.broadcasted_iota(jnp.int32, (ADAPTER_RANK, padded), 1)
    for i in range(n_dp):
        total = gps[me, i].astype(F32)
        for k in range(HEADS - 1):
            total += rgp[k, i].astype(F32)
        sgp[i] = jnp.where(spot == width, adapter.astype(F32), total).astype(BF)
    for a, b in ((sgm, gm_out), (sgh, gh_out), (sgp, gp_out)):
        loc.start(a, b, True)
    loc.finish()
    for c in mix_copies + q_copies + grads:
        c.wait_send()


def backward(layer, meta, d, h, weights, saved, n_dp):
    T = h.shape[0]
    L = T * HEADS
    n_blocks = L // GROUP
    raised = U_D + MODEL_WIDTH
    padded = (raised // (n_dp * HEADS) // 128 + 1) * 128
    quarter = MODEL_WIDTH // HEADS
    hidden_quarter = -(-(VALUE_WIDTH + HIDDEN_UNITS) // (HEADS * 128)) * 128
    outs = [
        ((T, MODEL_WIDTH), BF),
        ((6 * ADAPTER_RANK, quarter), BF),
        ((ADAPTER_RANK, hidden_quarter), BF),
        ((n_dp, ADAPTER_RANK, padded), BF),
    ]
    vm = pltpu.VMEM
    dma = pltpu.SemaphoreType.DMA
    return pl.pallas_call(
        functools.partial(backward_kernel, layer, n_blocks),
        out_shape=[jax.ShapeDtypeStruct(*s) for s in outs],
        in_specs=[pl.BlockSpec(memory_space=pltpu.SMEM)] + [ANY] * (2 + len(weights) + len(saved)),
        out_specs=[ANY] * len(outs),
        scratch_shapes=[vm(d.shape, d.dtype), vm(h.shape, h.dtype)]
        + weight_scratch(weights)
        + [vm(s.shape, s.dtype) for s in saved]
        + [vm(*s) for s in outs]
        + [
            vm((6 * ADAPTER_RANK, MODEL_WIDTH), BF),
            vm((ADAPTER_RANK, HEADS * hidden_quarter), BF),
            vm((ADAPTER_RANK, raised), BF),
            vm((HEADS, n_dp, ADAPTER_RANK, padded), BF),
            vm((HEADS - 1, 6 * ADAPTER_RANK, quarter), BF),
            vm((HEADS - 1, ADAPTER_RANK, hidden_quarter), BF),
            vm((HEADS - 1, n_dp, ADAPTER_RANK, padded), BF),
            vm((T, HIDDEN_UNITS), BF),
            vm((T, 2 * HIDDEN_UNITS), BF),
            vm((T, ADAPTER_COLUMNS), BF),
            vm((T, MODEL_WIDTH), BF),
            vm((T, MODEL_WIDTH), F32),
            vm((T, VALUE_WIDTH), BF),
            vm((HEADS - 1, T, DV), BF),
            vm((L, DV), BF),
            vm((L, DK), F32),
            vm((L, DK), BF),
            vm((DV, DK), F32),
            vm((n_blocks, DV, DK), BF),
            vm((n_blocks, 1, DK), F32),
            vm((L, DV), BF),
            vm((T, VALUE_WIDTH), BF),
            vm((HEADS - 1, T, CHUNK), BF),
            vm((HEADS, T, CHUNK), BF),
            vm((T, DK), BF),
            vm((HEADS - 1, FGATE_RANK, T), BF),
            vm((HEADS, FGATE_RANK, T), BF),
            vm((T, FROZEN), BF),
            dma((2 + len(weights) + len(saved) + len(outs),)),
            dma((3, HEADS)),
            dma((3, HEADS)),
            dma((5, HEADS)),
            dma((5, HEADS)),
        ],
        compiler_params=pltpu.CompilerParams(
            collective_id=3 + layer, has_side_effects=True, vmem_limit_bytes=VMEM_LIMIT
        ),
        cost_estimate=pl.CostEstimate(flops=2 * T * 16_000_000, bytes_accessed=45 << 20, transcendentals=T * 8192),
    )(meta, d, h, *weights, *saved)


UNITS = [(layer, w) for layer in range(2) for w in range(4)]


def model_kernel(n_blocks, meta, *refs):
    n_w, n_small, n_saved, n_z = 4, 5, 14, 4
    refs = list(refs)

    def take(n):
        out = refs[:n]
        del refs[:n]
        return out

    shards = take(n_w)
    f1_ref, ends_ref = take(2)
    small = take(n_small)
    outs = take(n_w)
    (f1_out,) = take(1)
    (x_out, c_out) = take(2)
    small_out = take(n_small)
    saved = [take(n_saved), take(n_saved)]
    held = take(n_w)
    held_f1 = take(1)[0]
    held_small = take(n_small)
    work = take(1 + n_saved + 7)
    qkv2, gl2, mix2, held_ends = take(4)
    (ins, zs, zr, ts, tr, xs, xr, ys, yr, fxs, fxr, fys, fyr, cs, cr, own, ms, mr, es, er, f1s, f1r, f1c, lsem, ssem, rsem) = take(26)
    core, z, s = lax.axis_index("section"), lax.axis_index("dp"), lax.axis_index("seq")
    other = 1 - core

    def remote(src, dst, send_sem, recv_sem, **where):
        return pltpu.make_async_remote_copy(
            src_ref=src, dst_ref=dst, send_sem=send_sem, recv_sem=recv_sem, device_id=where, device_id_type=MESH
        )

    def height(w):
        return shards[w].shape[1]

    def staged(w):
        return held[w].at[pl.ds(pl.multiple_of(z * height(w), 16), height(w))]

    fetch = [pltpu.make_async_copy(shards[w].at[0], staged(w), ins.at[w]) for w in range(n_w)]
    fetch += [pltpu.make_async_copy(a.at[0], b, ins.at[n_w + i]) for i, (a, b) in enumerate(zip(small, held_small))]
    fetch.append(pltpu.make_async_copy(ends_ref.at[0, :, 0], held_ends, ins.at[n_w + n_small]))
    fetch.append(pltpu.make_async_copy(f1_ref, held_f1.at[z], ins.at[n_w + n_small + 1]))
    for f in fetch:
        f.start()

    barrier = pltpu.get_barrier_semaphore()
    greeted = [dict(section=other)] + [dict(seq=s ^ k) for k in range(1, HEADS)]
    greeted += [dict(dp=lax.rem(z + gap, n_z)) for gap in range(1, n_z)]
    for where in greeted:
        pl.semaphore_signal(barrier, inc=1, device_id=where, device_id_type=MESH)
    pl.semaphore_wait(barrier, len(greeted))

    def part(u, j, start, size, strip=False):
        layer, w = UNITS[u]
        cols = shards[w].shape[2] // 2
        at, wide = (cols - STRIPS[w], STRIPS[w]) if strip else (0, cols - STRIPS[w])
        return outs[w].at[layer, pl.ds(pl.multiple_of(j * height(w) + start, 16), size), lanes(core * cols + at, wide)]

    def piece(u, j, q):
        r = height(UNITS[u][1])
        return part(u, j, q * (r // 4), r // 4)

    def half(u, j, q, low):
        r = height(UNITS[u][1])
        cut = (r // 8 + 15) // 16 * 16
        start, size = (0, cut) if low else (cut, r // 4 - cut)
        return part(u, j, q * (r // 4) + start, size)

    def block(u, j):
        layer, w = UNITS[u]
        cols = shards[w].shape[2] // 2
        return outs[w].at[layer, pl.ds(pl.multiple_of(j * height(w), 16), height(w)), lanes(core * cols, cols)]

    def whole_block(layer, w):
        return outs[w].at[layer, pl.ds(pl.multiple_of(z * height(w), 16), height(w))]

    def step(d):
        return 1 if d == 0 else -1

    def can_send(d, t):
        has_next = (z < n_z - 1) if d == 0 else (z > 0)
        first = z - step(d) * (t - 1)
        return jnp.logical_and(has_next, jnp.logical_and(first >= 0, first < n_z))

    def gets(d, t):
        first = z - step(d) * t
        return jnp.logical_and(first >= 0, first < n_z)

    def origin(d, t):
        return z - step(d) * t

    def z_copy(u, d, t):
        ref = piece(u, z - step(d) * (t - 1), s)
        return remote(ref, ref, zs.at[u, d, t - 1], zr.at[u, d, t - 1], dp=z + step(d))

    def t_copy(u, d, t):
        ref = part(u, z - step(d) * (t - 1), 0, height(UNITS[u][1]), True)
        return remote(ref, ref, ts.at[u, d, t - 1], tr.at[u, d, t - 1], dp=z + step(d))

    def x_copy(u, d, t):
        ref = piece(u, origin(d, t), s)
        return remote(ref, ref, xs.at[u, d, t - 1], xr.at[u, d, t - 1], seq=s ^ 1)

    def y_copy(u, d, t):
        ref = piece(u, origin(d, t), s)
        return remote(ref, ref, ys.at[u, d, t - 1], yr.at[u, d, t - 1], seq=s ^ 2)

    def fx_copy(u, d, t):
        ref = half(u, origin(d, t), s ^ 2, False)
        return remote(ref, ref, fxs.at[u, d, t - 1], fxr.at[u, d, t - 1], seq=s ^ 1)

    def fy_copy(u, d, t):
        ref = half(u, origin(d, t), s ^ 1, True)
        return remote(ref, ref, fys.at[u, d, t - 1], fyr.at[u, d, t - 1], seq=s ^ 2)

    def c_copy(u, d, t):
        ref = block(u, origin(d, t))
        return remote(ref, ref, cs.at[u, d, t - 1], cr.at[u, d, t - 1], section=other)

    def own_copy(w):
        return pltpu.make_async_copy(staged(w), whole_block(core, w), own.at[w])

    def own_cross(w):
        return remote(staged(w), whole_block(core, w), ms.at[n_small + w], mr.at[n_small + w], section=other)

    def start_own(u):
        layer, w = UNITS[u]

        if layer == 0:
            own_copy(w).wait()

        @pl.when(core != layer)
        def _():
            own_cross(w).wait_recv()

        for d in range(2):
            @pl.when(can_send(d, 1))
            def _():
                z_copy(u, d, 1).start()
                t_copy(u, d, 1).start()

    def take_z(u, t):
        for d in range(2):
            @pl.when(gets(d, t))
            def _():
                z_copy(u, d, t).wait_recv()
            if t < n_z - 1:
                @pl.when(can_send(d, t + 1))
                def _():
                    z_copy(u, d, t + 1).start()
            @pl.when(gets(d, t))
            def _():
                x_copy(u, d, t).start()
                y_copy(u, d, t).start()
                t_copy(u, d, t).wait_recv()
            if t < n_z - 1:
                @pl.when(can_send(d, t + 1))
                def _():
                    t_copy(u, d, t + 1).start()

    def take_xy(u, t):
        for d in range(2):
            @pl.when(gets(d, t))
            def _():
                x_copy(u, d, t).wait_recv()
                fy_copy(u, d, t).start()
                y_copy(u, d, t).wait_recv()
                fx_copy(u, d, t).start()

    def take_diagonal(u, t):
        for d in range(2):
            @pl.when(gets(d, t))
            def _():
                fy_copy(u, d, t).wait_recv()
                fx_copy(u, d, t).wait_recv()
                c_copy(u, d, t).start()

    def take_core(u):
        for d in range(2):
            for t in range(1, n_z):
                @pl.when(gets(d, t))
                def _():
                    c_copy(u, d, t).wait_recv()

    def f1_copy(gap):
        return remote(held_f1.at[z], f1_out.at[core, z], f1s.at[gap], f1r.at[gap], dp=lax.rem(z + gap, n_z))

    def launch(w):
        fetch[w].wait()
        own_copy(w).start()
        own_cross(w).start()

    launch(0)
    fetch[-1].wait()
    f1_sends = [f1_copy(gap) for gap in range(1, n_z)]
    for c in f1_sends:
        c.start()
    f1_own = pltpu.make_async_copy(held_f1.at[z], f1_out.at[core, z], own.at[n_w])
    f1_own.start()
    ends_to_x = remote(held_ends.at[1], x_out, es, er, section=other)
    ends_to_c = remote(held_ends.at[0], c_out, es, er, section=other)
    ends_x = pltpu.make_async_copy(held_ends.at[0], x_out, own.at[n_w + 1])
    ends_c = pltpu.make_async_copy(held_ends.at[1], c_out, own.at[n_w + 1])
    f1_cross = remote(f1_out.at[core], f1_out.at[core], f1c.at[0], f1c.at[1], section=other)
    start_own(0)
    launch(1)
    smalls = []

    def launch_rest():
        fetch[-2].wait()

        @pl.when(core == 0)
        def _():
            ends_to_x.start()
            ends_x.start()

        @pl.when(core == 1)
        def _():
            ends_to_c.start()
            ends_c.start()

        for i, (a, b) in enumerate(zip(held_small, small_out)):
            fetch[n_w + i].wait()
            mine = pltpu.make_async_copy(a, b.at[core], own.at[n_w + 2 + i])
            theirs = remote(a, b.at[core], ms.at[i], mr.at[i], section=other)
            mine.start()
            theirs.start()
            smalls.append((mine, theirs))
        for w in range(2, n_w):
            launch(w)
        f1_own.wait()
        for c in f1_sends:
            c.wait_recv()
        f1_cross.start()

    def settle_small():
        for mine, theirs in smalls:
            mine.wait()
            theirs.wait()
        for c in f1_sends:
            c.wait_send()
        f1_cross.wait()
        ends_x.wait()
        ends_to_x.wait()

    items = [(u, t) for u in range(len(UNITS)) for t in range(1, n_z)]
    ready, clock = [], 8.0
    for u, t in items:
        r, c = shards[UNITS[u][1]].shape[1:]
        clock += r // 4 * (c - 2 * STRIPS[UNITS[u][1]]) * 3 / LINK_BYTES_PER_US
        ready.append(clock)

    def gather_step(i):
        if i == 1:
            launch_rest()
        if i < len(items):
            u, t = items[i]
            if t == 1 and u + 1 < len(UNITS):
                start_own(u + 1)
            take_z(u, t)
        if 0 <= i - SKEW[0] < len(items):
            take_xy(*items[i - SKEW[0]])
        if 0 <= i - SKEW[1] < len(items):
            take_diagonal(*items[i - SKEW[1]])

    loc = Local(lsem)
    n_steps = len(items) + SKEW[1]
    works = [list(work), list(work)]
    for at, ref in ((4, qkv2), (5, gl2), (7, mix2)):
        works[1][at] = ref

    def both_layers():
        for layer in range(2):
            sources = dict(zip(NAMES[:4], outs))
            sources["f1"] = f1_out
            sources.update(zip(NAMES[5:], small_out))
            sources = {name: ref.at[layer] for name, ref in sources.items()}
            buffers = dict(zip(NAMES, held + [held_f1] + held_small))
            for what, us in forward_steps(
                layer, n_blocks, meta, loc, sources, buffers, works[layer], saved[layer], (ssem.at[layer], rsem.at[layer])
            ):
                yield layer, what, us
            if layer == 0:
                work[0][...] = work[1][...]

    steps, done, now, crossed, until = both_layers(), 0, 8.0, set(), None
    pending = next(steps)
    while pending is not None or done < n_steps:
        due = ready[min(max(done - 2, 0), len(ready) - 1)]
        blocked = False
        if pending is not None and pending[1] in NAMES[:4]:
            u = UNITS.index((pending[0], NAMES.index(pending[1])))
            blocked = done < min(3 * u + 3 + SKEW[1], n_steps)
            if not blocked:
                take_core(u)
                crossed.add(u)
                if pending[0] == 0:
                    own_cross(UNITS[u][1]).wait_send()
        elif pending is not None and pending[:2] == (0, "small"):
            blocked = done < 3
            if not blocked:
                settle_small()
                loc.start(x_out, work[0]).wait()
        elif pending is not None and pending[1] == "delay":
            until = now + pending[2] if until is None else until
            blocked = now < until and due < until
        if done < n_steps and (pending is None or blocked or due <= now):
            now = max(now, due)
            gather_step(done)
            done += 1
            continue
        now = now + pending[2] if until is None else max(now, until)
        until = None
        pending = next(steps, None)
    for u in range(len(UNITS)):
        if u not in crossed:
            take_core(u)
        for d in range(2):
            for t in range(1, n_z):
                @pl.when(can_send(d, t))
                def _():
                    z_copy(u, d, t).wait_send()
                    t_copy(u, d, t).wait_send()
                @pl.when(gets(d, t))
                def _():
                    x_copy(u, d, t).wait_send()
                    y_copy(u, d, t).wait_send()
                    fx_copy(u, d, t).wait_send()
                    fy_copy(u, d, t).wait_send()
                    c_copy(u, d, t).wait_send()


def forward_model(meta, shards, f1t, ends, small):
    shape, dma, vm = jax.ShapeDtypeStruct, pltpu.SemaphoreType.DMA, pltpu.VMEM
    T = ends.shape[3]
    L = T * HEADS
    n_blocks = L // GROUP
    saved = saved_shapes(T, L, n_blocks)
    n_w, n_small, n_u = len(shards), len(small), len(UNITS)
    outs = [shape((2, 4 * w.shape[1], w.shape[2]), w.dtype) for w in shards]
    outs.append(shape((2, 4) + f1t.shape, f1t.dtype))
    outs += [shape(ends.shape[3:], ends.dtype)] * 2
    outs += [shape((2,) + a.shape[1:], a.dtype) for a in small]
    outs += [shape(*s) for s in saved] * 2
    full = [vm((4 * w.shape[1], w.shape[2]), w.dtype) for w in shards]
    out = pl.pallas_call(
        functools.partial(model_kernel, n_blocks),
        out_shape=outs,
        in_specs=[pl.BlockSpec(memory_space=pltpu.SMEM)] + [ANY] * (n_w + 2 + n_small),
        out_specs=[ANY] * len(outs),
        scratch_shapes=full
        + [vm((4,) + f1t.shape, f1t.dtype)]
        + [vm(a.shape[1:], a.dtype) for a in small]
        + work_scratch(T, L, saved)
        + [vm((L, CHUNK), BF), vm((HEADS, FGATE_RANK, T), BF), vm((HEADS, T, DV), BF), vm((2,) + ends.shape[3:], BF)]
        + [dma((n_w + n_small + 2,))]
        + [dma((n_u, 2, 3)) for _ in range(14)]
        + [dma((n_w + n_small + 2,)), dma((n_small + n_w,)), dma((n_small + n_w,)), dma, dma, dma((4,)), dma((4,)), dma((2,))]
        + [dma((1 + 2 * (len(NAMES) + len(saved)),)), dma((2, 3, HEADS)), dma((2, 3, HEADS))],
        compiler_params=pltpu.CompilerParams(collective_id=0, has_side_effects=True, vmem_limit_bytes=VMEM_LIMIT),
    )(meta, *shards, f1t, ends, *small)
    weights = list(out[:5]) + list(out[7:12])
    return weights, out[5], out[6], out[12 : 12 + len(saved)], out[12 + len(saved) :]


def swap_sections(v):
    return lax.ppermute(v, "section", [(0, 1), (1, 0)])


def plain_gather(shards, f1t, ends, small):
    first = lax.axis_index("section") == 0
    both = lambda a: lax.all_gather(a, "section", axis=0)
    outs = [both(lax.all_gather(w[0], "dp", axis=0, tiled=True)) for w in shards]
    low = lax.all_gather(f1t, "dp", axis=1, tiled=True)
    outs.append(both(jnp.stack(jnp.split(low, 4, axis=1))))
    sent = swap_sections(jnp.where(first, ends[0, 1, 0], ends[0, 0, 0]))
    outs.append(jnp.where(first, ends[0, 0, 0], sent))
    outs.append(jnp.where(first, sent, ends[0, 1, 0]))
    return outs + [both(a[0]) for a in small]


def spread(parts, chosen):
    hot = (chosen[:, None] == jnp.arange(ADAPTERS, dtype=jnp.int32)[None, :]).astype(F32)
    return sum(parts[n][:, None] * hot[n][None, :, None, None] for n in range(parts.shape[0]))


def reduce_kernel(
    gm0, gh0, gp0, gm1, gh1, gp1, m_out, h_out, u_out,
    vm_, vh, vp, rm, rh, rp, am, ah, em, eh, ls, ss, rs, es, er,
):
    core, dp, me = lax.axis_index("section"), lax.axis_index("dp"), lax.axis_index("seq")
    n_dp = vp.shape[1]
    width = u_out.shape[1]
    loads = [
        pltpu.make_async_copy(a, b.at[l], ls.at[l, i])
        for l, three in enumerate(((gm0, gh0, gp0), (gm1, gh1, gp1)))
        for i, (a, b) in enumerate(zip(three, (vm_, vh, vp)))
    ]
    for c in loads:
        c.start()
    barrier = pltpu.get_barrier_semaphore()
    places = [dict(section=1 - core)] + [dict(seq=me ^ k) for k in range(1, HEADS)]
    for gap in range(1, n_dp):
        to = lax.rem(dp + gap, n_dp)
        places += [dict(dp=to), dict(section=1 - core, dp=to)]
    for where in places:
        pl.semaphore_signal(barrier, inc=1, device_id=where, device_id_type=MESH)
    for c in loads:
        c.wait()
    pl.semaphore_wait(barrier, len(places))
    slot = dp * 2 + core
    size = 6 * ADAPTER_COLUMNS // n_dp

    def first_projection(i):
        return i * size // ADAPTER_COLUMNS

    def parts(layer, to):
        at = pl.ds(pl.multiple_of(first_projection(to) * ADAPTER_RANK, ADAPTER_RANK), 2 * ADAPTER_RANK)
        return ((vm_.at[layer, at], rm.at[slot]), (vh.at[layer], rh.at[slot]), (vp.at[layer, to], rp.at[slot]))

    copies = []
    for gap in range(n_dp - 1, -1, -1):
        to = lax.rem(dp + gap, n_dp)
        for crossing in (0, 1):
            if crossing == 0 and gap == 0:
                continue
            section = 1 - core if crossing else core
            for i, (a, b) in enumerate(parts(section, to)):
                c = pltpu.make_async_remote_copy(
                    src_ref=a, dst_ref=b, send_sem=ss.at[crossing, gap, i], recv_sem=rs.at[crossing, gap, i],
                    device_id=dict(section=section, dp=to), device_id_type=MESH,
                )
                c.start()
                copies.append(c)
    at = pl.ds(pl.multiple_of(first_projection(dp) * ADAPTER_RANK, ADAPTER_RANK), 2 * ADAPTER_RANK)
    rm[slot] = vm_[core, at]
    rh[slot] = vh[core]
    rp[slot] = vp[core, dp]
    for c in copies:
        c.wait_recv()
    n = rm.shape[0]
    chosen = [rp[j, :, width : width + 1].astype(F32) for j in range(n)]
    for a in range(ADAPTERS):
        hot = [(c == float(a)).astype(F32) for c in chosen]
        at = slice(a * ADAPTER_RANK, (a + 1) * ADAPTER_RANK)

        def total(values):
            out = hot[0] * values(0).astype(F32)
            for j in range(1, n):
                out += hot[j] * values(j).astype(F32)
            return out

        for p in range(2):
            am[p * ADAPTER_COLUMNS + a * ADAPTER_RANK : p * ADAPTER_COLUMNS + (a + 1) * ADAPTER_RANK, :] = total(
                lambda j, p=p: rm[j, p * ADAPTER_RANK : (p + 1) * ADAPTER_RANK]
            )
        ah[at, :] = total(lambda j: rh[j])
        u_out[at, :] = total(lambda j: rp[j])[:, 0:width]
    own_m, own_h = size // HEADS, ADAPTER_COLUMNS // n_dp // HEADS
    base = dp * size - first_projection(dp) * ADAPTER_COLUMNS

    def m_rows(q):
        return am.at[pl.ds(pl.multiple_of(base + q * own_m, 16), own_m)]

    def h_rows(q):
        return ah.at[pl.ds(pl.multiple_of(dp * HEADS * own_h + q * own_h, 8), own_h)]

    last = []
    for k in range(1, HEADS):
        for i, (a, b) in enumerate(((m_rows(me ^ k), em.at[me]), (h_rows(me ^ k), eh.at[me]))):
            c = to_peer(a, b, es.at[i, k], er.at[i, k], me ^ k)
            c.start()
            last.append(c)
    em[me] = m_rows(me)[...]
    eh[me] = h_rows(me)[...]
    for c in last:
        c.wait_recv()
    for q in range(HEADS):
        m_out[:, q * em.shape[2] : (q + 1) * em.shape[2]] = em[q]
        h_out[:, q * eh.shape[2] : (q + 1) * eh.shape[2]] = eh[q]
    for c in copies + last:
        c.wait_send()


def reduce_gradients(early, late, n_dp):
    gm, gh, gp = early
    n = 2 * n_dp
    width = (U_D + MODEL_WIDTH) // (n_dp * HEADS)
    own_m, own_h = 6 * ADAPTER_COLUMNS // (n_dp * HEADS), ADAPTER_COLUMNS // (n_dp * HEADS)
    vm, dma, VM = pltpu.VMEM, pltpu.SemaphoreType.DMA, pl.BlockSpec(memory_space=pltpu.VMEM)
    shape = jax.ShapeDtypeStruct
    model, hidden, up = pl.pallas_call(
        reduce_kernel,
        out_shape=[
            shape((own_m, MODEL_WIDTH), F32),
            shape((own_h, HEADS * gh.shape[1]), F32),
            shape((ADAPTER_COLUMNS, width), F32),
        ],
        in_specs=[ANY] * 6,
        out_specs=[VM] * 3,
        scratch_shapes=[
            vm((2,) + gm.shape, BF),
            vm((2,) + gh.shape, BF),
            vm((2,) + gp.shape, BF),
            vm((n, 2 * ADAPTER_RANK, gm.shape[1]), BF),
            vm((n,) + gh.shape, BF),
            vm((n,) + gp.shape[1:], BF),
            vm((2 * ADAPTER_COLUMNS, gm.shape[1]), F32),
            vm((ADAPTER_COLUMNS, gh.shape[1]), F32),
            vm((HEADS, own_m, gm.shape[1]), F32),
            vm((HEADS, own_h, gh.shape[1]), F32),
            dma((2, 3)),
            dma((2, n_dp, 3)),
            dma((2, n_dp, 3)),
            dma((2, HEADS)),
            dma((2, HEADS)),
        ],
        compiler_params=pltpu.CompilerParams(collective_id=5, has_side_effects=True, vmem_limit_bytes=32 << 20),
    )(*early, *late)
    return model.T, hidden[:, : VALUE_WIDTH + HIDDEN_UNITS].T, up


def plain_reduce(early, late, n_dp):
    first = lax.axis_index("section") == 0
    dp = lax.axis_index("dp")
    kept = [jnp.where(first, a, b) for a, b in zip(early, late)]
    got = [swap_sections(jnp.where(first, b, a)) for a, b in zip(early, late)]
    gm, gh, gp = [jnp.stack(pair) for pair in zip(kept, got)]
    width = (U_D + MODEL_WIDTH) // (n_dp * HEADS)
    gm = lax.all_gather(gm, "dp", axis=0)
    gh = lax.all_gather(gh, "dp", axis=0)
    gp = lax.all_to_all(jnp.swapaxes(gp, 0, 1), "dp", split_axis=0, concat_axis=0, tiled=True)
    gp = gp.reshape(2 * n_dp, 1, ADAPTER_RANK, -1)
    n = gp.shape[0]
    chosen = gp[:, 0, 0, width].astype(jnp.int32)
    gm = spread(gm.reshape(n, 6, ADAPTER_RANK, -1).astype(F32), chosen).reshape(6 * ADAPTER_COLUMNS, -1)
    gh = spread(gh.reshape(n, 1, ADAPTER_RANK, -1).astype(F32), chosen).reshape(ADAPTER_COLUMNS, -1)
    gp = spread(gp.astype(F32), chosen).reshape(ADAPTER_COLUMNS, -1)

    def columns(v):
        size = v.shape[0] // n_dp
        v = lax.dynamic_slice_in_dim(v, dp * size, size, 0)
        return lax.all_to_all(v, "seq", split_axis=0, concat_axis=1, tiled=True).T

    return columns(gm), columns(gh)[: VALUE_WIDTH + HIDDEN_UNITS], gp[:, :width]


def local(
    ends,
    mixer_input_weight,
    forget_first_map,
    forget_second_map,
    forget_logit_bias,
    mixer_output_weight,
    feedforward_input_weight,
    feedforward_output_weight,
    adapter_model_first,
    adapter_hidden_first,
    adapter_second_maps,
    lengths,
    dealt_block_order,
    adapter_choice_per_seq,
):
    first = lax.axis_index("section") == 0
    mine = lambda a: jnp.where(first, a[0], a[1])
    order = mine(dealt_block_order)[0]
    n_blocks = order.shape[0]
    at = jnp.arange(n_blocks, dtype=jnp.int32)
    inverse = jnp.sum(at[:, None] * (order[:, None] == at[None, :]).astype(jnp.int32), axis=0)
    meta = jnp.concatenate([order, inverse, mine(adapter_choice_per_seq), mine(lengths)])
    n_dp = lax.axis_size("dp")
    own_kernels = n_dp == 4 and lax.axis_size("seq") == 4
    shards = [mixer_input_weight, mixer_output_weight, feedforward_input_weight, feedforward_output_weight]
    small = [
        forget_second_map,
        forget_logit_bias[:, None],
        adapter_model_first,
        adapter_hidden_first,
        adapter_second_maps,
    ]
    if own_kernels:
        weights, x, cotangent, early, late = forward_model(meta, shards, forget_first_map[0].T, ends, small)
    else:
        out = plain_gather(shards, forget_first_map[0].T, ends, small)
        weights, x, cotangent = list(out[:5]) + list(out[7:]), out[5], out[6]
        early = forward(0, meta, x, weights)
        late = forward(1, meta, early[0], weights)
    middle, *grads_late = backward(1, meta, cotangent, early[0], weights, late[1:], n_dp)
    entry, *grads_early = backward(0, meta, middle, x, weights, early[1:], n_dp)
    sent = swap_sections(jnp.where(first, late[0], entry))
    results = jnp.where(first, jnp.stack([entry, sent]), jnp.stack([sent, late[0]]))
    reduce = reduce_gradients if own_kernels else plain_reduce
    model, hidden, up = reduce(grads_early, grads_late, n_dp)
    return (results[None, :, None], model[None], hidden[None], up[None])


def solution(mesh):
    return jax.shard_map(
        local,
        mesh=mesh,
        in_specs=(
            P("section", None, "dp", "seq", None),
            P("section", "dp", None),
            P("section", "dp", None),
            P("section", None, None),
            P("section", None),
            P("section", "dp", None),
            P("section", "dp", None),
            P("section", "dp", None),
            P("section", None, None),
            P("section", None, None),
            P("section", None, None),
            P(None, "dp"),
            P(None, "dp", None),
            P(None, "dp"),
        ),
        out_specs=(
            P("section", None, "dp", "seq", None),
            P("section", None, ("dp", "seq")),
            P("section", None, ("dp", "seq")),
            P("section", None, ("dp", "seq")),
        ),
        check_vma=False,
    )
```

```python
import functools
import jax
import jax.numpy as jnp
from jax import lax
from jax.experimental import pallas as pl
from jax.experimental.pallas import tpu as pltpu

from jax.sharding import PartitionSpec as P

MODEL_WIDTH = 1024
HEADS = 4
KEY = 512
VALUE_WIDTH = 1024
HIDDEN_UNITS = 2816
FGATE_RANK = 16
GROUP = 64
ADAPTER_RANK = 16
ADAPTERS = 8
ADAPTER_COLUMNS = 128
VMEM_LIMIT = 60 << 20
LINK_BYTES_PER_US = 60e3
SKEW = (2, 4)
DELAYS = (8, 25, 20)
STRIPS = (256, 128, 384, 128)

MESH = pl.DeviceIdType.MESH
ANY = pl.BlockSpec(memory_space=pl.ANY)


BF = jnp.bfloat16
F32 = jnp.float32


def nn(a, b):
    return lax.dot_general(a, b, (((1,), (0,)), ((), ())), preferred_element_type=F32)


def nt(a, b):
    return lax.dot_general(a, b, (((1,), (1,)), ((), ())), preferred_element_type=F32)


def tn(a, b):
    return lax.dot_general(a, b, (((0,), (0,)), ((), ())), preferred_element_type=F32)


def silu_parts(v):
    sig = lax.logistic(v)
    return v * sig, sig


def inverse_rms(v):
    return lax.rsqrt(jnp.mean(v * v, axis=-1, keepdims=True) + 1e-06)


def rms_back(v, grad):
    r = inverse_rms(v)
    n = v * r
    return r * (grad - n * jnp.mean(grad * n, axis=-1, keepdims=True))


def lanes(start, size):
    return pl.ds(pl.multiple_of(start, 128), size)


def rows(start, size):
    return pl.ds(pl.multiple_of(start, size if size <= 64 else 64), size)


def greet_peers(me):
    barrier = pltpu.get_barrier_semaphore()
    for d in range(1, HEADS):
        pl.semaphore_signal(barrier, inc=1, device_id={"seq": me ^ d}, device_id_type=MESH)
    pl.semaphore_wait(barrier, HEADS - 1)


def to_peer(src, dst, ssem, rsem, peer):
    return pltpu.make_async_remote_copy(
        src_ref=src, dst_ref=dst, send_sem=ssem, recv_sem=rsem,
        device_id={"seq": peer}, device_id_type=MESH,
    )


class Local:
    def __init__(self, sems):
        self.sems, self.used, self.open = sems, 0, []

    def start(self, src, dst, wait_at_end=False):
        copy = pltpu.make_async_copy(src, dst, self.sems.at[self.used])
        self.used += 1
        copy.start()
        if wait_at_end:
            self.open.append(copy)
        return copy

    def finish(self):
        for copy in self.open:
            copy.wait()
        self.open = []


def picked(adapter, width):
    row = lax.broadcasted_iota(jnp.int32, (width, ADAPTER_RANK), 0)
    col = lax.broadcasted_iota(jnp.int32, (width, ADAPTER_RANK), 1)
    return (row == adapter * ADAPTER_RANK + col).astype(BF)


def column_mask(adapter):
    col = lax.broadcasted_iota(jnp.int32, (1, ADAPTER_COLUMNS), 1)
    low = adapter * ADAPTER_RANK
    return jnp.logical_and(col >= low, col < low + ADAPTER_RANK).astype(F32)


def lower_triangle(dtype):
    i = lax.broadcasted_iota(jnp.int32, (GROUP, GROUP), 0)
    j = lax.broadcasted_iota(jnp.int32, (GROUP, GROUP), 1)
    return (i >= j).astype(dtype)


DK = KEY // HEADS
DV = VALUE_WIDTH // HEADS
CHUNK = 2 * DK + DV
FROZEN = 2 * KEY + 2 * VALUE_WIDTH
TILE = 256
SCALE = DK ** (-0.5)

U_G = FROZEN
U_U = FROZEN + HIDDEN_UNITS
U_O = FROZEN + 2 * HIDDEN_UNITS
U_D = U_O + MODEL_WIDTH


def live_rows(n, length):
    at = lax.broadcasted_iota(jnp.int32, (GROUP, 1), 0) + n * GROUP
    return (at < length).astype(F32)


def forward_steps(layer, n_blocks, meta, loc, weights, buffers, work, outs, sems):
    w, v = weights, buffers
    (h, y, ad, og, qkv, gl, st, mix, yh, rh, ao, mid, af, gu, dn, normed, send, glsend, fg, state, gated, hidden) = work
    o_y, o_ad, o_og, o_qkv, o_gl, o_st, o_mix, o_yh, o_rh, o_ao, o_mid, o_af, o_gu, o_dn = outs
    ssem, rsem = sems
    me = lax.axis_index("seq")
    T = h.shape[0]
    per = T // GROUP
    adapter = meta[2 * n_blocks]
    length = meta[2 * n_blocks + 1]
    mask = column_mask(adapter)
    am, ah, au, mi, mo, fi, fo = [v[name] for name in ("am", "ah", "au", "mi", "mo", "fi", "fo")]

    def load(*names):
        return [loc.start(w[name], v[name]) for name in names]

    def wait(copies):
        for c in copies:
            c.wait()

    yield "small", 0
    small = load("f1", "f2", "b", "am", "au", "ah")
    yield None, 2
    hv = h[...].astype(F32)
    normed[...] = (hv * inverse_rms(hv)).astype(BF)
    wait(small)
    f1, f2, bias = v["f1"], v["f2"], v["b"]
    z_w = f1.shape[2]
    low = nt(f1[0], normed[:, 0:z_w])
    for j in range(1, f1.shape[0]):
        low += nt(f1[j], normed[:, j * z_w : (j + 1) * z_w])
    glsend[...] = low.astype(BF)
    low_copies = [to_peer(glsend, gl.at[me], ssem.at[0, d], rsem.at[0, d], me ^ d) for d in range(1, HEADS)]
    for c in low_copies:
        c.start()
    gl[me] = glsend[...]
    yield "delay", DELAYS[0]
    for p in range(4):
        cols = pl.ds(p * ADAPTER_COLUMNS, ADAPTER_COLUMNS)
        ad[:, cols] = (nn(normed[...], am[:, cols]) * mask).astype(BF)
    f2h = f2[:, lanes(me * DK, DK)]
    bh = bias[:, lanes(me * DK, DK)]
    for c in low_copies:
        c.wait_recv()
    for src in range(HEADS):
        logit = tn(gl[src], f2h) + bh
        fg[src * T : (src + 1) * T, :] = (jax.nn.log_sigmoid(logit) / 16.0).astype(BF)
    loc.start(gl, o_gl, True)
    loc.start(ad, o_ad, True)
    yield "mi", 0
    wait(load("mi"))

    def project(w_start, p, width):
        cols = lanes(w_start, width)
        return nn(normed[...], mi[:, cols]) + nn(ad[:, p * ADAPTER_COLUMNS : (p + 1) * ADAPTER_COLUMNS], au[:, cols])

    def chunk(head, ref):
        ref[:, 0:DK] = project(head * DK, 0, DK).astype(BF)
        ref[:, DK : 2 * DK] = project(KEY + head * DK, 1, DK).astype(BF)
        ref[:, 2 * DK : CHUNK] = project(2 * KEY + head * DV, 2, DV).astype(BF)

    qkv_copies = []
    for d in range(1, HEADS):
        yield None, 1
        chunk(me ^ d, send.at[d - 1])
        copy = to_peer(send.at[d - 1], qkv.at[rows(me * T, T)], ssem.at[1, d], rsem.at[1, d], me ^ d)
        copy.start()
        qkv_copies.append(copy)
    yield None, 1
    chunk(me, qkv.at[rows(me * T, T)])
    yield None, 1
    for j in range(VALUE_WIDTH // TILE):
        og[:, j * TILE : (j + 1) * TILE] = project(2 * KEY + VALUE_WIDTH + j * TILE, 3, TILE)
    loc.start(og, o_og, True)
    yield "delay", DELAYS[1]
    for c in qkv_copies:
        c.wait_recv()
    loc.start(qkv, o_qkv, True)
    tri = lower_triangle(BF)
    causal = lower_triangle(F32)
    state[...] = jnp.zeros_like(state)

    def advance(n, carry):
        at = pl.ds(meta[n_blocks + n] * GROUP, GROUP)
        summed = nn(tri, fg[at, :])
        total = summed[GROUP - 1 : GROUP]
        k = qkv[at, DK : 2 * DK].astype(F32) * live_rows(n, length)
        ku = (k * jnp.exp(total - summed)).astype(BF)
        update = tn(qkv[at, 2 * DK : CHUNK], ku)
        now = state[...]
        st[n] = now.astype(BF)
        state[...] = jnp.exp(total) * now + update
        return carry

    lax.fori_loop(0, n_blocks, advance, 0, unroll=4)
    loc.start(st, o_st, True)
    yield None, 4

    def mix_block(p):
        n = meta[p]
        at = rows(p * GROUP, GROUP)
        summed = nn(tri, fg[at, :])
        middle = summed[GROUP // 2 : GROUP // 2 + 1]
        q = qkv[at, 0:DK].astype(F32) * SCALE
        k = qkv[at, DK : 2 * DK].astype(F32) * live_rows(n, length)
        qe = (q * jnp.exp(summed - middle)).astype(BF)
        ke = (k * jnp.exp(middle - summed)).astype(BF)
        scores = jnp.where(causal > 0, nt(qe, ke), 0.0).astype(BF)
        o = nn(scores, qkv[at, 2 * DK : CHUNK]) + nt((q * jnp.exp(summed)).astype(BF), st[n])
        r = lax.rsqrt(jnp.mean(o * o, axis=-1, keepdims=True) + 1.0)
        yh[at, :] = (o * r).astype(BF)
        rh[at, :] = jnp.broadcast_to(r, (GROUP, DK))

    mix_copies = []
    for d in range(1, HEADS):
        yield None, 2
        peer = me ^ d
        lax.fori_loop(0, per, lambda j, c, peer=peer: (mix_block(peer * per + j), c)[1], 0, unroll=True)
        copy = to_peer(yh.at[rows(peer * T, T)], mix.at[me], ssem.at[2, d], rsem.at[2, d], peer)
        copy.start()
        mix_copies.append(copy)
    yield None, 2
    lax.fori_loop(0, per, lambda j, c: (mix_block(me * per + j), c)[1], 0, unroll=True)
    mix[me] = yh[rows(me * T, T), :]
    loc.start(yh, o_yh, True)
    loc.start(rh, o_rh, True)
    yield "mo", 0
    l_mo = load("mo")
    yield "delay", DELAYS[2]
    for c in mix_copies:
        c.wait_recv()
    loc.start(mix, o_mix, True)
    for hd in range(HEADS):
        cols = slice(hd * DV, (hd + 1) * DV)
        gated[:, cols] = (mix[hd].astype(F32) * silu_parts(og[:, cols])[0]).astype(BF)
    ao[...] = (nn(gated[...], ah[0:VALUE_WIDTH, :]) * mask).astype(BF)
    wait(l_mo)
    for j in range(MODEL_WIDTH // TILE):
        cols = slice(j * TILE, (j + 1) * TILE)
        mid[:, cols] = (
            h[:, cols].astype(F32) + nn(gated[...], mo[:, cols]) + nn(ao[...], au[:, U_O + j * TILE : U_O + (j + 1) * TILE])
        )
    loc.start(ao, o_ao, True)
    loc.start(mid, o_mid, True)
    yield None, 1
    mv = mid[...]
    normed[...] = (mv * inverse_rms(mv)).astype(BF)
    for p in range(2):
        cols = slice(p * ADAPTER_COLUMNS, (p + 1) * ADAPTER_COLUMNS)
        wide = slice((4 + p) * ADAPTER_COLUMNS, (5 + p) * ADAPTER_COLUMNS)
        af[:, cols] = (nn(normed[...], am[:, wide]) * mask).astype(BF)
    loc.start(af, o_af, True)
    yield "fi", 0
    wait(load("fi"))

    def up_tile(i, carry):
        a, b = lanes(i * TILE, TILE), lanes(HIDDEN_UNITS + i * TILE, TILE)
        gate = nn(normed[...], fi[:, a]) + nn(af[:, 0:ADAPTER_COLUMNS], au[:, lanes(U_G + i * TILE, TILE)])
        up = nn(normed[...], fi[:, b]) + nn(af[:, ADAPTER_COLUMNS:], au[:, lanes(U_U + i * TILE, TILE)])
        gu[:, a] = gate.astype(gu.dtype)
        gu[:, b] = up.astype(gu.dtype)
        hidden[:, a] = (silu_parts(gate)[0] * up).astype(BF)
        return carry

    tiles = HIDDEN_UNITS // TILE
    yield None, 3
    lax.fori_loop(0, tiles // 2, up_tile, 0)
    yield None, 3
    lax.fori_loop(tiles // 2, tiles, up_tile, 0)
    loc.start(gu, o_gu, True)
    dn[...] = (nn(hidden[...], ah[VALUE_WIDTH:, :]) * mask).astype(BF)
    loc.start(dn, o_dn, True)
    yield "fo", 0
    wait(load("fo"))
    yield None, 3
    for j in range(MODEL_WIDTH // TILE):
        cols = slice(j * TILE, (j + 1) * TILE)
        y[:, cols] = (
            mid[:, cols] + nn(hidden[...], fo[:, cols]) + nn(dn[...], au[:, U_D + j * TILE : U_D + (j + 1) * TILE])
        ).astype(BF)
    loc.start(y, o_y, True)
    loc.finish()
    for c in low_copies + qkv_copies + mix_copies:
        c.wait_send()


NAMES = ("mi", "mo", "fi", "fo", "f1", "f2", "b", "am", "ah", "au")


def forward_kernel(layer, n_blocks, meta, h_in, *refs):
    n_w, n_out = len(NAMES), 14
    ins, outs = refs[:n_w], refs[n_w : n_w + n_out]
    refs = refs[n_w + n_out :]
    buffers, work = dict(zip(NAMES, refs[:n_w])), refs[n_w:-3]
    lsem, ssem, rsem = refs[-3:]
    loc = Local(lsem)
    first = loc.start(h_in, work[0])
    greet_peers(lax.axis_index("seq"))
    first.wait()
    weights = {name: ref.at[layer] for name, ref in zip(NAMES, ins)}
    for _ in forward_steps(layer, n_blocks, meta, loc, weights, buffers, work, outs, (ssem, rsem)):
        pass


def weight_scratch(weights):
    return [pltpu.VMEM(w.shape[1:], w.dtype) for w in weights]


def saved_shapes(T, L, n_blocks):
    s = lambda shape, dtype=BF: (shape, dtype)
    return [
        s((T, MODEL_WIDTH)),
        s((T, 4 * ADAPTER_COLUMNS)),
        s((T, VALUE_WIDTH), F32),
        s((L, CHUNK)),
        s((HEADS, FGATE_RANK, T)),
        s((n_blocks, DV, DK)),
        s((HEADS, T, DV)),
        s((L, DV)),
        s((L, DK), F32),
        s((T, ADAPTER_COLUMNS)),
        s((T, MODEL_WIDTH), F32),
        s((T, 2 * ADAPTER_COLUMNS)),
        s((T, 2 * HIDDEN_UNITS)),
        s((T, ADAPTER_COLUMNS)),
    ]


def work_scratch(T, L, saved):
    vm = pltpu.VMEM
    return [vm((T, MODEL_WIDTH), BF)] + [vm(*s) for s in saved] + [
        vm((T, MODEL_WIDTH), BF),
        vm((HEADS - 1, T, CHUNK), BF),
        vm((FGATE_RANK, T), BF),
        vm((L, DK), BF),
        vm((DV, DK), F32),
        vm((T, VALUE_WIDTH), BF),
        vm((T, HIDDEN_UNITS), BF),
    ]


def forward(layer, meta, h, weights):
    T = h.shape[0]
    L = T * HEADS
    n_blocks = L // GROUP
    saved = saved_shapes(T, L, n_blocks)
    dma = pltpu.SemaphoreType.DMA
    return pl.pallas_call(
        functools.partial(forward_kernel, layer, n_blocks),
        out_shape=[jax.ShapeDtypeStruct(*s) for s in saved],
        in_specs=[pl.BlockSpec(memory_space=pltpu.SMEM)] + [ANY] * (1 + len(weights)),
        out_specs=[ANY] * len(saved),
        scratch_shapes=weight_scratch(weights)
        + work_scratch(T, L, saved)
        + [dma((1 + len(weights) + len(saved),)), dma((3, HEADS)), dma((3, HEADS))],
        compiler_params=pltpu.CompilerParams(
            collective_id=1 + layer, has_side_effects=True, vmem_limit_bytes=VMEM_LIMIT
        ),
    )(meta, h, *weights)


def backward_kernel(n_blocks, meta, d_in, *refs):
    refs = list(refs)

    def take(n):
        out = refs[:n]
        del refs[:n]
        return out

    n_w = len(NAMES)
    inputs = take(2)
    sources = take(n_w)
    kept = [take(13), take(13)]
    (e_out,) = take(1)
    grad_outs = [take(3), take(3)]
    d, h = take(2)
    mi, mo, fi, fo, f1, f2, bias, am, ah, au = take(n_w)
    ad, og, qkv, gl, st, mix, yh, rh, ao, mid, af, gu, dn = take(13)
    (e,) = take(1)
    grad_sums = [take(3), take(3)]
    (gm, gh, gp, gps, rgm2, rgh2, rgp2, hidden, wide, gad, big, grad, dog, sendm, dmr, logit, fg, gstate, gt, dt, don,
     hidden_gated, sendq, dqkv, dlog, sendl, dlr) = take(27)
    dproj = wide.at[:, pl.ds(MODEL_WIDTH, FROZEN)]
    lsem, ssem2, rsem2, gssem2, grsem2 = take(5)
    me = lax.axis_index("seq")
    loc = Local(lsem)
    buffers = dict(zip(NAMES, (mi, mo, fi, fo, f1, f2, bias, am, ah, au)))
    acts = dict(ad=ad, og=og, qkv=qkv, gl=gl, st=st, mix=mix, yh=yh, rh=rh, ao=ao, mid=mid, af=af, gu=gu, dn=dn)
    on_the_way = [{}, {}]

    def fetch(layer, *names):
        for name in names:
            if name == "d":
                c = loc.start(d_in, d)
            elif name == "h":
                c = loc.start(inputs[layer], h)
            elif name in buffers:
                c = loc.start(sources[NAMES.index(name)].at[layer], buffers[name])
            else:
                c = loc.start(kept[layer][list(acts).index(name)], acts[name])
            on_the_way[layer][name] = c

    fetch(1, "d", "au", "dn", "ah", "fo", "gu")
    greet_peers(me)
    fetch(1, "fi", "am", "mid", "mo", "og", "mix", "f2", "b", "gl", "yh", "rh", "qkv", "st", "ao", "af", "mi", "f1", "ad", "h")
    for layer in (1, 0):
        def arrive(*names, layer=layer):
            for name in names:
                on_the_way[layer][name].wait()

        backward_layer(
            layer, n_blocks, meta, me, loc, arrive, fetch if layer == 1 else None,
            d, h, mi, mo, fi, fo, f1, f2, bias, am, ah, au,
            ad, og, qkv, gl, st, mix, yh, rh, ao, mid, af, gu, dn,
            e, *grad_sums[layer], gm, gh, gp, gps, rgm2.at[layer], rgh2.at[layer], rgp2.at[layer],
            hidden, wide, gad, big, grad, dog, sendm, dmr, logit, fg, gstate, gt, dt, don,
            hidden_gated, sendq, dqkv, dlog, sendl, dlr, dproj,
            ssem2.at[layer], rsem2.at[layer], gssem2.at[layer], grsem2.at[layer],
        )
        for x, y in zip(grad_sums[layer], grad_outs[layer]):
            loc.start(x, y, True)
    loc.start(e, e_out, True)
    loc.finish()


def backward_layer(
    layer, n_blocks, meta, me, loc, arrive, fetch,
    d, h, mi, mo, fi, fo, f1, f2, bias, am, ah, au,
    ad, og, qkv, gl, st, mix, yh, rh, ao, mid, af, gu, dn,
    e, sgm, sgh, sgp, gm, gh, gp, gps, rgm, rgh, rgp,
    hidden, wide, gad, big, grad, dog, sendm, dmr, logit, fg, gstate, gt, dt, don,
    hidden_gated, sendq, dqkv, dlog, sendl, dlr, dproj,
    ssem, rsem, gssem, grsem,
):
    prefetch = (lambda *names: fetch(0, *names)) if fetch else (lambda *names: None)
    T = h.shape[0]
    per = T // GROUP
    adapter = meta[2 * n_blocks]
    length = meta[2 * n_blocks + 1]
    mask = column_mask(adapter)
    pick = picked(adapter, ADAPTER_COLUMNS)

    def narrow(v):
        return nn(v, pick).astype(BF)

    def outer(u, v):
        return tn(narrow(u), v).astype(BF)

    n_dp, width, padded = gps.shape[1], gp.shape[1] // (HEADS * gps.shape[1]), gps.shape[3]
    quarter, hidden_quarter = MODEL_WIDTH // HEADS, gh.shape[1] // HEADS
    n_late = -(-FROZEN // (HEADS * width))
    mix_rows = 4 * ADAPTER_RANK

    def place(dps):
        for i in dps:
            for q in range(HEADS):
                piece = gp[:, (i * HEADS + q) * width : (i * HEADS + q + 1) * width]
                gps[q, i] = jnp.concatenate([piece, jnp.zeros((ADAPTER_RANK, padded - width), BF)], axis=1)

    def grad_copies(late):
        copies = []
        at = slice(0, mix_rows) if late else slice(mix_rows, 6 * ADAPTER_RANK)
        dps = slice(0, n_late) if late else slice(n_late, n_dp)
        for k in range(1, HEADS):
            peer = me ^ k
            pairs = [
                (gm.at[at, lanes(peer * quarter, quarter)], rgm.at[k - 1, at]),
                (gps.at[peer, dps], rgp.at[k - 1, dps]),
            ]
            if not late:
                pairs.append((gh.at[:, lanes(peer * hidden_quarter, hidden_quarter)], rgh.at[k - 1]))
            for i, (a, b) in enumerate(pairs):
                j = i if late else 2 + i
                copies.append(to_peer(a, b, gssem.at[j, k], grsem.at[j, k], peer))
        return copies

    arrive("au", "dn") if layer == 0 else arrive("d", "au", "dn")
    gdown = (nt(d[...], au[:, U_D : U_D + MODEL_WIDTH]).astype(BF).astype(F32) * mask).astype(BF)
    gdown16 = narrow(gdown)
    gh[:, VALUE_WIDTH + HIDDEN_UNITS :] = jnp.zeros((ADAPTER_RANK, gh.shape[1] - VALUE_WIDTH - HIDDEN_UNITS), BF)
    gp[:, U_D : U_D + MODEL_WIDTH] = outer(dn[...], d[...])
    gad[...] = gdown
    arrive("ah", "fo", "gu")

    def down_tile(i, carry):
        a, b = lanes(i * TILE, TILE), lanes(HIDDEN_UNITS + i * TILE, TILE)
        at = pl.ds(pl.multiple_of(i * TILE, TILE), TILE)
        dh = nt(d[...], fo[at, :]) + nt(gad[...], ah[pl.ds(pl.multiple_of(VALUE_WIDTH + i * TILE, TILE), TILE), :])
        gate, up = gu[:, a].astype(F32), gu[:, b].astype(F32)
        act, sig = silu_parts(gate)
        hidden[:, a] = (act * up).astype(BF)
        wide[:, a] = (dh * up * sig * (1.0 + gate * (1.0 - sig))).astype(BF)
        wide[:, b] = (dh * act).astype(BF)
        return carry

    lax.fori_loop(0, HIDDEN_UNITS // TILE, down_tile, 0)
    prefetch("dn", "fo", "gu")
    gate_cols, up_cols = slice(0, HIDDEN_UNITS), slice(HIDDEN_UNITS, 2 * HIDDEN_UNITS)
    gg = (nt(wide[:, gate_cols], au[:, U_G : U_G + HIDDEN_UNITS]).astype(BF).astype(F32) * mask).astype(BF)
    gu2 = (nt(wide[:, up_cols], au[:, U_U : U_U + HIDDEN_UNITS]).astype(BF).astype(F32) * mask).astype(BF)
    gad2 = jnp.concatenate([gg, gu2], axis=1)
    big[:, 0 : 2 * ADAPTER_COLUMNS] = gad2
    arrive("fi", "am")

    def wide_tile(i, carry):
        at = pl.ds(pl.multiple_of(i * TILE, TILE), TILE)
        grad[:, lanes(i * TILE, TILE)] = nt(wide[...], fi[at, :]) + nt(
            big[:, 0 : 2 * ADAPTER_COLUMNS], am[at, 4 * ADAPTER_COLUMNS :]
        )
        return carry

    lax.fori_loop(0, MODEL_WIDTH // TILE, wide_tile, 0)
    prefetch("fi")
    arrive("mid")
    mv = mid[...]
    grad_mid = d[...].astype(F32) + rms_back(mv, grad[...])
    grad[...] = grad_mid
    attn = grad_mid.astype(BF)
    e[...] = attn
    gout = (nt(attn, au[:, U_O : U_O + MODEL_WIDTH]).astype(BF).astype(F32) * mask).astype(BF)
    gad[...] = gout
    arrive("mo", "og", "mix")

    def gate_back(head, out):
        at = rows(head * DV, DV)
        cols = lanes(head * DV, DV)
        gg_ = nt(e[...], mo[at, :]) + nt(gad[...], ah[at, :])
        o = og[:, cols]
        act, sig = silu_parts(o)
        out[...] = (gg_ * act).astype(BF)
        m = mix[head].astype(F32)
        dog[:, cols] = (gg_ * m * sig * (1.0 + o * (1.0 - sig))).astype(BF)
        hidden_gated[:, cols] = (m * act).astype(BF)

    mix_copies = []
    for k in range(1, HEADS):
        peer = me ^ k
        gate_back(peer, sendm.at[k - 1])
        copy = to_peer(sendm.at[k - 1], dmr.at[rows(me * T, T)], ssem.at[0, k], rsem.at[0, k], peer)
        copy.start()
        mix_copies.append(copy)
    gate_back(me, dmr.at[rows(me * T, T)])

    prefetch("mo", "ah", "og", "mix")
    arrive("f2", "b", "gl", "yh", "rh", "qkv", "st")
    f2h = f2[:, lanes(me * DK, DK)]
    bh = bias[:, lanes(me * DK, DK)]
    for src in range(HEADS):
        lg = tn(gl[src], f2h) + bh
        logit[src * T : (src + 1) * T, :] = lg
        fg[src * T : (src + 1) * T, :] = (jax.nn.log_sigmoid(lg) / 16.0).astype(BF)
    tri = lower_triangle(BF)
    causal = lower_triangle(F32)
    for c in mix_copies:
        c.wait_recv()
    gstate[...] = jnp.zeros_like(gstate)

    def retreat(i, carry):
        n = n_blocks - 1 - i
        at = pl.ds(meta[n_blocks + n] * GROUP, GROUP)
        here = rows(n * GROUP, GROUP)
        dm = dmr[at, :].astype(F32)
        yv = yh[at, :].astype(F32)
        r = rh[at, 0:1]
        do = (r * (dm - yv * jnp.mean(dm * yv, axis=-1, keepdims=True))).astype(BF)
        don[here, :] = do
        summed = nn(tri, fg[at, :])
        total = jnp.exp(summed[GROUP - 1 : GROUP])
        qs = (qkv[at, 0:DK].astype(F32) * SCALE * jnp.exp(summed)).astype(BF)
        now = gstate[...]
        gt[n] = now.astype(BF)
        decayed = total * now
        dt[n] = jnp.sum(decayed * st[n].astype(F32), axis=0, keepdims=True)
        gstate[...] = decayed + tn(do, qs)
        return carry

    lax.fori_loop(0, n_blocks, retreat, 0, unroll=4)

    def back_block(p, out, j):
        n = meta[p]
        at = rows(p * GROUP, GROUP)
        here = pl.ds(n * GROUP, GROUP)
        to = rows(j * GROUP, GROUP)
        live = live_rows(n, length)
        summed = nn(tri, fg[at, :])
        middle = summed[GROUP // 2 : GROUP // 2 + 1]
        total = summed[GROUP - 1 : GROUP]
        e1, e2 = jnp.exp(summed - middle), jnp.exp(middle - summed)
        es, eu = jnp.exp(summed), jnp.exp(total - summed)
        q = qkv[at, 0:DK].astype(F32) * SCALE
        k = qkv[at, DK : 2 * DK].astype(F32) * live
        v = qkv[at, 2 * DK : CHUNK]
        do, state_t, grad_t = don[here, :], st[n], gt[n]
        qe, ke, qs, ku = q * e1, k * e2, q * es, k * eu
        qeb, keb = qe.astype(BF), ke.astype(BF)
        scores = jnp.where(causal > 0, nt(qeb, keb), 0.0).astype(BF)
        dscores = jnp.where(causal > 0, nt(do, v), 0.0).astype(BF)
        dv = tn(scores, do) + nt(ku.astype(BF), grad_t)
        dqs = nn(do, state_t)
        dku = nn(v, grad_t)
        dqe = nn(dscores, keb)
        dke = tn(dscores, qeb)
        out[to, 0:DK] = (SCALE * (dqe * e1 + dqs * es)).astype(BF)
        out[to, DK : 2 * DK] = (live * (dke * e2 + dku * eu)).astype(BF)
        out[to, 2 * DK : CHUNK] = dv.astype(BF)
        kk = dku * ku
        dsum = dqe * qe + dqs * qs - dke * ke - kk
        dtotal = dt[n] + jnp.sum(kk, axis=0, keepdims=True)
        high = dsum.astype(BF)
        lowp = (dsum - high.astype(F32)).astype(BF)
        df = tn(tri, high) + tn(tri, lowp) + dtotal
        df = df.astype(BF).astype(F32)
        dlog[to, :] = (df * lax.logistic(-logit[at, :]) / 16.0).astype(BF)

    q_copies = []

    def back_rows(dest, out, low_out):
        lax.fori_loop(0, per, lambda j, c: (back_block(dest * per + j, out, j), c)[1], 0, unroll=2)
        low_out[...] = nt(f2h, dlog[...]).astype(BF)

    for k in range(1, HEADS):
        peer = me ^ k
        back_rows(peer, sendq.at[k - 1], sendl.at[k - 1])
        copies = (
            to_peer(sendq.at[k - 1], dqkv.at[me], ssem.at[1, k], rsem.at[1, k], peer),
            to_peer(sendl.at[k - 1], dlr.at[me], ssem.at[2, k], rsem.at[2, k], peer),
        )
        for copy in copies:
            copy.start()
        q_copies += copies
    back_rows(me, dqkv.at[me], dlr.at[me])

    arrive("af", "ao")
    mv = mid[...]
    normed_mid = (mv * inverse_rms(mv)).astype(BF)
    gh[:, VALUE_WIDTH : VALUE_WIDTH + HIDDEN_UNITS] = tn(gdown16, hidden[...]).astype(BF)
    gm[4 * ADAPTER_RANK : 5 * ADAPTER_RANK, :] = outer(big[:, 0:ADAPTER_COLUMNS], normed_mid)
    gm[5 * ADAPTER_RANK : 6 * ADAPTER_RANK, :] = outer(big[:, ADAPTER_COLUMNS : 2 * ADAPTER_COLUMNS], normed_mid)
    gp[:, U_G : U_G + HIDDEN_UNITS] = outer(af[:, 0:ADAPTER_COLUMNS], wide[:, gate_cols])
    gp[:, U_U : U_U + HIDDEN_UNITS] = outer(af[:, ADAPTER_COLUMNS:], wide[:, up_cols])
    gp[:, U_O : U_O + MODEL_WIDTH] = outer(ao[...], e[...])
    gh[:, 0:VALUE_WIDTH] = outer(gad[...], hidden_gated[...])
    place(range(n_late, n_dp))
    grads = grad_copies(False)
    for c in grads:
        c.start()
    prefetch("mid", "af", "ao", "qkv", "gl", "st", "yh", "rh", "f2", "b")

    arrive("mi", "f1", "ad", "h")
    hv = h[...].astype(F32)
    hr = inverse_rms(hv)
    big[...] = (hv * hr).astype(BF)
    for c in q_copies:
        c.wait_recv()
    for hd in range(HEADS):
        dproj[:, hd * DK : (hd + 1) * DK] = dqkv[hd, :, 0:DK]
        dproj[:, KEY + hd * DK : KEY + (hd + 1) * DK] = dqkv[hd, :, DK : 2 * DK]
        dproj[:, 2 * KEY + hd * DV : 2 * KEY + (hd + 1) * DV] = dqkv[hd, :, 2 * DK : CHUNK]
    dproj[:, 2 * KEY + VALUE_WIDTH :] = dog[...]
    dlow = dlr[0].astype(F32)
    for hd in range(1, HEADS):
        dlow += dlr[hd].astype(F32)
    dlowb = dlow.astype(BF)
    spans = ((0, KEY), (KEY, KEY), (2 * KEY, VALUE_WIDTH), (2 * KEY + VALUE_WIDTH, VALUE_WIDTH))
    for p, (start, span) in enumerate(spans):
        block = slice(p * ADAPTER_COLUMNS, (p + 1) * ADAPTER_COLUMNS)
        piece = dproj[:, start : start + span]
        ga = (nt(piece, au[:, start : start + span]).astype(BF).astype(F32) * mask).astype(BF)
        wide[:, block] = ga
        gm[p * ADAPTER_RANK : (p + 1) * ADAPTER_RANK, :] = outer(ga, big[...])
        gp[:, start : start + span] = outer(ad[:, block], piece)
    place(range(n_late))
    late_grads = grad_copies(True)
    for c in late_grads:
        c.start()
    z_w = f1.shape[2]
    tiles = f1.shape[0]
    back = []
    for j in range(tiles):
        at = slice(j * z_w, (j + 1) * z_w)
        back.append(
            nt(dproj[...], mi[at, :]) + nt(wide[:, 0 : 4 * ADAPTER_COLUMNS], am[at, 0 : 4 * ADAPTER_COLUMNS]) + tn(dlowb, f1[j])
        )
    dn_ = jnp.concatenate(back, axis=1)
    n = hv * hr
    e[...] = (grad[...] + hr * (dn_ - n * jnp.mean(dn_ * n, axis=-1, keepdims=True))).astype(BF)
    if layer == 1:
        d[...] = e[...]
    prefetch("au", "am", "mi", "f1", "ad", "h")
    grads += late_grads
    for c in grads:
        c.wait_recv()

    def summed_over_seq(own, got):
        total = own.astype(F32)
        for k in range(HEADS - 1):
            total += got[k].astype(F32)
        return total.astype(BF)

    sgm[...] = summed_over_seq(gm[:, lanes(me * quarter, quarter)], rgm)
    sgh[...] = summed_over_seq(gh[:, lanes(me * hidden_quarter, hidden_quarter)], rgh)
    spot = lax.broadcasted_iota(jnp.int32, (ADAPTER_RANK, padded), 1)
    for i in range(n_dp):
        total = gps[me, i].astype(F32)
        for k in range(HEADS - 1):
            total += rgp[k, i].astype(F32)
        sgp[i] = jnp.where(spot == width, adapter.astype(F32), total).astype(BF)
    for c in mix_copies + q_copies + grads:
        c.wait_send()


def backward(meta, d, x, h1, weights, early, late, n_dp):
    T = x.shape[0]
    L = T * HEADS
    n_blocks = L // GROUP
    raised = U_D + MODEL_WIDTH
    padded = (raised // (n_dp * HEADS) // 128 + 1) * 128
    quarter = MODEL_WIDTH // HEADS
    hidden_quarter = -(-(VALUE_WIDTH + HIDDEN_UNITS) // (HEADS * 128)) * 128
    outs = [
        ((T, MODEL_WIDTH), BF),
        ((6 * ADAPTER_RANK, quarter), BF),
        ((ADAPTER_RANK, hidden_quarter), BF),
        ((n_dp, ADAPTER_RANK, padded), BF),
    ]
    vm = pltpu.VMEM
    dma = pltpu.SemaphoreType.DMA
    return pl.pallas_call(
        functools.partial(backward_kernel, n_blocks),
        out_shape=[jax.ShapeDtypeStruct(*s) for s in outs[:1] + 2 * outs[1:]],
        in_specs=[pl.BlockSpec(memory_space=pltpu.SMEM)] + [ANY] * (3 + len(weights) + 2 * len(early)),
        out_specs=[ANY] * (2 * len(outs) - 1),
        scratch_shapes=[vm(d.shape, d.dtype), vm(x.shape, x.dtype)]
        + weight_scratch(weights)
        + [vm(s.shape, s.dtype) for s in early]
        + [vm(*s) for s in outs[:1] + 2 * outs[1:]]
        + [
            vm((6 * ADAPTER_RANK, MODEL_WIDTH), BF),
            vm((ADAPTER_RANK, HEADS * hidden_quarter), BF),
            vm((ADAPTER_RANK, raised), BF),
            vm((HEADS, n_dp, ADAPTER_RANK, padded), BF),
            vm((2, HEADS - 1, 6 * ADAPTER_RANK, quarter), BF),
            vm((2, HEADS - 1, ADAPTER_RANK, hidden_quarter), BF),
            vm((2, HEADS - 1, n_dp, ADAPTER_RANK, padded), BF),
            vm((T, HIDDEN_UNITS), BF),
            vm((T, 2 * HIDDEN_UNITS), BF),
            vm((T, ADAPTER_COLUMNS), BF),
            vm((T, MODEL_WIDTH), BF),
            vm((T, MODEL_WIDTH), F32),
            vm((T, VALUE_WIDTH), BF),
            vm((HEADS - 1, T, DV), BF),
            vm((L, DV), BF),
            vm((L, DK), F32),
            vm((L, DK), BF),
            vm((DV, DK), F32),
            vm((n_blocks, DV, DK), BF),
            vm((n_blocks, 1, DK), F32),
            vm((L, DV), BF),
            vm((T, VALUE_WIDTH), BF),
            vm((HEADS - 1, T, CHUNK), BF),
            vm((HEADS, T, CHUNK), BF),
            vm((T, DK), BF),
            vm((HEADS - 1, FGATE_RANK, T), BF),
            vm((HEADS, FGATE_RANK, T), BF),
            dma((2 * (2 + len(weights) + len(early) + len(outs)),)),
            dma((2, 3, HEADS)),
            dma((2, 3, HEADS)),
            dma((2, 5, HEADS)),
            dma((2, 5, HEADS)),
        ],
        compiler_params=pltpu.CompilerParams(
            collective_id=3, has_side_effects=True, vmem_limit_bytes=VMEM_LIMIT
        ),
        cost_estimate=pl.CostEstimate(flops=4 * T * 16_000_000, bytes_accessed=90 << 20, transcendentals=T * 16384),
    )(meta, d, x, h1, *weights, *early, *late)


UNITS = [(layer, w) for layer in range(2) for w in range(4)]


def model_kernel(n_blocks, meta, *refs):
    n_w, n_small, n_saved, n_z = 4, 5, 14, 4
    refs = list(refs)

    def take(n):
        out = refs[:n]
        del refs[:n]
        return out

    shards = take(n_w)
    f1_ref, ends_ref = take(2)
    small = take(n_small)
    outs = take(n_w)
    (f1_out,) = take(1)
    (x_out, c_out) = take(2)
    small_out = take(n_small)
    saved = [take(n_saved), take(n_saved)]
    held = take(n_w)
    held_f1 = take(1)[0]
    held_small = take(n_small)
    work = take(1 + n_saved + 7)
    qkv2, gl2, mix2, held_ends = take(4)
    (ins, zs, zr, ts, tr, xs, xr, ys, yr, fxs, fxr, fys, fyr, cs, cr, own, ms, mr, es, er, f1s, f1r, f1c, lsem, ssem, rsem) = take(26)
    core, z, s = lax.axis_index("section"), lax.axis_index("dp"), lax.axis_index("seq")
    other = 1 - core

    def remote(src, dst, send_sem, recv_sem, **where):
        return pltpu.make_async_remote_copy(
            src_ref=src, dst_ref=dst, send_sem=send_sem, recv_sem=recv_sem, device_id=where, device_id_type=MESH
        )

    def height(w):
        return shards[w].shape[1]

    def staged(w):
        return held[w].at[pl.ds(pl.multiple_of(z * height(w), 16), height(w))]

    fetch = [pltpu.make_async_copy(shards[w].at[0], staged(w), ins.at[w]) for w in range(n_w)]
    fetch += [pltpu.make_async_copy(a.at[0], b, ins.at[n_w + i]) for i, (a, b) in enumerate(zip(small, held_small))]
    fetch.append(pltpu.make_async_copy(ends_ref.at[0, :, 0], held_ends, ins.at[n_w + n_small]))
    fetch.append(pltpu.make_async_copy(f1_ref, held_f1.at[z], ins.at[n_w + n_small + 1]))
    for f in fetch:
        f.start()

    barrier = pltpu.get_barrier_semaphore()
    greeted = [dict(section=other)] + [dict(seq=s ^ k) for k in range(1, HEADS)]
    greeted += [dict(dp=lax.rem(z + gap, n_z)) for gap in range(1, n_z)]
    for where in greeted:
        pl.semaphore_signal(barrier, inc=1, device_id=where, device_id_type=MESH)
    pl.semaphore_wait(barrier, len(greeted))

    def part(u, j, start, size, strip=False):
        layer, w = UNITS[u]
        cols = shards[w].shape[2] // 2
        at, wide = (cols - STRIPS[w], STRIPS[w]) if strip else (0, cols - STRIPS[w])
        return outs[w].at[layer, pl.ds(pl.multiple_of(j * height(w) + start, 16), size), lanes(core * cols + at, wide)]

    def piece(u, j, q):
        r = height(UNITS[u][1])
        return part(u, j, q * (r // 4), r // 4)

    def half(u, j, q, low):
        r = height(UNITS[u][1])
        cut = (r // 8 + 15) // 16 * 16
        start, size = (0, cut) if low else (cut, r // 4 - cut)
        return part(u, j, q * (r // 4) + start, size)

    def block(u, j):
        layer, w = UNITS[u]
        cols = shards[w].shape[2] // 2
        return outs[w].at[layer, pl.ds(pl.multiple_of(j * height(w), 16), height(w)), lanes(core * cols, cols)]

    def whole_block(layer, w):
        return outs[w].at[layer, pl.ds(pl.multiple_of(z * height(w), 16), height(w))]

    def step(d):
        return 1 if d == 0 else -1

    def can_send(d, t):
        has_next = (z < n_z - 1) if d == 0 else (z > 0)
        first = z - step(d) * (t - 1)
        return jnp.logical_and(has_next, jnp.logical_and(first >= 0, first < n_z))

    def gets(d, t):
        first = z - step(d) * t
        return jnp.logical_and(first >= 0, first < n_z)

    def origin(d, t):
        return z - step(d) * t

    def z_copy(u, d, t):
        ref = piece(u, z - step(d) * (t - 1), s)
        return remote(ref, ref, zs.at[u, d, t - 1], zr.at[u, d, t - 1], dp=z + step(d))

    def t_copy(u, d, t):
        ref = part(u, z - step(d) * (t - 1), 0, height(UNITS[u][1]), True)
        return remote(ref, ref, ts.at[u, d, t - 1], tr.at[u, d, t - 1], dp=z + step(d))

    def x_copy(u, d, t):
        ref = piece(u, origin(d, t), s)
        return remote(ref, ref, xs.at[u, d, t - 1], xr.at[u, d, t - 1], seq=s ^ 1)

    def y_copy(u, d, t):
        ref = piece(u, origin(d, t), s)
        return remote(ref, ref, ys.at[u, d, t - 1], yr.at[u, d, t - 1], seq=s ^ 2)

    def fx_copy(u, d, t):
        ref = half(u, origin(d, t), s ^ 2, False)
        return remote(ref, ref, fxs.at[u, d, t - 1], fxr.at[u, d, t - 1], seq=s ^ 1)

    def fy_copy(u, d, t):
        ref = half(u, origin(d, t), s ^ 1, True)
        return remote(ref, ref, fys.at[u, d, t - 1], fyr.at[u, d, t - 1], seq=s ^ 2)

    def c_copy(u, d, t):
        ref = block(u, origin(d, t))
        return remote(ref, ref, cs.at[u, d, t - 1], cr.at[u, d, t - 1], section=other)

    def own_copy(w):
        return pltpu.make_async_copy(staged(w), whole_block(core, w), own.at[w])

    def own_cross(w):
        return remote(staged(w), whole_block(core, w), ms.at[n_small + w], mr.at[n_small + w], section=other)

    def start_own(u):
        layer, w = UNITS[u]

        if layer == 0:
            own_copy(w).wait()

        @pl.when(core != layer)
        def _():
            own_cross(w).wait_recv()

        for d in range(2):
            @pl.when(can_send(d, 1))
            def _():
                z_copy(u, d, 1).start()
                if STRIPS[w]:
                    t_copy(u, d, 1).start()

    def take_z(u, t):
        for d in range(2):
            @pl.when(gets(d, t))
            def _():
                z_copy(u, d, t).wait_recv()
            if t < n_z - 1:
                @pl.when(can_send(d, t + 1))
                def _():
                    z_copy(u, d, t + 1).start()
            @pl.when(gets(d, t))
            def _():
                x_copy(u, d, t).start()
                y_copy(u, d, t).start()
                if STRIPS[UNITS[u][1]]:
                    t_copy(u, d, t).wait_recv()
            if t < n_z - 1 and STRIPS[UNITS[u][1]]:
                @pl.when(can_send(d, t + 1))
                def _():
                    t_copy(u, d, t + 1).start()

    def take_xy(u, t):
        for d in range(2):
            @pl.when(gets(d, t))
            def _():
                x_copy(u, d, t).wait_recv()
                fy_copy(u, d, t).start()
                y_copy(u, d, t).wait_recv()
                fx_copy(u, d, t).start()

    def take_diagonal(u, t):
        for d in range(2):
            @pl.when(gets(d, t))
            def _():
                fy_copy(u, d, t).wait_recv()
                fx_copy(u, d, t).wait_recv()
                c_copy(u, d, t).start()

    def take_core(u):
        for d in range(2):
            for t in range(1, n_z):
                @pl.when(gets(d, t))
                def _():
                    c_copy(u, d, t).wait_recv()

    def f1_copy(gap):
        return remote(held_f1.at[z], f1_out.at[core, z], f1s.at[gap], f1r.at[gap], dp=lax.rem(z + gap, n_z))

    def launch(w):
        fetch[w].wait()
        own_copy(w).start()
        own_cross(w).start()

    launch(0)
    fetch[-1].wait()
    f1_sends = [f1_copy(gap) for gap in range(1, n_z)]
    for c in f1_sends:
        c.start()
    f1_own = pltpu.make_async_copy(held_f1.at[z], f1_out.at[core, z], own.at[n_w])
    f1_own.start()
    ends_to_x = remote(held_ends.at[1], x_out, es, er, section=other)
    ends_to_c = remote(held_ends.at[0], c_out, es, er, section=other)
    ends_x = pltpu.make_async_copy(held_ends.at[0], x_out, own.at[n_w + 1])
    ends_c = pltpu.make_async_copy(held_ends.at[1], c_out, own.at[n_w + 1])
    f1_cross = remote(f1_out.at[core], f1_out.at[core], f1c.at[0], f1c.at[1], section=other)
    start_own(0)
    launch(1)
    smalls = []

    def launch_rest():
        fetch[-2].wait()

        @pl.when(core == 0)
        def _():
            ends_to_x.start()
            ends_x.start()

        @pl.when(core == 1)
        def _():
            ends_to_c.start()
            ends_c.start()

        for i, (a, b) in enumerate(zip(held_small, small_out)):
            fetch[n_w + i].wait()
            mine = pltpu.make_async_copy(a, b.at[core], own.at[n_w + 2 + i])
            theirs = remote(a, b.at[core], ms.at[i], mr.at[i], section=other)
            mine.start()
            theirs.start()
            smalls.append((mine, theirs))
        for w in range(2, n_w):
            launch(w)
        f1_own.wait()
        for c in f1_sends:
            c.wait_recv()
        f1_cross.start()

    def settle_small():
        for mine, theirs in smalls:
            mine.wait()
            theirs.wait()
        for c in f1_sends:
            c.wait_send()
        f1_cross.wait()
        ends_x.wait()
        ends_to_x.wait()

    items = [(u, t) for u in range(len(UNITS)) for t in range(1, n_z)]
    ready, clock = [], 8.0
    for u, t in items:
        r, c = shards[UNITS[u][1]].shape[1:]
        clock += r // 4 * (c - 2 * STRIPS[UNITS[u][1]]) * 3 / LINK_BYTES_PER_US
        ready.append(clock)

    def gather_step(i):
        if i == 1:
            launch_rest()
        if i < len(items):
            u, t = items[i]
            if t == 1 and u + 1 < len(UNITS):
                start_own(u + 1)
            take_z(u, t)
        if 0 <= i - SKEW[0] < len(items):
            take_xy(*items[i - SKEW[0]])
        if 0 <= i - SKEW[1] < len(items):
            take_diagonal(*items[i - SKEW[1]])

    loc = Local(lsem)
    n_steps = len(items) + SKEW[1]
    works = [list(work), list(work)]
    for at, ref in ((4, qkv2), (5, gl2), (7, mix2)):
        works[1][at] = ref

    def both_layers():
        for layer in range(2):
            sources = dict(zip(NAMES[:4], outs))
            sources["f1"] = f1_out
            sources.update(zip(NAMES[5:], small_out))
            sources = {name: ref.at[layer] for name, ref in sources.items()}
            buffers = dict(zip(NAMES, held + [held_f1] + held_small))
            for what, us in forward_steps(
                layer, n_blocks, meta, loc, sources, buffers, works[layer], saved[layer], (ssem.at[layer], rsem.at[layer])
            ):
                yield layer, what, us
            if layer == 0:
                work[0][...] = work[1][...]

    steps, done, now, crossed, until = both_layers(), 0, 8.0, set(), None
    pending = next(steps)
    while pending is not None or done < n_steps:
        due = ready[min(max(done - 2, 0), len(ready) - 1)]
        blocked = False
        if pending is not None and pending[1] in NAMES[:4]:
            u = UNITS.index((pending[0], NAMES.index(pending[1])))
            blocked = done < min(3 * u + 3 + SKEW[1], n_steps)
            if not blocked:
                take_core(u)
                crossed.add(u)
                if pending[0] == 0:
                    own_cross(UNITS[u][1]).wait_send()
        elif pending is not None and pending[:2] == (0, "small"):
            blocked = done < 3
            if not blocked:
                settle_small()
                loc.start(x_out, work[0]).wait()
        elif pending is not None and pending[1] == "delay":
            until = now + pending[2] if until is None else until
            blocked = now < until and due < until
        if done < n_steps and (pending is None or blocked or due <= now):
            now = max(now, due)
            gather_step(done)
            done += 1
            continue
        now = now + pending[2] if until is None else max(now, until)
        until = None
        pending = next(steps, None)
    for u in range(len(UNITS)):
        if u not in crossed:
            take_core(u)
        for d in range(2):
            for t in range(1, n_z):
                @pl.when(can_send(d, t))
                def _():
                    z_copy(u, d, t).wait_send()
                    if STRIPS[UNITS[u][1]]:
                        t_copy(u, d, t).wait_send()
                @pl.when(gets(d, t))
                def _():
                    x_copy(u, d, t).wait_send()
                    y_copy(u, d, t).wait_send()
                    fx_copy(u, d, t).wait_send()
                    fy_copy(u, d, t).wait_send()
                    c_copy(u, d, t).wait_send()


def forward_model(meta, shards, f1t, ends, small):
    shape, dma, vm = jax.ShapeDtypeStruct, pltpu.SemaphoreType.DMA, pltpu.VMEM
    T = ends.shape[3]
    L = T * HEADS
    n_blocks = L // GROUP
    saved = saved_shapes(T, L, n_blocks)
    n_w, n_small, n_u = len(shards), len(small), len(UNITS)
    outs = [shape((2, 4 * w.shape[1], w.shape[2]), w.dtype) for w in shards]
    outs.append(shape((2, 4) + f1t.shape, f1t.dtype))
    outs += [shape(ends.shape[3:], ends.dtype)] * 2
    outs += [shape((2,) + a.shape[1:], a.dtype) for a in small]
    outs += [shape(*s) for s in saved] * 2
    full = [vm((4 * w.shape[1], w.shape[2]), w.dtype) for w in shards]
    out = pl.pallas_call(
        functools.partial(model_kernel, n_blocks),
        out_shape=outs,
        in_specs=[pl.BlockSpec(memory_space=pltpu.SMEM)] + [ANY] * (n_w + 2 + n_small),
        out_specs=[ANY] * len(outs),
        scratch_shapes=full
        + [vm((4,) + f1t.shape, f1t.dtype)]
        + [vm(a.shape[1:], a.dtype) for a in small]
        + work_scratch(T, L, saved)
        + [vm((L, CHUNK), BF), vm((HEADS, FGATE_RANK, T), BF), vm((HEADS, T, DV), BF), vm((2,) + ends.shape[3:], BF)]
        + [dma((n_w + n_small + 2,))]
        + [dma((n_u, 2, 3)) for _ in range(14)]
        + [dma((n_w + n_small + 2,)), dma((n_small + n_w,)), dma((n_small + n_w,)), dma, dma, dma((4,)), dma((4,)), dma((2,))]
        + [dma((1 + 2 * (len(NAMES) + len(saved)),)), dma((2, 3, HEADS)), dma((2, 3, HEADS))],
        compiler_params=pltpu.CompilerParams(collective_id=0, has_side_effects=True, vmem_limit_bytes=VMEM_LIMIT),
    )(meta, *shards, f1t, ends, *small)
    weights = list(out[:5]) + list(out[7:12])
    return weights, out[5], out[6], out[12 : 12 + len(saved)], out[12 + len(saved) :]


def swap_sections(v):
    return lax.ppermute(v, "section", [(0, 1), (1, 0)])


def plain_gather(shards, f1t, ends, small):
    first = lax.axis_index("section") == 0
    both = lambda a: lax.all_gather(a, "section", axis=0)
    outs = [both(lax.all_gather(w[0], "dp", axis=0, tiled=True)) for w in shards]
    low = lax.all_gather(f1t, "dp", axis=1, tiled=True)
    outs.append(both(jnp.stack(jnp.split(low, 4, axis=1))))
    sent = swap_sections(jnp.where(first, ends[0, 1, 0], ends[0, 0, 0]))
    outs.append(jnp.where(first, ends[0, 0, 0], sent))
    outs.append(jnp.where(first, sent, ends[0, 1, 0]))
    return outs + [both(a[0]) for a in small]


def spread(parts, chosen):
    hot = (chosen[:, None] == jnp.arange(ADAPTERS, dtype=jnp.int32)[None, :]).astype(F32)
    return sum(parts[n][:, None] * hot[n][None, :, None, None] for n in range(parts.shape[0]))


def reduce_kernel(
    gm0, gh0, gp0, gm1, gh1, gp1, m_out, h_out, u_out,
    vm_, vh, vp, rm, rh, rp, am, ah, em, eh, ls, ss, rs, es, er,
):
    core, dp, me = lax.axis_index("section"), lax.axis_index("dp"), lax.axis_index("seq")
    n_dp = vp.shape[1]
    width = u_out.shape[1]
    loads = [
        pltpu.make_async_copy(a, b.at[l], ls.at[l, i])
        for l, three in enumerate(((gm0, gh0, gp0), (gm1, gh1, gp1)))
        for i, (a, b) in enumerate(zip(three, (vm_, vh, vp)))
    ]
    for c in loads:
        c.start()
    barrier = pltpu.get_barrier_semaphore()
    places = [dict(section=1 - core)] + [dict(seq=me ^ k) for k in range(1, HEADS)]
    for gap in range(1, n_dp):
        to = lax.rem(dp + gap, n_dp)
        places += [dict(dp=to), dict(section=1 - core, dp=to)]
    for where in places:
        pl.semaphore_signal(barrier, inc=1, device_id=where, device_id_type=MESH)
    for c in loads:
        c.wait()
    pl.semaphore_wait(barrier, len(places))
    slot = dp * 2 + core
    size = 6 * ADAPTER_COLUMNS // n_dp

    def first_projection(i):
        return i * size // ADAPTER_COLUMNS

    def parts(layer, to):
        at = pl.ds(pl.multiple_of(first_projection(to) * ADAPTER_RANK, ADAPTER_RANK), 2 * ADAPTER_RANK)
        return ((vm_.at[layer, at], rm.at[slot]), (vh.at[layer], rh.at[slot]), (vp.at[layer, to], rp.at[slot]))

    copies = []
    for gap in range(n_dp - 1, -1, -1):
        to = lax.rem(dp + gap, n_dp)
        for crossing in (0, 1):
            if crossing == 0 and gap == 0:
                continue
            section = 1 - core if crossing else core
            for i, (a, b) in enumerate(parts(section, to)):
                c = pltpu.make_async_remote_copy(
                    src_ref=a, dst_ref=b, send_sem=ss.at[crossing, gap, i], recv_sem=rs.at[crossing, gap, i],
                    device_id=dict(section=section, dp=to), device_id_type=MESH,
                )
                c.start()
                copies.append(c)
    at = pl.ds(pl.multiple_of(first_projection(dp) * ADAPTER_RANK, ADAPTER_RANK), 2 * ADAPTER_RANK)
    rm[slot] = vm_[core, at]
    rh[slot] = vh[core]
    rp[slot] = vp[core, dp]
    for c in copies:
        c.wait_recv()
    n = rm.shape[0]
    chosen = [rp[j, :, width : width + 1].astype(F32) for j in range(n)]
    for a in range(ADAPTERS):
        hot = [(c == float(a)).astype(F32) for c in chosen]
        at = slice(a * ADAPTER_RANK, (a + 1) * ADAPTER_RANK)

        def total(values):
            out = hot[0] * values(0).astype(F32)
            for j in range(1, n):
                out += hot[j] * values(j).astype(F32)
            return out

        for p in range(2):
            am[p * ADAPTER_COLUMNS + a * ADAPTER_RANK : p * ADAPTER_COLUMNS + (a + 1) * ADAPTER_RANK, :] = total(
                lambda j, p=p: rm[j, p * ADAPTER_RANK : (p + 1) * ADAPTER_RANK]
            )
        ah[at, :] = total(lambda j: rh[j])
        u_out[at, :] = total(lambda j: rp[j])[:, 0:width]
    own_m, own_h = size // HEADS, ADAPTER_COLUMNS // n_dp // HEADS
    base = dp * size - first_projection(dp) * ADAPTER_COLUMNS

    def m_rows(q):
        return am.at[pl.ds(pl.multiple_of(base + q * own_m, 16), own_m)]

    def h_rows(q):
        return ah.at[pl.ds(pl.multiple_of(dp * HEADS * own_h + q * own_h, 8), own_h)]

    last = []
    for k in range(1, HEADS):
        for i, (a, b) in enumerate(((m_rows(me ^ k), em.at[me]), (h_rows(me ^ k), eh.at[me]))):
            c = to_peer(a, b, es.at[i, k], er.at[i, k], me ^ k)
            c.start()
            last.append(c)
    em[me] = m_rows(me)[...]
    eh[me] = h_rows(me)[...]
    for c in last:
        c.wait_recv()
    for q in range(HEADS):
        m_out[:, q * em.shape[2] : (q + 1) * em.shape[2]] = em[q]
        h_out[:, q * eh.shape[2] : (q + 1) * eh.shape[2]] = eh[q]
    for c in copies + last:
        c.wait_send()


def reduce_gradients(early, late, n_dp):
    gm, gh, gp = early
    n = 2 * n_dp
    width = (U_D + MODEL_WIDTH) // (n_dp * HEADS)
    own_m, own_h = 6 * ADAPTER_COLUMNS // (n_dp * HEADS), ADAPTER_COLUMNS // (n_dp * HEADS)
    vm, dma, VM = pltpu.VMEM, pltpu.SemaphoreType.DMA, pl.BlockSpec(memory_space=pltpu.VMEM)
    shape = jax.ShapeDtypeStruct
    model, hidden, up = pl.pallas_call(
        reduce_kernel,
        out_shape=[
            shape((own_m, MODEL_WIDTH), F32),
            shape((own_h, HEADS * gh.shape[1]), F32),
            shape((ADAPTER_COLUMNS, width), F32),
        ],
        in_specs=[ANY] * 6,
        out_specs=[VM] * 3,
        scratch_shapes=[
            vm((2,) + gm.shape, BF),
            vm((2,) + gh.shape, BF),
            vm((2,) + gp.shape, BF),
            vm((n, 2 * ADAPTER_RANK, gm.shape[1]), BF),
            vm((n,) + gh.shape, BF),
            vm((n,) + gp.shape[1:], BF),
            vm((2 * ADAPTER_COLUMNS, gm.shape[1]), F32),
            vm((ADAPTER_COLUMNS, gh.shape[1]), F32),
            vm((HEADS, own_m, gm.shape[1]), F32),
            vm((HEADS, own_h, gh.shape[1]), F32),
            dma((2, 3)),
            dma((2, n_dp, 3)),
            dma((2, n_dp, 3)),
            dma((2, HEADS)),
            dma((2, HEADS)),
        ],
        compiler_params=pltpu.CompilerParams(collective_id=5, has_side_effects=True, vmem_limit_bytes=32 << 20),
    )(*early, *late)
    return model.T, hidden[:, : VALUE_WIDTH + HIDDEN_UNITS].T, up


def plain_reduce(early, late, n_dp):
    first = lax.axis_index("section") == 0
    dp = lax.axis_index("dp")
    kept = [jnp.where(first, a, b) for a, b in zip(early, late)]
    got = [swap_sections(jnp.where(first, b, a)) for a, b in zip(early, late)]
    gm, gh, gp = [jnp.stack(pair) for pair in zip(kept, got)]
    width = (U_D + MODEL_WIDTH) // (n_dp * HEADS)
    gm = lax.all_gather(gm, "dp", axis=0)
    gh = lax.all_gather(gh, "dp", axis=0)
    gp = lax.all_to_all(jnp.swapaxes(gp, 0, 1), "dp", split_axis=0, concat_axis=0, tiled=True)
    gp = gp.reshape(2 * n_dp, 1, ADAPTER_RANK, -1)
    n = gp.shape[0]
    chosen = gp[:, 0, 0, width].astype(jnp.int32)
    gm = spread(gm.reshape(n, 6, ADAPTER_RANK, -1).astype(F32), chosen).reshape(6 * ADAPTER_COLUMNS, -1)
    gh = spread(gh.reshape(n, 1, ADAPTER_RANK, -1).astype(F32), chosen).reshape(ADAPTER_COLUMNS, -1)
    gp = spread(gp.astype(F32), chosen).reshape(ADAPTER_COLUMNS, -1)

    def columns(v):
        size = v.shape[0] // n_dp
        v = lax.dynamic_slice_in_dim(v, dp * size, size, 0)
        return lax.all_to_all(v, "seq", split_axis=0, concat_axis=1, tiled=True).T

    return columns(gm), columns(gh)[: VALUE_WIDTH + HIDDEN_UNITS], gp[:, :width]


def local(
    ends,
    mixer_input_weight,
    forget_first_map,
    forget_second_map,
    forget_logit_bias,
    mixer_output_weight,
    feedforward_input_weight,
    feedforward_output_weight,
    adapter_model_first,
    adapter_hidden_first,
    adapter_second_maps,
    lengths,
    dealt_block_order,
    adapter_choice_per_seq,
):
    first = lax.axis_index("section") == 0
    mine = lambda a: jnp.where(first, a[0], a[1])
    order = mine(dealt_block_order)[0]
    n_blocks = order.shape[0]
    at = jnp.arange(n_blocks, dtype=jnp.int32)
    inverse = jnp.sum(at[:, None] * (order[:, None] == at[None, :]).astype(jnp.int32), axis=0)
    meta = jnp.concatenate([order, inverse, mine(adapter_choice_per_seq), mine(lengths)])
    n_dp = lax.axis_size("dp")
    own_kernels = n_dp == 4 and lax.axis_size("seq") == 4
    shards = [mixer_input_weight, mixer_output_weight, feedforward_input_weight, feedforward_output_weight]
    small = [
        forget_second_map,
        forget_logit_bias[:, None],
        adapter_model_first,
        adapter_hidden_first,
        adapter_second_maps,
    ]
    if own_kernels:
        weights, x, cotangent, early, late = forward_model(meta, shards, forget_first_map[0].T, ends, small)
    else:
        out = plain_gather(shards, forget_first_map[0].T, ends, small)
        weights, x, cotangent = list(out[:5]) + list(out[7:]), out[5], out[6]
        early = forward(0, meta, x, weights)
        late = forward(1, meta, early[0], weights)
    entry, *grads = backward(meta, cotangent, x, early[0], weights, early[1:], late[1:], n_dp)
    grads_early, grads_late = grads[:3], grads[3:]
    sent = swap_sections(jnp.where(first, late[0], entry))
    results = jnp.where(first, jnp.stack([entry, sent]), jnp.stack([sent, late[0]]))
    reduce = reduce_gradients if own_kernels else plain_reduce
    model, hidden, up = reduce(grads_early, grads_late, n_dp)
    return (results[None, :, None], model[None], hidden[None], up[None])


def solution(mesh):
    return jax.shard_map(
        local,
        mesh=mesh,
        in_specs=(
            P("section", None, "dp", "seq", None),
            P("section", "dp", None),
            P("section", "dp", None),
            P("section", None, None),
            P("section", None),
            P("section", "dp", None),
            P("section", "dp", None),
            P("section", "dp", None),
            P("section", None, None),
            P("section", None, None),
            P("section", None, None),
            P(None, "dp"),
            P(None, "dp", None),
            P(None, "dp"),
        ),
        out_specs=(
            P("section", None, "dp", "seq", None),
            P("section", None, ("dp", "seq")),
            P("section", None, ("dp", "seq")),
            P("section", None, ("dp", "seq")),
        ),
        check_vma=False,
    )
```

```python
import functools
import jax
import jax.numpy as jnp
from jax import lax
from jax.experimental import pallas as pl
from jax.experimental.pallas import tpu as pltpu

from jax.sharding import PartitionSpec as P

MODEL_WIDTH = 1024
HEADS = 4
KEY = 512
VALUE_WIDTH = 1024
HIDDEN_UNITS = 2816
FGATE_RANK = 16
GROUP = 64
ADAPTER_RANK = 16
ADAPTERS = 8
ADAPTER_COLUMNS = 128
VMEM_LIMIT = 60 << 20
LINK_BYTES_PER_US = 60e3
SKEW = (2, 4)
DELAYS = (8, 25, 20)
STRIPS = (256, 128, 384, 128)

MESH = pl.DeviceIdType.MESH
ANY = pl.BlockSpec(memory_space=pl.ANY)


BF = jnp.bfloat16
F32 = jnp.float32


def nn(a, b):
    return lax.dot_general(a, b, (((1,), (0,)), ((), ())), preferred_element_type=F32)


def nt(a, b):
    return lax.dot_general(a, b, (((1,), (1,)), ((), ())), preferred_element_type=F32)


def tn(a, b):
    return lax.dot_general(a, b, (((0,), (0,)), ((), ())), preferred_element_type=F32)


def silu_parts(v):
    sig = lax.logistic(v)
    return v * sig, sig


def inverse_rms(v):
    return lax.rsqrt(jnp.mean(v * v, axis=-1, keepdims=True) + 1e-06)


def rms_back(v, grad):
    r = inverse_rms(v)
    n = v * r
    return r * (grad - n * jnp.mean(grad * n, axis=-1, keepdims=True))


def lanes(start, size):
    return pl.ds(pl.multiple_of(start, 128), size)


def rows(start, size):
    return pl.ds(pl.multiple_of(start, size if size <= 64 else 64), size)


def greet_peers(me):
    barrier = pltpu.get_barrier_semaphore()
    for d in range(1, HEADS):
        pl.semaphore_signal(barrier, inc=1, device_id={"seq": me ^ d}, device_id_type=MESH)
    pl.semaphore_wait(barrier, HEADS - 1)


def to_peer(src, dst, ssem, rsem, peer):
    return pltpu.make_async_remote_copy(
        src_ref=src, dst_ref=dst, send_sem=ssem, recv_sem=rsem,
        device_id={"seq": peer}, device_id_type=MESH,
    )


class Local:
    def __init__(self, sems):
        self.sems, self.used, self.open = sems, 0, []

    def start(self, src, dst, wait_at_end=False):
        copy = pltpu.make_async_copy(src, dst, self.sems.at[self.used])
        self.used += 1
        copy.start()
        if wait_at_end:
            self.open.append(copy)
        return copy

    def finish(self):
        for copy in self.open:
            copy.wait()
        self.open = []


def picked(adapter, width):
    row = lax.broadcasted_iota(jnp.int32, (width, ADAPTER_RANK), 0)
    col = lax.broadcasted_iota(jnp.int32, (width, ADAPTER_RANK), 1)
    return (row == adapter * ADAPTER_RANK + col).astype(BF)


def column_mask(adapter):
    col = lax.broadcasted_iota(jnp.int32, (1, ADAPTER_COLUMNS), 1)
    low = adapter * ADAPTER_RANK
    return jnp.logical_and(col >= low, col < low + ADAPTER_RANK).astype(F32)


def lower_triangle(dtype):
    i = lax.broadcasted_iota(jnp.int32, (GROUP, GROUP), 0)
    j = lax.broadcasted_iota(jnp.int32, (GROUP, GROUP), 1)
    return (i >= j).astype(dtype)


DK = KEY // HEADS
DV = VALUE_WIDTH // HEADS
CHUNK = 2 * DK + DV
FROZEN = 2 * KEY + 2 * VALUE_WIDTH
TILE = 256
SCALE = DK ** (-0.5)

U_G = FROZEN
U_U = FROZEN + HIDDEN_UNITS
U_O = FROZEN + 2 * HIDDEN_UNITS
U_D = U_O + MODEL_WIDTH


def live_rows(n, length):
    at = lax.broadcasted_iota(jnp.int32, (GROUP, 1), 0) + n * GROUP
    return (at < length).astype(F32)


def forward_steps(layer, n_blocks, meta, loc, weights, buffers, work, outs, sems):
    w, v = weights, buffers
    (h, y, ad, og, qkv, gl, st, mix, yh, rh, ao, mid, af, gu, dn, normed, send, glsend, fg, state, gated, hidden) = work
    o_y, o_ad, o_og, o_qkv, o_gl, o_st, o_mix, o_yh, o_rh, o_ao, o_mid, o_af, o_gu, o_dn = outs
    ssem, rsem = sems
    me = lax.axis_index("seq")
    T = h.shape[0]
    per = T // GROUP
    adapter = meta[2 * n_blocks]
    length = meta[2 * n_blocks + 1]
    mask = column_mask(adapter)
    am, ah, au, mi, mo, fi, fo = [v[name] for name in ("am", "ah", "au", "mi", "mo", "fi", "fo")]

    def load(*names):
        return [loc.start(w[name], v[name]) for name in names]

    def wait(copies):
        for c in copies:
            c.wait()

    yield "small", 0
    small = load("f1", "f2", "b", "am", "au", "ah")
    yield None, 2
    hv = h[...].astype(F32)
    normed[...] = (hv * inverse_rms(hv)).astype(BF)
    wait(small)
    f1, f2, bias = v["f1"], v["f2"], v["b"]
    z_w = f1.shape[2]
    low = nt(f1[0], normed[:, 0:z_w])
    for j in range(1, f1.shape[0]):
        low += nt(f1[j], normed[:, j * z_w : (j + 1) * z_w])
    glsend[...] = low.astype(BF)
    low_copies = [to_peer(glsend, gl.at[me], ssem.at[0, d], rsem.at[0, d], me ^ d) for d in range(1, HEADS)]
    for c in low_copies:
        c.start()
    gl[me] = glsend[...]
    yield "delay", DELAYS[0]
    for p in range(4):
        cols = pl.ds(p * ADAPTER_COLUMNS, ADAPTER_COLUMNS)
        ad[:, cols] = (nn(normed[...], am[:, cols]) * mask).astype(BF)
    f2h = f2[:, lanes(me * DK, DK)]
    bh = bias[:, lanes(me * DK, DK)]
    for c in low_copies:
        c.wait_recv()
    for src in range(HEADS):
        logit = tn(gl[src], f2h) + bh
        fg[src * T : (src + 1) * T, :] = (jax.nn.log_sigmoid(logit) / 16.0).astype(BF)
    loc.start(gl, o_gl, True)
    loc.start(ad, o_ad, True)
    yield "mi", 0
    wait(load("mi"))

    def project(w_start, p, width):
        cols = lanes(w_start, width)
        return nn(normed[...], mi[:, cols]) + nn(ad[:, p * ADAPTER_COLUMNS : (p + 1) * ADAPTER_COLUMNS], au[:, cols])

    def chunk(head, ref):
        ref[:, 0:DK] = project(head * DK, 0, DK).astype(BF)
        ref[:, DK : 2 * DK] = project(KEY + head * DK, 1, DK).astype(BF)
        ref[:, 2 * DK : CHUNK] = project(2 * KEY + head * DV, 2, DV).astype(BF)

    qkv_copies = []
    for d in (3, 1, 2):
        yield None, 1
        chunk(me ^ d, send.at[d - 1])
        copy = to_peer(send.at[d - 1], qkv.at[rows(me * T, T)], ssem.at[1, d], rsem.at[1, d], me ^ d)
        copy.start()
        qkv_copies.append(copy)
    yield None, 1
    chunk(me, qkv.at[rows(me * T, T)])
    yield None, 1
    for j in range(VALUE_WIDTH // TILE):
        og[:, j * TILE : (j + 1) * TILE] = project(2 * KEY + VALUE_WIDTH + j * TILE, 3, TILE)
    loc.start(og, o_og, True)
    yield "delay", DELAYS[1]
    for c in qkv_copies:
        c.wait_recv()
    loc.start(qkv, o_qkv, True)
    tri = lower_triangle(BF)
    causal = lower_triangle(F32)
    state[...] = jnp.zeros_like(state)

    def advance(n, carry):
        at = pl.ds(meta[n_blocks + n] * GROUP, GROUP)
        summed = nn(tri, fg[at, :])
        total = summed[GROUP - 1 : GROUP]
        k = qkv[at, DK : 2 * DK].astype(F32) * live_rows(n, length)
        ku = (k * jnp.exp(total - summed)).astype(BF)
        update = tn(qkv[at, 2 * DK : CHUNK], ku)
        now = state[...]
        st[n] = now.astype(BF)
        state[...] = jnp.exp(total) * now + update
        return carry

    lax.fori_loop(0, n_blocks, advance, 0, unroll=8)
    loc.start(st, o_st, True)
    yield None, 4

    def mix_block(p):
        n = meta[p]
        at = rows(p * GROUP, GROUP)
        summed = nn(tri, fg[at, :])
        middle = summed[GROUP // 2 : GROUP // 2 + 1]
        q = qkv[at, 0:DK].astype(F32) * SCALE
        k = qkv[at, DK : 2 * DK].astype(F32) * live_rows(n, length)
        qe = (q * jnp.exp(summed - middle)).astype(BF)
        ke = (k * jnp.exp(middle - summed)).astype(BF)
        scores = jnp.where(causal > 0, nt(qe, ke), 0.0).astype(BF)
        o = nn(scores, qkv[at, 2 * DK : CHUNK]) + nt((q * jnp.exp(summed)).astype(BF), st[n])
        r = lax.rsqrt(jnp.mean(o * o, axis=-1, keepdims=True) + 1.0)
        yh[at, :] = (o * r).astype(BF)
        rh[at, :] = jnp.broadcast_to(r, (GROUP, DK))

    mix_copies = []
    for d in (3, 1, 2):
        yield None, 2
        peer = me ^ d
        lax.fori_loop(0, per, lambda j, c, peer=peer: (mix_block(peer * per + j), c)[1], 0, unroll=True)
        copy = to_peer(yh.at[rows(peer * T, T)], mix.at[me], ssem.at[2, d], rsem.at[2, d], peer)
        copy.start()
        mix_copies.append(copy)
    yield None, 2
    lax.fori_loop(0, per, lambda j, c: (mix_block(me * per + j), c)[1], 0, unroll=True)
    mix[me] = yh[rows(me * T, T), :]
    loc.start(yh, o_yh, True)
    loc.start(rh, o_rh, True)
    yield "mo", 0
    l_mo = load("mo")
    yield "delay", DELAYS[2]
    for c in mix_copies:
        c.wait_recv()
    loc.start(mix, o_mix, True)
    for hd in range(HEADS):
        cols = slice(hd * DV, (hd + 1) * DV)
        gated[:, cols] = (mix[hd].astype(F32) * silu_parts(og[:, cols])[0]).astype(BF)
    ao[...] = (nn(gated[...], ah[0:VALUE_WIDTH, :]) * mask).astype(BF)
    wait(l_mo)
    for j in range(MODEL_WIDTH // TILE):
        cols = slice(j * TILE, (j + 1) * TILE)
        mid[:, cols] = (
            h[:, cols].astype(F32) + nn(gated[...], mo[:, cols]) + nn(ao[...], au[:, U_O + j * TILE : U_O + (j + 1) * TILE])
        )
    loc.start(ao, o_ao, True)
    loc.start(mid, o_mid, True)
    yield None, 1
    mv = mid[...]
    normed[...] = (mv * inverse_rms(mv)).astype(BF)
    for p in range(2):
        cols = slice(p * ADAPTER_COLUMNS, (p + 1) * ADAPTER_COLUMNS)
        wide = slice((4 + p) * ADAPTER_COLUMNS, (5 + p) * ADAPTER_COLUMNS)
        af[:, cols] = (nn(normed[...], am[:, wide]) * mask).astype(BF)
    loc.start(af, o_af, True)
    yield "fi", 0
    wait(load("fi"))

    def up_tile(i, carry):
        a, b = lanes(i * TILE, TILE), lanes(HIDDEN_UNITS + i * TILE, TILE)
        gate = nn(normed[...], fi[:, a]) + nn(af[:, 0:ADAPTER_COLUMNS], au[:, lanes(U_G + i * TILE, TILE)])
        up = nn(normed[...], fi[:, b]) + nn(af[:, ADAPTER_COLUMNS:], au[:, lanes(U_U + i * TILE, TILE)])
        gu[:, a] = gate.astype(gu.dtype)
        gu[:, b] = up.astype(gu.dtype)
        hidden[:, a] = (silu_parts(gate)[0] * up).astype(BF)
        return carry

    tiles = HIDDEN_UNITS // TILE
    yield None, 3
    lax.fori_loop(0, tiles // 2, up_tile, 0)
    yield None, 3
    lax.fori_loop(tiles // 2, tiles, up_tile, 0)
    loc.start(gu, o_gu, True)
    dn[...] = (nn(hidden[...], ah[VALUE_WIDTH:, :]) * mask).astype(BF)
    loc.start(dn, o_dn, True)
    yield "fo", 0
    wait(load("fo"))
    yield None, 3
    for j in range(MODEL_WIDTH // TILE):
        cols = slice(j * TILE, (j + 1) * TILE)
        y[:, cols] = (
            mid[:, cols] + nn(hidden[...], fo[:, cols]) + nn(dn[...], au[:, U_D + j * TILE : U_D + (j + 1) * TILE])
        ).astype(BF)
    loc.start(y, o_y, True)
    loc.finish()
    for c in low_copies + qkv_copies + mix_copies:
        c.wait_send()


NAMES = ("mi", "mo", "fi", "fo", "f1", "f2", "b", "am", "ah", "au")


def forward_kernel(layer, n_blocks, meta, h_in, *refs):
    n_w, n_out = len(NAMES), 14
    ins, outs = refs[:n_w], refs[n_w : n_w + n_out]
    refs = refs[n_w + n_out :]
    buffers, work = dict(zip(NAMES, refs[:n_w])), refs[n_w:-3]
    lsem, ssem, rsem = refs[-3:]
    loc = Local(lsem)
    first = loc.start(h_in, work[0])
    greet_peers(lax.axis_index("seq"))
    first.wait()
    weights = {name: ref.at[layer] for name, ref in zip(NAMES, ins)}
    for _ in forward_steps(layer, n_blocks, meta, loc, weights, buffers, work, outs, (ssem, rsem)):
        pass


def weight_scratch(weights):
    return [pltpu.VMEM(w.shape[1:], w.dtype) for w in weights]


def saved_shapes(T, L, n_blocks):
    s = lambda shape, dtype=BF: (shape, dtype)
    return [
        s((T, MODEL_WIDTH)),
        s((T, 4 * ADAPTER_COLUMNS)),
        s((T, VALUE_WIDTH), F32),
        s((L, CHUNK)),
        s((HEADS, FGATE_RANK, T)),
        s((n_blocks, DV, DK)),
        s((HEADS, T, DV)),
        s((L, DV)),
        s((L, DK), F32),
        s((T, ADAPTER_COLUMNS)),
        s((T, MODEL_WIDTH), F32),
        s((T, 2 * ADAPTER_COLUMNS)),
        s((T, 2 * HIDDEN_UNITS)),
        s((T, ADAPTER_COLUMNS)),
    ]


def work_scratch(T, L, saved):
    vm = pltpu.VMEM
    return [vm((T, MODEL_WIDTH), BF)] + [vm(*s) for s in saved] + [
        vm((T, MODEL_WIDTH), BF),
        vm((HEADS - 1, T, CHUNK), BF),
        vm((FGATE_RANK, T), BF),
        vm((L, DK), BF),
        vm((DV, DK), F32),
        vm((T, VALUE_WIDTH), BF),
        vm((T, HIDDEN_UNITS), BF),
    ]


def forward(layer, meta, h, weights):
    T = h.shape[0]
    L = T * HEADS
    n_blocks = L // GROUP
    saved = saved_shapes(T, L, n_blocks)
    dma = pltpu.SemaphoreType.DMA
    return pl.pallas_call(
        functools.partial(forward_kernel, layer, n_blocks),
        out_shape=[jax.ShapeDtypeStruct(*s) for s in saved],
        in_specs=[pl.BlockSpec(memory_space=pltpu.SMEM)] + [ANY] * (1 + len(weights)),
        out_specs=[ANY] * len(saved),
        scratch_shapes=weight_scratch(weights)
        + work_scratch(T, L, saved)
        + [dma((1 + len(weights) + len(saved),)), dma((3, HEADS)), dma((3, HEADS))],
        compiler_params=pltpu.CompilerParams(
            collective_id=1 + layer, has_side_effects=True, vmem_limit_bytes=VMEM_LIMIT
        ),
    )(meta, h, *weights)


def backward_kernel(n_blocks, meta, d_in, *refs):
    refs = list(refs)

    def take(n):
        out = refs[:n]
        del refs[:n]
        return out

    n_w = len(NAMES)
    inputs = take(2)
    sources = take(n_w)
    kept = [take(13), take(13)]
    (e_out,) = take(1)
    grad_outs = [take(3), take(3)]
    d, h = take(2)
    mi, mo, fi, fo, f1, f2, bias, am, ah, au = take(n_w)
    ad, og, qkv, gl, st, mix, yh, rh, ao, mid, af, gu, dn = take(13)
    (e,) = take(1)
    grad_sums = [take(3), take(3)]
    (gm, gh, gp, gps, rgm2, rgh2, rgp2, hidden, wide, gad, big, grad, dog, sendm, dmr, logit, fg, gstate, gt, dt, don,
     hidden_gated, sendq, dqkv, dlog, sendl, dlr) = take(27)
    dproj = wide.at[:, pl.ds(MODEL_WIDTH, FROZEN)]
    lsem, ssem2, rsem2, gssem2, grsem2 = take(5)
    me = lax.axis_index("seq")
    loc = Local(lsem)
    buffers = dict(zip(NAMES, (mi, mo, fi, fo, f1, f2, bias, am, ah, au)))
    acts = dict(ad=ad, og=og, qkv=qkv, gl=gl, st=st, mix=mix, yh=yh, rh=rh, ao=ao, mid=mid, af=af, gu=gu, dn=dn)
    on_the_way = [{}, {}]

    def fetch(layer, *names):
        for name in names:
            if name == "d":
                c = loc.start(d_in, d)
            elif name == "h":
                c = loc.start(inputs[layer], h)
            elif name in buffers:
                c = loc.start(sources[NAMES.index(name)].at[layer], buffers[name])
            else:
                c = loc.start(kept[layer][list(acts).index(name)], acts[name])
            on_the_way[layer][name] = c

    fetch(1, "d", "au", "dn", "ah", "fo", "gu")
    greet_peers(me)
    fetch(1, "fi", "am", "mid", "mo", "og", "mix", "f2", "b", "gl", "yh", "rh", "qkv", "st", "ao", "af", "mi", "f1", "ad", "h")
    finish = None
    for layer in (1, 0):
        def arrive(*names, layer=layer):
            for name in names:
                on_the_way[layer][name].wait()

        finish = backward_layer(
            layer, n_blocks, meta, me, loc, arrive, fetch if layer == 1 else None, finish, grad_outs[layer],
            d, h, mi, mo, fi, fo, f1, f2, bias, am, ah, au,
            ad, og, qkv, gl, st, mix, yh, rh, ao, mid, af, gu, dn,
            e, *grad_sums[layer], gm, gh, gp, gps, rgm2.at[layer], rgh2.at[layer], rgp2.at[layer],
            hidden, wide, gad, big, grad, dog, sendm, dmr, logit, fg, gstate, gt, dt, don,
            hidden_gated, sendq, dqkv, dlog, sendl, dlr, dproj,
            ssem2.at[layer], rsem2.at[layer], gssem2.at[layer], grsem2.at[layer],
        )
    loc.start(e, e_out, True)
    finish()
    loc.finish()


def backward_layer(
    layer, n_blocks, meta, me, loc, arrive, fetch, window, grad_outs,
    d, h, mi, mo, fi, fo, f1, f2, bias, am, ah, au,
    ad, og, qkv, gl, st, mix, yh, rh, ao, mid, af, gu, dn,
    e, sgm, sgh, sgp, gm, gh, gp, gps, rgm, rgh, rgp,
    hidden, wide, gad, big, grad, dog, sendm, dmr, logit, fg, gstate, gt, dt, don,
    hidden_gated, sendq, dqkv, dlog, sendl, dlr, dproj,
    ssem, rsem, gssem, grsem,
):
    prefetch = (lambda *names: fetch(0, *names)) if fetch else (lambda *names: None)
    T = h.shape[0]
    per = T // GROUP
    adapter = meta[2 * n_blocks]
    length = meta[2 * n_blocks + 1]
    mask = column_mask(adapter)
    pick = picked(adapter, ADAPTER_COLUMNS)

    def narrow(v):
        return nn(v, pick).astype(BF)

    def outer(u, v):
        return tn(narrow(u), v).astype(BF)

    n_dp, width, padded = gps.shape[1], gp.shape[1] // (HEADS * gps.shape[1]), gps.shape[3]
    quarter, hidden_quarter = MODEL_WIDTH // HEADS, gh.shape[1] // HEADS
    n_late = -(-FROZEN // (HEADS * width))
    mix_rows = 4 * ADAPTER_RANK

    def place(dps):
        for i in dps:
            for q in range(HEADS):
                piece = gp[:, (i * HEADS + q) * width : (i * HEADS + q + 1) * width]
                gps[q, i] = jnp.concatenate([piece, jnp.zeros((ADAPTER_RANK, padded - width), BF)], axis=1)

    def grad_copies(late):
        copies = []
        at = slice(0, mix_rows) if late else slice(mix_rows, 6 * ADAPTER_RANK)
        dps = slice(0, n_late) if late else slice(n_late, n_dp)
        for k in range(1, HEADS):
            peer = me ^ k
            pairs = [
                (gm.at[at, lanes(peer * quarter, quarter)], rgm.at[k - 1, at]),
                (gps.at[peer, dps], rgp.at[k - 1, dps]),
            ]
            if not late:
                pairs.append((gh.at[:, lanes(peer * hidden_quarter, hidden_quarter)], rgh.at[k - 1]))
            for i, (a, b) in enumerate(pairs):
                j = i if late else 2 + i
                copies.append(to_peer(a, b, gssem.at[j, k], grsem.at[j, k], peer))
        return copies

    arrive("au", "dn") if layer == 0 else arrive("d", "au", "dn")
    gdown = (nt(d[...], au[:, U_D : U_D + MODEL_WIDTH]).astype(BF).astype(F32) * mask).astype(BF)
    gdown16 = narrow(gdown)
    if layer == 1:
        gh[:, VALUE_WIDTH + HIDDEN_UNITS :] = jnp.zeros((ADAPTER_RANK, gh.shape[1] - VALUE_WIDTH - HIDDEN_UNITS), BF)
    gp[:, U_D : U_D + MODEL_WIDTH] = outer(dn[...], d[...])
    gad[...] = gdown
    arrive("ah", "fo", "gu")

    def down_tile(i, carry):
        a, b = lanes(i * TILE, TILE), lanes(HIDDEN_UNITS + i * TILE, TILE)
        at = pl.ds(pl.multiple_of(i * TILE, TILE), TILE)
        dh = nt(d[...], fo[at, :]) + nt(gad[...], ah[pl.ds(pl.multiple_of(VALUE_WIDTH + i * TILE, TILE), TILE), :])
        gate, up = gu[:, a].astype(F32), gu[:, b].astype(F32)
        act, sig = silu_parts(gate)
        hidden[:, a] = (act * up).astype(BF)
        wide[:, a] = (dh * up * sig * (1.0 + gate * (1.0 - sig))).astype(BF)
        wide[:, b] = (dh * act).astype(BF)
        return carry

    lax.fori_loop(0, HIDDEN_UNITS // TILE, down_tile, 0)
    prefetch("dn", "fo", "gu")
    gate_cols, up_cols = slice(0, HIDDEN_UNITS), slice(HIDDEN_UNITS, 2 * HIDDEN_UNITS)
    gg = (nt(wide[:, gate_cols], au[:, U_G : U_G + HIDDEN_UNITS]).astype(BF).astype(F32) * mask).astype(BF)
    gu2 = (nt(wide[:, up_cols], au[:, U_U : U_U + HIDDEN_UNITS]).astype(BF).astype(F32) * mask).astype(BF)
    gad2 = jnp.concatenate([gg, gu2], axis=1)
    big[:, 0 : 2 * ADAPTER_COLUMNS] = gad2
    arrive("fi", "am")

    def wide_tile(i, carry):
        at = pl.ds(pl.multiple_of(i * TILE, TILE), TILE)
        grad[:, lanes(i * TILE, TILE)] = nt(wide[...], fi[at, :]) + nt(
            big[:, 0 : 2 * ADAPTER_COLUMNS], am[at, 4 * ADAPTER_COLUMNS :]
        )
        return carry

    lax.fori_loop(0, MODEL_WIDTH // TILE, wide_tile, 0)
    prefetch("fi")
    arrive("mid")
    mv = mid[...]
    grad_mid = d[...].astype(F32) + rms_back(mv, grad[...])
    grad[...] = grad_mid
    attn = grad_mid.astype(BF)
    e[...] = attn
    gout = (nt(attn, au[:, U_O : U_O + MODEL_WIDTH]).astype(BF).astype(F32) * mask).astype(BF)
    gad[...] = gout
    arrive("mo", "og", "mix")

    def gate_back(head, out):
        at = rows(head * DV, DV)
        cols = lanes(head * DV, DV)
        gg_ = nt(e[...], mo[at, :]) + nt(gad[...], ah[at, :])
        o = og[:, cols]
        act, sig = silu_parts(o)
        out[...] = (gg_ * act).astype(BF)
        m = mix[head].astype(F32)
        dog[:, cols] = (gg_ * m * sig * (1.0 + o * (1.0 - sig))).astype(BF)
        hidden_gated[:, cols] = (m * act).astype(BF)

    mix_copies = []
    for k in (3, 1, 2):
        peer = me ^ k
        gate_back(peer, sendm.at[k - 1])
        copy = to_peer(sendm.at[k - 1], dmr.at[rows(me * T, T)], ssem.at[0, k], rsem.at[0, k], peer)
        copy.start()
        mix_copies.append(copy)
    gate_back(me, dmr.at[rows(me * T, T)])

    prefetch("mo", "ah", "og", "mix")
    if window:
        window()
    arrive("af")
    mv = mid[...]
    normed_mid = (mv * inverse_rms(mv)).astype(BF)
    gm[4 * ADAPTER_RANK : 5 * ADAPTER_RANK, :] = outer(big[:, 0:ADAPTER_COLUMNS], normed_mid)
    gm[5 * ADAPTER_RANK : 6 * ADAPTER_RANK, :] = outer(big[:, ADAPTER_COLUMNS : 2 * ADAPTER_COLUMNS], normed_mid)
    gp[:, U_G : U_G + HIDDEN_UNITS] = outer(af[:, 0:ADAPTER_COLUMNS], wide[:, gate_cols])
    gp[:, U_U : U_U + HIDDEN_UNITS] = outer(af[:, ADAPTER_COLUMNS:], wide[:, up_cols])
    arrive("f2", "b", "gl", "yh", "rh", "qkv", "st")
    f2h = f2[:, lanes(me * DK, DK)]
    bh = bias[:, lanes(me * DK, DK)]
    for src in range(HEADS):
        lg = tn(gl[src], f2h) + bh
        logit[src * T : (src + 1) * T, :] = lg
        fg[src * T : (src + 1) * T, :] = (jax.nn.log_sigmoid(lg) / 16.0).astype(BF)
    tri = lower_triangle(BF)
    causal = lower_triangle(F32)
    for c in mix_copies:
        c.wait_recv()
    gstate[...] = jnp.zeros_like(gstate)

    def retreat(i, carry):
        n = n_blocks - 1 - i
        at = pl.ds(meta[n_blocks + n] * GROUP, GROUP)
        here = rows(n * GROUP, GROUP)
        dm = dmr[at, :].astype(F32)
        yv = yh[at, :].astype(F32)
        r = rh[at, 0:1]
        do = (r * (dm - yv * jnp.mean(dm * yv, axis=-1, keepdims=True))).astype(BF)
        don[here, :] = do
        summed = nn(tri, fg[at, :])
        total = jnp.exp(summed[GROUP - 1 : GROUP])
        qs = (qkv[at, 0:DK].astype(F32) * SCALE * jnp.exp(summed)).astype(BF)
        now = gstate[...]
        gt[n] = now.astype(BF)
        decayed = total * now
        dt[n] = jnp.sum(decayed * st[n].astype(F32), axis=0, keepdims=True)
        gstate[...] = decayed + tn(do, qs)
        return carry

    lax.fori_loop(0, n_blocks, retreat, 0, unroll=8)

    def back_block(p, out, j):
        n = meta[p]
        at = rows(p * GROUP, GROUP)
        here = pl.ds(n * GROUP, GROUP)
        to = rows(j * GROUP, GROUP)
        live = live_rows(n, length)
        summed = nn(tri, fg[at, :])
        middle = summed[GROUP // 2 : GROUP // 2 + 1]
        total = summed[GROUP - 1 : GROUP]
        e1, e2 = jnp.exp(summed - middle), jnp.exp(middle - summed)
        es, eu = jnp.exp(summed), jnp.exp(total - summed)
        q = qkv[at, 0:DK].astype(F32) * SCALE
        k = qkv[at, DK : 2 * DK].astype(F32) * live
        v = qkv[at, 2 * DK : CHUNK]
        do, state_t, grad_t = don[here, :], st[n], gt[n]
        qe, ke, qs, ku = q * e1, k * e2, q * es, k * eu
        qeb, keb = qe.astype(BF), ke.astype(BF)
        scores = jnp.where(causal > 0, nt(qeb, keb), 0.0).astype(BF)
        dscores = jnp.where(causal > 0, nt(do, v), 0.0).astype(BF)
        dv = tn(scores, do) + nt(ku.astype(BF), grad_t)
        dqs = nn(do, state_t)
        dku = nn(v, grad_t)
        dqe = nn(dscores, keb)
        dke = tn(dscores, qeb)
        out[to, 0:DK] = (SCALE * (dqe * e1 + dqs * es)).astype(BF)
        out[to, DK : 2 * DK] = (live * (dke * e2 + dku * eu)).astype(BF)
        out[to, 2 * DK : CHUNK] = dv.astype(BF)
        kk = dku * ku
        dsum = dqe * qe + dqs * qs - dke * ke - kk
        dtotal = dt[n] + jnp.sum(kk, axis=0, keepdims=True)
        high = dsum.astype(BF)
        lowp = (dsum - high.astype(F32)).astype(BF)
        df = tn(tri, high) + tn(tri, lowp) + dtotal
        df = df.astype(BF).astype(F32)
        dlog[to, :] = (df * lax.logistic(-logit[at, :]) / 16.0).astype(BF)

    q_copies = []

    def back_rows(dest, out, low_out):
        lax.fori_loop(0, per, lambda j, c: (back_block(dest * per + j, out, j), c)[1], 0, unroll=True)
        low_out[...] = nt(f2h, dlog[...]).astype(BF)

    for k in (3, 1, 2):
        peer = me ^ k
        back_rows(peer, sendq.at[k - 1], sendl.at[k - 1])
        copies = (
            to_peer(sendq.at[k - 1], dqkv.at[me], ssem.at[1, k], rsem.at[1, k], peer),
            to_peer(sendl.at[k - 1], dlr.at[me], ssem.at[2, k], rsem.at[2, k], peer),
        )
        for copy in copies:
            copy.start()
        q_copies += copies
    back_rows(me, dqkv.at[me], dlr.at[me])

    arrive("ao")
    gh[:, VALUE_WIDTH : VALUE_WIDTH + HIDDEN_UNITS] = tn(gdown16, hidden[...]).astype(BF)
    gp[:, U_O : U_O + MODEL_WIDTH] = outer(ao[...], e[...])
    gh[:, 0:VALUE_WIDTH] = outer(gad[...], hidden_gated[...])
    place(range(n_late, n_dp))
    grads = grad_copies(False)
    for c in grads:
        c.start()
    prefetch("mid", "af", "ao", "qkv", "gl", "st", "yh", "rh", "f2", "b")

    arrive("mi", "f1", "ad", "h")
    hv = h[...].astype(F32)
    hr = inverse_rms(hv)
    big[...] = (hv * hr).astype(BF)
    for c in q_copies:
        c.wait_recv()
    for hd in range(HEADS):
        dproj[:, hd * DK : (hd + 1) * DK] = dqkv[hd, :, 0:DK]
        dproj[:, KEY + hd * DK : KEY + (hd + 1) * DK] = dqkv[hd, :, DK : 2 * DK]
        dproj[:, 2 * KEY + hd * DV : 2 * KEY + (hd + 1) * DV] = dqkv[hd, :, 2 * DK : CHUNK]
    dproj[:, 2 * KEY + VALUE_WIDTH :] = dog[...]
    dlow = dlr[0].astype(F32)
    for hd in range(1, HEADS):
        dlow += dlr[hd].astype(F32)
    dlowb = dlow.astype(BF)
    spans = ((0, KEY), (KEY, KEY), (2 * KEY, VALUE_WIDTH), (2 * KEY + VALUE_WIDTH, VALUE_WIDTH))
    for p, (start, span) in enumerate(spans):
        block = slice(p * ADAPTER_COLUMNS, (p + 1) * ADAPTER_COLUMNS)
        piece = dproj[:, start : start + span]
        ga = (nt(piece, au[:, start : start + span]).astype(BF).astype(F32) * mask).astype(BF)
        wide[:, block] = ga
        gm[p * ADAPTER_RANK : (p + 1) * ADAPTER_RANK, :] = outer(ga, big[...])
        gp[:, start : start + span] = outer(ad[:, block], piece)
    place(range(n_late))
    late_grads = grad_copies(True)
    for c in late_grads:
        c.start()
    z_w = f1.shape[2]
    tiles = f1.shape[0]
    back = []
    for j in range(tiles):
        at = slice(j * z_w, (j + 1) * z_w)
        back.append(
            nt(dproj[...], mi[at, :]) + nt(wide[:, 0 : 4 * ADAPTER_COLUMNS], am[at, 0 : 4 * ADAPTER_COLUMNS]) + tn(dlowb, f1[j])
        )
    dn_ = jnp.concatenate(back, axis=1)
    n = hv * hr
    e[...] = (grad[...] + hr * (dn_ - n * jnp.mean(dn_ * n, axis=-1, keepdims=True))).astype(BF)
    if layer == 1:
        d[...] = e[...]
    prefetch("au", "am", "mi", "f1", "ad", "h")
    grads += late_grads
    for c in mix_copies + q_copies:
        c.wait_send()

    def finish():
        for c in grads:
            c.wait_recv()

        def summed_over_seq(own, got):
            total = own.astype(F32)
            for k in range(HEADS - 1):
                total += got[k].astype(F32)
            return total.astype(BF)

        sgm[...] = summed_over_seq(gm[:, lanes(me * quarter, quarter)], rgm)
        sgh[...] = summed_over_seq(gh[:, lanes(me * hidden_quarter, hidden_quarter)], rgh)
        spot = lax.broadcasted_iota(jnp.int32, (ADAPTER_RANK, padded), 1)
        for i in range(n_dp):
            total = gps[me, i].astype(F32)
            for k in range(HEADS - 1):
                total += rgp[k, i].astype(F32)
            sgp[i] = jnp.where(spot == width, adapter.astype(F32), total).astype(BF)
        for c in grads:
            c.wait_send()
        for a, b in zip((sgm, sgh, sgp), grad_outs):
            loc.start(a, b, True)

    return finish


def backward(meta, d, x, h1, weights, early, late, n_dp):
    T = x.shape[0]
    L = T * HEADS
    n_blocks = L // GROUP
    raised = U_D + MODEL_WIDTH
    padded = (raised // (n_dp * HEADS) // 128 + 1) * 128
    quarter = MODEL_WIDTH // HEADS
    hidden_quarter = -(-(VALUE_WIDTH + HIDDEN_UNITS) // (HEADS * 128)) * 128
    outs = [
        ((T, MODEL_WIDTH), BF),
        ((6 * ADAPTER_RANK, quarter), BF),
        ((ADAPTER_RANK, hidden_quarter), BF),
        ((n_dp, ADAPTER_RANK, padded), BF),
    ]
    vm = pltpu.VMEM
    dma = pltpu.SemaphoreType.DMA
    return pl.pallas_call(
        functools.partial(backward_kernel, n_blocks),
        out_shape=[jax.ShapeDtypeStruct(*s) for s in outs[:1] + 2 * outs[1:]],
        in_specs=[pl.BlockSpec(memory_space=pltpu.SMEM)] + [ANY] * (3 + len(weights) + 2 * len(early)),
        out_specs=[ANY] * (2 * len(outs) - 1),
        scratch_shapes=[vm(d.shape, d.dtype), vm(x.shape, x.dtype)]
        + weight_scratch(weights)
        + [vm(s.shape, s.dtype) for s in early]
        + [vm(*s) for s in outs[:1] + 2 * outs[1:]]
        + [
            vm((6 * ADAPTER_RANK, MODEL_WIDTH), BF),
            vm((ADAPTER_RANK, HEADS * hidden_quarter), BF),
            vm((ADAPTER_RANK, raised), BF),
            vm((HEADS, n_dp, ADAPTER_RANK, padded), BF),
            vm((2, HEADS - 1, 6 * ADAPTER_RANK, quarter), BF),
            vm((2, HEADS - 1, ADAPTER_RANK, hidden_quarter), BF),
            vm((2, HEADS - 1, n_dp, ADAPTER_RANK, padded), BF),
            vm((T, HIDDEN_UNITS), BF),
            vm((T, 2 * HIDDEN_UNITS), BF),
            vm((T, ADAPTER_COLUMNS), BF),
            vm((T, MODEL_WIDTH), BF),
            vm((T, MODEL_WIDTH), F32),
            vm((T, VALUE_WIDTH), BF),
            vm((HEADS - 1, T, DV), BF),
            vm((L, DV), BF),
            vm((L, DK), F32),
            vm((L, DK), BF),
            vm((DV, DK), F32),
            vm((n_blocks, DV, DK), BF),
            vm((n_blocks, 1, DK), F32),
            vm((L, DV), BF),
            vm((T, VALUE_WIDTH), BF),
            vm((HEADS - 1, T, CHUNK), BF),
            vm((HEADS, T, CHUNK), BF),
            vm((T, DK), BF),
            vm((HEADS - 1, FGATE_RANK, T), BF),
            vm((HEADS, FGATE_RANK, T), BF),
            dma((2 * (2 + len(weights) + len(early) + len(outs)),)),
            dma((2, 3, HEADS)),
            dma((2, 3, HEADS)),
            dma((2, 5, HEADS)),
            dma((2, 5, HEADS)),
        ],
        compiler_params=pltpu.CompilerParams(
            collective_id=3, has_side_effects=True, vmem_limit_bytes=VMEM_LIMIT
        ),
        cost_estimate=pl.CostEstimate(flops=4 * T * 16_000_000, bytes_accessed=90 << 20, transcendentals=T * 16384),
    )(meta, d, x, h1, *weights, *early, *late)


UNITS = [(layer, w) for layer in range(2) for w in range(4)]


def model_kernel(n_blocks, meta, *refs):
    n_w, n_small, n_saved, n_z = 4, 5, 14, 4
    refs = list(refs)

    def take(n):
        out = refs[:n]
        del refs[:n]
        return out

    shards = take(n_w)
    f1_ref, ends_ref = take(2)
    small = take(n_small)
    outs = take(n_w)
    (f1_out,) = take(1)
    (x_out, c_out) = take(2)
    small_out = take(n_small)
    saved = [take(n_saved), take(n_saved)]
    held = take(n_w)
    held_f1 = take(1)[0]
    held_small = take(n_small)
    work = take(1 + n_saved + 7)
    qkv2, gl2, mix2, held_ends = take(4)
    (ins, zs, zr, ts, tr, xs, xr, ys, yr, fxs, fxr, fys, fyr, cs, cr, own, ms, mr, es, er, f1s, f1r, f1c, lsem, ssem, rsem) = take(26)
    core, z, s = lax.axis_index("section"), lax.axis_index("dp"), lax.axis_index("seq")
    other = 1 - core

    def remote(src, dst, send_sem, recv_sem, **where):
        return pltpu.make_async_remote_copy(
            src_ref=src, dst_ref=dst, send_sem=send_sem, recv_sem=recv_sem, device_id=where, device_id_type=MESH
        )

    def height(w):
        return shards[w].shape[1]

    def staged(w):
        return held[w].at[pl.ds(pl.multiple_of(z * height(w), 16), height(w))]

    fetch = [pltpu.make_async_copy(shards[w].at[0], staged(w), ins.at[w]) for w in range(n_w)]
    fetch += [pltpu.make_async_copy(a.at[0], b, ins.at[n_w + i]) for i, (a, b) in enumerate(zip(small, held_small))]
    fetch.append(pltpu.make_async_copy(ends_ref.at[0, :, 0], held_ends, ins.at[n_w + n_small]))
    fetch.append(pltpu.make_async_copy(f1_ref, held_f1.at[z], ins.at[n_w + n_small + 1]))
    for f in fetch:
        f.start()

    barrier = pltpu.get_barrier_semaphore()
    greeted = [dict(section=other)] + [dict(seq=s ^ k) for k in range(1, HEADS)]
    greeted += [dict(dp=lax.rem(z + gap, n_z)) for gap in range(1, n_z)]
    for where in greeted:
        pl.semaphore_signal(barrier, inc=1, device_id=where, device_id_type=MESH)
    pl.semaphore_wait(barrier, len(greeted))

    def part(u, j, start, size, strip=False):
        layer, w = UNITS[u]
        cols = shards[w].shape[2] // 2
        at, wide = (cols - STRIPS[w], STRIPS[w]) if strip else (0, cols - STRIPS[w])
        return outs[w].at[layer, pl.ds(pl.multiple_of(j * height(w) + start, 16), size), lanes(core * cols + at, wide)]

    def piece(u, j, q):
        r = height(UNITS[u][1])
        return part(u, j, q * (r // 4), r // 4)

    def half(u, j, q, low):
        r = height(UNITS[u][1])
        cut = (r // 8 + 15) // 16 * 16
        start, size = (0, cut) if low else (cut, r // 4 - cut)
        return part(u, j, q * (r // 4) + start, size)

    def block(u, j):
        layer, w = UNITS[u]
        cols = shards[w].shape[2] // 2
        return outs[w].at[layer, pl.ds(pl.multiple_of(j * height(w), 16), height(w)), lanes(core * cols, cols)]

    def whole_block(layer, w):
        return outs[w].at[layer, pl.ds(pl.multiple_of(z * height(w), 16), height(w))]

    def step(d):
        return 1 if d == 0 else -1

    def can_send(d, t):
        has_next = (z < n_z - 1) if d == 0 else (z > 0)
        first = z - step(d) * (t - 1)
        return jnp.logical_and(has_next, jnp.logical_and(first >= 0, first < n_z))

    def gets(d, t):
        first = z - step(d) * t
        return jnp.logical_and(first >= 0, first < n_z)

    def origin(d, t):
        return z - step(d) * t

    def z_copy(u, d, t):
        ref = piece(u, z - step(d) * (t - 1), s)
        return remote(ref, ref, zs.at[u, d, t - 1], zr.at[u, d, t - 1], dp=z + step(d))

    def t_copy(u, d, t):
        ref = part(u, z - step(d) * (t - 1), 0, height(UNITS[u][1]), True)
        return remote(ref, ref, ts.at[u, d, t - 1], tr.at[u, d, t - 1], dp=z + step(d))

    def x_copy(u, d, t):
        ref = piece(u, origin(d, t), s)
        return remote(ref, ref, xs.at[u, d, t - 1], xr.at[u, d, t - 1], seq=s ^ 1)

    def y_copy(u, d, t):
        ref = piece(u, origin(d, t), s)
        return remote(ref, ref, ys.at[u, d, t - 1], yr.at[u, d, t - 1], seq=s ^ 2)

    def fx_copy(u, d, t):
        ref = half(u, origin(d, t), s ^ 2, False)
        return remote(ref, ref, fxs.at[u, d, t - 1], fxr.at[u, d, t - 1], seq=s ^ 1)

    def fy_copy(u, d, t):
        ref = half(u, origin(d, t), s ^ 1, True)
        return remote(ref, ref, fys.at[u, d, t - 1], fyr.at[u, d, t - 1], seq=s ^ 2)

    def c_copy(u, d, t):
        ref = block(u, origin(d, t))
        return remote(ref, ref, cs.at[u, d, t - 1], cr.at[u, d, t - 1], section=other)

    def own_copy(w):
        return pltpu.make_async_copy(staged(w), whole_block(core, w), own.at[w])

    def own_cross(w):
        return remote(staged(w), whole_block(core, w), ms.at[n_small + w], mr.at[n_small + w], section=other)

    def start_own(u):
        layer, w = UNITS[u]

        if layer == 0:
            own_copy(w).wait()

        @pl.when(core != layer)
        def _():
            own_cross(w).wait_recv()

        for d in range(2):
            @pl.when(can_send(d, 1))
            def _():
                z_copy(u, d, 1).start()
                if STRIPS[w]:
                    t_copy(u, d, 1).start()

    def take_z(u, t):
        for d in range(2):
            @pl.when(gets(d, t))
            def _():
                z_copy(u, d, t).wait_recv()
            if t < n_z - 1:
                @pl.when(can_send(d, t + 1))
                def _():
                    z_copy(u, d, t + 1).start()
            @pl.when(gets(d, t))
            def _():
                x_copy(u, d, t).start()
                y_copy(u, d, t).start()
                if STRIPS[UNITS[u][1]]:
                    t_copy(u, d, t).wait_recv()
            if t < n_z - 1 and STRIPS[UNITS[u][1]]:
                @pl.when(can_send(d, t + 1))
                def _():
                    t_copy(u, d, t + 1).start()

    def take_xy(u, t):
        for d in range(2):
            @pl.when(gets(d, t))
            def _():
                x_copy(u, d, t).wait_recv()
                fy_copy(u, d, t).start()
                y_copy(u, d, t).wait_recv()
                fx_copy(u, d, t).start()

    def take_diagonal(u, t):
        for d in range(2):
            @pl.when(gets(d, t))
            def _():
                fy_copy(u, d, t).wait_recv()
                fx_copy(u, d, t).wait_recv()
                c_copy(u, d, t).start()

    def take_core(u):
        for d in range(2):
            for t in range(1, n_z):
                @pl.when(gets(d, t))
                def _():
                    c_copy(u, d, t).wait_recv()

    def f1_copy(gap):
        return remote(held_f1.at[z], f1_out.at[core, z], f1s.at[gap], f1r.at[gap], dp=lax.rem(z + gap, n_z))

    def launch(w):
        fetch[w].wait()
        own_copy(w).start()
        own_cross(w).start()

    launch(0)
    fetch[-1].wait()
    f1_sends = [f1_copy(gap) for gap in range(1, n_z)]
    for c in f1_sends:
        c.start()
    f1_own = pltpu.make_async_copy(held_f1.at[z], f1_out.at[core, z], own.at[n_w])
    f1_own.start()
    ends_to_x = remote(held_ends.at[1], x_out, es, er, section=other)
    ends_to_c = remote(held_ends.at[0], c_out, es, er, section=other)
    ends_x = pltpu.make_async_copy(held_ends.at[0], x_out, own.at[n_w + 1])
    ends_c = pltpu.make_async_copy(held_ends.at[1], c_out, own.at[n_w + 1])
    f1_cross = remote(f1_out.at[core], f1_out.at[core], f1c.at[0], f1c.at[1], section=other)
    start_own(0)
    launch(1)
    smalls = []

    def launch_rest():
        fetch[-2].wait()

        @pl.when(core == 0)
        def _():
            ends_to_x.start()
            ends_x.start()

        @pl.when(core == 1)
        def _():
            ends_to_c.start()
            ends_c.start()

        for i, (a, b) in enumerate(zip(held_small, small_out)):
            fetch[n_w + i].wait()
            mine = pltpu.make_async_copy(a, b.at[core], own.at[n_w + 2 + i])
            theirs = remote(a, b.at[core], ms.at[i], mr.at[i], section=other)
            mine.start()
            theirs.start()
            smalls.append((mine, theirs))
        for w in range(2, n_w):
            launch(w)
        f1_own.wait()
        for c in f1_sends:
            c.wait_recv()
        f1_cross.start()

    def settle_small():
        for mine, theirs in smalls:
            mine.wait()
            theirs.wait()
        for c in f1_sends:
            c.wait_send()
        f1_cross.wait()
        ends_x.wait()
        ends_to_x.wait()

    items = [(u, t) for u in range(len(UNITS)) for t in range(1, n_z)]
    ready, clock = [], 8.0
    for u, t in items:
        r, c = shards[UNITS[u][1]].shape[1:]
        clock += r // 4 * (c - 2 * STRIPS[UNITS[u][1]]) * 3 / LINK_BYTES_PER_US
        ready.append(clock)

    def gather_step(i):
        if i == 1:
            launch_rest()
        if i < len(items):
            u, t = items[i]
            if t == 1 and u + 1 < len(UNITS):
                start_own(u + 1)
            take_z(u, t)
        if 0 <= i - SKEW[0] < len(items):
            take_xy(*items[i - SKEW[0]])
        if 0 <= i - SKEW[1] < len(items):
            take_diagonal(*items[i - SKEW[1]])

    loc = Local(lsem)
    n_steps = len(items) + SKEW[1]
    works = [list(work), list(work)]
    for at, ref in ((4, qkv2), (5, gl2), (7, mix2)):
        works[1][at] = ref

    def both_layers():
        for layer in range(2):
            sources = dict(zip(NAMES[:4], outs))
            sources["f1"] = f1_out
            sources.update(zip(NAMES[5:], small_out))
            sources = {name: ref.at[layer] for name, ref in sources.items()}
            buffers = dict(zip(NAMES, held + [held_f1] + held_small))
            for what, us in forward_steps(
                layer, n_blocks, meta, loc, sources, buffers, works[layer], saved[layer], (ssem.at[layer], rsem.at[layer])
            ):
                yield layer, what, us
            if layer == 0:
                work[0][...] = work[1][...]

    steps, done, now, crossed, until = both_layers(), 0, 8.0, set(), None
    pending = next(steps)
    while pending is not None or done < n_steps:
        due = ready[min(max(done - 2, 0), len(ready) - 1)]
        blocked = False
        if pending is not None and pending[1] in NAMES[:4]:
            u = UNITS.index((pending[0], NAMES.index(pending[1])))
            blocked = done < min(3 * u + 3 + SKEW[1], n_steps)
            if not blocked:
                take_core(u)
                crossed.add(u)
                if pending[0] == 0:
                    own_cross(UNITS[u][1]).wait_send()
        elif pending is not None and pending[:2] == (0, "small"):
            blocked = done < 3
            if not blocked:
                settle_small()
                loc.start(x_out, work[0]).wait()
        elif pending is not None and pending[1] == "delay":
            until = now + pending[2] if until is None else until
            blocked = now < until and due < until
        if done < n_steps and (pending is None or blocked or due <= now):
            now = max(now, due)
            gather_step(done)
            done += 1
            continue
        now = now + pending[2] if until is None else max(now, until)
        until = None
        pending = next(steps, None)
    for u in range(len(UNITS)):
        if u not in crossed:
            take_core(u)
        for d in range(2):
            for t in range(1, n_z):
                @pl.when(can_send(d, t))
                def _():
                    z_copy(u, d, t).wait_send()
                    if STRIPS[UNITS[u][1]]:
                        t_copy(u, d, t).wait_send()
                @pl.when(gets(d, t))
                def _():
                    x_copy(u, d, t).wait_send()
                    y_copy(u, d, t).wait_send()
                    fx_copy(u, d, t).wait_send()
                    fy_copy(u, d, t).wait_send()
                    c_copy(u, d, t).wait_send()


def forward_model(meta, shards, f1t, ends, small):
    shape, dma, vm = jax.ShapeDtypeStruct, pltpu.SemaphoreType.DMA, pltpu.VMEM
    T = ends.shape[3]
    L = T * HEADS
    n_blocks = L // GROUP
    saved = saved_shapes(T, L, n_blocks)
    n_w, n_small, n_u = len(shards), len(small), len(UNITS)
    outs = [shape((2, 4 * w.shape[1], w.shape[2]), w.dtype) for w in shards]
    outs.append(shape((2, 4) + f1t.shape, f1t.dtype))
    outs += [shape(ends.shape[3:], ends.dtype)] * 2
    outs += [shape((2,) + a.shape[1:], a.dtype) for a in small]
    outs += [shape(*s) for s in saved] * 2
    full = [vm((4 * w.shape[1], w.shape[2]), w.dtype) for w in shards]
    out = pl.pallas_call(
        functools.partial(model_kernel, n_blocks),
        out_shape=outs,
        in_specs=[pl.BlockSpec(memory_space=pltpu.SMEM)] + [ANY] * (n_w + 2 + n_small),
        out_specs=[ANY] * len(outs),
        scratch_shapes=full
        + [vm((4,) + f1t.shape, f1t.dtype)]
        + [vm(a.shape[1:], a.dtype) for a in small]
        + work_scratch(T, L, saved)
        + [vm((L, CHUNK), BF), vm((HEADS, FGATE_RANK, T), BF), vm((HEADS, T, DV), BF), vm((2,) + ends.shape[3:], BF)]
        + [dma((n_w + n_small + 2,))]
        + [dma((n_u, 2, 3)) for _ in range(14)]
        + [dma((n_w + n_small + 2,)), dma((n_small + n_w,)), dma((n_small + n_w,)), dma, dma, dma((4,)), dma((4,)), dma((2,))]
        + [dma((1 + 2 * (len(NAMES) + len(saved)),)), dma((2, 3, HEADS)), dma((2, 3, HEADS))],
        compiler_params=pltpu.CompilerParams(collective_id=0, has_side_effects=True, vmem_limit_bytes=VMEM_LIMIT),
    )(meta, *shards, f1t, ends, *small)
    weights = list(out[:5]) + list(out[7:12])
    return weights, out[5], out[6], out[12 : 12 + len(saved)], out[12 + len(saved) :]


def swap_sections(v):
    return lax.ppermute(v, "section", [(0, 1), (1, 0)])


def plain_gather(shards, f1t, ends, small):
    first = lax.axis_index("section") == 0
    both = lambda a: lax.all_gather(a, "section", axis=0)
    outs = [both(lax.all_gather(w[0], "dp", axis=0, tiled=True)) for w in shards]
    low = lax.all_gather(f1t, "dp", axis=1, tiled=True)
    outs.append(both(jnp.stack(jnp.split(low, 4, axis=1))))
    sent = swap_sections(jnp.where(first, ends[0, 1, 0], ends[0, 0, 0]))
    outs.append(jnp.where(first, ends[0, 0, 0], sent))
    outs.append(jnp.where(first, sent, ends[0, 1, 0]))
    return outs + [both(a[0]) for a in small]


def spread(parts, chosen):
    hot = (chosen[:, None] == jnp.arange(ADAPTERS, dtype=jnp.int32)[None, :]).astype(F32)
    return sum(parts[n][:, None] * hot[n][None, :, None, None] for n in range(parts.shape[0]))


def reduce_kernel(
    gm0, gh0, gp0, gm1, gh1, gp1, entry, last_y, m_out, h_out, u_out, ends_out,
    vm_, vh, vp, rm, rh, rp, am, ah, em, eh, ends, ls, ss, rs, es, er, xl, xo, xs, xr,
):
    core, dp, me = lax.axis_index("section"), lax.axis_index("dp"), lax.axis_index("seq")
    n_dp = vp.shape[1]
    width = u_out.shape[1]
    loads = [
        pltpu.make_async_copy(a, b.at[l], ls.at[l, i])
        for l, three in enumerate(((gm0, gh0, gp0), (gm1, gh1, gp1)))
        for i, (a, b) in enumerate(zip(three, (vm_, vh, vp)))
    ]
    for c in loads:
        c.start()
    ends_in = [pltpu.make_async_copy(a, ends.at[i], xl.at[i]) for i, a in enumerate((entry, last_y))]
    for c in ends_in:
        c.start()
    barrier = pltpu.get_barrier_semaphore()
    places = [dict(section=1 - core)] + [dict(seq=me ^ k) for k in range(1, HEADS)]
    for gap in range(1, n_dp):
        to = lax.rem(dp + gap, n_dp)
        places += [dict(dp=to), dict(section=1 - core, dp=to)]
    for where in places:
        pl.semaphore_signal(barrier, inc=1, device_id=where, device_id_type=MESH)
    for c in loads:
        c.wait()
    pl.semaphore_wait(barrier, len(places))
    slot = dp * 2 + core
    size = 6 * ADAPTER_COLUMNS // n_dp

    def first_projection(i):
        return i * size // ADAPTER_COLUMNS

    def parts(layer, to):
        at = pl.ds(pl.multiple_of(first_projection(to) * ADAPTER_RANK, ADAPTER_RANK), 2 * ADAPTER_RANK)
        return ((vm_.at[layer, at], rm.at[slot]), (vh.at[layer], rh.at[slot]), (vp.at[layer, to], rp.at[slot]))

    copies = []
    for gap in range(n_dp - 1, -1, -1):
        to = lax.rem(dp + gap, n_dp)
        for crossing in (0, 1):
            if crossing == 0 and gap == 0:
                continue
            section = 1 - core if crossing else core
            for i, (a, b) in enumerate(parts(section, to)):
                c = pltpu.make_async_remote_copy(
                    src_ref=a, dst_ref=b, send_sem=ss.at[crossing, gap, i], recv_sem=rs.at[crossing, gap, i],
                    device_id=dict(section=section, dp=to), device_id_type=MESH,
                )
                c.start()
                copies.append(c)
    for c in ends_in:
        c.wait()
    ends_own = pltpu.make_async_copy(ends.at[core], ends_out.at[core], xo)
    ends_cross = pltpu.make_async_remote_copy(
        src_ref=ends.at[1 - core], dst_ref=ends_out.at[core], send_sem=xs, recv_sem=xr,
        device_id=dict(section=1 - core), device_id_type=MESH,
    )
    ends_own.start()
    ends_cross.start()
    at = pl.ds(pl.multiple_of(first_projection(dp) * ADAPTER_RANK, ADAPTER_RANK), 2 * ADAPTER_RANK)
    rm[slot] = vm_[core, at]
    rh[slot] = vh[core]
    rp[slot] = vp[core, dp]
    for c in copies:
        c.wait_recv()
    n = rm.shape[0]
    chosen = [rp[j, :, width : width + 1].astype(F32) for j in range(n)]
    for a in range(ADAPTERS):
        hot = [(c == float(a)).astype(F32) for c in chosen]
        at = slice(a * ADAPTER_RANK, (a + 1) * ADAPTER_RANK)

        def total(values):
            out = hot[0] * values(0).astype(F32)
            for j in range(1, n):
                out += hot[j] * values(j).astype(F32)
            return out

        for p in range(2):
            am[p * ADAPTER_COLUMNS + a * ADAPTER_RANK : p * ADAPTER_COLUMNS + (a + 1) * ADAPTER_RANK, :] = total(
                lambda j, p=p: rm[j, p * ADAPTER_RANK : (p + 1) * ADAPTER_RANK]
            )
        ah[at, :] = total(lambda j: rh[j])
        u_out[at, :] = total(lambda j: rp[j])[:, 0:width]
    own_m, own_h = size // HEADS, ADAPTER_COLUMNS // n_dp // HEADS
    base = dp * size - first_projection(dp) * ADAPTER_COLUMNS

    def m_rows(q):
        return am.at[pl.ds(pl.multiple_of(base + q * own_m, 16), own_m)]

    def h_rows(q):
        return ah.at[pl.ds(pl.multiple_of(dp * HEADS * own_h + q * own_h, 8), own_h)]

    last = []
    for k in range(1, HEADS):
        for i, (a, b) in enumerate(((m_rows(me ^ k), em.at[me]), (h_rows(me ^ k), eh.at[me]))):
            c = to_peer(a, b, es.at[i, k], er.at[i, k], me ^ k)
            c.start()
            last.append(c)
    em[me] = m_rows(me)[...]
    eh[me] = h_rows(me)[...]
    for c in last:
        c.wait_recv()
    for q in range(HEADS):
        m_out[:, q * em.shape[2] : (q + 1) * em.shape[2]] = em[q]
        h_out[:, q * eh.shape[2] : (q + 1) * eh.shape[2]] = eh[q]
    for c in copies + last:
        c.wait_send()
    ends_own.wait()
    ends_cross.wait()


def reduce_gradients(early, late, entry, y, n_dp):
    gm, gh, gp = early
    n = 2 * n_dp
    width = (U_D + MODEL_WIDTH) // (n_dp * HEADS)
    own_m, own_h = 6 * ADAPTER_COLUMNS // (n_dp * HEADS), ADAPTER_COLUMNS // (n_dp * HEADS)
    vm, dma, VM = pltpu.VMEM, pltpu.SemaphoreType.DMA, pl.BlockSpec(memory_space=pltpu.VMEM)
    shape = jax.ShapeDtypeStruct
    model, hidden, up, ends = pl.pallas_call(
        reduce_kernel,
        out_shape=[
            shape((own_m, MODEL_WIDTH), F32),
            shape((own_h, HEADS * gh.shape[1]), F32),
            shape((ADAPTER_COLUMNS, width), F32),
            shape((2,) + y.shape, y.dtype),
        ],
        in_specs=[ANY] * 8,
        out_specs=[VM] * 3 + [ANY],
        scratch_shapes=[
            vm((2,) + gm.shape, BF),
            vm((2,) + gh.shape, BF),
            vm((2,) + gp.shape, BF),
            vm((n, 2 * ADAPTER_RANK, gm.shape[1]), BF),
            vm((n,) + gh.shape, BF),
            vm((n,) + gp.shape[1:], BF),
            vm((2 * ADAPTER_COLUMNS, gm.shape[1]), F32),
            vm((ADAPTER_COLUMNS, gh.shape[1]), F32),
            vm((HEADS, own_m, gm.shape[1]), F32),
            vm((HEADS, own_h, gh.shape[1]), F32),
            vm((2,) + y.shape, y.dtype),
            dma((2, 3)),
            dma((2, n_dp, 3)),
            dma((2, n_dp, 3)),
            dma((2, HEADS)),
            dma((2, HEADS)),
            dma((2,)),
            dma,
            dma,
            dma,
        ],
        compiler_params=pltpu.CompilerParams(collective_id=5, has_side_effects=True, vmem_limit_bytes=VMEM_LIMIT),
    )(*early, *late, entry, y)
    return model.T, hidden[:, : VALUE_WIDTH + HIDDEN_UNITS].T, up, ends


def plain_reduce(early, late, n_dp):
    first = lax.axis_index("section") == 0
    dp = lax.axis_index("dp")
    kept = [jnp.where(first, a, b) for a, b in zip(early, late)]
    got = [swap_sections(jnp.where(first, b, a)) for a, b in zip(early, late)]
    gm, gh, gp = [jnp.stack(pair) for pair in zip(kept, got)]
    width = (U_D + MODEL_WIDTH) // (n_dp * HEADS)
    gm = lax.all_gather(gm, "dp", axis=0)
    gh = lax.all_gather(gh, "dp", axis=0)
    gp = lax.all_to_all(jnp.swapaxes(gp, 0, 1), "dp", split_axis=0, concat_axis=0, tiled=True)
    gp = gp.reshape(2 * n_dp, 1, ADAPTER_RANK, -1)
    n = gp.shape[0]
    chosen = gp[:, 0, 0, width].astype(jnp.int32)
    gm = spread(gm.reshape(n, 6, ADAPTER_RANK, -1).astype(F32), chosen).reshape(6 * ADAPTER_COLUMNS, -1)
    gh = spread(gh.reshape(n, 1, ADAPTER_RANK, -1).astype(F32), chosen).reshape(ADAPTER_COLUMNS, -1)
    gp = spread(gp.astype(F32), chosen).reshape(ADAPTER_COLUMNS, -1)

    def columns(v):
        size = v.shape[0] // n_dp
        v = lax.dynamic_slice_in_dim(v, dp * size, size, 0)
        return lax.all_to_all(v, "seq", split_axis=0, concat_axis=1, tiled=True).T

    return columns(gm), columns(gh)[: VALUE_WIDTH + HIDDEN_UNITS], gp[:, :width]


def local(
    ends,
    mixer_input_weight,
    forget_first_map,
    forget_second_map,
    forget_logit_bias,
    mixer_output_weight,
    feedforward_input_weight,
    feedforward_output_weight,
    adapter_model_first,
    adapter_hidden_first,
    adapter_second_maps,
    lengths,
    dealt_block_order,
    adapter_choice_per_seq,
):
    first = lax.axis_index("section") == 0
    mine = lambda a: jnp.where(first, a[0], a[1])
    order = mine(dealt_block_order)[0]
    n_blocks = order.shape[0]
    at = jnp.arange(n_blocks, dtype=jnp.int32)
    inverse = jnp.sum(at[:, None] * (order[:, None] == at[None, :]).astype(jnp.int32), axis=0)
    meta = jnp.concatenate([order, inverse, mine(adapter_choice_per_seq), mine(lengths)])
    n_dp = lax.axis_size("dp")
    own_kernels = n_dp == 4 and lax.axis_size("seq") == 4
    shards = [mixer_input_weight, mixer_output_weight, feedforward_input_weight, feedforward_output_weight]
    small = [
        forget_second_map,
        forget_logit_bias[:, None],
        adapter_model_first,
        adapter_hidden_first,
        adapter_second_maps,
    ]
    if own_kernels:
        weights, x, cotangent, early, late = forward_model(meta, shards, forget_first_map[0].T, ends, small)
    else:
        out = plain_gather(shards, forget_first_map[0].T, ends, small)
        weights, x, cotangent = list(out[:5]) + list(out[7:]), out[5], out[6]
        early = forward(0, meta, x, weights)
        late = forward(1, meta, early[0], weights)
    entry, *grads = backward(meta, cotangent, x, early[0], weights, early[1:], late[1:], n_dp)
    grads_early, grads_late = grads[:3], grads[3:]
    if own_kernels:
        model, hidden, up, results = reduce_gradients(grads_early, grads_late, entry, late[0], n_dp)
    else:
        sent = swap_sections(jnp.where(first, late[0], entry))
        results = jnp.where(first, jnp.stack([entry, sent]), jnp.stack([sent, late[0]]))
        model, hidden, up = plain_reduce(grads_early, grads_late, n_dp)
    return (results[None, :, None], model[None], hidden[None], up[None])


def solution(mesh):
    return jax.shard_map(
        local,
        mesh=mesh,
        in_specs=(
            P("section", None, "dp", "seq", None),
            P("section", "dp", None),
            P("section", "dp", None),
            P("section", None, None),
            P("section", None),
            P("section", "dp", None),
            P("section", "dp", None),
            P("section", "dp", None),
            P("section", None, None),
            P("section", None, None),
            P("section", None, None),
            P(None, "dp"),
            P(None, "dp", None),
            P(None, "dp"),
        ),
        out_specs=(
            P("section", None, "dp", "seq", None),
            P("section", None, ("dp", "seq")),
            P("section", None, ("dp", "seq")),
            P("section", None, ("dp", "seq")),
        ),
        check_vma=False,
    )
```

```python
import functools
import jax
import jax.numpy as jnp
from jax import lax
from jax.experimental import pallas as pl
from jax.experimental.pallas import tpu as pltpu

from jax.sharding import PartitionSpec as P

MODEL_WIDTH = 1024
HEADS = 4
KEY = 512
VALUE_WIDTH = 1024
HIDDEN_UNITS = 2816
FGATE_RANK = 16
GROUP = 64
ADAPTER_RANK = 16
ADAPTERS = 8
ADAPTER_COLUMNS = 128
VMEM_LIMIT = 60 << 20
LINK_BYTES_PER_US = 60e3
SKEW = (2, 4)
DELAYS = (8, 25, 20)
STRIPS = (256, 128, 384, 128)

MESH = pl.DeviceIdType.MESH
ANY = pl.BlockSpec(memory_space=pl.ANY)


BF = jnp.bfloat16
F32 = jnp.float32


def nn(a, b):
    return lax.dot_general(a, b, (((1,), (0,)), ((), ())), preferred_element_type=F32)


def nt(a, b):
    return lax.dot_general(a, b, (((1,), (1,)), ((), ())), preferred_element_type=F32)


def tn(a, b):
    return lax.dot_general(a, b, (((0,), (0,)), ((), ())), preferred_element_type=F32)


def silu_parts(v):
    sig = lax.logistic(v)
    return v * sig, sig


def inverse_rms(v):
    return lax.rsqrt(jnp.mean(v * v, axis=-1, keepdims=True) + 1e-06)


def rms_back(v, grad):
    r = inverse_rms(v)
    n = v * r
    return r * (grad - n * jnp.mean(grad * n, axis=-1, keepdims=True))


def lanes(start, size):
    return pl.ds(pl.multiple_of(start, 128), size)


def rows(start, size):
    return pl.ds(pl.multiple_of(start, size if size <= 64 else 64), size)


def greet_peers(me):
    barrier = pltpu.get_barrier_semaphore()
    for d in range(1, HEADS):
        pl.semaphore_signal(barrier, inc=1, device_id={"seq": me ^ d}, device_id_type=MESH)
    pl.semaphore_wait(barrier, HEADS - 1)


def to_peer(src, dst, ssem, rsem, peer):
    return pltpu.make_async_remote_copy(
        src_ref=src, dst_ref=dst, send_sem=ssem, recv_sem=rsem,
        device_id={"seq": peer}, device_id_type=MESH,
    )


class Local:
    def __init__(self, sems):
        self.sems, self.used, self.open = sems, 0, []

    def start(self, src, dst, wait_at_end=False):
        copy = pltpu.make_async_copy(src, dst, self.sems.at[self.used])
        self.used += 1
        copy.start()
        if wait_at_end:
            self.open.append(copy)
        return copy

    def finish(self):
        for copy in self.open:
            copy.wait()
        self.open = []


def picked(adapter, width):
    row = lax.broadcasted_iota(jnp.int32, (width, ADAPTER_RANK), 0)
    col = lax.broadcasted_iota(jnp.int32, (width, ADAPTER_RANK), 1)
    return (row == adapter * ADAPTER_RANK + col).astype(BF)


def column_mask(adapter):
    col = lax.broadcasted_iota(jnp.int32, (1, ADAPTER_COLUMNS), 1)
    low = adapter * ADAPTER_RANK
    return jnp.logical_and(col >= low, col < low + ADAPTER_RANK).astype(F32)


def lower_triangle(dtype):
    i = lax.broadcasted_iota(jnp.int32, (GROUP, GROUP), 0)
    j = lax.broadcasted_iota(jnp.int32, (GROUP, GROUP), 1)
    return (i >= j).astype(dtype)


DK = KEY // HEADS
DV = VALUE_WIDTH // HEADS
CHUNK = 2 * DK + DV
FROZEN = 2 * KEY + 2 * VALUE_WIDTH
TILE = 256
SCALE = DK ** (-0.5)

U_G = FROZEN
U_U = FROZEN + HIDDEN_UNITS
U_O = FROZEN + 2 * HIDDEN_UNITS
U_D = U_O + MODEL_WIDTH


def live_rows(n, length):
    at = lax.broadcasted_iota(jnp.int32, (GROUP, 1), 0) + n * GROUP
    return (at < length).astype(F32)


def forward_steps(layer, n_blocks, meta, loc, weights, buffers, work, outs, sems):
    w, v = weights, buffers
    (h, y, ad, og, qkv, gl, st, mix, yh, rh, ao, mid, af, gu, dn, normed, send, glsend, fg, state, gated, hidden) = work
    o_y, o_ad, o_og, o_qkv, o_gl, o_st, o_mix, o_yh, o_rh, o_ao, o_mid, o_af, o_gu, o_dn = outs
    ssem, rsem = sems
    me = lax.axis_index("seq")
    T = h.shape[0]
    per = T // GROUP
    adapter = meta[2 * n_blocks]
    length = meta[2 * n_blocks + 1]
    mask = column_mask(adapter)
    am, ah, au, mi, mo, fi, fo = [v[name] for name in ("am", "ah", "au", "mi", "mo", "fi", "fo")]

    def load(*names):
        return [loc.start(w[name], v[name]) for name in names]

    def wait(copies):
        for c in copies:
            c.wait()

    yield "small", 0
    small = load("f1", "f2", "b", "am", "au", "ah")
    yield None, 2
    hv = h[...].astype(F32)
    normed[...] = (hv * inverse_rms(hv)).astype(BF)
    wait(small)
    f1, f2, bias = v["f1"], v["f2"], v["b"]
    z_w = f1.shape[2]
    low = nt(f1[0], normed[:, 0:z_w])
    for j in range(1, f1.shape[0]):
        low += nt(f1[j], normed[:, j * z_w : (j + 1) * z_w])
    glsend[...] = low.astype(BF)
    low_copies = [to_peer(glsend, gl.at[me], ssem.at[0, d], rsem.at[0, d], me ^ d) for d in range(1, HEADS)]
    for c in low_copies:
        c.start()
    gl[me] = glsend[...]
    yield "delay", DELAYS[0]
    for p in range(4):
        cols = pl.ds(p * ADAPTER_COLUMNS, ADAPTER_COLUMNS)
        ad[:, cols] = (nn(normed[...], am[:, cols]) * mask).astype(BF)
    f2h = f2[:, lanes(me * DK, DK)]
    bh = bias[:, lanes(me * DK, DK)]
    for c in low_copies:
        c.wait_recv()
    for src in range(HEADS):
        logit = tn(gl[src], f2h) + bh
        fg[src * T : (src + 1) * T, :] = (jax.nn.log_sigmoid(logit) / 16.0).astype(BF)
    loc.start(gl, o_gl, True)
    loc.start(ad, o_ad, True)
    yield "mi", 0
    wait(load("mi"))

    def project(w_start, p, width):
        cols = lanes(w_start, width)
        return nn(normed[...], mi[:, cols]) + nn(ad[:, p * ADAPTER_COLUMNS : (p + 1) * ADAPTER_COLUMNS], au[:, cols])

    def chunk(head, ref):
        ref[:, 0:DK] = project(head * DK, 0, DK).astype(BF)
        ref[:, DK : 2 * DK] = project(KEY + head * DK, 1, DK).astype(BF)
        ref[:, 2 * DK : CHUNK] = project(2 * KEY + head * DV, 2, DV).astype(BF)

    qkv_copies = []
    for d in (3, 1, 2):
        yield None, 1
        chunk(me ^ d, send.at[d - 1])
        copy = to_peer(send.at[d - 1], qkv.at[rows(me * T, T)], ssem.at[1, d], rsem.at[1, d], me ^ d)
        copy.start()
        qkv_copies.append(copy)
    yield None, 1
    chunk(me, qkv.at[rows(me * T, T)])
    yield None, 1
    for j in range(VALUE_WIDTH // TILE):
        og[:, j * TILE : (j + 1) * TILE] = project(2 * KEY + VALUE_WIDTH + j * TILE, 3, TILE)
    loc.start(og, o_og, True)
    yield "delay", DELAYS[1]
    for c in qkv_copies:
        c.wait_recv()
    loc.start(qkv, o_qkv, True)
    tri = lower_triangle(BF)
    causal = lower_triangle(F32)
    state[...] = jnp.zeros_like(state)

    def advance(n, carry):
        at = pl.ds(meta[n_blocks + n] * GROUP, GROUP)
        summed = nn(tri, fg[at, :])
        total = summed[GROUP - 1 : GROUP]
        k = qkv[at, DK : 2 * DK].astype(F32) * live_rows(n, length)
        ku = (k * jnp.exp(total - summed)).astype(BF)
        update = tn(qkv[at, 2 * DK : CHUNK], ku)
        now = state[...]
        st[n] = now.astype(BF)
        state[...] = jnp.exp(total) * now + update
        return carry

    lax.fori_loop(0, n_blocks, advance, 0, unroll=8)
    loc.start(st, o_st, True)
    yield None, 4

    def mix_block(p):
        n = meta[p]
        at = rows(p * GROUP, GROUP)
        summed = nn(tri, fg[at, :])
        middle = summed[GROUP // 2 : GROUP // 2 + 1]
        q = qkv[at, 0:DK].astype(F32) * SCALE
        k = qkv[at, DK : 2 * DK].astype(F32) * live_rows(n, length)
        qe = (q * jnp.exp(summed - middle)).astype(BF)
        ke = (k * jnp.exp(middle - summed)).astype(BF)
        scores = jnp.where(causal > 0, nt(qe, ke), 0.0).astype(BF)
        o = nn(scores, qkv[at, 2 * DK : CHUNK]) + nt((q * jnp.exp(summed)).astype(BF), st[n])
        r = lax.rsqrt(jnp.mean(o * o, axis=-1, keepdims=True) + 1.0)
        yh[at, :] = (o * r).astype(BF)
        rh[at, :] = jnp.broadcast_to(r, (GROUP, DK))

    mix_copies = []
    for d in (3, 1, 2):
        yield None, 2
        peer = me ^ d
        lax.fori_loop(0, per, lambda j, c, peer=peer: (mix_block(peer * per + j), c)[1], 0, unroll=True)
        copy = to_peer(yh.at[rows(peer * T, T)], mix.at[me], ssem.at[2, d], rsem.at[2, d], peer)
        copy.start()
        mix_copies.append(copy)
    yield None, 2
    lax.fori_loop(0, per, lambda j, c: (mix_block(me * per + j), c)[1], 0, unroll=True)
    mix[me] = yh[rows(me * T, T), :]
    loc.start(yh, o_yh, True)
    loc.start(rh, o_rh, True)
    yield "mo", 0
    l_mo = load("mo")
    yield "delay", DELAYS[2]
    for c in mix_copies:
        c.wait_recv()
    loc.start(mix, o_mix, True)
    for hd in range(HEADS):
        cols = slice(hd * DV, (hd + 1) * DV)
        gated[:, cols] = (mix[hd].astype(F32) * silu_parts(og[:, cols])[0]).astype(BF)
    ao[...] = (nn(gated[...], ah[0:VALUE_WIDTH, :]) * mask).astype(BF)
    wait(l_mo)
    for j in range(MODEL_WIDTH // TILE):
        cols = slice(j * TILE, (j + 1) * TILE)
        mid[:, cols] = (
            h[:, cols].astype(F32) + nn(gated[...], mo[:, cols]) + nn(ao[...], au[:, U_O + j * TILE : U_O + (j + 1) * TILE])
        )
    loc.start(ao, o_ao, True)
    loc.start(mid, o_mid, True)
    yield None, 1
    mv = mid[...]
    normed[...] = (mv * inverse_rms(mv)).astype(BF)
    for p in range(2):
        cols = slice(p * ADAPTER_COLUMNS, (p + 1) * ADAPTER_COLUMNS)
        wide = slice((4 + p) * ADAPTER_COLUMNS, (5 + p) * ADAPTER_COLUMNS)
        af[:, cols] = (nn(normed[...], am[:, wide]) * mask).astype(BF)
    loc.start(af, o_af, True)
    yield "fi", 0
    wait(load("fi"))

    def up_tile(i, carry):
        a, b = lanes(i * TILE, TILE), lanes(HIDDEN_UNITS + i * TILE, TILE)
        gate = nn(normed[...], fi[:, a]) + nn(af[:, 0:ADAPTER_COLUMNS], au[:, lanes(U_G + i * TILE, TILE)])
        up = nn(normed[...], fi[:, b]) + nn(af[:, ADAPTER_COLUMNS:], au[:, lanes(U_U + i * TILE, TILE)])
        gu[:, a] = gate.astype(gu.dtype)
        gu[:, b] = up.astype(gu.dtype)
        hidden[:, a] = (silu_parts(gate)[0] * up).astype(BF)
        return carry

    tiles = HIDDEN_UNITS // TILE
    yield None, 3
    lax.fori_loop(0, tiles // 2, up_tile, 0)
    yield None, 3
    lax.fori_loop(tiles // 2, tiles, up_tile, 0)
    loc.start(gu, o_gu, True)
    dn[...] = (nn(hidden[...], ah[VALUE_WIDTH:, :]) * mask).astype(BF)
    loc.start(dn, o_dn, True)
    yield "fo", 0
    wait(load("fo"))
    yield None, 3
    for j in range(MODEL_WIDTH // TILE):
        cols = slice(j * TILE, (j + 1) * TILE)
        y[:, cols] = (
            mid[:, cols] + nn(hidden[...], fo[:, cols]) + nn(dn[...], au[:, U_D + j * TILE : U_D + (j + 1) * TILE])
        ).astype(BF)
    loc.start(y, o_y, True)
    loc.finish()
    for c in low_copies + qkv_copies + mix_copies:
        c.wait_send()


NAMES = ("mi", "mo", "fi", "fo", "f1", "f2", "b", "am", "ah", "au")


def forward_kernel(layer, n_blocks, meta, h_in, *refs):
    n_w, n_out = len(NAMES), 14
    ins, outs = refs[:n_w], refs[n_w : n_w + n_out]
    refs = refs[n_w + n_out :]
    buffers, work = dict(zip(NAMES, refs[:n_w])), refs[n_w:-3]
    lsem, ssem, rsem = refs[-3:]
    loc = Local(lsem)
    first = loc.start(h_in, work[0])
    greet_peers(lax.axis_index("seq"))
    first.wait()
    weights = {name: ref.at[layer] for name, ref in zip(NAMES, ins)}
    for _ in forward_steps(layer, n_blocks, meta, loc, weights, buffers, work, outs, (ssem, rsem)):
        pass


def weight_scratch(weights):
    return [pltpu.VMEM(w.shape[1:], w.dtype) for w in weights]


def saved_shapes(T, L, n_blocks):
    s = lambda shape, dtype=BF: (shape, dtype)
    return [
        s((T, MODEL_WIDTH)),
        s((T, 4 * ADAPTER_COLUMNS)),
        s((T, VALUE_WIDTH), F32),
        s((L, CHUNK)),
        s((HEADS, FGATE_RANK, T)),
        s((n_blocks, DV, DK)),
        s((HEADS, T, DV)),
        s((L, DV)),
        s((L, DK), F32),
        s((T, ADAPTER_COLUMNS)),
        s((T, MODEL_WIDTH), F32),
        s((T, 2 * ADAPTER_COLUMNS)),
        s((T, 2 * HIDDEN_UNITS)),
        s((T, ADAPTER_COLUMNS)),
    ]


def work_scratch(T, L, saved):
    vm = pltpu.VMEM
    return [vm((T, MODEL_WIDTH), BF)] + [vm(*s) for s in saved] + [
        vm((T, MODEL_WIDTH), BF),
        vm((HEADS - 1, T, CHUNK), BF),
        vm((FGATE_RANK, T), BF),
        vm((L, DK), BF),
        vm((DV, DK), F32),
        vm((T, VALUE_WIDTH), BF),
        vm((T, HIDDEN_UNITS), BF),
    ]


def forward(layer, meta, h, weights):
    T = h.shape[0]
    L = T * HEADS
    n_blocks = L // GROUP
    saved = saved_shapes(T, L, n_blocks)
    dma = pltpu.SemaphoreType.DMA
    return pl.pallas_call(
        functools.partial(forward_kernel, layer, n_blocks),
        out_shape=[jax.ShapeDtypeStruct(*s) for s in saved],
        in_specs=[pl.BlockSpec(memory_space=pltpu.SMEM)] + [ANY] * (1 + len(weights)),
        out_specs=[ANY] * len(saved),
        scratch_shapes=weight_scratch(weights)
        + work_scratch(T, L, saved)
        + [dma((1 + len(weights) + len(saved),)), dma((3, HEADS)), dma((3, HEADS))],
        compiler_params=pltpu.CompilerParams(
            collective_id=1 + layer, has_side_effects=True, vmem_limit_bytes=VMEM_LIMIT
        ),
    )(meta, h, *weights)


def backward_kernel(n_blocks, meta, d_in, *refs):
    refs = list(refs)

    def take(n):
        out = refs[:n]
        del refs[:n]
        return out

    n_w = len(NAMES)
    inputs = take(2)
    sources = take(n_w)
    kept = [take(13), take(13)]
    (e_out,) = take(1)
    grad_outs = [take(3), take(3)]
    d, h = take(2)
    mi, mo, fi, fo, f1, f2, bias, am, ah, au = take(n_w)
    ad, og, qkv, gl, st, mix, yh, rh, ao, mid, af, gu, dn = take(13)
    (e,) = take(1)
    grad_sums = [take(3), take(3)]
    (gm, gh, gp, gps, rgm2, rgh2, rgp2, hidden, wide, gad, big, grad, dog, sendm, dmr, logit, fg, gstate, gt, dt, don,
     hidden_gated, sendq, dqkv, dlog, sendl, dlr) = take(27)
    dproj = wide.at[:, pl.ds(MODEL_WIDTH, FROZEN)]
    lsem, ssem2, rsem2, gssem2, grsem2 = take(5)
    me = lax.axis_index("seq")
    loc = Local(lsem)
    buffers = dict(zip(NAMES, (mi, mo, fi, fo, f1, f2, bias, am, ah, au)))
    acts = dict(ad=ad, og=og, qkv=qkv, gl=gl, st=st, mix=mix, yh=yh, rh=rh, ao=ao, mid=mid, af=af, gu=gu, dn=dn)
    on_the_way = [{}, {}]

    def fetch(layer, *names):
        for name in names:
            if name == "d":
                c = loc.start(d_in, d)
            elif name == "h":
                c = loc.start(inputs[layer], h)
            elif name in buffers:
                c = loc.start(sources[NAMES.index(name)].at[layer], buffers[name])
            else:
                c = loc.start(kept[layer][list(acts).index(name)], acts[name])
            on_the_way[layer][name] = c

    fetch(1, "d", "au", "dn", "ah", "fo", "gu")
    greet_peers(me)
    fetch(1, "fi", "am", "mid", "mo", "og", "mix", "f2", "b", "gl", "yh", "rh", "qkv", "st", "ao", "af", "mi", "f1", "ad", "h")
    finish = None
    for layer in (1, 0):
        def arrive(*names, layer=layer):
            for name in names:
                on_the_way[layer][name].wait()

        finish = backward_layer(
            layer, n_blocks, meta, me, loc, arrive, fetch if layer == 1 else None, finish, grad_outs[layer],
            d, h, mi, mo, fi, fo, f1, f2, bias, am, ah, au,
            ad, og, qkv, gl, st, mix, yh, rh, ao, mid, af, gu, dn,
            e, *grad_sums[layer], gm, gh, gp, gps, rgm2.at[layer], rgh2.at[layer], rgp2.at[layer],
            hidden, wide, gad, big, grad, dog, sendm, dmr, logit, fg, gstate, gt, dt, don,
            hidden_gated, sendq, dqkv, dlog, sendl, dlr, dproj,
            ssem2.at[layer], rsem2.at[layer], gssem2.at[layer], grsem2.at[layer],
        )
    loc.start(e, e_out, True)
    finish()
    loc.finish()


def backward_layer(
    layer, n_blocks, meta, me, loc, arrive, fetch, window, grad_outs,
    d, h, mi, mo, fi, fo, f1, f2, bias, am, ah, au,
    ad, og, qkv, gl, st, mix, yh, rh, ao, mid, af, gu, dn,
    e, sgm, sgh, sgp, gm, gh, gp, gps, rgm, rgh, rgp,
    hidden, wide, gad, big, grad, dog, sendm, dmr, logit, fg, gstate, gt, dt, don,
    hidden_gated, sendq, dqkv, dlog, sendl, dlr, dproj,
    ssem, rsem, gssem, grsem,
):
    prefetch = (lambda *names: fetch(0, *names)) if fetch else (lambda *names: None)
    T = h.shape[0]
    per = T // GROUP
    adapter = meta[2 * n_blocks]
    length = meta[2 * n_blocks + 1]
    mask = column_mask(adapter)
    pick = picked(adapter, ADAPTER_COLUMNS)

    def narrow(v):
        return nn(v, pick).astype(BF)

    def outer(u, v):
        return tn(narrow(u), v).astype(BF)

    n_dp, width, padded = gps.shape[1], gp.shape[1] // (HEADS * gps.shape[1]), gps.shape[3]
    quarter, hidden_quarter = MODEL_WIDTH // HEADS, gh.shape[1] // HEADS
    n_late = -(-FROZEN // (HEADS * width))
    mix_rows = 4 * ADAPTER_RANK

    def place(dps):
        for i in dps:
            for q in range(HEADS):
                piece = gp[:, (i * HEADS + q) * width : (i * HEADS + q + 1) * width]
                gps[q, i] = jnp.concatenate([piece, jnp.zeros((ADAPTER_RANK, padded - width), BF)], axis=1)

    def grad_copies(late):
        copies = []
        at = slice(0, mix_rows) if late else slice(mix_rows, 6 * ADAPTER_RANK)
        dps = slice(0, n_late) if late else slice(n_late, n_dp)
        for k in range(1, HEADS):
            peer = me ^ k
            pairs = [
                (gm.at[at, lanes(peer * quarter, quarter)], rgm.at[k - 1, at]),
                (gps.at[peer, dps], rgp.at[k - 1, dps]),
            ]
            if not late:
                pairs.append((gh.at[:, lanes(peer * hidden_quarter, hidden_quarter)], rgh.at[k - 1]))
            for i, (a, b) in enumerate(pairs):
                j = i if late else 2 + i
                copies.append(to_peer(a, b, gssem.at[j, k], grsem.at[j, k], peer))
        return copies

    arrive("au", "dn") if layer == 0 else arrive("d", "au", "dn")
    gdown = (nt(d[...], au[:, U_D : U_D + MODEL_WIDTH]).astype(BF).astype(F32) * mask).astype(BF)
    gdown16 = narrow(gdown)
    if layer == 1:
        gh[:, VALUE_WIDTH + HIDDEN_UNITS :] = jnp.zeros((ADAPTER_RANK, gh.shape[1] - VALUE_WIDTH - HIDDEN_UNITS), BF)
    gp[:, U_D : U_D + MODEL_WIDTH] = outer(dn[...], d[...])
    gad[...] = gdown
    arrive("ah", "fo", "gu")

    def down_tile(i, carry):
        a, b = lanes(i * TILE, TILE), lanes(HIDDEN_UNITS + i * TILE, TILE)
        at = pl.ds(pl.multiple_of(i * TILE, TILE), TILE)
        dh = nt(d[...], fo[at, :]) + nt(gad[...], ah[pl.ds(pl.multiple_of(VALUE_WIDTH + i * TILE, TILE), TILE), :])
        gate, up = gu[:, a].astype(F32), gu[:, b].astype(F32)
        act, sig = silu_parts(gate)
        hidden[:, a] = (act * up).astype(BF)
        wide[:, a] = (dh * up * sig * (1.0 + gate * (1.0 - sig))).astype(BF)
        wide[:, b] = (dh * act).astype(BF)
        return carry

    lax.fori_loop(0, HIDDEN_UNITS // TILE, down_tile, 0)
    prefetch("dn", "fo", "gu")
    gate_cols, up_cols = slice(0, HIDDEN_UNITS), slice(HIDDEN_UNITS, 2 * HIDDEN_UNITS)
    gg = (nt(wide[:, gate_cols], au[:, U_G : U_G + HIDDEN_UNITS]).astype(BF).astype(F32) * mask).astype(BF)
    gu2 = (nt(wide[:, up_cols], au[:, U_U : U_U + HIDDEN_UNITS]).astype(BF).astype(F32) * mask).astype(BF)
    gad2 = jnp.concatenate([gg, gu2], axis=1)
    big[:, 0 : 2 * ADAPTER_COLUMNS] = gad2
    arrive("fi", "am")

    def wide_tile(i, carry):
        at = pl.ds(pl.multiple_of(i * TILE, TILE), TILE)
        grad[:, lanes(i * TILE, TILE)] = nt(wide[...], fi[at, :]) + nt(
            big[:, 0 : 2 * ADAPTER_COLUMNS], am[at, 4 * ADAPTER_COLUMNS :]
        )
        return carry

    lax.fori_loop(0, MODEL_WIDTH // TILE, wide_tile, 0)
    prefetch("fi")
    arrive("mid")
    mv = mid[...]
    grad_mid = d[...].astype(F32) + rms_back(mv, grad[...])
    grad[...] = grad_mid
    attn = grad_mid.astype(BF)
    e[...] = attn
    gout = (nt(attn, au[:, U_O : U_O + MODEL_WIDTH]).astype(BF).astype(F32) * mask).astype(BF)
    gad[...] = gout
    arrive("mo", "og", "mix")

    def gate_back(head, out):
        at = rows(head * DV, DV)
        cols = lanes(head * DV, DV)
        gg_ = nt(e[...], mo[at, :]) + nt(gad[...], ah[at, :])
        o = og[:, cols]
        act, sig = silu_parts(o)
        out[...] = (gg_ * act).astype(BF)
        m = mix[head].astype(F32)
        dog[:, cols] = (gg_ * m * sig * (1.0 + o * (1.0 - sig))).astype(BF)
        hidden_gated[:, cols] = (m * act).astype(BF)

    mix_copies = []
    for k in (3, 1, 2):
        peer = me ^ k
        gate_back(peer, sendm.at[k - 1])
        copy = to_peer(sendm.at[k - 1], dmr.at[rows(me * T, T)], ssem.at[0, k], rsem.at[0, k], peer)
        copy.start()
        mix_copies.append(copy)
    gate_back(me, dmr.at[rows(me * T, T)])

    prefetch("mo", "ah", "og", "mix")
    if window:
        window()
    arrive("af")
    mv = mid[...]
    normed_mid = (mv * inverse_rms(mv)).astype(BF)
    gm[4 * ADAPTER_RANK : 5 * ADAPTER_RANK, :] = outer(big[:, 0:ADAPTER_COLUMNS], normed_mid)
    gm[5 * ADAPTER_RANK : 6 * ADAPTER_RANK, :] = outer(big[:, ADAPTER_COLUMNS : 2 * ADAPTER_COLUMNS], normed_mid)
    gp[:, U_G : U_G + HIDDEN_UNITS] = outer(af[:, 0:ADAPTER_COLUMNS], wide[:, gate_cols])
    gp[:, U_U : U_U + HIDDEN_UNITS] = outer(af[:, ADAPTER_COLUMNS:], wide[:, up_cols])
    arrive("f2", "b", "gl", "yh", "rh", "qkv", "st")
    f2h = f2[:, lanes(me * DK, DK)]
    bh = bias[:, lanes(me * DK, DK)]
    for src in range(HEADS):
        lg = tn(gl[src], f2h) + bh
        logit[src * T : (src + 1) * T, :] = lg
        fg[src * T : (src + 1) * T, :] = (jax.nn.log_sigmoid(lg) / 16.0).astype(BF)
    tri = lower_triangle(BF)
    causal = lower_triangle(F32)
    for c in mix_copies:
        c.wait_recv()
    gstate[...] = jnp.zeros_like(gstate)

    def retreat(i, carry):
        n = n_blocks - 1 - i
        at = pl.ds(meta[n_blocks + n] * GROUP, GROUP)
        here = rows(n * GROUP, GROUP)
        dm = dmr[at, :].astype(F32)
        yv = yh[at, :].astype(F32)
        r = rh[at, 0:1]
        do = (r * (dm - yv * jnp.mean(dm * yv, axis=-1, keepdims=True))).astype(BF)
        don[here, :] = do
        summed = nn(tri, fg[at, :])
        total = jnp.exp(summed[GROUP - 1 : GROUP])
        qs = (qkv[at, 0:DK].astype(F32) * SCALE * jnp.exp(summed)).astype(BF)
        now = gstate[...]
        gt[n] = now.astype(BF)
        decayed = total * now
        dt[n] = jnp.sum(decayed * st[n].astype(F32), axis=0, keepdims=True)
        gstate[...] = decayed + tn(do, qs)
        return carry

    lax.fori_loop(0, n_blocks, retreat, 0, unroll=8)

    def back_block(p, out, j):
        n = meta[p]
        at = rows(p * GROUP, GROUP)
        here = pl.ds(n * GROUP, GROUP)
        to = rows(j * GROUP, GROUP)
        live = live_rows(n, length)
        summed = nn(tri, fg[at, :])
        middle = summed[GROUP // 2 : GROUP // 2 + 1]
        total = summed[GROUP - 1 : GROUP]
        e1, e2 = jnp.exp(summed - middle), jnp.exp(middle - summed)
        es, eu = jnp.exp(summed), jnp.exp(total - summed)
        q = qkv[at, 0:DK].astype(F32) * SCALE
        k = qkv[at, DK : 2 * DK].astype(F32) * live
        v = qkv[at, 2 * DK : CHUNK]
        do, state_t, grad_t = don[here, :], st[n], gt[n]
        qe, ke, qs, ku = q * e1, k * e2, q * es, k * eu
        qeb, keb = qe.astype(BF), ke.astype(BF)
        scores = jnp.where(causal > 0, nt(qeb, keb), 0.0).astype(BF)
        dscores = jnp.where(causal > 0, nt(do, v), 0.0).astype(BF)
        dv = tn(scores, do) + nt(ku.astype(BF), grad_t)
        dqs = nn(do, state_t)
        dku = nn(v, grad_t)
        dqe = nn(dscores, keb)
        dke = tn(dscores, qeb)
        out[to, 0:DK] = (SCALE * (dqe * e1 + dqs * es)).astype(BF)
        out[to, DK : 2 * DK] = (live * (dke * e2 + dku * eu)).astype(BF)
        out[to, 2 * DK : CHUNK] = dv.astype(BF)
        kk = dku * ku
        dsum = dqe * qe + dqs * qs - dke * ke - kk
        dtotal = dt[n] + jnp.sum(kk, axis=0, keepdims=True)
        high = dsum.astype(BF)
        lowp = (dsum - high.astype(F32)).astype(BF)
        df = tn(tri, high) + tn(tri, lowp) + dtotal
        df = df.astype(BF).astype(F32)
        dlog[to, :] = (df * lax.logistic(-logit[at, :]) / 16.0).astype(BF)

    q_copies = []

    def back_rows(dest, out, low_out):
        lax.fori_loop(0, per, lambda j, c: (back_block(dest * per + j, out, j), c)[1], 0, unroll=True)
        low_out[...] = nt(f2h, dlog[...]).astype(BF)

    for k in (3, 1, 2):
        peer = me ^ k
        back_rows(peer, sendq.at[k - 1], sendl.at[k - 1])
        copies = (
            to_peer(sendq.at[k - 1], dqkv.at[me], ssem.at[1, k], rsem.at[1, k], peer),
            to_peer(sendl.at[k - 1], dlr.at[me], ssem.at[2, k], rsem.at[2, k], peer),
        )
        for copy in copies:
            copy.start()
        q_copies += copies
    back_rows(me, dqkv.at[me], dlr.at[me])

    arrive("ao")
    gh[:, VALUE_WIDTH : VALUE_WIDTH + HIDDEN_UNITS] = tn(gdown16, hidden[...]).astype(BF)
    gp[:, U_O : U_O + MODEL_WIDTH] = outer(ao[...], e[...])
    gh[:, 0:VALUE_WIDTH] = outer(gad[...], hidden_gated[...])
    place(range(n_late, n_dp))
    grads = grad_copies(False)
    for c in grads:
        c.start()
    prefetch("mid", "af", "ao", "qkv", "gl", "st", "yh", "rh", "f2", "b")

    arrive("mi", "f1", "ad", "h")
    hv = h[...].astype(F32)
    hr = inverse_rms(hv)
    big[...] = (hv * hr).astype(BF)
    for c in q_copies:
        c.wait_recv()
    for hd in range(HEADS):
        dproj[:, hd * DK : (hd + 1) * DK] = dqkv[hd, :, 0:DK]
        dproj[:, KEY + hd * DK : KEY + (hd + 1) * DK] = dqkv[hd, :, DK : 2 * DK]
        dproj[:, 2 * KEY + hd * DV : 2 * KEY + (hd + 1) * DV] = dqkv[hd, :, 2 * DK : CHUNK]
    dproj[:, 2 * KEY + VALUE_WIDTH :] = dog[...]
    dlow = dlr[0].astype(F32)
    for hd in range(1, HEADS):
        dlow += dlr[hd].astype(F32)
    dlowb = dlow.astype(BF)
    spans = ((0, KEY), (KEY, KEY), (2 * KEY, VALUE_WIDTH), (2 * KEY + VALUE_WIDTH, VALUE_WIDTH))
    for p, (start, span) in enumerate(spans):
        block = slice(p * ADAPTER_COLUMNS, (p + 1) * ADAPTER_COLUMNS)
        piece = dproj[:, start : start + span]
        ga = (nt(piece, au[:, start : start + span]).astype(BF).astype(F32) * mask).astype(BF)
        wide[:, block] = ga
        gm[p * ADAPTER_RANK : (p + 1) * ADAPTER_RANK, :] = outer(ga, big[...])
        gp[:, start : start + span] = outer(ad[:, block], piece)
    place(range(n_late))
    late_grads = grad_copies(True)
    for c in late_grads:
        c.start()
    z_w = f1.shape[2]
    tiles = f1.shape[0]
    back = []
    for j in range(tiles):
        at = slice(j * z_w, (j + 1) * z_w)
        back.append(
            nt(dproj[...], mi[at, :]) + nt(wide[:, 0 : 4 * ADAPTER_COLUMNS], am[at, 0 : 4 * ADAPTER_COLUMNS]) + tn(dlowb, f1[j])
        )
    dn_ = jnp.concatenate(back, axis=1)
    n = hv * hr
    e[...] = (grad[...] + hr * (dn_ - n * jnp.mean(dn_ * n, axis=-1, keepdims=True))).astype(BF)
    if layer == 1:
        d[...] = e[...]
    prefetch("au", "am", "mi", "f1", "ad", "h")
    grads += late_grads
    for c in mix_copies + q_copies:
        c.wait_send()

    def finish():
        for c in grads:
            c.wait_recv()

        def summed_over_seq(own, got):
            total = own.astype(F32)
            for k in range(HEADS - 1):
                total += got[k].astype(F32)
            return total.astype(BF)

        sgm[...] = summed_over_seq(gm[:, lanes(me * quarter, quarter)], rgm)
        sgh[...] = summed_over_seq(gh[:, lanes(me * hidden_quarter, hidden_quarter)], rgh)
        spot = lax.broadcasted_iota(jnp.int32, (ADAPTER_RANK, padded), 1)
        for i in range(n_dp):
            total = gps[me, i].astype(F32)
            for k in range(HEADS - 1):
                total += rgp[k, i].astype(F32)
            sgp[i] = jnp.where(spot == width, adapter.astype(F32), total).astype(BF)
        for c in grads:
            c.wait_send()
        for a, b in zip((sgm, sgh, sgp), grad_outs):
            loc.start(a, b, True)

    return finish


def backward(meta, d, x, h1, weights, early, late, n_dp):
    T = x.shape[0]
    L = T * HEADS
    n_blocks = L // GROUP
    raised = U_D + MODEL_WIDTH
    padded = (raised // (n_dp * HEADS) // 128 + 1) * 128
    quarter = MODEL_WIDTH // HEADS
    hidden_quarter = -(-(VALUE_WIDTH + HIDDEN_UNITS) // (HEADS * 128)) * 128
    outs = [
        ((T, MODEL_WIDTH), BF),
        ((6 * ADAPTER_RANK, quarter), BF),
        ((ADAPTER_RANK, hidden_quarter), BF),
        ((n_dp, ADAPTER_RANK, padded), BF),
    ]
    vm = pltpu.VMEM
    dma = pltpu.SemaphoreType.DMA
    return pl.pallas_call(
        functools.partial(backward_kernel, n_blocks),
        out_shape=[jax.ShapeDtypeStruct(*s) for s in outs[:1] + 2 * outs[1:]],
        in_specs=[pl.BlockSpec(memory_space=pltpu.SMEM)] + [ANY] * (3 + len(weights) + 2 * len(early)),
        out_specs=[ANY] * (2 * len(outs) - 1),
        scratch_shapes=[vm(d.shape, d.dtype), vm(x.shape, x.dtype)]
        + weight_scratch(weights)
        + [vm(s.shape, s.dtype) for s in early]
        + [vm(*s) for s in outs[:1] + 2 * outs[1:]]
        + [
            vm((6 * ADAPTER_RANK, MODEL_WIDTH), BF),
            vm((ADAPTER_RANK, HEADS * hidden_quarter), BF),
            vm((ADAPTER_RANK, raised), BF),
            vm((HEADS, n_dp, ADAPTER_RANK, padded), BF),
            vm((2, HEADS - 1, 6 * ADAPTER_RANK, quarter), BF),
            vm((2, HEADS - 1, ADAPTER_RANK, hidden_quarter), BF),
            vm((2, HEADS - 1, n_dp, ADAPTER_RANK, padded), BF),
            vm((T, HIDDEN_UNITS), BF),
            vm((T, 2 * HIDDEN_UNITS), BF),
            vm((T, ADAPTER_COLUMNS), BF),
            vm((T, MODEL_WIDTH), BF),
            vm((T, MODEL_WIDTH), F32),
            vm((T, VALUE_WIDTH), BF),
            vm((HEADS - 1, T, DV), BF),
            vm((L, DV), BF),
            vm((L, DK), F32),
            vm((L, DK), BF),
            vm((DV, DK), F32),
            vm((n_blocks, DV, DK), BF),
            vm((n_blocks, 1, DK), F32),
            vm((L, DV), BF),
            vm((T, VALUE_WIDTH), BF),
            vm((HEADS - 1, T, CHUNK), BF),
            vm((HEADS, T, CHUNK), BF),
            vm((T, DK), BF),
            vm((HEADS - 1, FGATE_RANK, T), BF),
            vm((HEADS, FGATE_RANK, T), BF),
            dma((2 * (2 + len(weights) + len(early) + len(outs)),)),
            dma((2, 3, HEADS)),
            dma((2, 3, HEADS)),
            dma((2, 5, HEADS)),
            dma((2, 5, HEADS)),
        ],
        compiler_params=pltpu.CompilerParams(
            collective_id=3, has_side_effects=True, vmem_limit_bytes=VMEM_LIMIT
        ),
        cost_estimate=pl.CostEstimate(flops=4 * T * 16_000_000, bytes_accessed=90 << 20, transcendentals=T * 16384),
    )(meta, d, x, h1, *weights, *early, *late)


UNITS = [(layer, w) for layer in range(2) for w in range(4)]


def model_kernel(n_blocks, meta, *refs):
    n_w, n_small, n_saved, n_z = 4, 5, 14, 4
    refs = list(refs)

    def take(n):
        out = refs[:n]
        del refs[:n]
        return out

    shards = take(n_w)
    f1_ref, ends_ref = take(2)
    small = take(n_small)
    outs = take(n_w)
    (f1_out,) = take(1)
    (x_out, c_out) = take(2)
    small_out = take(n_small)
    saved = [take(n_saved), take(n_saved)]
    held = take(n_w)
    held_f1 = take(1)[0]
    held_small = take(n_small)
    work = take(1 + n_saved + 7)
    qkv2, gl2, mix2, held_ends = take(4)
    (ins, zs, zr, ts, tr, xs, xr, ys, yr, fxs, fxr, fys, fyr, cs, cr, own, ms, mr, es, er, f1s, f1r, f1c, lsem, ssem, rsem) = take(26)
    core, z, s = lax.axis_index("section"), lax.axis_index("dp"), lax.axis_index("seq")
    other = 1 - core

    def remote(src, dst, send_sem, recv_sem, **where):
        return pltpu.make_async_remote_copy(
            src_ref=src, dst_ref=dst, send_sem=send_sem, recv_sem=recv_sem, device_id=where, device_id_type=MESH
        )

    def height(w):
        return shards[w].shape[1]

    def staged(w):
        return held[w].at[pl.ds(pl.multiple_of(z * height(w), 16), height(w))]

    fetch = [pltpu.make_async_copy(shards[w].at[0], staged(w), ins.at[w]) for w in range(n_w)]
    fetch += [pltpu.make_async_copy(a.at[0], b, ins.at[n_w + i]) for i, (a, b) in enumerate(zip(small, held_small))]
    fetch.append(pltpu.make_async_copy(ends_ref.at[0, :, 0], held_ends, ins.at[n_w + n_small]))
    fetch.append(pltpu.make_async_copy(f1_ref, held_f1.at[z], ins.at[n_w + n_small + 1]))
    for f in fetch:
        f.start()

    barrier = pltpu.get_barrier_semaphore()
    greeted = [dict(section=other)] + [dict(seq=s ^ k) for k in range(1, HEADS)]
    greeted += [dict(dp=lax.rem(z + gap, n_z)) for gap in range(1, n_z)]
    for where in greeted:
        pl.semaphore_signal(barrier, inc=1, device_id=where, device_id_type=MESH)
    pl.semaphore_wait(barrier, len(greeted))

    def part(u, j, start, size, strip=False):
        layer, w = UNITS[u]
        cols = shards[w].shape[2] // 2
        at, wide = (cols - STRIPS[w], STRIPS[w]) if strip else (0, cols - STRIPS[w])
        return outs[w].at[layer, pl.ds(pl.multiple_of(j * height(w) + start, 16), size), lanes(core * cols + at, wide)]

    def piece(u, j, q):
        r = height(UNITS[u][1])
        return part(u, j, q * (r // 4), r // 4)

    def half(u, j, q, low):
        r = height(UNITS[u][1])
        cut = (r // 8 + 15) // 16 * 16
        start, size = (0, cut) if low else (cut, r // 4 - cut)
        return part(u, j, q * (r // 4) + start, size)

    def block(u, j):
        layer, w = UNITS[u]
        cols = shards[w].shape[2] // 2
        return outs[w].at[layer, pl.ds(pl.multiple_of(j * height(w), 16), height(w)), lanes(core * cols, cols)]

    def whole_block(layer, w):
        return outs[w].at[layer, pl.ds(pl.multiple_of(z * height(w), 16), height(w))]

    def step(d):
        return 1 if d == 0 else -1

    def can_send(d, t):
        has_next = (z < n_z - 1) if d == 0 else (z > 0)
        first = z - step(d) * (t - 1)
        return jnp.logical_and(has_next, jnp.logical_and(first >= 0, first < n_z))

    def gets(d, t):
        first = z - step(d) * t
        return jnp.logical_and(first >= 0, first < n_z)

    def origin(d, t):
        return z - step(d) * t

    def z_copy(u, d, t):
        ref = piece(u, z - step(d) * (t - 1), s)
        return remote(ref, ref, zs.at[u, d, t - 1], zr.at[u, d, t - 1], dp=z + step(d))

    def t_copy(u, d, t):
        ref = part(u, z - step(d) * (t - 1), 0, height(UNITS[u][1]), True)
        return remote(ref, ref, ts.at[u, d, t - 1], tr.at[u, d, t - 1], dp=z + step(d))

    def x_copy(u, d, t):
        ref = piece(u, origin(d, t), s)
        return remote(ref, ref, xs.at[u, d, t - 1], xr.at[u, d, t - 1], seq=s ^ 1)

    def y_copy(u, d, t):
        ref = piece(u, origin(d, t), s)
        return remote(ref, ref, ys.at[u, d, t - 1], yr.at[u, d, t - 1], seq=s ^ 2)

    def fx_copy(u, d, t):
        ref = half(u, origin(d, t), s ^ 2, False)
        return remote(ref, ref, fxs.at[u, d, t - 1], fxr.at[u, d, t - 1], seq=s ^ 1)

    def fy_copy(u, d, t):
        ref = half(u, origin(d, t), s ^ 1, True)
        return remote(ref, ref, fys.at[u, d, t - 1], fyr.at[u, d, t - 1], seq=s ^ 2)

    def c_copy(u, d, t):
        ref = block(u, origin(d, t))
        return remote(ref, ref, cs.at[u, d, t - 1], cr.at[u, d, t - 1], section=other)

    def own_copy(w):
        return pltpu.make_async_copy(staged(w), whole_block(core, w), own.at[w])

    def own_cross(w):
        return remote(staged(w), whole_block(core, w), ms.at[n_small + w], mr.at[n_small + w], section=other)

    def start_own(u):
        layer, w = UNITS[u]

        if layer == 0:
            own_copy(w).wait()

        @pl.when(core != layer)
        def _():
            own_cross(w).wait_recv()

        for d in range(2):
            @pl.when(can_send(d, 1))
            def _():
                z_copy(u, d, 1).start()
                if STRIPS[w]:
                    t_copy(u, d, 1).start()

    def take_z(u, t):
        for d in range(2):
            @pl.when(gets(d, t))
            def _():
                z_copy(u, d, t).wait_recv()
            if t < n_z - 1:
                @pl.when(can_send(d, t + 1))
                def _():
                    z_copy(u, d, t + 1).start()
            @pl.when(gets(d, t))
            def _():
                x_copy(u, d, t).start()
                y_copy(u, d, t).start()
                if STRIPS[UNITS[u][1]]:
                    t_copy(u, d, t).wait_recv()
            if t < n_z - 1 and STRIPS[UNITS[u][1]]:
                @pl.when(can_send(d, t + 1))
                def _():
                    t_copy(u, d, t + 1).start()

    def take_xy(u, t):
        for d in range(2):
            @pl.when(gets(d, t))
            def _():
                x_copy(u, d, t).wait_recv()
                fy_copy(u, d, t).start()
                y_copy(u, d, t).wait_recv()
                fx_copy(u, d, t).start()

    def take_diagonal(u, t):
        for d in range(2):
            @pl.when(gets(d, t))
            def _():
                fy_copy(u, d, t).wait_recv()
                fx_copy(u, d, t).wait_recv()
                c_copy(u, d, t).start()

    def take_core(u):
        for d in range(2):
            for t in range(1, n_z):
                @pl.when(gets(d, t))
                def _():
                    c_copy(u, d, t).wait_recv()

    def f1_copy(gap):
        return remote(held_f1.at[z], f1_out.at[core, z], f1s.at[gap], f1r.at[gap], dp=lax.rem(z + gap, n_z))

    def launch(w):
        fetch[w].wait()
        own_copy(w).start()
        own_cross(w).start()

    launch(0)
    fetch[-1].wait()
    f1_sends = [f1_copy(gap) for gap in range(1, n_z)]
    for c in f1_sends:
        c.start()
    f1_own = pltpu.make_async_copy(held_f1.at[z], f1_out.at[core, z], own.at[n_w])
    f1_own.start()
    ends_to_x = remote(held_ends.at[1], x_out, es, er, section=other)
    ends_to_c = remote(held_ends.at[0], c_out, es, er, section=other)
    ends_x = pltpu.make_async_copy(held_ends.at[0], x_out, own.at[n_w + 1])
    ends_c = pltpu.make_async_copy(held_ends.at[1], c_out, own.at[n_w + 1])
    f1_cross = remote(f1_out.at[core], f1_out.at[core], f1c.at[0], f1c.at[1], section=other)
    start_own(0)
    launch(1)
    smalls = []

    def launch_rest():
        fetch[-2].wait()

        @pl.when(core == 0)
        def _():
            ends_to_x.start()
            ends_x.start()

        @pl.when(core == 1)
        def _():
            ends_to_c.start()
            ends_c.start()

        for i, (a, b) in enumerate(zip(held_small, small_out)):
            fetch[n_w + i].wait()
            mine = pltpu.make_async_copy(a, b.at[core], own.at[n_w + 2 + i])
            theirs = remote(a, b.at[core], ms.at[i], mr.at[i], section=other)
            mine.start()
            theirs.start()
            smalls.append((mine, theirs))
        for w in range(2, n_w):
            launch(w)
        f1_own.wait()
        for c in f1_sends:
            c.wait_recv()
        f1_cross.start()

    def settle_small():
        for mine, theirs in smalls:
            mine.wait()
            theirs.wait()
        for c in f1_sends:
            c.wait_send()
        f1_cross.wait()
        ends_x.wait()
        ends_to_x.wait()

    items = [(u, t) for u in range(len(UNITS)) for t in range(1, n_z)]
    ready, clock = [], 8.0
    for u, t in items:
        r, c = shards[UNITS[u][1]].shape[1:]
        clock += r // 4 * (c - 2 * STRIPS[UNITS[u][1]]) * 3 / LINK_BYTES_PER_US
        ready.append(clock)

    def gather_step(i):
        if i == 1:
            launch_rest()
        if i < len(items):
            u, t = items[i]
            if t == 1 and u + 1 < len(UNITS):
                start_own(u + 1)
            take_z(u, t)
        if 0 <= i - SKEW[0] < len(items):
            take_xy(*items[i - SKEW[0]])
        if 0 <= i - SKEW[1] < len(items):
            take_diagonal(*items[i - SKEW[1]])

    loc = Local(lsem)
    n_steps = len(items) + SKEW[1]
    works = [list(work), list(work)]
    for at, ref in ((4, qkv2), (5, gl2), (7, mix2)):
        works[1][at] = ref

    def both_layers():
        for layer in range(2):
            sources = dict(zip(NAMES[:4], outs))
            sources["f1"] = f1_out
            sources.update(zip(NAMES[5:], small_out))
            sources = {name: ref.at[layer] for name, ref in sources.items()}
            buffers = dict(zip(NAMES, held + [held_f1] + held_small))
            for what, us in forward_steps(
                layer, n_blocks, meta, loc, sources, buffers, works[layer], saved[layer], (ssem.at[layer], rsem.at[layer])
            ):
                yield layer, what, us
            if layer == 0:
                work[0][...] = work[1][...]

    steps, done, now, crossed, until = both_layers(), 0, 8.0, set(), None
    pending = next(steps)
    while pending is not None or done < n_steps:
        due = ready[min(max(done - 2, 0), len(ready) - 1)]
        blocked = False
        if pending is not None and pending[1] in NAMES[:4]:
            u = UNITS.index((pending[0], NAMES.index(pending[1])))
            blocked = done < min(3 * u + 3 + SKEW[1], n_steps)
            if not blocked:
                take_core(u)
                crossed.add(u)
                if pending[0] == 0:
                    own_cross(UNITS[u][1]).wait_send()
        elif pending is not None and pending[:2] == (0, "small"):
            blocked = done < 3
            if not blocked:
                settle_small()
                loc.start(x_out, work[0]).wait()
        elif pending is not None and pending[1] == "delay":
            until = now + pending[2] if until is None else until
            blocked = now < until and due < until
        if done < n_steps and (pending is None or blocked or due <= now):
            now = max(now, due)
            gather_step(done)
            done += 1
            continue
        now = now + pending[2] if until is None else max(now, until)
        until = None
        pending = next(steps, None)
    for u in range(len(UNITS)):
        if u not in crossed:
            take_core(u)
        for d in range(2):
            for t in range(1, n_z):
                @pl.when(can_send(d, t))
                def _():
                    z_copy(u, d, t).wait_send()
                    if STRIPS[UNITS[u][1]]:
                        t_copy(u, d, t).wait_send()
                @pl.when(gets(d, t))
                def _():
                    x_copy(u, d, t).wait_send()
                    y_copy(u, d, t).wait_send()
                    fx_copy(u, d, t).wait_send()
                    fy_copy(u, d, t).wait_send()
                    c_copy(u, d, t).wait_send()


def forward_model(meta, shards, f1t, ends, small):
    shape, dma, vm = jax.ShapeDtypeStruct, pltpu.SemaphoreType.DMA, pltpu.VMEM
    T = ends.shape[3]
    L = T * HEADS
    n_blocks = L // GROUP
    saved = saved_shapes(T, L, n_blocks)
    n_w, n_small, n_u = len(shards), len(small), len(UNITS)
    outs = [shape((2, 4 * w.shape[1], w.shape[2]), w.dtype) for w in shards]
    outs.append(shape((2, 4) + f1t.shape, f1t.dtype))
    outs += [shape(ends.shape[3:], ends.dtype)] * 2
    outs += [shape((2,) + a.shape[1:], a.dtype) for a in small]
    outs += [shape(*s) for s in saved] * 2
    full = [vm((4 * w.shape[1], w.shape[2]), w.dtype) for w in shards]
    out = pl.pallas_call(
        functools.partial(model_kernel, n_blocks),
        out_shape=outs,
        in_specs=[pl.BlockSpec(memory_space=pltpu.SMEM)] + [ANY] * (n_w + 2 + n_small),
        out_specs=[ANY] * len(outs),
        scratch_shapes=full
        + [vm((4,) + f1t.shape, f1t.dtype)]
        + [vm(a.shape[1:], a.dtype) for a in small]
        + work_scratch(T, L, saved)
        + [vm((L, CHUNK), BF), vm((HEADS, FGATE_RANK, T), BF), vm((HEADS, T, DV), BF), vm((2,) + ends.shape[3:], BF)]
        + [dma((n_w + n_small + 2,))]
        + [dma((n_u, 2, 3)) for _ in range(14)]
        + [dma((n_w + n_small + 2,)), dma((n_small + n_w,)), dma((n_small + n_w,)), dma, dma, dma((4,)), dma((4,)), dma((2,))]
        + [dma((1 + 2 * (len(NAMES) + len(saved)),)), dma((2, 3, HEADS)), dma((2, 3, HEADS))],
        compiler_params=pltpu.CompilerParams(collective_id=0, has_side_effects=True, vmem_limit_bytes=VMEM_LIMIT),
    )(meta, *shards, f1t, ends, *small)
    weights = list(out[:5]) + list(out[7:12])
    return weights, out[5], out[6], out[12 : 12 + len(saved)], out[12 + len(saved) :]


def swap_sections(v):
    return lax.ppermute(v, "section", [(0, 1), (1, 0)])


def plain_gather(shards, f1t, ends, small):
    first = lax.axis_index("section") == 0
    both = lambda a: lax.all_gather(a, "section", axis=0)
    outs = [both(lax.all_gather(w[0], "dp", axis=0, tiled=True)) for w in shards]
    low = lax.all_gather(f1t, "dp", axis=1, tiled=True)
    outs.append(both(jnp.stack(jnp.split(low, 4, axis=1))))
    sent = swap_sections(jnp.where(first, ends[0, 1, 0], ends[0, 0, 0]))
    outs.append(jnp.where(first, ends[0, 0, 0], sent))
    outs.append(jnp.where(first, sent, ends[0, 1, 0]))
    return outs + [both(a[0]) for a in small]


def spread(parts, chosen):
    hot = (chosen[:, None] == jnp.arange(ADAPTERS, dtype=jnp.int32)[None, :]).astype(F32)
    return sum(parts[n][:, None] * hot[n][None, :, None, None] for n in range(parts.shape[0]))


def reduce_kernel(
    gm0, gh0, gp0, gm1, gh1, gp1, entry, last_y, m_out, h_out, u_out, ends_out,
    vm_, vh, vp, rm, rh, rp, am, ah, em, eh, ends, ls, ss, rs, es, er, xl, xo, xs, xr,
):
    core, dp, me = lax.axis_index("section"), lax.axis_index("dp"), lax.axis_index("seq")
    n_dp = vp.shape[1]
    width = u_out.shape[1]
    loads = [
        pltpu.make_async_copy(a, b.at[l], ls.at[l, i])
        for l, three in enumerate(((gm0, gh0, gp0), (gm1, gh1, gp1)))
        for i, (a, b) in enumerate(zip(three, (vm_, vh, vp)))
    ]
    for c in loads:
        c.start()
    ends_in = [pltpu.make_async_copy(a, ends.at[i], xl.at[i]) for i, a in enumerate((entry, last_y))]
    for c in ends_in:
        c.start()
    barrier = pltpu.get_barrier_semaphore()
    places = [dict(section=1 - core)] + [dict(seq=me ^ k) for k in range(1, HEADS)]
    for gap in range(1, n_dp):
        to = lax.rem(dp + gap, n_dp)
        places += [dict(dp=to), dict(section=1 - core, dp=to)]
    for where in places:
        pl.semaphore_signal(barrier, inc=1, device_id=where, device_id_type=MESH)
    for c in loads:
        c.wait()
    pl.semaphore_wait(barrier, len(places))
    slot = dp * 2 + core
    size = 6 * ADAPTER_COLUMNS // n_dp

    def first_projection(i):
        return i * size // ADAPTER_COLUMNS

    def parts(layer, to):
        at = pl.ds(pl.multiple_of(first_projection(to) * ADAPTER_RANK, ADAPTER_RANK), 2 * ADAPTER_RANK)
        return ((vm_.at[layer, at], rm.at[slot]), (vh.at[layer], rh.at[slot]), (vp.at[layer, to], rp.at[slot]))

    copies = []
    for gap in range(n_dp - 1, -1, -1):
        to = lax.rem(dp + gap, n_dp)
        for crossing in (0, 1):
            if crossing == 0 and gap == 0:
                continue
            section = 1 - core if crossing else core
            for i, (a, b) in enumerate(parts(section, to)):
                c = pltpu.make_async_remote_copy(
                    src_ref=a, dst_ref=b, send_sem=ss.at[crossing, gap, i], recv_sem=rs.at[crossing, gap, i],
                    device_id=dict(section=section, dp=to), device_id_type=MESH,
                )
                c.start()
                copies.append(c)
    for c in ends_in:
        c.wait()
    ends_own = pltpu.make_async_copy(ends.at[core], ends_out.at[core], xo)
    ends_cross = pltpu.make_async_remote_copy(
        src_ref=ends.at[1 - core], dst_ref=ends_out.at[core], send_sem=xs, recv_sem=xr,
        device_id=dict(section=1 - core), device_id_type=MESH,
    )
    ends_own.start()
    ends_cross.start()
    at = pl.ds(pl.multiple_of(first_projection(dp) * ADAPTER_RANK, ADAPTER_RANK), 2 * ADAPTER_RANK)
    rm[slot] = vm_[core, at]
    rh[slot] = vh[core]
    rp[slot] = vp[core, dp]
    for c in copies:
        c.wait_recv()
    n = rm.shape[0]
    chosen = [rp[j, :, width : width + 1].astype(F32) for j in range(n)]
    for a in range(ADAPTERS):
        hot = [(c == float(a)).astype(F32) for c in chosen]
        at = slice(a * ADAPTER_RANK, (a + 1) * ADAPTER_RANK)

        def total(values):
            out = hot[0] * values(0).astype(F32)
            for j in range(1, n):
                out += hot[j] * values(j).astype(F32)
            return out

        for p in range(2):
            am[p * ADAPTER_COLUMNS + a * ADAPTER_RANK : p * ADAPTER_COLUMNS + (a + 1) * ADAPTER_RANK, :] = total(
                lambda j, p=p: rm[j, p * ADAPTER_RANK : (p + 1) * ADAPTER_RANK]
            )
        ah[at, :] = total(lambda j: rh[j])
        u_out[at, :] = total(lambda j: rp[j])[:, 0:width]
    own_m, own_h = size // HEADS, ADAPTER_COLUMNS // n_dp // HEADS
    base = dp * size - first_projection(dp) * ADAPTER_COLUMNS

    def m_rows(q):
        return am.at[pl.ds(pl.multiple_of(base + q * own_m, 16), own_m)]

    def h_rows(q):
        return ah.at[pl.ds(pl.multiple_of(dp * HEADS * own_h + q * own_h, 8), own_h)]

    last = []
    for k in range(1, HEADS):
        for i, (a, b) in enumerate(((m_rows(me ^ k), em.at[me]), (h_rows(me ^ k), eh.at[me]))):
            c = to_peer(a, b, es.at[i, k], er.at[i, k], me ^ k)
            c.start()
            last.append(c)
    em[me] = m_rows(me)[...]
    eh[me] = h_rows(me)[...]
    for c in last:
        c.wait_recv()
    for q in range(HEADS):
        m_out[:, q * em.shape[2] : (q + 1) * em.shape[2]] = em[q]
        h_out[:, q * eh.shape[2] : (q + 1) * eh.shape[2]] = eh[q]
    for c in copies + last:
        c.wait_send()
    ends_own.wait()
    ends_cross.wait()


def reduce_gradients(early, late, entry, y, n_dp):
    gm, gh, gp = early
    n = 2 * n_dp
    width = (U_D + MODEL_WIDTH) // (n_dp * HEADS)
    own_m, own_h = 6 * ADAPTER_COLUMNS // (n_dp * HEADS), ADAPTER_COLUMNS // (n_dp * HEADS)
    vm, dma, VM = pltpu.VMEM, pltpu.SemaphoreType.DMA, pl.BlockSpec(memory_space=pltpu.VMEM)
    shape = jax.ShapeDtypeStruct
    model, hidden, up, ends = pl.pallas_call(
        reduce_kernel,
        out_shape=[
            shape((own_m, MODEL_WIDTH), F32),
            shape((own_h, HEADS * gh.shape[1]), F32),
            shape((ADAPTER_COLUMNS, width), F32),
            shape((2,) + y.shape, y.dtype),
        ],
        in_specs=[ANY] * 8,
        out_specs=[VM] * 3 + [ANY],
        scratch_shapes=[
            vm((2,) + gm.shape, BF),
            vm((2,) + gh.shape, BF),
            vm((2,) + gp.shape, BF),
            vm((n, 2 * ADAPTER_RANK, gm.shape[1]), BF),
            vm((n,) + gh.shape, BF),
            vm((n,) + gp.shape[1:], BF),
            vm((2 * ADAPTER_COLUMNS, gm.shape[1]), F32),
            vm((ADAPTER_COLUMNS, gh.shape[1]), F32),
            vm((HEADS, own_m, gm.shape[1]), F32),
            vm((HEADS, own_h, gh.shape[1]), F32),
            vm((2,) + y.shape, y.dtype),
            dma((2, 3)),
            dma((2, n_dp, 3)),
            dma((2, n_dp, 3)),
            dma((2, HEADS)),
            dma((2, HEADS)),
            dma((2,)),
            dma,
            dma,
            dma,
        ],
        compiler_params=pltpu.CompilerParams(collective_id=5, has_side_effects=True, vmem_limit_bytes=VMEM_LIMIT),
    )(*early, *late, entry, y)
    return model.T, hidden[:, : VALUE_WIDTH + HIDDEN_UNITS].T, up, ends


def plain_reduce(early, late, n_dp):
    first = lax.axis_index("section") == 0
    dp = lax.axis_index("dp")
    kept = [jnp.where(first, a, b) for a, b in zip(early, late)]
    got = [swap_sections(jnp.where(first, b, a)) for a, b in zip(early, late)]
    gm, gh, gp = [jnp.stack(pair) for pair in zip(kept, got)]
    width = (U_D + MODEL_WIDTH) // (n_dp * HEADS)
    gm = lax.all_gather(gm, "dp", axis=0)
    gh = lax.all_gather(gh, "dp", axis=0)
    gp = lax.all_to_all(jnp.swapaxes(gp, 0, 1), "dp", split_axis=0, concat_axis=0, tiled=True)
    gp = gp.reshape(2 * n_dp, 1, ADAPTER_RANK, -1)
    n = gp.shape[0]
    chosen = gp[:, 0, 0, width].astype(jnp.int32)
    gm = spread(gm.reshape(n, 6, ADAPTER_RANK, -1).astype(F32), chosen).reshape(6 * ADAPTER_COLUMNS, -1)
    gh = spread(gh.reshape(n, 1, ADAPTER_RANK, -1).astype(F32), chosen).reshape(ADAPTER_COLUMNS, -1)
    gp = spread(gp.astype(F32), chosen).reshape(ADAPTER_COLUMNS, -1)

    def columns(v):
        size = v.shape[0] // n_dp
        v = lax.dynamic_slice_in_dim(v, dp * size, size, 0)
        return lax.all_to_all(v, "seq", split_axis=0, concat_axis=1, tiled=True).T

    return columns(gm), columns(gh)[: VALUE_WIDTH + HIDDEN_UNITS], gp[:, :width]


def local(
    ends,
    mixer_input_weight,
    forget_first_map,
    forget_second_map,
    forget_logit_bias,
    mixer_output_weight,
    feedforward_input_weight,
    feedforward_output_weight,
    adapter_model_first,
    adapter_hidden_first,
    adapter_second_maps,
    lengths,
    dealt_block_order,
    adapter_choice_per_seq,
):
    first = lax.axis_index("section") == 0
    told = jnp.concatenate([dealt_block_order[:, 0], adapter_choice_per_seq, lengths], axis=1)
    told = jnp.where(first, told[0], told[1])
    order = told[:-2]
    n_blocks = order.shape[0]
    at = jnp.arange(n_blocks, dtype=jnp.int32)
    inverse = jnp.sum(at[:, None] * (order[:, None] == at[None, :]).astype(jnp.int32), axis=0)
    meta = jnp.concatenate([order, inverse, told[-2:]])
    n_dp = lax.axis_size("dp")
    own_kernels = n_dp == 4 and lax.axis_size("seq") == 4
    shards = [mixer_input_weight, mixer_output_weight, feedforward_input_weight, feedforward_output_weight]
    small = [
        forget_second_map,
        forget_logit_bias[:, None],
        adapter_model_first,
        adapter_hidden_first,
        adapter_second_maps,
    ]
    if own_kernels:
        weights, x, cotangent, early, late = forward_model(meta, shards, forget_first_map[0].T, ends, small)
    else:
        out = plain_gather(shards, forget_first_map[0].T, ends, small)
        weights, x, cotangent = list(out[:5]) + list(out[7:]), out[5], out[6]
        early = forward(0, meta, x, weights)
        late = forward(1, meta, early[0], weights)
    entry, *grads = backward(meta, cotangent, x, early[0], weights, early[1:], late[1:], n_dp)
    grads_early, grads_late = grads[:3], grads[3:]
    if own_kernels:
        model, hidden, up, results = reduce_gradients(grads_early, grads_late, entry, late[0], n_dp)
    else:
        sent = swap_sections(jnp.where(first, late[0], entry))
        results = jnp.where(first, jnp.stack([entry, sent]), jnp.stack([sent, late[0]]))
        model, hidden, up = plain_reduce(grads_early, grads_late, n_dp)
    return (results[None, :, None], model[None], hidden[None], up[None])


def solution(mesh):
    return jax.shard_map(
        local,
        mesh=mesh,
        in_specs=(
            P("section", None, "dp", "seq", None),
            P("section", "dp", None),
            P("section", "dp", None),
            P("section", None, None),
            P("section", None),
            P("section", "dp", None),
            P("section", "dp", None),
            P("section", "dp", None),
            P("section", None, None),
            P("section", None, None),
            P("section", None, None),
            P(None, "dp"),
            P(None, "dp", None),
            P(None, "dp"),
        ),
        out_specs=(
            P("section", None, "dp", "seq", None),
            P("section", None, ("dp", "seq")),
            P("section", None, ("dp", "seq")),
            P("section", None, ("dp", "seq")),
        ),
        check_vma=False,
    )
```

```python
import functools
import jax
import jax.numpy as jnp
from jax import lax
from jax.experimental import pallas as pl
from jax.experimental.pallas import tpu as pltpu

from jax.sharding import PartitionSpec as P

MODEL_WIDTH = 1024
HEADS = 4
KEY = 512
VALUE_WIDTH = 1024
HIDDEN_UNITS = 2816
FGATE_RANK = 16
GROUP = 64
ADAPTER_RANK = 16
ADAPTERS = 8
ADAPTER_COLUMNS = 128
VMEM_LIMIT = 60 << 20
LINK_BYTES_PER_US = 60e3
SKEW = (2, 4)
DELAYS = (8, 25, 20)
STRIPS = (256, 128, 384, 128)

MESH = pl.DeviceIdType.MESH
ANY = pl.BlockSpec(memory_space=pl.ANY)


BF = jnp.bfloat16
F32 = jnp.float32


def nn(a, b):
    return lax.dot_general(a, b, (((1,), (0,)), ((), ())), preferred_element_type=F32)


def nt(a, b):
    return lax.dot_general(a, b, (((1,), (1,)), ((), ())), preferred_element_type=F32)


def tn(a, b):
    return lax.dot_general(a, b, (((0,), (0,)), ((), ())), preferred_element_type=F32)


def silu_parts(v):
    sig = lax.logistic(v)
    return v * sig, sig


def inverse_rms(v):
    return lax.rsqrt(jnp.mean(v * v, axis=-1, keepdims=True) + 1e-06)


def rms_back(v, grad):
    r = inverse_rms(v)
    n = v * r
    return r * (grad - n * jnp.mean(grad * n, axis=-1, keepdims=True))


def lanes(start, size):
    return pl.ds(pl.multiple_of(start, 128), size)


def rows(start, size):
    return pl.ds(pl.multiple_of(start, size if size <= 64 else 64), size)


def greet_peers(me):
    barrier = pltpu.get_barrier_semaphore()
    for d in range(1, HEADS):
        pl.semaphore_signal(barrier, inc=1, device_id={"seq": me ^ d}, device_id_type=MESH)
    pl.semaphore_wait(barrier, HEADS - 1)


def to_peer(src, dst, ssem, rsem, peer):
    return pltpu.make_async_remote_copy(
        src_ref=src, dst_ref=dst, send_sem=ssem, recv_sem=rsem,
        device_id={"seq": peer}, device_id_type=MESH,
    )


class Local:
    def __init__(self, sems):
        self.sems, self.used, self.open = sems, 0, []

    def start(self, src, dst, wait_at_end=False):
        copy = pltpu.make_async_copy(src, dst, self.sems.at[self.used])
        self.used += 1
        copy.start()
        if wait_at_end:
            self.open.append(copy)
        return copy

    def finish(self):
        for copy in self.open:
            copy.wait()
        self.open = []


def picked(adapter, width):
    row = lax.broadcasted_iota(jnp.int32, (width, ADAPTER_RANK), 0)
    col = lax.broadcasted_iota(jnp.int32, (width, ADAPTER_RANK), 1)
    return (row == adapter * ADAPTER_RANK + col).astype(BF)


def column_mask(adapter):
    col = lax.broadcasted_iota(jnp.int32, (1, ADAPTER_COLUMNS), 1)
    low = adapter * ADAPTER_RANK
    return jnp.logical_and(col >= low, col < low + ADAPTER_RANK).astype(F32)


def lower_triangle(dtype):
    i = lax.broadcasted_iota(jnp.int32, (GROUP, GROUP), 0)
    j = lax.broadcasted_iota(jnp.int32, (GROUP, GROUP), 1)
    return (i >= j).astype(dtype)


DK = KEY // HEADS
DV = VALUE_WIDTH // HEADS
CHUNK = 2 * DK + DV
FROZEN = 2 * KEY + 2 * VALUE_WIDTH
TILE = 256
SCALE = DK ** (-0.5)

U_G = FROZEN
U_U = FROZEN + HIDDEN_UNITS
U_O = FROZEN + 2 * HIDDEN_UNITS
U_D = U_O + MODEL_WIDTH


def live_rows(n, length):
    at = lax.broadcasted_iota(jnp.int32, (GROUP, 1), 0) + n * GROUP
    return (at < length).astype(F32)


def forward_steps(layer, n_blocks, meta, loc, weights, buffers, work, outs, sems):
    w, v = weights, buffers
    (h, y, ad, og, qkv, gl, st, mix, yh, rh, ao, mid, af, gu, dn, normed, send, glsend, fg, state, gated, hidden) = work
    o_y, o_ad, o_og, o_qkv, o_gl, o_st, o_mix, o_yh, o_rh, o_ao, o_mid, o_af, o_gu, o_dn = outs
    ssem, rsem = sems
    me = lax.axis_index("seq")
    T = h.shape[0]
    per = T // GROUP
    adapter = meta[2 * n_blocks]
    length = meta[2 * n_blocks + 1]
    mask = column_mask(adapter)
    am, ah, au, mi, mo, fi, fo = [v[name] for name in ("am", "ah", "au", "mi", "mo", "fi", "fo")]

    def load(*names):
        return [loc.start(w[name], v[name]) for name in names]

    def wait(copies):
        for c in copies:
            c.wait()

    yield "small", 0
    small = load("f1", "f2", "b", "am", "au", "ah")
    yield None, 2
    hv = h[...].astype(F32)
    normed[...] = (hv * inverse_rms(hv)).astype(BF)
    wait(small)
    f1, f2, bias = v["f1"], v["f2"], v["b"]
    z_w = f1.shape[2]
    low = nt(f1[0], normed[:, 0:z_w])
    for j in range(1, f1.shape[0]):
        low += nt(f1[j], normed[:, j * z_w : (j + 1) * z_w])
    glsend[...] = low.astype(BF)
    low_copies = [to_peer(glsend, gl.at[me], ssem.at[0, d], rsem.at[0, d], me ^ d) for d in range(1, HEADS)]
    for c in low_copies:
        c.start()
    gl[me] = glsend[...]
    yield "delay", DELAYS[0]
    for p in range(4):
        cols = pl.ds(p * ADAPTER_COLUMNS, ADAPTER_COLUMNS)
        ad[:, cols] = (nn(normed[...], am[:, cols]) * mask).astype(BF)
    f2h = f2[:, lanes(me * DK, DK)]
    bh = bias[:, lanes(me * DK, DK)]
    for c in low_copies:
        c.wait_recv()
    for src in range(HEADS):
        logit = tn(gl[src], f2h) + bh
        fg[src * T : (src + 1) * T, :] = (jax.nn.log_sigmoid(logit) / 16.0).astype(BF)
    loc.start(gl, o_gl, True)
    loc.start(ad, o_ad, True)
    yield "mi", 0
    wait(load("mi"))

    def project(w_start, p, width):
        cols = lanes(w_start, width)
        return nn(normed[...], mi[:, cols]) + nn(ad[:, p * ADAPTER_COLUMNS : (p + 1) * ADAPTER_COLUMNS], au[:, cols])

    def chunk(head, ref):
        ref[:, 0:DK] = project(head * DK, 0, DK).astype(BF)
        ref[:, DK : 2 * DK] = project(KEY + head * DK, 1, DK).astype(BF)
        ref[:, 2 * DK : CHUNK] = project(2 * KEY + head * DV, 2, DV).astype(BF)

    qkv_copies = []
    for d in (3, 1, 2):
        yield None, 1
        chunk(me ^ d, send.at[d - 1])
        copy = to_peer(send.at[d - 1], qkv.at[rows(me * T, T)], ssem.at[1, d], rsem.at[1, d], me ^ d)
        copy.start()
        qkv_copies.append(copy)
    yield None, 1
    chunk(me, qkv.at[rows(me * T, T)])
    yield None, 1
    for j in range(VALUE_WIDTH // TILE):
        og[:, j * TILE : (j + 1) * TILE] = project(2 * KEY + VALUE_WIDTH + j * TILE, 3, TILE)
    loc.start(og, o_og, True)
    yield "delay", DELAYS[1]
    for c in qkv_copies:
        c.wait_recv()
    loc.start(qkv, o_qkv, True)
    tri = lower_triangle(BF)
    causal = lower_triangle(F32)
    state[...] = jnp.zeros_like(state)

    def advance(n, carry):
        at = pl.ds(meta[n_blocks + n] * GROUP, GROUP)
        summed = nn(tri, fg[at, :])
        total = summed[GROUP - 1 : GROUP]
        k = qkv[at, DK : 2 * DK].astype(F32) * live_rows(n, length)
        ku = (k * jnp.exp(total - summed)).astype(BF)
        update = tn(qkv[at, 2 * DK : CHUNK], ku)
        now = state[...]
        st[n] = now.astype(BF)
        state[...] = jnp.exp(total) * now + update
        return carry

    lax.fori_loop(0, n_blocks, advance, 0, unroll=8)
    loc.start(st, o_st, True)
    yield None, 4

    def mix_block(p):
        n = meta[p]
        at = rows(p * GROUP, GROUP)
        summed = nn(tri, fg[at, :])
        middle = summed[GROUP // 2 : GROUP // 2 + 1]
        q = qkv[at, 0:DK].astype(F32) * SCALE
        k = qkv[at, DK : 2 * DK].astype(F32) * live_rows(n, length)
        qe = (q * jnp.exp(summed - middle)).astype(BF)
        ke = (k * jnp.exp(middle - summed)).astype(BF)
        scores = jnp.where(causal > 0, nt(qe, ke), 0.0).astype(BF)
        o = nn(scores, qkv[at, 2 * DK : CHUNK]) + nt((q * jnp.exp(summed)).astype(BF), st[n])
        r = lax.rsqrt(jnp.mean(o * o, axis=-1, keepdims=True) + 1.0)
        yh[at, :] = (o * r).astype(BF)
        rh[at, :] = jnp.broadcast_to(r, (GROUP, DK))

    mix_copies = []
    for d in (3, 1, 2):
        yield None, 2
        peer = me ^ d
        lax.fori_loop(0, per, lambda j, c, peer=peer: (mix_block(peer * per + j), c)[1], 0, unroll=True)
        copy = to_peer(yh.at[rows(peer * T, T)], mix.at[me], ssem.at[2, d], rsem.at[2, d], peer)
        copy.start()
        mix_copies.append(copy)
    yield None, 2
    lax.fori_loop(0, per, lambda j, c: (mix_block(me * per + j), c)[1], 0, unroll=True)
    mix[me] = yh[rows(me * T, T), :]
    loc.start(yh, o_yh, True)
    loc.start(rh, o_rh, True)
    yield "mo", 0
    l_mo = load("mo")
    yield "delay", DELAYS[2]
    for c in mix_copies:
        c.wait_recv()
    loc.start(mix, o_mix, True)
    for hd in range(HEADS):
        cols = slice(hd * DV, (hd + 1) * DV)
        gated[:, cols] = (mix[hd].astype(F32) * silu_parts(og[:, cols])[0]).astype(BF)
    ao[...] = (nn(gated[...], ah[0:VALUE_WIDTH, :]) * mask).astype(BF)
    wait(l_mo)
    for j in range(MODEL_WIDTH // TILE):
        cols = slice(j * TILE, (j + 1) * TILE)
        mid[:, cols] = (
            h[:, cols].astype(F32) + nn(gated[...], mo[:, cols]) + nn(ao[...], au[:, U_O + j * TILE : U_O + (j + 1) * TILE])
        )
    loc.start(ao, o_ao, True)
    loc.start(mid, o_mid, True)
    yield None, 1
    mv = mid[...]
    normed[...] = (mv * inverse_rms(mv)).astype(BF)
    for p in range(2):
        cols = slice(p * ADAPTER_COLUMNS, (p + 1) * ADAPTER_COLUMNS)
        wide = slice((4 + p) * ADAPTER_COLUMNS, (5 + p) * ADAPTER_COLUMNS)
        af[:, cols] = (nn(normed[...], am[:, wide]) * mask).astype(BF)
    loc.start(af, o_af, True)
    yield "fi", 0
    wait(load("fi"))

    def up_tile(i, carry):
        a, b = lanes(i * TILE, TILE), lanes(HIDDEN_UNITS + i * TILE, TILE)
        gate = nn(normed[...], fi[:, a]) + nn(af[:, 0:ADAPTER_COLUMNS], au[:, lanes(U_G + i * TILE, TILE)])
        up = nn(normed[...], fi[:, b]) + nn(af[:, ADAPTER_COLUMNS:], au[:, lanes(U_U + i * TILE, TILE)])
        gu[:, a] = gate.astype(gu.dtype)
        gu[:, b] = up.astype(gu.dtype)
        hidden[:, a] = (silu_parts(gate)[0] * up).astype(BF)
        return carry

    tiles = HIDDEN_UNITS // TILE
    yield None, 3
    lax.fori_loop(0, tiles // 2, up_tile, 0)
    yield None, 3
    lax.fori_loop(tiles // 2, tiles, up_tile, 0)
    loc.start(gu, o_gu, True)
    dn[...] = (nn(hidden[...], ah[VALUE_WIDTH:, :]) * mask).astype(BF)
    loc.start(dn, o_dn, True)
    yield "fo", 0
    wait(load("fo"))
    yield None, 3
    for j in range(MODEL_WIDTH // TILE):
        cols = slice(j * TILE, (j + 1) * TILE)
        y[:, cols] = (
            mid[:, cols] + nn(hidden[...], fo[:, cols]) + nn(dn[...], au[:, U_D + j * TILE : U_D + (j + 1) * TILE])
        ).astype(BF)
    loc.start(y, o_y, True)
    loc.finish()
    for c in low_copies + qkv_copies + mix_copies:
        c.wait_send()


NAMES = ("mi", "mo", "fi", "fo", "f1", "f2", "b", "am", "ah", "au")


def forward_kernel(layer, n_blocks, meta, h_in, *refs):
    n_w, n_out = len(NAMES), 14
    ins, outs = refs[:n_w], refs[n_w : n_w + n_out]
    refs = refs[n_w + n_out :]
    buffers, work = dict(zip(NAMES, refs[:n_w])), refs[n_w:-3]
    lsem, ssem, rsem = refs[-3:]
    loc = Local(lsem)
    first = loc.start(h_in, work[0])
    greet_peers(lax.axis_index("seq"))
    first.wait()
    weights = {name: ref.at[layer] for name, ref in zip(NAMES, ins)}
    for _ in forward_steps(layer, n_blocks, meta, loc, weights, buffers, work, outs, (ssem, rsem)):
        pass


def weight_scratch(weights):
    return [pltpu.VMEM(w.shape[1:], w.dtype) for w in weights]


def saved_shapes(T, L, n_blocks):
    s = lambda shape, dtype=BF: (shape, dtype)
    return [
        s((T, MODEL_WIDTH)),
        s((T, 4 * ADAPTER_COLUMNS)),
        s((T, VALUE_WIDTH), F32),
        s((L, CHUNK)),
        s((HEADS, FGATE_RANK, T)),
        s((n_blocks, DV, DK)),
        s((HEADS, T, DV)),
        s((L, DV)),
        s((L, DK), F32),
        s((T, ADAPTER_COLUMNS)),
        s((T, MODEL_WIDTH), F32),
        s((T, 2 * ADAPTER_COLUMNS)),
        s((T, 2 * HIDDEN_UNITS)),
        s((T, ADAPTER_COLUMNS)),
    ]


def work_scratch(T, L, saved):
    vm = pltpu.VMEM
    return [vm((T, MODEL_WIDTH), BF)] + [vm(*s) for s in saved] + [
        vm((T, MODEL_WIDTH), BF),
        vm((HEADS - 1, T, CHUNK), BF),
        vm((FGATE_RANK, T), BF),
        vm((L, DK), BF),
        vm((DV, DK), F32),
        vm((T, VALUE_WIDTH), BF),
        vm((T, HIDDEN_UNITS), BF),
    ]


def forward(layer, meta, h, weights):
    T = h.shape[0]
    L = T * HEADS
    n_blocks = L // GROUP
    saved = saved_shapes(T, L, n_blocks)
    dma = pltpu.SemaphoreType.DMA
    return pl.pallas_call(
        functools.partial(forward_kernel, layer, n_blocks),
        out_shape=[jax.ShapeDtypeStruct(*s) for s in saved],
        in_specs=[pl.BlockSpec(memory_space=pltpu.SMEM)] + [ANY] * (1 + len(weights)),
        out_specs=[ANY] * len(saved),
        scratch_shapes=weight_scratch(weights)
        + work_scratch(T, L, saved)
        + [dma((1 + len(weights) + len(saved),)), dma((3, HEADS)), dma((3, HEADS))],
        compiler_params=pltpu.CompilerParams(
            collective_id=1 + layer, has_side_effects=True, vmem_limit_bytes=VMEM_LIMIT
        ),
    )(meta, h, *weights)


def backward_kernel(n_blocks, meta, d_in, *refs):
    refs = list(refs)

    def take(n):
        out = refs[:n]
        del refs[:n]
        return out

    n_w = len(NAMES)
    inputs = take(2)
    sources = take(n_w)
    kept = [take(13), take(13)]
    (e_out,) = take(1)
    grad_outs = [take(3), take(3)]
    d, h = take(2)
    mi, mo, fi, fo, f1, f2, bias, am, ah, au = take(n_w)
    ad, og, qkv, gl, st, mix, yh, rh, ao, mid, af, gu, dn = take(13)
    (e,) = take(1)
    grad_sums = [take(3), take(3)]
    (gm, gh, gp, gps, rgm2, rgh2, rgp2, hidden, wide, gad, big, grad, dog, sendm, dmr, logit, fg, gstate, gt, dt, don,
     hidden_gated, sendq, dqkv, dlog, sendl, dlr) = take(27)
    dproj = wide.at[:, pl.ds(MODEL_WIDTH, FROZEN)]
    lsem, ssem2, rsem2, gssem2, grsem2 = take(5)
    me = lax.axis_index("seq")
    loc = Local(lsem)
    buffers = dict(zip(NAMES, (mi, mo, fi, fo, f1, f2, bias, am, ah, au)))
    acts = dict(ad=ad, og=og, qkv=qkv, gl=gl, st=st, mix=mix, yh=yh, rh=rh, ao=ao, mid=mid, af=af, gu=gu, dn=dn)
    on_the_way = [{}, {}]

    def fetch(layer, *names):
        for name in names:
            if name == "d":
                c = loc.start(d_in, d)
            elif name == "h":
                c = loc.start(inputs[layer], h)
            elif name in buffers:
                c = loc.start(sources[NAMES.index(name)].at[layer], buffers[name])
            else:
                c = loc.start(kept[layer][list(acts).index(name)], acts[name])
            on_the_way[layer][name] = c

    barrier = pltpu.get_barrier_semaphore()
    for k in range(1, HEADS):
        pl.semaphore_signal(barrier, inc=1, device_id={"seq": me ^ k}, device_id_type=MESH)
    fetch(1, "d", "au", "dn", "ah", "fo", "gu")
    fetch(1, "fi", "am", "mid", "mo", "og", "mix", "f2", "b", "gl", "yh", "rh", "qkv", "st", "ao", "af", "mi", "f1", "ad", "h")
    pl.semaphore_wait(barrier, HEADS - 1)
    finish = None
    for layer in (1, 0):
        def arrive(*names, layer=layer):
            for name in names:
                on_the_way[layer][name].wait()

        finish = backward_layer(
            layer, n_blocks, meta, me, loc, arrive, fetch if layer == 1 else None, finish, grad_outs[layer],
            d, h, mi, mo, fi, fo, f1, f2, bias, am, ah, au,
            ad, og, qkv, gl, st, mix, yh, rh, ao, mid, af, gu, dn,
            e, *grad_sums[layer], gm, gh, gp, gps, rgm2.at[layer], rgh2.at[layer], rgp2.at[layer],
            hidden, wide, gad, big, grad, dog, sendm, dmr, logit, fg, gstate, gt, dt, don,
            hidden_gated, sendq, dqkv, dlog, sendl, dlr, dproj,
            ssem2.at[layer], rsem2.at[layer], gssem2.at[layer], grsem2.at[layer],
        )
    loc.start(e, e_out, True)
    finish()
    loc.finish()


def backward_layer(
    layer, n_blocks, meta, me, loc, arrive, fetch, window, grad_outs,
    d, h, mi, mo, fi, fo, f1, f2, bias, am, ah, au,
    ad, og, qkv, gl, st, mix, yh, rh, ao, mid, af, gu, dn,
    e, sgm, sgh, sgp, gm, gh, gp, gps, rgm, rgh, rgp,
    hidden, wide, gad, big, grad, dog, sendm, dmr, logit, fg, gstate, gt, dt, don,
    hidden_gated, sendq, dqkv, dlog, sendl, dlr, dproj,
    ssem, rsem, gssem, grsem,
):
    prefetch = (lambda *names: fetch(0, *names)) if fetch else (lambda *names: None)
    T = h.shape[0]
    per = T // GROUP
    adapter = meta[2 * n_blocks]
    length = meta[2 * n_blocks + 1]
    mask = column_mask(adapter)
    pick = picked(adapter, ADAPTER_COLUMNS)

    def narrow(v):
        return nn(v, pick).astype(BF)

    def outer(u, v):
        return tn(narrow(u), v).astype(BF)

    n_dp, width, padded = gps.shape[1], gp.shape[1] // (HEADS * gps.shape[1]), gps.shape[3]
    quarter, hidden_quarter = MODEL_WIDTH // HEADS, gh.shape[1] // HEADS
    n_late = -(-FROZEN // (HEADS * width))
    mix_rows = 4 * ADAPTER_RANK

    def place(dps):
        for i in dps:
            for q in range(HEADS):
                piece = gp[:, (i * HEADS + q) * width : (i * HEADS + q + 1) * width]
                gps[q, i] = jnp.concatenate([piece, jnp.zeros((ADAPTER_RANK, padded - width), BF)], axis=1)

    def grad_copies(late):
        copies = []
        at = slice(0, mix_rows) if late else slice(mix_rows, 6 * ADAPTER_RANK)
        dps = slice(0, n_late) if late else slice(n_late, n_dp)
        for k in range(1, HEADS):
            peer = me ^ k
            pairs = [
                (gm.at[at, lanes(peer * quarter, quarter)], rgm.at[k - 1, at]),
                (gps.at[peer, dps], rgp.at[k - 1, dps]),
            ]
            if not late:
                pairs.append((gh.at[:, lanes(peer * hidden_quarter, hidden_quarter)], rgh.at[k - 1]))
            for i, (a, b) in enumerate(pairs):
                j = i if late else 2 + i
                copies.append(to_peer(a, b, gssem.at[j, k], grsem.at[j, k], peer))
        return copies

    arrive("au", "dn") if layer == 0 else arrive("d", "au", "dn")
    gdown = (nt(d[...], au[:, U_D : U_D + MODEL_WIDTH]).astype(BF).astype(F32) * mask).astype(BF)
    gdown16 = narrow(gdown)
    if layer == 1:
        gh[:, VALUE_WIDTH + HIDDEN_UNITS :] = jnp.zeros((ADAPTER_RANK, gh.shape[1] - VALUE_WIDTH - HIDDEN_UNITS), BF)
    gp[:, U_D : U_D + MODEL_WIDTH] = outer(dn[...], d[...])
    gad[...] = gdown
    arrive("ah", "fo", "gu")

    def down_tile(i, carry):
        a, b = lanes(i * TILE, TILE), lanes(HIDDEN_UNITS + i * TILE, TILE)
        at = pl.ds(pl.multiple_of(i * TILE, TILE), TILE)
        dh = nt(d[...], fo[at, :]) + nt(gad[...], ah[pl.ds(pl.multiple_of(VALUE_WIDTH + i * TILE, TILE), TILE), :])
        gate, up = gu[:, a].astype(F32), gu[:, b].astype(F32)
        act, sig = silu_parts(gate)
        hidden[:, a] = (act * up).astype(BF)
        wide[:, a] = (dh * up * sig * (1.0 + gate * (1.0 - sig))).astype(BF)
        wide[:, b] = (dh * act).astype(BF)
        return carry

    lax.fori_loop(0, HIDDEN_UNITS // TILE, down_tile, 0)
    prefetch("dn", "fo", "gu")
    gate_cols, up_cols = slice(0, HIDDEN_UNITS), slice(HIDDEN_UNITS, 2 * HIDDEN_UNITS)
    gg = (nt(wide[:, gate_cols], au[:, U_G : U_G + HIDDEN_UNITS]).astype(BF).astype(F32) * mask).astype(BF)
    gu2 = (nt(wide[:, up_cols], au[:, U_U : U_U + HIDDEN_UNITS]).astype(BF).astype(F32) * mask).astype(BF)
    gad2 = jnp.concatenate([gg, gu2], axis=1)
    big[:, 0 : 2 * ADAPTER_COLUMNS] = gad2
    arrive("fi", "am")

    def wide_tile(i, carry):
        at = pl.ds(pl.multiple_of(i * TILE, TILE), TILE)
        grad[:, lanes(i * TILE, TILE)] = nt(wide[...], fi[at, :]) + nt(
            big[:, 0 : 2 * ADAPTER_COLUMNS], am[at, 4 * ADAPTER_COLUMNS :]
        )
        return carry

    lax.fori_loop(0, MODEL_WIDTH // TILE, wide_tile, 0)
    prefetch("fi")
    arrive("mid")
    mv = mid[...]
    grad_mid = d[...].astype(F32) + rms_back(mv, grad[...])
    grad[...] = grad_mid
    attn = grad_mid.astype(BF)
    e[...] = attn
    gout = (nt(attn, au[:, U_O : U_O + MODEL_WIDTH]).astype(BF).astype(F32) * mask).astype(BF)
    gad[...] = gout
    arrive("mo", "og", "mix")

    def gate_back(head, out):
        at = rows(head * DV, DV)
        cols = lanes(head * DV, DV)
        gg_ = nt(e[...], mo[at, :]) + nt(gad[...], ah[at, :])
        o = og[:, cols]
        act, sig = silu_parts(o)
        out[...] = (gg_ * act).astype(BF)
        m = mix[head].astype(F32)
        dog[:, cols] = (gg_ * m * sig * (1.0 + o * (1.0 - sig))).astype(BF)
        hidden_gated[:, cols] = (m * act).astype(BF)

    mix_copies = []
    for k in (3, 1, 2):
        peer = me ^ k
        gate_back(peer, sendm.at[k - 1])
        copy = to_peer(sendm.at[k - 1], dmr.at[rows(me * T, T)], ssem.at[0, k], rsem.at[0, k], peer)
        copy.start()
        mix_copies.append(copy)
    gate_back(me, dmr.at[rows(me * T, T)])

    prefetch("mo", "ah", "og", "mix")
    if window:
        window()
    arrive("af")
    mv = mid[...]
    normed_mid = (mv * inverse_rms(mv)).astype(BF)
    gm[4 * ADAPTER_RANK : 5 * ADAPTER_RANK, :] = outer(big[:, 0:ADAPTER_COLUMNS], normed_mid)
    gm[5 * ADAPTER_RANK : 6 * ADAPTER_RANK, :] = outer(big[:, ADAPTER_COLUMNS : 2 * ADAPTER_COLUMNS], normed_mid)
    gp[:, U_G : U_G + HIDDEN_UNITS] = outer(af[:, 0:ADAPTER_COLUMNS], wide[:, gate_cols])
    gp[:, U_U : U_U + HIDDEN_UNITS] = outer(af[:, ADAPTER_COLUMNS:], wide[:, up_cols])
    arrive("f2", "b", "gl", "yh", "rh", "qkv", "st")
    f2h = f2[:, lanes(me * DK, DK)]
    bh = bias[:, lanes(me * DK, DK)]
    for src in range(HEADS):
        lg = tn(gl[src], f2h) + bh
        logit[src * T : (src + 1) * T, :] = lg
        fg[src * T : (src + 1) * T, :] = (jax.nn.log_sigmoid(lg) / 16.0).astype(BF)
    tri = lower_triangle(BF)
    causal = lower_triangle(F32)
    for c in mix_copies:
        c.wait_recv()
    gstate[...] = jnp.zeros_like(gstate)

    def retreat(i, carry):
        n = n_blocks - 1 - i
        at = pl.ds(meta[n_blocks + n] * GROUP, GROUP)
        here = rows(n * GROUP, GROUP)
        dm = dmr[at, :].astype(F32)
        yv = yh[at, :].astype(F32)
        r = rh[at, 0:1]
        do = (r * (dm - yv * jnp.mean(dm * yv, axis=-1, keepdims=True))).astype(BF)
        don[here, :] = do
        summed = nn(tri, fg[at, :])
        total = jnp.exp(summed[GROUP - 1 : GROUP])
        qs = (qkv[at, 0:DK].astype(F32) * SCALE * jnp.exp(summed)).astype(BF)
        now = gstate[...]
        gt[n] = now.astype(BF)
        decayed = total * now
        dt[n] = jnp.sum(decayed * st[n].astype(F32), axis=0, keepdims=True)
        gstate[...] = decayed + tn(do, qs)
        return carry

    lax.fori_loop(0, n_blocks, retreat, 0, unroll=8)

    def back_block(p, out, j):
        n = meta[p]
        at = rows(p * GROUP, GROUP)
        here = pl.ds(n * GROUP, GROUP)
        to = rows(j * GROUP, GROUP)
        live = live_rows(n, length)
        summed = nn(tri, fg[at, :])
        middle = summed[GROUP // 2 : GROUP // 2 + 1]
        total = summed[GROUP - 1 : GROUP]
        e1, e2 = jnp.exp(summed - middle), jnp.exp(middle - summed)
        es, eu = jnp.exp(summed), jnp.exp(total - summed)
        q = qkv[at, 0:DK].astype(F32) * SCALE
        k = qkv[at, DK : 2 * DK].astype(F32) * live
        v = qkv[at, 2 * DK : CHUNK]
        do, state_t, grad_t = don[here, :], st[n], gt[n]
        qe, ke, qs, ku = q * e1, k * e2, q * es, k * eu
        qeb, keb = qe.astype(BF), ke.astype(BF)
        scores = jnp.where(causal > 0, nt(qeb, keb), 0.0).astype(BF)
        dscores = jnp.where(causal > 0, nt(do, v), 0.0).astype(BF)
        dv = tn(scores, do) + nt(ku.astype(BF), grad_t)
        dqs = nn(do, state_t)
        dku = nn(v, grad_t)
        dqe = nn(dscores, keb)
        dke = tn(dscores, qeb)
        out[to, 0:DK] = (SCALE * (dqe * e1 + dqs * es)).astype(BF)
        out[to, DK : 2 * DK] = (live * (dke * e2 + dku * eu)).astype(BF)
        out[to, 2 * DK : CHUNK] = dv.astype(BF)
        kk = dku * ku
        dsum = dqe * qe + dqs * qs - dke * ke - kk
        dtotal = dt[n] + jnp.sum(kk, axis=0, keepdims=True)
        high = dsum.astype(BF)
        lowp = (dsum - high.astype(F32)).astype(BF)
        df = tn(tri, high) + tn(tri, lowp) + dtotal
        df = df.astype(BF).astype(F32)
        dlog[to, :] = (df * lax.logistic(-logit[at, :]) / 16.0).astype(BF)

    q_copies = []

    def back_rows(dest, out, low_out):
        lax.fori_loop(0, per, lambda j, c: (back_block(dest * per + j, out, j), c)[1], 0, unroll=True)
        low_out[...] = nt(f2h, dlog[...]).astype(BF)

    for k in (3, 1, 2):
        peer = me ^ k
        back_rows(peer, sendq.at[k - 1], sendl.at[k - 1])
        copies = (
            to_peer(sendq.at[k - 1], dqkv.at[me], ssem.at[1, k], rsem.at[1, k], peer),
            to_peer(sendl.at[k - 1], dlr.at[me], ssem.at[2, k], rsem.at[2, k], peer),
        )
        for copy in copies:
            copy.start()
        q_copies += copies
    back_rows(me, dqkv.at[me], dlr.at[me])

    arrive("ao")
    gh[:, VALUE_WIDTH : VALUE_WIDTH + HIDDEN_UNITS] = tn(gdown16, hidden[...]).astype(BF)
    gp[:, U_O : U_O + MODEL_WIDTH] = outer(ao[...], e[...])
    gh[:, 0:VALUE_WIDTH] = outer(gad[...], hidden_gated[...])
    place(range(n_late, n_dp))
    grads = grad_copies(False)
    for c in grads:
        c.start()
    prefetch("mid", "af", "ao", "qkv", "gl", "st", "yh", "rh", "f2", "b")

    arrive("mi", "f1", "ad", "h")
    hv = h[...].astype(F32)
    hr = inverse_rms(hv)
    big[...] = (hv * hr).astype(BF)
    for c in q_copies:
        c.wait_recv()
    for hd in range(HEADS):
        dproj[:, hd * DK : (hd + 1) * DK] = dqkv[hd, :, 0:DK]
        dproj[:, KEY + hd * DK : KEY + (hd + 1) * DK] = dqkv[hd, :, DK : 2 * DK]
        dproj[:, 2 * KEY + hd * DV : 2 * KEY + (hd + 1) * DV] = dqkv[hd, :, 2 * DK : CHUNK]
    dproj[:, 2 * KEY + VALUE_WIDTH :] = dog[...]
    dlow = dlr[0].astype(F32)
    for hd in range(1, HEADS):
        dlow += dlr[hd].astype(F32)
    dlowb = dlow.astype(BF)
    spans = ((0, KEY), (KEY, KEY), (2 * KEY, VALUE_WIDTH), (2 * KEY + VALUE_WIDTH, VALUE_WIDTH))
    for p, (start, span) in enumerate(spans):
        block = slice(p * ADAPTER_COLUMNS, (p + 1) * ADAPTER_COLUMNS)
        piece = dproj[:, start : start + span]
        ga = (nt(piece, au[:, start : start + span]).astype(BF).astype(F32) * mask).astype(BF)
        wide[:, block] = ga
        gm[p * ADAPTER_RANK : (p + 1) * ADAPTER_RANK, :] = outer(ga, big[...])
        gp[:, start : start + span] = outer(ad[:, block], piece)
    place(range(n_late))
    late_grads = grad_copies(True)
    for c in late_grads:
        c.start()
    z_w = f1.shape[2]
    tiles = f1.shape[0]
    back = []
    for j in range(tiles):
        at = slice(j * z_w, (j + 1) * z_w)
        back.append(
            nt(dproj[...], mi[at, :]) + nt(wide[:, 0 : 4 * ADAPTER_COLUMNS], am[at, 0 : 4 * ADAPTER_COLUMNS]) + tn(dlowb, f1[j])
        )
    dn_ = jnp.concatenate(back, axis=1)
    n = hv * hr
    e[...] = (grad[...] + hr * (dn_ - n * jnp.mean(dn_ * n, axis=-1, keepdims=True))).astype(BF)
    if layer == 1:
        d[...] = e[...]
    prefetch("au", "am", "mi", "f1", "ad", "h")
    grads += late_grads
    for c in mix_copies + q_copies:
        c.wait_send()

    def finish():
        for c in grads:
            c.wait_recv()

        def summed_over_seq(own, got):
            total = own.astype(F32)
            for k in range(HEADS - 1):
                total += got[k].astype(F32)
            return total.astype(BF)

        sgm[...] = summed_over_seq(gm[:, lanes(me * quarter, quarter)], rgm)
        sgh[...] = summed_over_seq(gh[:, lanes(me * hidden_quarter, hidden_quarter)], rgh)
        spot = lax.broadcasted_iota(jnp.int32, (ADAPTER_RANK, padded), 1)
        for i in range(n_dp):
            total = gps[me, i].astype(F32)
            for k in range(HEADS - 1):
                total += rgp[k, i].astype(F32)
            sgp[i] = jnp.where(spot == width, adapter.astype(F32), total).astype(BF)
        for c in grads:
            c.wait_send()
        for a, b in zip((sgm, sgh, sgp), grad_outs):
            loc.start(a, b, True)

    return finish


def backward(meta, d, x, h1, weights, early, late, n_dp):
    T = x.shape[0]
    L = T * HEADS
    n_blocks = L // GROUP
    raised = U_D + MODEL_WIDTH
    padded = (raised // (n_dp * HEADS) // 128 + 1) * 128
    quarter = MODEL_WIDTH // HEADS
    hidden_quarter = -(-(VALUE_WIDTH + HIDDEN_UNITS) // (HEADS * 128)) * 128
    outs = [
        ((T, MODEL_WIDTH), BF),
        ((6 * ADAPTER_RANK, quarter), BF),
        ((ADAPTER_RANK, hidden_quarter), BF),
        ((n_dp, ADAPTER_RANK, padded), BF),
    ]
    vm = pltpu.VMEM
    dma = pltpu.SemaphoreType.DMA
    return pl.pallas_call(
        functools.partial(backward_kernel, n_blocks),
        out_shape=[jax.ShapeDtypeStruct(*s) for s in outs[:1] + 2 * outs[1:]],
        in_specs=[pl.BlockSpec(memory_space=pltpu.SMEM)] + [ANY] * (3 + len(weights) + 2 * len(early)),
        out_specs=[ANY] * (2 * len(outs) - 1),
        scratch_shapes=[vm(d.shape, d.dtype), vm(x.shape, x.dtype)]
        + weight_scratch(weights)
        + [vm(s.shape, s.dtype) for s in early]
        + [vm(*s) for s in outs[:1] + 2 * outs[1:]]
        + [
            vm((6 * ADAPTER_RANK, MODEL_WIDTH), BF),
            vm((ADAPTER_RANK, HEADS * hidden_quarter), BF),
            vm((ADAPTER_RANK, raised), BF),
            vm((HEADS, n_dp, ADAPTER_RANK, padded), BF),
            vm((2, HEADS - 1, 6 * ADAPTER_RANK, quarter), BF),
            vm((2, HEADS - 1, ADAPTER_RANK, hidden_quarter), BF),
            vm((2, HEADS - 1, n_dp, ADAPTER_RANK, padded), BF),
            vm((T, HIDDEN_UNITS), BF),
            vm((T, 2 * HIDDEN_UNITS), BF),
            vm((T, ADAPTER_COLUMNS), BF),
            vm((T, MODEL_WIDTH), BF),
            vm((T, MODEL_WIDTH), F32),
            vm((T, VALUE_WIDTH), BF),
            vm((HEADS - 1, T, DV), BF),
            vm((L, DV), BF),
            vm((L, DK), F32),
            vm((L, DK), BF),
            vm((DV, DK), F32),
            vm((n_blocks, DV, DK), BF),
            vm((n_blocks, 1, DK), F32),
            vm((L, DV), BF),
            vm((T, VALUE_WIDTH), BF),
            vm((HEADS - 1, T, CHUNK), BF),
            vm((HEADS, T, CHUNK), BF),
            vm((T, DK), BF),
            vm((HEADS - 1, FGATE_RANK, T), BF),
            vm((HEADS, FGATE_RANK, T), BF),
            dma((2 * (2 + len(weights) + len(early) + len(outs)),)),
            dma((2, 3, HEADS)),
            dma((2, 3, HEADS)),
            dma((2, 5, HEADS)),
            dma((2, 5, HEADS)),
        ],
        compiler_params=pltpu.CompilerParams(
            collective_id=3, has_side_effects=True, vmem_limit_bytes=VMEM_LIMIT
        ),
        cost_estimate=pl.CostEstimate(flops=4 * T * 16_000_000, bytes_accessed=90 << 20, transcendentals=T * 16384),
    )(meta, d, x, h1, *weights, *early, *late)


UNITS = [(layer, w) for layer in range(2) for w in range(4)]


def model_kernel(n_blocks, meta, *refs):
    n_w, n_small, n_saved, n_z = 4, 5, 14, 4
    refs = list(refs)

    def take(n):
        out = refs[:n]
        del refs[:n]
        return out

    shards = take(n_w)
    f1_ref, ends_ref = take(2)
    small = take(n_small)
    outs = take(n_w)
    (f1_out,) = take(1)
    (x_out, c_out) = take(2)
    small_out = take(n_small)
    saved = [take(n_saved), take(n_saved)]
    held = take(n_w)
    held_f1 = take(1)[0]
    held_small = take(n_small)
    work = take(1 + n_saved + 7)
    qkv2, gl2, mix2, held_ends = take(4)
    (ins, zs, zr, ts, tr, xs, xr, ys, yr, fxs, fxr, fys, fyr, cs, cr, own, ms, mr, es, er, f1s, f1r, f1c, lsem, ssem, rsem) = take(26)
    core, z, s = lax.axis_index("section"), lax.axis_index("dp"), lax.axis_index("seq")
    other = 1 - core

    def remote(src, dst, send_sem, recv_sem, **where):
        return pltpu.make_async_remote_copy(
            src_ref=src, dst_ref=dst, send_sem=send_sem, recv_sem=recv_sem, device_id=where, device_id_type=MESH
        )

    def height(w):
        return shards[w].shape[1]

    def staged(w):
        return held[w].at[pl.ds(pl.multiple_of(z * height(w), 16), height(w))]

    fetch = [pltpu.make_async_copy(shards[w].at[0], staged(w), ins.at[w]) for w in range(n_w)]
    fetch += [pltpu.make_async_copy(a.at[0], b, ins.at[n_w + i]) for i, (a, b) in enumerate(zip(small, held_small))]
    fetch.append(pltpu.make_async_copy(ends_ref.at[0, :, 0], held_ends, ins.at[n_w + n_small]))
    fetch.append(pltpu.make_async_copy(f1_ref, held_f1.at[z], ins.at[n_w + n_small + 1]))
    for f in fetch:
        f.start()

    barrier = pltpu.get_barrier_semaphore()
    greeted = [dict(section=other)] + [dict(seq=s ^ k) for k in range(1, HEADS)]
    greeted += [dict(dp=lax.rem(z + gap, n_z)) for gap in range(1, n_z)]
    for where in greeted:
        pl.semaphore_signal(barrier, inc=1, device_id=where, device_id_type=MESH)
    pl.semaphore_wait(barrier, len(greeted))

    def part(u, j, start, size, strip=False):
        layer, w = UNITS[u]
        cols = shards[w].shape[2] // 2
        at, wide = (cols - STRIPS[w], STRIPS[w]) if strip else (0, cols - STRIPS[w])
        return outs[w].at[layer, pl.ds(pl.multiple_of(j * height(w) + start, 16), size), lanes(core * cols + at, wide)]

    def piece(u, j, q):
        r = height(UNITS[u][1])
        return part(u, j, q * (r // 4), r // 4)

    def half(u, j, q, low):
        r = height(UNITS[u][1])
        cut = (r // 8 + 15) // 16 * 16
        start, size = (0, cut) if low else (cut, r // 4 - cut)
        return part(u, j, q * (r // 4) + start, size)

    def block(u, j):
        layer, w = UNITS[u]
        cols = shards[w].shape[2] // 2
        return outs[w].at[layer, pl.ds(pl.multiple_of(j * height(w), 16), height(w)), lanes(core * cols, cols)]

    def whole_block(layer, w):
        return outs[w].at[layer, pl.ds(pl.multiple_of(z * height(w), 16), height(w))]

    def step(d):
        return 1 if d == 0 else -1

    def can_send(d, t):
        has_next = (z < n_z - 1) if d == 0 else (z > 0)
        first = z - step(d) * (t - 1)
        return jnp.logical_and(has_next, jnp.logical_and(first >= 0, first < n_z))

    def gets(d, t):
        first = z - step(d) * t
        return jnp.logical_and(first >= 0, first < n_z)

    def origin(d, t):
        return z - step(d) * t

    def z_copy(u, d, t):
        ref = piece(u, z - step(d) * (t - 1), s)
        return remote(ref, ref, zs.at[u, d, t - 1], zr.at[u, d, t - 1], dp=z + step(d))

    def t_copy(u, d, t):
        ref = part(u, z - step(d) * (t - 1), 0, height(UNITS[u][1]), True)
        return remote(ref, ref, ts.at[u, d, t - 1], tr.at[u, d, t - 1], dp=z + step(d))

    def x_copy(u, d, t):
        ref = piece(u, origin(d, t), s)
        return remote(ref, ref, xs.at[u, d, t - 1], xr.at[u, d, t - 1], seq=s ^ 1)

    def y_copy(u, d, t):
        ref = piece(u, origin(d, t), s)
        return remote(ref, ref, ys.at[u, d, t - 1], yr.at[u, d, t - 1], seq=s ^ 2)

    def fx_copy(u, d, t):
        ref = half(u, origin(d, t), s ^ 2, False)
        return remote(ref, ref, fxs.at[u, d, t - 1], fxr.at[u, d, t - 1], seq=s ^ 1)

    def fy_copy(u, d, t):
        ref = half(u, origin(d, t), s ^ 1, True)
        return remote(ref, ref, fys.at[u, d, t - 1], fyr.at[u, d, t - 1], seq=s ^ 2)

    def c_copy(u, d, t):
        ref = block(u, origin(d, t))
        return remote(ref, ref, cs.at[u, d, t - 1], cr.at[u, d, t - 1], section=other)

    def own_copy(w):
        return pltpu.make_async_copy(staged(w), whole_block(core, w), own.at[w])

    def own_cross(w):
        return remote(staged(w), whole_block(core, w), ms.at[n_small + w], mr.at[n_small + w], section=other)

    def start_own(u):
        layer, w = UNITS[u]

        if layer == 0:
            own_copy(w).wait()

        @pl.when(core != layer)
        def _():
            own_cross(w).wait_recv()

        for d in range(2):
            @pl.when(can_send(d, 1))
            def _():
                z_copy(u, d, 1).start()
                if STRIPS[w]:
                    t_copy(u, d, 1).start()

    def take_z(u, t):
        for d in range(2):
            @pl.when(gets(d, t))
            def _():
                z_copy(u, d, t).wait_recv()
            if t < n_z - 1:
                @pl.when(can_send(d, t + 1))
                def _():
                    z_copy(u, d, t + 1).start()
            @pl.when(gets(d, t))
            def _():
                x_copy(u, d, t).start()
                y_copy(u, d, t).start()
                if STRIPS[UNITS[u][1]]:
                    t_copy(u, d, t).wait_recv()
            if t < n_z - 1 and STRIPS[UNITS[u][1]]:
                @pl.when(can_send(d, t + 1))
                def _():
                    t_copy(u, d, t + 1).start()

    def take_xy(u, t):
        for d in range(2):
            @pl.when(gets(d, t))
            def _():
                x_copy(u, d, t).wait_recv()
                fy_copy(u, d, t).start()
                y_copy(u, d, t).wait_recv()
                fx_copy(u, d, t).start()

    def take_diagonal(u, t):
        for d in range(2):
            @pl.when(gets(d, t))
            def _():
                fy_copy(u, d, t).wait_recv()
                fx_copy(u, d, t).wait_recv()
                c_copy(u, d, t).start()

    def take_core(u):
        for d in range(2):
            for t in range(1, n_z):
                @pl.when(gets(d, t))
                def _():
                    c_copy(u, d, t).wait_recv()

    def f1_copy(gap):
        return remote(held_f1.at[z], f1_out.at[core, z], f1s.at[gap], f1r.at[gap], dp=lax.rem(z + gap, n_z))

    def launch(w):
        fetch[w].wait()
        own_copy(w).start()
        own_cross(w).start()

    launch(0)
    fetch[-1].wait()
    f1_sends = [f1_copy(gap) for gap in range(1, n_z)]
    for c in f1_sends:
        c.start()
    f1_own = pltpu.make_async_copy(held_f1.at[z], f1_out.at[core, z], own.at[n_w])
    f1_own.start()
    ends_to_x = remote(held_ends.at[1], x_out, es, er, section=other)
    ends_to_c = remote(held_ends.at[0], c_out, es, er, section=other)
    ends_x = pltpu.make_async_copy(held_ends.at[0], x_out, own.at[n_w + 1])
    ends_c = pltpu.make_async_copy(held_ends.at[1], c_out, own.at[n_w + 1])
    f1_cross = remote(f1_out.at[core], f1_out.at[core], f1c.at[0], f1c.at[1], section=other)
    start_own(0)
    launch(1)
    smalls = []

    def launch_rest():
        fetch[-2].wait()

        @pl.when(core == 0)
        def _():
            ends_to_x.start()
            ends_x.start()

        @pl.when(core == 1)
        def _():
            ends_to_c.start()
            ends_c.start()

        for i, (a, b) in enumerate(zip(held_small, small_out)):
            fetch[n_w + i].wait()
            mine = pltpu.make_async_copy(a, b.at[core], own.at[n_w + 2 + i])
            theirs = remote(a, b.at[core], ms.at[i], mr.at[i], section=other)
            mine.start()
            theirs.start()
            smalls.append((mine, theirs))
        for w in range(2, n_w):
            launch(w)
        f1_own.wait()
        for c in f1_sends:
            c.wait_recv()
        f1_cross.start()

    def settle_small():
        for mine, theirs in smalls:
            mine.wait()
            theirs.wait()
        for c in f1_sends:
            c.wait_send()
        f1_cross.wait()
        ends_x.wait()
        ends_to_x.wait()

    items = [(u, t) for u in range(len(UNITS)) for t in range(1, n_z)]
    ready, clock = [], 8.0
    for u, t in items:
        r, c = shards[UNITS[u][1]].shape[1:]
        clock += r // 4 * (c - 2 * STRIPS[UNITS[u][1]]) * 3 / LINK_BYTES_PER_US
        ready.append(clock)

    def gather_step(i):
        if i == 1:
            launch_rest()
        if i < len(items):
            u, t = items[i]
            if t == 1 and u + 1 < len(UNITS):
                start_own(u + 1)
            take_z(u, t)
        if 0 <= i - SKEW[0] < len(items):
            take_xy(*items[i - SKEW[0]])
        if 0 <= i - SKEW[1] < len(items):
            take_diagonal(*items[i - SKEW[1]])

    loc = Local(lsem)
    n_steps = len(items) + SKEW[1]
    works = [list(work), list(work)]
    for at, ref in ((4, qkv2), (5, gl2), (7, mix2)):
        works[1][at] = ref

    def both_layers():
        for layer in range(2):
            sources = dict(zip(NAMES[:4], outs))
            sources["f1"] = f1_out
            sources.update(zip(NAMES[5:], small_out))
            sources = {name: ref.at[layer] for name, ref in sources.items()}
            buffers = dict(zip(NAMES, held + [held_f1] + held_small))
            for what, us in forward_steps(
                layer, n_blocks, meta, loc, sources, buffers, works[layer], saved[layer], (ssem.at[layer], rsem.at[layer])
            ):
                yield layer, what, us
            if layer == 0:
                work[0][...] = work[1][...]

    steps, done, now, crossed, until = both_layers(), 0, 8.0, set(), None
    pending = next(steps)
    while pending is not None or done < n_steps:
        due = ready[min(max(done - 2, 0), len(ready) - 1)]
        blocked = False
        if pending is not None and pending[1] in NAMES[:4]:
            u = UNITS.index((pending[0], NAMES.index(pending[1])))
            blocked = done < min(3 * u + 3 + SKEW[1], n_steps)
            if not blocked:
                take_core(u)
                crossed.add(u)
                if pending[0] == 0:
                    own_cross(UNITS[u][1]).wait_send()
        elif pending is not None and pending[:2] == (0, "small"):
            blocked = done < 3
            if not blocked:
                settle_small()
                loc.start(x_out, work[0]).wait()
        elif pending is not None and pending[1] == "delay":
            until = now + pending[2] if until is None else until
            blocked = now < until and due < until
        if done < n_steps and (pending is None or blocked or due <= now):
            now = max(now, due)
            gather_step(done)
            done += 1
            continue
        now = now + pending[2] if until is None else max(now, until)
        until = None
        pending = next(steps, None)
    for u in range(len(UNITS)):
        if u not in crossed:
            take_core(u)
        for d in range(2):
            for t in range(1, n_z):
                @pl.when(can_send(d, t))
                def _():
                    z_copy(u, d, t).wait_send()
                    if STRIPS[UNITS[u][1]]:
                        t_copy(u, d, t).wait_send()
                @pl.when(gets(d, t))
                def _():
                    x_copy(u, d, t).wait_send()
                    y_copy(u, d, t).wait_send()
                    fx_copy(u, d, t).wait_send()
                    fy_copy(u, d, t).wait_send()
                    c_copy(u, d, t).wait_send()


def forward_model(meta, shards, f1t, ends, small):
    shape, dma, vm = jax.ShapeDtypeStruct, pltpu.SemaphoreType.DMA, pltpu.VMEM
    T = ends.shape[3]
    L = T * HEADS
    n_blocks = L // GROUP
    saved = saved_shapes(T, L, n_blocks)
    n_w, n_small, n_u = len(shards), len(small), len(UNITS)
    outs = [shape((2, 4 * w.shape[1], w.shape[2]), w.dtype) for w in shards]
    outs.append(shape((2, 4) + f1t.shape, f1t.dtype))
    outs += [shape(ends.shape[3:], ends.dtype)] * 2
    outs += [shape((2,) + a.shape[1:], a.dtype) for a in small]
    outs += [shape(*s) for s in saved] * 2
    full = [vm((4 * w.shape[1], w.shape[2]), w.dtype) for w in shards]
    out = pl.pallas_call(
        functools.partial(model_kernel, n_blocks),
        out_shape=outs,
        in_specs=[pl.BlockSpec(memory_space=pltpu.SMEM)] + [ANY] * (n_w + 2 + n_small),
        out_specs=[ANY] * len(outs),
        scratch_shapes=full
        + [vm((4,) + f1t.shape, f1t.dtype)]
        + [vm(a.shape[1:], a.dtype) for a in small]
        + work_scratch(T, L, saved)
        + [vm((L, CHUNK), BF), vm((HEADS, FGATE_RANK, T), BF), vm((HEADS, T, DV), BF), vm((2,) + ends.shape[3:], BF)]
        + [dma((n_w + n_small + 2,))]
        + [dma((n_u, 2, 3)) for _ in range(14)]
        + [dma((n_w + n_small + 2,)), dma((n_small + n_w,)), dma((n_small + n_w,)), dma, dma, dma((4,)), dma((4,)), dma((2,))]
        + [dma((1 + 2 * (len(NAMES) + len(saved)),)), dma((2, 3, HEADS)), dma((2, 3, HEADS))],
        compiler_params=pltpu.CompilerParams(collective_id=0, has_side_effects=True, vmem_limit_bytes=VMEM_LIMIT),
    )(meta, *shards, f1t, ends, *small)
    weights = list(out[:5]) + list(out[7:12])
    return weights, out[5], out[6], out[12 : 12 + len(saved)], out[12 + len(saved) :]


def swap_sections(v):
    return lax.ppermute(v, "section", [(0, 1), (1, 0)])


def plain_gather(shards, f1t, ends, small):
    first = lax.axis_index("section") == 0
    both = lambda a: lax.all_gather(a, "section", axis=0)
    outs = [both(lax.all_gather(w[0], "dp", axis=0, tiled=True)) for w in shards]
    low = lax.all_gather(f1t, "dp", axis=1, tiled=True)
    outs.append(both(jnp.stack(jnp.split(low, 4, axis=1))))
    sent = swap_sections(jnp.where(first, ends[0, 1, 0], ends[0, 0, 0]))
    outs.append(jnp.where(first, ends[0, 0, 0], sent))
    outs.append(jnp.where(first, sent, ends[0, 1, 0]))
    return outs + [both(a[0]) for a in small]


def spread(parts, chosen):
    hot = (chosen[:, None] == jnp.arange(ADAPTERS, dtype=jnp.int32)[None, :]).astype(F32)
    return sum(parts[n][:, None] * hot[n][None, :, None, None] for n in range(parts.shape[0]))


def reduce_kernel(
    gm0, gh0, gp0, gm1, gh1, gp1, entry, last_y, m_out, h_out, u_out, ends_out,
    vm_, vh, vp, rm, rh, rp, am, ah, em, eh, ends, ls, ss, rs, es, er, xl, xo, xs, xr,
):
    core, dp, me = lax.axis_index("section"), lax.axis_index("dp"), lax.axis_index("seq")
    n_dp = vp.shape[1]
    width = u_out.shape[1]
    loads = [
        pltpu.make_async_copy(a, b.at[l], ls.at[l, i])
        for l, three in enumerate(((gm0, gh0, gp0), (gm1, gh1, gp1)))
        for i, (a, b) in enumerate(zip(three, (vm_, vh, vp)))
    ]
    for c in loads:
        c.start()
    ends_in = [pltpu.make_async_copy(a, ends.at[i], xl.at[i]) for i, a in enumerate((entry, last_y))]
    for c in ends_in:
        c.start()
    barrier = pltpu.get_barrier_semaphore()
    places = [dict(section=1 - core)] + [dict(seq=me ^ k) for k in range(1, HEADS)]
    for gap in range(1, n_dp):
        to = lax.rem(dp + gap, n_dp)
        places += [dict(dp=to), dict(section=1 - core, dp=to)]
    for where in places:
        pl.semaphore_signal(barrier, inc=1, device_id=where, device_id_type=MESH)
    for c in loads:
        c.wait()
    pl.semaphore_wait(barrier, len(places))
    slot = dp * 2 + core
    size = 6 * ADAPTER_COLUMNS // n_dp

    def first_projection(i):
        return i * size // ADAPTER_COLUMNS

    def parts(layer, to):
        at = pl.ds(pl.multiple_of(first_projection(to) * ADAPTER_RANK, ADAPTER_RANK), 2 * ADAPTER_RANK)
        return ((vm_.at[layer, at], rm.at[slot]), (vh.at[layer], rh.at[slot]), (vp.at[layer, to], rp.at[slot]))

    copies = []
    for gap in range(n_dp - 1, -1, -1):
        to = lax.rem(dp + gap, n_dp)
        for crossing in (0, 1):
            if crossing == 0 and gap == 0:
                continue
            section = 1 - core if crossing else core
            for i, (a, b) in enumerate(parts(section, to)):
                c = pltpu.make_async_remote_copy(
                    src_ref=a, dst_ref=b, send_sem=ss.at[crossing, gap, i], recv_sem=rs.at[crossing, gap, i],
                    device_id=dict(section=section, dp=to), device_id_type=MESH,
                )
                c.start()
                copies.append(c)
    for c in ends_in:
        c.wait()
    ends_own = pltpu.make_async_copy(ends.at[core], ends_out.at[core], xo)
    ends_cross = pltpu.make_async_remote_copy(
        src_ref=ends.at[1 - core], dst_ref=ends_out.at[core], send_sem=xs, recv_sem=xr,
        device_id=dict(section=1 - core), device_id_type=MESH,
    )
    ends_own.start()
    ends_cross.start()
    at = pl.ds(pl.multiple_of(first_projection(dp) * ADAPTER_RANK, ADAPTER_RANK), 2 * ADAPTER_RANK)
    rm[slot] = vm_[core, at]
    rh[slot] = vh[core]
    rp[slot] = vp[core, dp]
    for c in copies:
        c.wait_recv()
    n = rm.shape[0]
    chosen = [rp[j, :, width : width + 1].astype(F32) for j in range(n)]
    for a in range(ADAPTERS):
        hot = [(c == float(a)).astype(F32) for c in chosen]
        at = slice(a * ADAPTER_RANK, (a + 1) * ADAPTER_RANK)

        def total(values):
            out = hot[0] * values(0).astype(F32)
            for j in range(1, n):
                out += hot[j] * values(j).astype(F32)
            return out

        for p in range(2):
            am[p * ADAPTER_COLUMNS + a * ADAPTER_RANK : p * ADAPTER_COLUMNS + (a + 1) * ADAPTER_RANK, :] = total(
                lambda j, p=p: rm[j, p * ADAPTER_RANK : (p + 1) * ADAPTER_RANK]
            )
        ah[at, :] = total(lambda j: rh[j])
        u_out[at, :] = total(lambda j: rp[j])[:, 0:width]
    own_m, own_h = size // HEADS, ADAPTER_COLUMNS // n_dp // HEADS
    base = dp * size - first_projection(dp) * ADAPTER_COLUMNS

    def m_rows(q):
        return am.at[pl.ds(pl.multiple_of(base + q * own_m, 16), own_m)]

    def h_rows(q):
        return ah.at[pl.ds(pl.multiple_of(dp * HEADS * own_h + q * own_h, 8), own_h)]

    last = []
    for k in range(1, HEADS):
        for i, (a, b) in enumerate(((m_rows(me ^ k), em.at[me]), (h_rows(me ^ k), eh.at[me]))):
            c = to_peer(a, b, es.at[i, k], er.at[i, k], me ^ k)
            c.start()
            last.append(c)
    em[me] = m_rows(me)[...]
    eh[me] = h_rows(me)[...]
    for c in last:
        c.wait_recv()
    for q in range(HEADS):
        m_out[:, q * em.shape[2] : (q + 1) * em.shape[2]] = em[q]
        start = q * eh.shape[2]
        wide = min(eh.shape[2], h_out.shape[1] - start)
        h_out[:, start : start + wide] = eh[q, :, 0:wide]
    for c in copies + last:
        c.wait_send()
    ends_own.wait()
    ends_cross.wait()


def reduce_gradients(early, late, entry, y, n_dp):
    gm, gh, gp = early
    n = 2 * n_dp
    width = (U_D + MODEL_WIDTH) // (n_dp * HEADS)
    own_m, own_h = 6 * ADAPTER_COLUMNS // (n_dp * HEADS), ADAPTER_COLUMNS // (n_dp * HEADS)
    vm, dma, VM = pltpu.VMEM, pltpu.SemaphoreType.DMA, pl.BlockSpec(memory_space=pltpu.VMEM)
    shape = jax.ShapeDtypeStruct
    model, hidden, up, ends = pl.pallas_call(
        reduce_kernel,
        out_shape=[
            shape((own_m, MODEL_WIDTH), F32),
            shape((own_h, VALUE_WIDTH + HIDDEN_UNITS), F32),
            shape((ADAPTER_COLUMNS, width), F32),
            shape((2,) + y.shape, y.dtype),
        ],
        in_specs=[ANY] * 8,
        out_specs=[VM] * 3 + [ANY],
        scratch_shapes=[
            vm((2,) + gm.shape, BF),
            vm((2,) + gh.shape, BF),
            vm((2,) + gp.shape, BF),
            vm((n, 2 * ADAPTER_RANK, gm.shape[1]), BF),
            vm((n,) + gh.shape, BF),
            vm((n,) + gp.shape[1:], BF),
            vm((2 * ADAPTER_COLUMNS, gm.shape[1]), F32),
            vm((ADAPTER_COLUMNS, gh.shape[1]), F32),
            vm((HEADS, own_m, gm.shape[1]), F32),
            vm((HEADS, own_h, gh.shape[1]), F32),
            vm((2,) + y.shape, y.dtype),
            dma((2, 3)),
            dma((2, n_dp, 3)),
            dma((2, n_dp, 3)),
            dma((2, HEADS)),
            dma((2, HEADS)),
            dma((2,)),
            dma,
            dma,
            dma,
        ],
        compiler_params=pltpu.CompilerParams(collective_id=5, has_side_effects=True, vmem_limit_bytes=VMEM_LIMIT),
    )(*early, *late, entry, y)
    return model.T, hidden.T, up, ends


def plain_reduce(early, late, n_dp):
    first = lax.axis_index("section") == 0
    dp = lax.axis_index("dp")
    kept = [jnp.where(first, a, b) for a, b in zip(early, late)]
    got = [swap_sections(jnp.where(first, b, a)) for a, b in zip(early, late)]
    gm, gh, gp = [jnp.stack(pair) for pair in zip(kept, got)]
    width = (U_D + MODEL_WIDTH) // (n_dp * HEADS)
    gm = lax.all_gather(gm, "dp", axis=0)
    gh = lax.all_gather(gh, "dp", axis=0)
    gp = lax.all_to_all(jnp.swapaxes(gp, 0, 1), "dp", split_axis=0, concat_axis=0, tiled=True)
    gp = gp.reshape(2 * n_dp, 1, ADAPTER_RANK, -1)
    n = gp.shape[0]
    chosen = gp[:, 0, 0, width].astype(jnp.int32)
    gm = spread(gm.reshape(n, 6, ADAPTER_RANK, -1).astype(F32), chosen).reshape(6 * ADAPTER_COLUMNS, -1)
    gh = spread(gh.reshape(n, 1, ADAPTER_RANK, -1).astype(F32), chosen).reshape(ADAPTER_COLUMNS, -1)
    gp = spread(gp.astype(F32), chosen).reshape(ADAPTER_COLUMNS, -1)

    def columns(v):
        size = v.shape[0] // n_dp
        v = lax.dynamic_slice_in_dim(v, dp * size, size, 0)
        return lax.all_to_all(v, "seq", split_axis=0, concat_axis=1, tiled=True).T

    return columns(gm), columns(gh)[: VALUE_WIDTH + HIDDEN_UNITS], gp[:, :width]


def local(
    ends,
    mixer_input_weight,
    forget_first_map,
    forget_second_map,
    forget_logit_bias,
    mixer_output_weight,
    feedforward_input_weight,
    feedforward_output_weight,
    adapter_model_first,
    adapter_hidden_first,
    adapter_second_maps,
    lengths,
    dealt_block_order,
    adapter_choice_per_seq,
):
    first = lax.axis_index("section") == 0
    told = jnp.concatenate([dealt_block_order[:, 0], adapter_choice_per_seq, lengths], axis=1)
    told = jnp.where(first, told[0], told[1])
    order = told[:-2]
    n_blocks = order.shape[0]
    at = jnp.arange(n_blocks, dtype=jnp.int32)
    inverse = jnp.sum(at[:, None] * (order[:, None] == at[None, :]).astype(jnp.int32), axis=0)
    meta = jnp.concatenate([order, inverse, told[-2:]])
    n_dp = lax.axis_size("dp")
    own_kernels = n_dp == 4 and lax.axis_size("seq") == 4
    shards = [mixer_input_weight, mixer_output_weight, feedforward_input_weight, feedforward_output_weight]
    small = [
        forget_second_map,
        forget_logit_bias[:, None],
        adapter_model_first,
        adapter_hidden_first,
        adapter_second_maps,
    ]
    if own_kernels:
        weights, x, cotangent, early, late = forward_model(meta, shards, forget_first_map[0].T, ends, small)
    else:
        out = plain_gather(shards, forget_first_map[0].T, ends, small)
        weights, x, cotangent = list(out[:5]) + list(out[7:]), out[5], out[6]
        early = forward(0, meta, x, weights)
        late = forward(1, meta, early[0], weights)
    entry, *grads = backward(meta, cotangent, x, early[0], weights, early[1:], late[1:], n_dp)
    grads_early, grads_late = grads[:3], grads[3:]
    if own_kernels:
        model, hidden, up, results = reduce_gradients(grads_early, grads_late, entry, late[0], n_dp)
    else:
        sent = swap_sections(jnp.where(first, late[0], entry))
        results = jnp.where(first, jnp.stack([entry, sent]), jnp.stack([sent, late[0]]))
        model, hidden, up = plain_reduce(grads_early, grads_late, n_dp)
    return (results[None, :, None], model[None], hidden[None], up[None])


def solution(mesh):
    return jax.shard_map(
        local,
        mesh=mesh,
        in_specs=(
            P("section", None, "dp", "seq", None),
            P("section", "dp", None),
            P("section", "dp", None),
            P("section", None, None),
            P("section", None),
            P("section", "dp", None),
            P("section", "dp", None),
            P("section", "dp", None),
            P("section", None, None),
            P("section", None, None),
            P("section", None, None),
            P(None, "dp"),
            P(None, "dp", None),
            P(None, "dp"),
        ),
        out_specs=(
            P("section", None, "dp", "seq", None),
            P("section", None, ("dp", "seq")),
            P("section", None, ("dp", "seq")),
            P("section", None, ("dp", "seq")),
        ),
        check_vma=False,
    )
```
